32 devices in a mesh: ens: 2 (over x), lon: 16 (over z, y, core).
Axes of the slice: x: 2, y: 2, z: 4, core: 2. Of those that a mesh axis runs over, the one named last changes fastest.
Arguments:
- tracer: float32 [32, 128, 512], P('ens', 'lon'), parts along dimension 0, may hold values from -6 to 6
- zonal_flow: float32 [32, 128, 512], P('ens', 'lon'), parts along dimension 0, may hold values from -10.8 to 10.8
- meridional_flow: float32 [32, 128, 512], P('ens', 'lon'), parts along dimension 0, may hold values from -10.8 to 10.8
- level_count: int32 [128, 512], P('lon'), may hold values from 0 to 16
- diffusivity: float32 [128, 512], P('lon'), may hold values from 0.02 to 0.2
- surface: float32 [128, 512], P('lon'), may hold values from 0.05 to 0.5
Outputs:
- tracer_next: float32 [32, 128, 512], P('ens', 'lon'), parts along dimension 0
- zonal_next: float32 [32, 128, 512], P('ens', 'lon'), parts along dimension 0
- meridional_next: float32 [32, 128, 512], P('ens', 'lon'), parts along dimension 0
- surface_height: float32 [128, 1024], P('lon', 'ens'), parts along dimension 1
The draws below stay inside these ranges and needn't reach their ends.
There are 2 independent parts, one for each index of `ens`. The reference program is written for one: setup_inputs(seed, part) draws one part's arguments, and reference() takes and returns one part's arrays. A program takes and returns all parts, laid end to end along the dimension named above; an argument that names none is the same for every part. Nothing has to cross between parts.
All inputs are finite; a program needn't handle non-finite values.
Results may differ from the reference program's by a relative error of at most 0.0001.
Values sent between devices are 32-bit elements; how exact they have to be, the bound alone decides.
No kernel may reach another device: no remote copies, remote signals or barrier semaphores. Data moves between devices by JAX's collectives and lax.ppermute only.
A program may use at most 64 MiB of HBM per device.

```python
import math
import jax
import jax.numpy as jnp

K = 16
NY = 512
ITERS = 6
NX = 128


def draw_zonal_flow(key, part):
    key = jax.random.fold_in(key, 11)
    position = (jnp.arange(NX, dtype=jnp.float32) + 0.5) / NX
    values = jnp.clip(jax.random.normal(key, (K, NX, NY), jnp.float32), -6.0, 6.0)
    spread = 0.6 + 1.2 * position
    values = values * spread[None, :, None]
    return values


def draw_meridional_flow(key, part):
    key = jax.random.fold_in(key, 12)
    position = (jnp.arange(NX, dtype=jnp.float32) + 0.5) / NX
    values = jnp.clip(jax.random.normal(key, (K, NX, NY), jnp.float32), -6.0, 6.0)
    spread = 0.6 + 1.2 * position
    values = values * spread[None, :, None]
    return values


def plant(entries, stream_key, low, largest):
    longest = entries.shape.index(max(entries.shape))
    spots = []
    for shift in (0, 1):
        where = [jax.random.randint(jax.random.fold_in(stream_key, axis), (), 0, length) for axis, length in enumerate(entries.shape)]
        where[longest] = (where[longest] + shift) % entries.shape[longest]
        spots.append(tuple(where))
    return entries.at[spots[0]].set(low).at[spots[1]].set(largest)


def steps_of(stream_key, shape, cuts, low, high):
    loudness = 1.0
    for dim, blocks in cuts:
        draws = jax.random.uniform(jax.random.fold_in(jax.random.fold_in(stream_key, 6), dim), (blocks,), jnp.float32, low / len(cuts), high / len(cuts))
        loudness = loudness * jnp.repeat(jnp.exp(draws), shape[dim] // blocks).reshape((-1,) + (1,) * (len(shape) - 1 - dim))
    return loudness


def normal_values(rng, dims, deviation, reach, cuts=(), kind=jnp.bfloat16):
    loudness = steps_of(rng, dims, cuts, -0.22, 0.18) if cuts else 1.0
    values = jax.random.normal(rng, dims, jnp.float32) * deviation * loudness
    return jnp.minimum(jnp.maximum(values, -reach), reach).astype(kind)


def setup_inputs(seed: int = 0, part: int = 0) -> dict:
    streams_of = jax.random.split(jax.random.key(seed), 7)
    own_keys = jax.random.split(jax.random.fold_in(streams_of[6], part), 7)
    return {
        "tracer": normal_values(own_keys[0], (K, NX, NY), 1.0, 6.0, ((1, 16),), jnp.float32),
        "zonal_flow": draw_zonal_flow(jax.random.fold_in(jax.random.fold_in(streams_of[6], part), 71), part),
        "meridional_flow": draw_meridional_flow(jax.random.fold_in(jax.random.fold_in(streams_of[6], part), 71), part),
        "level_count": plant(jax.random.randint(streams_of[3], (NX, NY), 0, K + 1), jax.random.fold_in(streams_of[3], 1), 0, K).astype(jnp.int32),
        "diffusivity": jnp.clip(jnp.exp(math.log(0.2) - 2.3025851 * jax.random.uniform(streams_of[4], (NX, NY), jnp.float32) ** steps_of(streams_of[4], (NX, NY), ((0, 16),), -0.2, 0.2)), 0.02, 0.2),
        "surface": jnp.clip(jnp.exp(math.log(0.5) - 2.3025851 * jax.random.uniform(streams_of[5], (NX, NY), jnp.float32) ** steps_of(streams_of[5], (NX, NY), ((0, 16),), -0.2, 0.2)), 0.05, 0.5),
    }


vertical_mix = 0.1
advection = 0.25
coriolis_scale = 0.3
gravity = 0.5
corner_weight = 0.25
center_base = 5.0


def pad_full(fields, sign_flip):
    north_row = jnp.flip(fields[:, :, :, NY - 1], 2) * sign_flip[:, None, None]
    south_row = jnp.zeros_like(north_row)
    rows_done = jnp.concatenate([south_row[..., None], fields, north_row[..., None]], axis=3)
    return jnp.concatenate([rows_done[:, :, -1:], rows_done, rows_done[:, :, :1]], axis=2)


def nine_point(padded, ocean_mask, surface):
    center_cells = padded[1:-1, 1:-1]
    edge_sum = padded[2:, 1:-1] + padded[:-2, 1:-1] + padded[1:-1, 2:] + padded[1:-1, :-2]
    corner_sum = padded[2:, 2:] + padded[2:, :-2] + padded[:-2, 2:] + padded[:-2, :-2]
    return ocean_mask * ((center_base + surface) * center_cells - edge_sum - corner_weight * corner_sum)


def baroclinic(padded, tracer, zonal_flow, meridional_flow, level_mask, diffusivity):
    center_cells = padded[:, :, 1:-1, 1:-1]
    east_side = padded[:, :, 2:, 1:-1]
    west_side = padded[:, :, :-2, 1:-1]
    north_side = padded[:, :, 1:-1, 2:]
    south_side = padded[:, :, 1:-1, :-2]
    edge_sum = east_side + west_side + north_side + south_side
    mask_sum = edge_sum[3]
    deeper = jnp.concatenate([center_cells[:, 1:], jnp.zeros_like(center_cells[:, :1])], axis=1)
    shallower = jnp.concatenate([jnp.zeros_like(center_cells[:, :1]), center_cells[:, :-1]], axis=1)
    vertical_term = deeper[0] + shallower[0] - (deeper[3] + shallower[3]) * tracer
    carried = zonal_flow * (east_side[0] - west_side[0]) + meridional_flow * (north_side[0] - south_side[0])
    tracer_next = level_mask * (tracer + diffusivity * (edge_sum[0] - mask_sum * tracer)
                                + vertical_mix * vertical_term - advection * carried)
    latitude = (jnp.arange(NY, dtype=jnp.float32) + 0.5) / NY
    planetary = coriolis_scale * (2.0 * latitude - 1.0)
    zonal_step = level_mask * (zonal_flow + diffusivity * (edge_sum[1] - mask_sum * zonal_flow)
                               + planetary * meridional_flow)
    meridional_step = level_mask * (meridional_flow + diffusivity * (edge_sum[2] - mask_sum * meridional_flow)
                                    - planetary * zonal_flow)
    return tracer_next, zonal_step, meridional_step


def column_sum(zonal_step, meridional_step):
    thickness = 0.5 * (0.5 + jnp.arange(K, dtype=jnp.float32) / K)
    return jnp.sum(thickness[:, None, None] * (zonal_step + meridional_step), axis=0)


def operate(direction, ocean_mask, surface):
    padded = pad_full(direction[None, None], jnp.ones((1,), jnp.float32))[0, 0]
    return nine_point(padded, ocean_mask, surface)


def reference(tracer, zonal_flow, meridional_flow, level_count, diffusivity, surface):
    levels = jnp.arange(K, dtype=jnp.int32)[:, None, None]
    level_mask = (levels < level_count[None]).astype(jnp.float32)
    stacked = jnp.stack([level_mask * tracer, level_mask * zonal_flow, level_mask * meridional_flow, level_mask])
    padded = pad_full(stacked, jnp.array([1.0, -1.0, -1.0, 1.0], jnp.float32))
    tracer_next, zonal_step, meridional_step = baroclinic(padded, tracer, zonal_flow, meridional_flow,
                                                          level_mask, diffusivity)
    forcing = column_sum(zonal_step, meridional_step)
    ocean_mask = level_mask[0]
    solution = jnp.zeros_like(forcing)
    residual = forcing
    direction = forcing
    norm_now = jnp.sum(residual * residual)
    for iteration in range(ITERS):
        applied = operate(direction, ocean_mask, surface)
        step_size = norm_now / jnp.sum(direction * applied)
        solution = solution + step_size * direction
        residual = residual - step_size * applied
        if iteration + 1 < ITERS:
            norm_next = jnp.sum(residual * residual)
            direction = residual + (norm_next / norm_now) * direction
            norm_now = norm_next
    height_padded = pad_full(solution[None, None], jnp.ones((1,), jnp.float32))[0, 0]
    east_height = height_padded[2:, 1:-1]
    north_height = height_padded[1:-1, 2:]
    zonal_next = level_mask * (zonal_step - gravity * (east_height - solution)[None])
    meridional_next = level_mask * (meridional_step - gravity * (north_height - solution)[None])
    return tracer_next, zonal_next, meridional_next, solution
```

```python
import functools

import jax
import jax.numpy as jnp
from jax import lax
from jax.experimental import pallas as pl
from jax.experimental.pallas import tpu as pltpu
from jax.sharding import PartitionSpec as P

K = 16
NY = 512
ITERS = 6
COLS = 8
EXT = 3 * COLS
LANES = 128
PACK = 80
BASIS = ITERS + 1

vertical_mix = 0.1
advection = 0.25
coriolis_scale = 0.3
gravity = 0.5
corner_weight = 0.25
shift = 5.0
scale = 4.0
LANE_P = 16
LANE_LC = 32
LANE_DIFF = 33
LANE_MT = 40
LANE_MU = 56
LANE_MV = 72

f32 = jnp.float32


def iota(shape, dim):
    return lax.broadcasted_iota(jnp.int32, shape, dim)


def thickness(k):
    return 0.5 * (0.5 + k / K)


def planetary(shape):
    latitude = (iota(shape, 1).astype(f32) + 0.5) / NY
    return coriolis_scale * (2.0 * latitude - 1.0)


def roll(value, amount, axis):
    return pltpu.roll(value, amount % value.shape[axis], axis)


def level_sum(value):
    weight = 0.5 * (0.5 + iota(value.shape, 0).astype(f32) / K)
    return jnp.sum(weight * value, axis=0, keepdims=True)


def two_sum(a, b):
    s = a + b
    t = s - a
    return s, (a - (s - t)) + (b - t)


def fast_two_sum(a, b):
    s = a + b
    return s, b - (s - a)


def split(a):
    c = 4097.0 * a
    high = c - (c - a)
    return high, a - high


def two_prod(a, b, a_parts=None, b_parts=None):
    ah, al = split(a) if a_parts is None else a_parts
    bh, bl = split(b) if b_parts is None else b_parts
    p = a * b
    return p, ((ah * bh - p) + ah * bl + al * bh) + al * bl


def pair_mul(a, b):
    p, e = two_prod(a[0], b[0])
    return p, e + (a[0] * b[1] + a[1] * b[0])


def pair_add(a, b):
    s, e = two_sum(a[0], b[0])
    return s, e + (a[1] + b[1])


def pair_norm(a):
    return fast_two_sum(a[0], a[1])


def pair_scale(a, factor):
    p, e = two_prod(a[0], factor)
    return p, e + a[1] * factor


def pair_tree(terms):
    while len(terms) > 1:
        pairs = [pair_add(terms[i], terms[i + 1]) for i in range(0, len(terms) - 1, 2)]
        terms = pairs + terms[len(terms) - len(terms) % 2:]
    return terms[0]


def pair_rows(a):
    for step in (4, 2, 1):
        a = pair_add(a, (roll(a[0], step, 0), roll(a[1], step, 0)))
    return a


def pack_kernel(tracer, zonal, meridional, count, diffusivity, surface, inner, outer):
    shape = (COLS, NY)
    even = lax.axis_index("lon") % 2 == 0
    lc = count[...].astype(f32)
    diff = diffusivity[...]
    row, lane = iota(shape, 0), iota(shape, 1)
    tile_lane = iota((COLS, LANES), 1)
    total = jnp.zeros(shape, f32)
    turn = jnp.zeros(shape, f32)
    flux_x = jnp.zeros(shape, f32)
    flux_y = jnp.zeros(shape, f32)
    fold = jnp.zeros((COLS, LANES), f32)

    def put(tile, at, column):
        return jnp.where(tile_lane == at, column, tile)

    for k in range(K):
        mask = (lc > k).astype(f32)
        u, v = zonal[k], meridional[k]
        mt, mu, mv = mask * tracer[k], mask * u, mask * v
        p = mu + mv
        total += thickness(k) * p
        turn += thickness(k) * (mv - mu)
        flux_x += thickness(k) * (mask * roll(p, -1, 0) - roll(mask, -1, 0) * p)
        flux_y += thickness(k) * (mask * roll(p, -1, 1) - roll(mask, -1, 1) * p)
        fold = put(fold, LANE_P + k, p[:, NY - 1:])
        for base, field in ((0, mt), (1, mu), (2, mv)):
            west, east = field[:1], field[COLS - 1:]
            at = 2 * COLS + base * K + k
            inner[at:at + 1] = jnp.where(even, east, west)
            outer[at:at + 1] = jnp.where(even, west, east)
            fold = put(fold, LANE_MT + base * K + k, field[:, NY - 1:])
    fold = put(fold, LANE_LC, lc[:, NY - 1:])
    fold = put(fold, LANE_DIFF, diff[:, NY - 1:])
    flux_x = jnp.where(row == COLS - 1, 0.0, flux_x)
    flux_y = jnp.where(lane == NY - 1, 0.0, flux_y)
    west_flux = jnp.where(row == 0, 0.0, roll(flux_x, 1, 0))
    south_flux = jnp.where(lane == 0, 0.0, roll(flux_y, 1, 1))
    forcing = total + planetary(shape) * turn + diff * (
        flux_x - west_flux + flux_y - south_flux
    )
    coded = jnp.where(lc > 0, surface[...], -1.0)
    zeros = jnp.zeros((COLS, NY - LANES), f32)
    for pack, mine, other in ((inner, COLS - 1, 0), (outer, 0, COLS - 1)):
        pack[0:COLS] = forcing
        pack[COLS:2 * COLS] = coded
        edge_lc = jnp.where(even, lc[mine:mine + 1], lc[other:other + 1])
        edge_diff = jnp.where(even, diff[mine:mine + 1], diff[other:other + 1])
        pack[64:72] = jnp.where(row == 0, edge_lc, jnp.where(row == 1, edge_diff, 0.0))
        pack[72:80] = jnp.concatenate([fold, zeros], axis=1)


def interface_flux(mine, theirs):
    level = iota((K, NY), 0).astype(f32)
    p_mine = mine[32:48] + mine[48:64]
    p_theirs = theirs[32:48] + theirs[48:64]
    return level_sum(
        jnp.where(level < mine[64:65], p_theirs, 0.0)
        - jnp.where(level < theirs[64:65], p_mine, 0.0)
    )


def halo_kernel(inner, outer, sibling, beyond, forcing, coded, tile, flipped):
    shape = (EXT, NY)
    even = lax.axis_index("lon") % 2 == 0
    flux_in = interface_flux(inner, sibling)
    flux_out = interface_flux(outer, beyond)
    row = iota(shape, 0)

    def arrange(at):
        own = inner[at:at + COLS]
        east, west = sibling[at:at + COLS], beyond[at:at + COLS]
        first = jnp.where(even, west, east)
        last = jnp.where(even, east, west)
        return jnp.concatenate([first, own, last], axis=0)

    def choose(a, b):
        return jnp.where(even, a, b)

    west_own = choose(outer[65:66] * flux_out, inner[65:66] * flux_in)
    west_far = choose(beyond[65:66] * flux_out, sibling[65:66] * flux_in)
    east_own = choose(inner[65:66] * flux_in, outer[65:66] * flux_out)
    east_far = choose(sibling[65:66] * flux_in, beyond[65:66] * flux_out)
    change = jnp.where(
        row == COLS - 1,
        -west_far,
        jnp.where(
            row == COLS,
            west_own,
            jnp.where(row == 2 * COLS - 1, east_own, jnp.where(row == 2 * COLS, -east_far, 0.0)),
        ),
    )
    full = arrange(0) + change
    code = arrange(COLS)
    forcing[...] = full
    coded[...] = code
    lane = iota((EXT, LANES), 1)
    fold = arrange(72)[:, :LANES]
    for j in range(COLS):
        at = NY - 1 - j
        fold = jnp.where(lane == j, full[:, at:at + 1], fold)
        fold = jnp.where(lane == COLS + j, code[:, at:at + 1], fold)
    tile[...] = fold
    flipped[...] = jnp.concatenate([fold[EXT - 1 - i:EXT - i] for i in range(EXT)], axis=0)


def basis_kernel(forcing, coded, tile, mirror, vectors, gram):
    width = NY + LANES
    lane = iota((EXT, LANES), 1)
    mine, theirs = tile[...], mirror[...]
    level = (lane - LANE_P).astype(f32)
    weight = jnp.where((lane >= LANE_P) & (lane < LANE_P + K), 0.5 * (0.5 + level / K), 0.0)
    mask_mine = (level < mine[:, LANE_LC:LANE_LC + 1]).astype(f32)
    mask_theirs = (level < theirs[:, LANE_LC:LANE_LC + 1]).astype(f32)
    flux = -jnp.sum(weight * (mask_mine * theirs + mask_theirs * mine), axis=1, keepdims=True)
    own_change = mine[:, LANE_DIFF:LANE_DIFF + 1] * flux
    far_change = theirs[:, LANE_DIFF:LANE_DIFF + 1] * flux
    north = jnp.where(lane < COLS, theirs, 0.0)
    north = north + jnp.where(lane == 0, far_change, 0.0)
    body_lane = iota((EXT, NY), 1)
    south = forcing[...] + jnp.where(body_lane == NY - 1, own_change, 0.0)
    north_code = jnp.where(lane < COLS, roll(theirs, -COLS, 1), -1.0)
    code = jnp.concatenate([coded[...], north_code], axis=1)
    ocean = code > 0
    centre = jnp.where(ocean, code / scale, 0.0)
    around = jnp.where(ocean, 1.0 / scale, 0.0)
    wide_lane = iota((EXT, width), 1)

    def operate(q):
        along = roll(q, -1, 1) + jnp.where(wide_lane == 0, 0.0, roll(q, 1, 1))
        beside = q + corner_weight * along
        return centre * q - around * (along + roll(beside, 1, 0) + roll(beside, -1, 0))

    v = [jnp.concatenate([south, north], axis=1)]
    v.append(operate(v[0]))
    for j in range(2, BASIS):
        v.append(2.0 * operate(v[-1]) - v[-2])
    for j in range(ITERS):
        vectors[j * EXT:(j + 1) * EXT] = v[j]
    own = [[q[COLS:2 * COLS, c * LANES:(c + 1) * LANES] for c in range(NY // LANES)] for q in v]
    parts = [[split(q) for q in row] for row in own]
    sub = iota((COLS, LANES), 0)
    tile_lane = iota((COLS, LANES), 1)
    sums = {}
    for i in range(BASIS):
        for j in range(i, BASIS):
            terms = [
                two_prod(own[i][c], own[j][c], parts[i][c], parts[j][c])
                for c in range(NY // LANES)
            ]
            sums[i, j] = sums[j, i] = pair_rows(pair_tree(terms))
    out = jnp.zeros((COLS, LANES), f32)
    for i in range(BASIS):
        column = (jnp.zeros((COLS, LANES), f32), jnp.zeros((COLS, LANES), f32))
        for j in range(BASIS):
            column = tuple(jnp.where(sub == j, s, c) for s, c in zip(sums[i, j], column))
        step = LANES // 2
        while step:
            column = pair_add(column, (roll(column[0], step, 1), roll(column[1], step, 1)))
            step //= 2
        column = pair_norm(column)
        out = jnp.where(tile_lane == i, column[0], out)
        out = jnp.where(tile_lane == LANES // 2 + i, column[1], out)
    gram[...] = out


def coefficients(gram):
    shape = (COLS, LANES)
    tiles = [gram[i * COLS:(i + 1) * COLS] for i in range(gram.shape[0] // COLS)]
    total = pair_norm(pair_tree([(t, roll(t, LANES // 2, 1)) for t in tiles]))
    wide = lambda column: jnp.broadcast_to(column, shape)
    matrix = [tuple(wide(part[:, j:j + 1]) for part in total) for j in range(BASIS)]
    sub = iota(shape, 0)
    first = (sub == 0).astype(f32)
    zero = jnp.zeros(shape, f32)

    def apply(b):
        half = scale / 2
        up = [half * jnp.where(sub == 0, 0.0, roll(part, 1, 0)) for part in b]
        up = [jnp.where(sub == 1, 2.0 * part, part) for part in up]
        down = [half * jnp.where(sub == COLS - 1, 0.0, roll(part, -1, 0)) for part in b]
        four = tuple(4.0 * part for part in b)
        return pair_norm(pair_add(pair_add(four, b), pair_add(tuple(up), tuple(down))))

    def times(vector, count):
        terms = []
        for j in range(count):
            at = tuple(wide(part[j:j + 1]) for part in vector)
            terms.append(pair_mul(matrix[j], at))
        return pair_norm(pair_tree(terms))

    def dot(a, b):
        s = pair_rows(pair_mul(a, b))
        return s[0] + s[1]

    residual = (first, zero)
    image = matrix[0]
    direction = residual
    solution = zero
    norm_now = wide(matrix[0][0][:1])
    floor = 1e-13 * norm_now
    alive = norm_now > 0
    for iteration in range(ITERS):
        applied = apply(direction)
        applied_image = times(applied, iteration + 2)
        curvature = dot(direction, applied_image)
        alive = alive & (curvature > 0)
        step = jnp.where(alive, norm_now / jnp.where(alive, curvature, 1.0), 0.0)
        solution = solution + step * direction[0]
        if iteration + 1 < ITERS:
            back = -step
            residual = pair_norm(pair_add(residual, pair_scale(applied, back)))
            image = pair_norm(pair_add(image, pair_scale(applied_image, back)))
            norm_next = dot(residual, image)
            ratio = jnp.where(alive, norm_next / jnp.where(alive, norm_now, 1.0), 0.0)
            direction = pair_norm(pair_add(residual, pair_scale(direction, ratio)))
            norm_now = norm_next
            alive = alive & (norm_now > floor)
    return solution


def finish_kernel(gram, vectors, zonal, meridional, count, zonal_next, meridional_next, height):
    x = coefficients(gram)
    total = jnp.zeros((EXT, NY + LANES), f32)
    for j in range(ITERS):
        total += x[j:j + 1, :1] * vectors[j * EXT:(j + 1) * EXT]
    own = total[COLS:2 * COLS, :NY]
    height[...] = own
    east = gravity * (roll(total, -1, 0)[COLS:2 * COLS, :NY] - own)
    north = gravity * (roll(total, -1, 1)[COLS:2 * COLS, :NY] - own)
    lc = count[...]
    for k in range(K):
        zonal_next[k] = zonal[k] - jnp.where(lc > k, east, 0.0)
        meridional_next[k] = meridional[k] - jnp.where(lc > k, north, 0.0)


def step_kernel(
    tracer, zonal, meridional, count, diffusivity, sibling, beyond, mirror,
    tracer_next, zonal_step, meridional_step,
):
    shape = (COLS, NY)
    even = lax.axis_index("lon") % 2 == 0
    row, lane = iota(shape, 0), iota(shape, 1)
    lc = count[...].astype(f32)
    diff = diffusivity[...]
    turn = planetary(shape)
    north_tile = mirror[COLS:2 * COLS]
    sib_lc, out_lc = sibling[64:65], beyond[64:65]
    west_lc, east_lc = jnp.where(even, out_lc, sib_lc), jnp.where(even, sib_lc, out_lc)
    north_lc = north_tile[:, LANE_LC:LANE_LC + 1]

    def around(field, west, east, north):
        return (
            jnp.where(row == COLS - 1, east, roll(field, -1, 0)),
            jnp.where(row == 0, west, roll(field, 1, 0)),
            jnp.where(lane == NY - 1, north, roll(field, -1, 1)),
            jnp.where(lane == 0, 0.0, roll(field, 1, 1)),
        )

    def edges(base, k):
        at = 2 * COLS + base * K + k
        a, b = sibling[at:at + 1], beyond[at:at + 1]
        return jnp.where(even, b, a), jnp.where(even, a, b)

    def masked(k):
        if k < 0 or k >= K:
            return jnp.zeros(shape, f32), jnp.zeros(shape, f32)
        mask = (lc > k).astype(f32)
        return mask, mask * tracer[k]

    below, here = masked(-1), masked(0)
    for k in range(K):
        above = masked(k + 1)
        mask, mt = here
        t, u, v = tracer[k], zonal[k], meridional[k]
        mask_sum = sum(
            around(
                mask,
                (west_lc > k).astype(f32),
                (east_lc > k).astype(f32),
                (north_lc > k).astype(f32),
            )
        )
        fields = []
        for base, field, sign in ((0, mt, 1.0), (1, mask * u, -1.0), (2, mask * v, -1.0)):
            at = LANE_MT + base * K + k
            fields.append(around(field, *edges(base, k), sign * north_tile[:, at:at + 1]))
        te, tw, tn, ts = fields[0]
        vertical = above[1] + below[1] - (above[0] + below[0]) * t
        tracer_next[k] = mask * (
            t
            + diff * (te + tw + tn + ts - mask_sum * t)
            + vertical_mix * vertical
            - advection * (u * (te - tw) + v * (tn - ts))
        )
        zonal_step[k] = mask * (u + diff * (sum(fields[1]) - mask_sum * u) + turn * v)
        meridional_step[k] = mask * (v + diff * (sum(fields[2]) - mask_sum * v) - turn * u)
        below, here = here, above


def call(kernel, shapes, *args, flops=0):
    moved = 4 * sum(a.size for a in args) + 4 * sum(
        functools.reduce(lambda x, y: x * y, s, 1) for s in shapes
    )
    space = pl.BlockSpec(memory_space=pltpu.VMEM)
    return pl.pallas_call(
        kernel,
        out_shape=[jax.ShapeDtypeStruct(s, f32) for s in shapes],
        in_specs=[space] * len(args),
        out_specs=[space] * len(shapes),
        compiler_params=pltpu.CompilerParams(vmem_limit_bytes=32 * 1024 * 1024),
        cost_estimate=pl.CostEstimate(flops=flops, bytes_accessed=moved, transcendentals=0),
    )(*args)


def body(tracer, zonal, meridional, count, diffusivity, surface):
    size = lax.axis_size("lon")
    block = (K, COLS, NY)

    def permute(value, pairs):
        return lax.ppermute(value, "lon", pairs)

    siblings = [(i, i ^ 1) for i in range(size)]
    outward = [(i, (i + 1 if i % 2 else i - 1) % size) for i in range(size)]
    mirrored = [(i, size - 1 - i) for i in range(size)]
    inner, outer = call(
        pack_kernel, [(PACK, NY)] * 2, tracer, zonal, meridional, count, diffusivity, surface
    )
    beyond = permute(outer, outward)
    sibling = permute(inner, siblings)
    forcing, coded, tile, flipped = call(
        halo_kernel,
        [(EXT, NY), (EXT, NY), (EXT, LANES), (EXT, LANES)],
        inner, outer, sibling, beyond,
    )
    mirror = permute(flipped, mirrored)
    vectors, gram = call(
        basis_kernel,
        [(ITERS * EXT, NY + LANES), (COLS, LANES)],
        forcing, coded, tile, mirror,
    )
    tracer_next, zonal_step, meridional_step = call(
        step_kernel, [block] * 3,
        tracer, zonal, meridional, count, diffusivity, sibling, beyond, mirror,
        flops=65536 * 80,
    )
    reach = 1
    while reach < size:
        across = reach ^ 1 if reach > 1 else 1
        gram = jnp.concatenate(
            [gram, permute(gram, [(i, i ^ across) for i in range(size)])], axis=0
        )
        reach *= 2
    zonal_next, meridional_next, height = call(
        finish_kernel, [block, block, (COLS, NY)],
        gram, vectors, zonal_step, meridional_step, count,
    )
    return tracer_next, zonal_next, meridional_next, height


def solution(mesh):
    column = P("lon", None)
    field = P("ens", "lon", None)
    return jax.shard_map(
        body,
        mesh=mesh,
        in_specs=(field, field, field, column, column, column),
        out_specs=(field, field, field, P("lon", "ens")),
        check_vma=False,
    )
```

```python
import functools

import jax
import jax.numpy as jnp
from jax import lax
from jax.experimental import pallas as pl
from jax.experimental.pallas import tpu as pltpu
from jax.sharding import PartitionSpec as P

K = 16
NY = 512
ITERS = 6
COLS = 8
EXT = 3 * COLS
LANES = 128
PACK = 80
BASIS = ITERS + 1
CHUNKS = 4

vertical_mix = 0.1
advection = 0.25
coriolis_scale = 0.3
gravity = 0.5
corner_weight = 0.25
shift = 5.0
scale = 4.0
LANE_P = 16
LANE_LC = 32
LANE_DIFF = 33
LANE_MT = 40
LANE_MU = 56
LANE_MV = 72

f32 = jnp.float32


def iota(shape, dim):
    return lax.broadcasted_iota(jnp.int32, shape, dim)


def thickness(k):
    return 0.5 * (0.5 + k / K)


def planetary(shape):
    latitude = (iota(shape, 1).astype(f32) + 0.5) / NY
    return coriolis_scale * (2.0 * latitude - 1.0)


def roll(value, amount, axis):
    return pltpu.roll(value, amount % value.shape[axis], axis)


def level_sum(value):
    weight = 0.5 * (0.5 + iota(value.shape, 0).astype(f32) / K)
    return jnp.sum(weight * value, axis=0, keepdims=True)


def two_sum(a, b):
    s = a + b
    t = s - a
    return s, (a - (s - t)) + (b - t)


def fast_two_sum(a, b):
    s = a + b
    return s, b - (s - a)


def split(a):
    c = 4097.0 * a
    high = c - (c - a)
    return high, a - high


def two_prod(a, b, a_parts=None, b_parts=None):
    ah, al = split(a) if a_parts is None else a_parts
    bh, bl = split(b) if b_parts is None else b_parts
    p = a * b
    return p, ((ah * bh - p) + ah * bl + al * bh) + al * bl


def pair_mul(a, b):
    p, e = two_prod(a[0], b[0])
    return p, e + (a[0] * b[1] + a[1] * b[0])


def pair_add(a, b):
    s, e = two_sum(a[0], b[0])
    return s, e + (a[1] + b[1])


def pair_norm(a):
    return fast_two_sum(a[0], a[1])


def pair_scale(a, factor):
    p, e = two_prod(a[0], factor)
    return p, e + a[1] * factor


def pair_tree(terms):
    while len(terms) > 1:
        pairs = [pair_add(terms[i], terms[i + 1]) for i in range(0, len(terms) - 1, 2)]
        terms = pairs + terms[len(terms) - len(terms) % 2:]
    return terms[0]


def pair_rows(a):
    for step in (4, 2, 1):
        a = pair_add(a, (roll(a[0], step, 0), roll(a[1], step, 0)))
    return a


def pack_kernel(
    tracer_in, zonal_in, meridional_in, count_in, diffusivity_in, surface_in, inner, outer,
    tracer, zonal, meridional, count, diffusivity, surface, sems,
):
    shape = (COLS, NY)
    even = lax.axis_index("lon") % 2 == 0
    small = [
        pltpu.make_async_copy(a, b, sems.at[i])
        for i, (a, b) in enumerate(
            ((count_in, count), (diffusivity_in, diffusivity), (surface_in, surface))
        )
    ]
    large = []
    for c in range(CHUNKS):
        part = pl.ds(c * K // CHUNKS, K // CHUNKS)
        large.append(
            [
                pltpu.make_async_copy(a.at[part], b.at[part], sems.at[3 + 3 * c + i])
                for i, (a, b) in enumerate(
                    ((zonal_in, zonal), (meridional_in, meridional), (tracer_in, tracer))
                )
            ]
        )
    for copy in small + sum(large, []):
        copy.start()
    for copy in small:
        copy.wait()
    lc = count[...].astype(f32)
    diff = diffusivity[...]
    row, lane = iota(shape, 0), iota(shape, 1)
    tile_lane = iota((COLS, LANES), 1)
    total = jnp.zeros(shape, f32)
    turn = jnp.zeros(shape, f32)
    flux_x = jnp.zeros(shape, f32)
    flux_y = jnp.zeros(shape, f32)
    fold = jnp.zeros((COLS, LANES), f32)

    def put(tile, at, column):
        return jnp.where(tile_lane == at, column, tile)

    for k in range(K):
        if k % (K // CHUNKS) == 0:
            for copy in large[k // (K // CHUNKS)]:
                copy.wait()
        mask = (lc > k).astype(f32)
        u, v = zonal[k], meridional[k]
        mt, mu, mv = mask * tracer[k], mask * u, mask * v
        p = mu + mv
        total += thickness(k) * p
        turn += thickness(k) * (mv - mu)
        flux_x += thickness(k) * (mask * roll(p, -1, 0) - roll(mask, -1, 0) * p)
        flux_y += thickness(k) * (mask * roll(p, -1, 1) - roll(mask, -1, 1) * p)
        fold = put(fold, LANE_P + k, p[:, NY - 1:])
        for base, field in ((0, mt), (1, mu), (2, mv)):
            west, east = field[:1], field[COLS - 1:]
            at = 2 * COLS + base * K + k
            inner[at:at + 1] = jnp.where(even, east, west)
            outer[at:at + 1] = jnp.where(even, west, east)
            fold = put(fold, LANE_MT + base * K + k, field[:, NY - 1:])
    fold = put(fold, LANE_LC, lc[:, NY - 1:])
    fold = put(fold, LANE_DIFF, diff[:, NY - 1:])
    flux_x = jnp.where(row == COLS - 1, 0.0, flux_x)
    flux_y = jnp.where(lane == NY - 1, 0.0, flux_y)
    west_flux = jnp.where(row == 0, 0.0, roll(flux_x, 1, 0))
    south_flux = jnp.where(lane == 0, 0.0, roll(flux_y, 1, 1))
    forcing = total + planetary(shape) * turn + diff * (
        flux_x - west_flux + flux_y - south_flux
    )
    coded = jnp.where(lc > 0, surface[...], -1.0)
    zeros = jnp.zeros((COLS, NY - LANES), f32)
    for pack, mine, other in ((inner, COLS - 1, 0), (outer, 0, COLS - 1)):
        pack[0:COLS] = forcing
        pack[COLS:2 * COLS] = coded
        edge_lc = jnp.where(even, lc[mine:mine + 1], lc[other:other + 1])
        edge_diff = jnp.where(even, diff[mine:mine + 1], diff[other:other + 1])
        pack[64:72] = jnp.where(row == 0, edge_lc, jnp.where(row == 1, edge_diff, 0.0))
        pack[72:80] = jnp.concatenate([fold, zeros], axis=1)


def interface_flux(mine, theirs):
    level = iota((K, NY), 0).astype(f32)
    p_mine = mine[32:48] + mine[48:64]
    p_theirs = theirs[32:48] + theirs[48:64]
    return level_sum(
        jnp.where(level < mine[64:65], p_theirs, 0.0)
        - jnp.where(level < theirs[64:65], p_mine, 0.0)
    )


def halo_kernel(inner, outer, sibling, beyond, forcing, coded, tile, flipped):
    shape = (EXT, NY)
    even = lax.axis_index("lon") % 2 == 0
    flux_in = interface_flux(inner, sibling)
    flux_out = interface_flux(outer, beyond)
    row = iota(shape, 0)

    def arrange(at):
        own = inner[at:at + COLS]
        east, west = sibling[at:at + COLS], beyond[at:at + COLS]
        first = jnp.where(even, west, east)
        last = jnp.where(even, east, west)
        return jnp.concatenate([first, own, last], axis=0)

    def choose(a, b):
        return jnp.where(even, a, b)

    west_own = choose(outer[65:66] * flux_out, inner[65:66] * flux_in)
    west_far = choose(beyond[65:66] * flux_out, sibling[65:66] * flux_in)
    east_own = choose(inner[65:66] * flux_in, outer[65:66] * flux_out)
    east_far = choose(sibling[65:66] * flux_in, beyond[65:66] * flux_out)
    change = jnp.where(
        row == COLS - 1,
        -west_far,
        jnp.where(
            row == COLS,
            west_own,
            jnp.where(row == 2 * COLS - 1, east_own, jnp.where(row == 2 * COLS, -east_far, 0.0)),
        ),
    )
    full = arrange(0) + change
    code = arrange(COLS)
    forcing[...] = full
    coded[...] = code
    lane = iota((EXT, LANES), 1)
    fold = arrange(72)[:, :LANES]
    for j in range(COLS):
        at = NY - 1 - j
        fold = jnp.where(lane == j, full[:, at:at + 1], fold)
        fold = jnp.where(lane == COLS + j, code[:, at:at + 1], fold)
    tile[...] = fold
    flipped[...] = jnp.concatenate([fold[EXT - 1 - i:EXT - i] for i in range(EXT)], axis=0)


def basis_kernel(forcing, coded, tile, mirror, vectors, gram):
    width = NY + LANES
    lane = iota((EXT, LANES), 1)
    mine, theirs = tile[...], mirror[...]
    level = (lane - LANE_P).astype(f32)
    weight = jnp.where((lane >= LANE_P) & (lane < LANE_P + K), 0.5 * (0.5 + level / K), 0.0)
    mask_mine = (level < mine[:, LANE_LC:LANE_LC + 1]).astype(f32)
    mask_theirs = (level < theirs[:, LANE_LC:LANE_LC + 1]).astype(f32)
    flux = -jnp.sum(weight * (mask_mine * theirs + mask_theirs * mine), axis=1, keepdims=True)
    own_change = mine[:, LANE_DIFF:LANE_DIFF + 1] * flux
    far_change = theirs[:, LANE_DIFF:LANE_DIFF + 1] * flux
    north = jnp.where(lane < COLS, theirs, 0.0)
    north = north + jnp.where(lane == 0, far_change, 0.0)
    body_lane = iota((EXT, NY), 1)
    south = forcing[...] + jnp.where(body_lane == NY - 1, own_change, 0.0)
    north_code = jnp.where(lane < COLS, roll(theirs, -COLS, 1), -1.0)
    code = jnp.concatenate([coded[...], north_code], axis=1)
    ocean = code > 0
    centre = jnp.where(ocean, code / scale, 0.0)
    around = jnp.where(ocean, 1.0 / scale, 0.0)
    wide_lane = iota((EXT, width), 1)

    def operate(q):
        along = roll(q, -1, 1) + jnp.where(wide_lane == 0, 0.0, roll(q, 1, 1))
        beside = q + corner_weight * along
        return centre * q - around * (along + roll(beside, 1, 0) + roll(beside, -1, 0))

    v = [jnp.concatenate([south, north], axis=1)]
    v.append(operate(v[0]))
    for j in range(2, BASIS):
        v.append(2.0 * operate(v[-1]) - v[-2])
    for j in range(ITERS):
        vectors[j * EXT:(j + 1) * EXT] = v[j]
    own = [[q[COLS:2 * COLS, c * LANES:(c + 1) * LANES] for c in range(NY // LANES)] for q in v]
    parts = [[split(q) for q in row] for row in own]
    sub = iota((COLS, LANES), 0)
    tile_lane = iota((COLS, LANES), 1)
    sums = {}
    for i in range(BASIS):
        for j in range(i, BASIS):
            terms = [
                two_prod(own[i][c], own[j][c], parts[i][c], parts[j][c])
                for c in range(NY // LANES)
            ]
            sums[i, j] = sums[j, i] = pair_rows(pair_tree(terms))
    out = jnp.zeros((COLS, LANES), f32)
    for i in range(BASIS):
        column = (jnp.zeros((COLS, LANES), f32), jnp.zeros((COLS, LANES), f32))
        for j in range(BASIS):
            column = tuple(jnp.where(sub == j, s, c) for s, c in zip(sums[i, j], column))
        step = LANES // 2
        while step:
            column = pair_add(column, (roll(column[0], step, 1), roll(column[1], step, 1)))
            step //= 2
        column = pair_norm(column)
        out = jnp.where(tile_lane == i, column[0], out)
        out = jnp.where(tile_lane == LANES // 2 + i, column[1], out)
    gram[...] = out


def coefficients(gram):
    shape = (COLS, LANES)
    tiles = [gram[i * COLS:(i + 1) * COLS] for i in range(gram.shape[0] // COLS)]
    total = pair_norm(pair_tree([(t, roll(t, LANES // 2, 1)) for t in tiles]))
    wide = lambda column: jnp.broadcast_to(column, shape)
    matrix = [tuple(wide(part[:, j:j + 1]) for part in total) for j in range(BASIS)]
    sub = iota(shape, 0)
    first = (sub == 0).astype(f32)
    zero = jnp.zeros(shape, f32)

    def apply(b):
        half = scale / 2
        up = [half * jnp.where(sub == 0, 0.0, roll(part, 1, 0)) for part in b]
        up = [jnp.where(sub == 1, 2.0 * part, part) for part in up]
        down = [half * jnp.where(sub == COLS - 1, 0.0, roll(part, -1, 0)) for part in b]
        four = tuple(4.0 * part for part in b)
        return pair_norm(pair_add(pair_add(four, b), pair_add(tuple(up), tuple(down))))

    def times(vector, count):
        terms = []
        for j in range(count):
            at = tuple(wide(part[j:j + 1]) for part in vector)
            terms.append(pair_mul(matrix[j], at))
        return pair_norm(pair_tree(terms))

    def dot(a, b):
        s = pair_rows(pair_mul(a, b))
        return s[0] + s[1]

    residual = (first, zero)
    image = matrix[0]
    direction = residual
    solution = zero
    norm_now = wide(matrix[0][0][:1])
    floor = 1e-13 * norm_now
    alive = norm_now > 0
    for iteration in range(ITERS):
        applied = apply(direction)
        applied_image = times(applied, iteration + 2)
        curvature = dot(direction, applied_image)
        alive = alive & (curvature > 0)
        step = jnp.where(alive, norm_now / jnp.where(alive, curvature, 1.0), 0.0)
        solution = solution + step * direction[0]
        if iteration + 1 < ITERS:
            back = -step
            residual = pair_norm(pair_add(residual, pair_scale(applied, back)))
            image = pair_norm(pair_add(image, pair_scale(applied_image, back)))
            norm_next = dot(residual, image)
            ratio = jnp.where(alive, norm_next / jnp.where(alive, norm_now, 1.0), 0.0)
            direction = pair_norm(pair_add(residual, pair_scale(direction, ratio)))
            norm_now = norm_next
            alive = alive & (norm_now > floor)
    return solution


def finish_kernel(gram, vectors, zonal, meridional, levels, zonal_next, meridional_next, height):
    x = coefficients(gram)
    total = jnp.zeros((EXT, NY + LANES), f32)
    for j in range(ITERS):
        total += x[j:j + 1, :1] * vectors[j * EXT:(j + 1) * EXT]
    own = total[COLS:2 * COLS, :NY]
    height[...] = own
    east = gravity * (roll(total, -1, 0)[COLS:2 * COLS, :NY] - own)
    north = gravity * (roll(total, -1, 1)[COLS:2 * COLS, :NY] - own)
    lc = levels[...]
    for k in range(K):
        zonal_next[k] = zonal[k] - jnp.where(lc > k, east, 0.0)
        meridional_next[k] = meridional[k] - jnp.where(lc > k, north, 0.0)


def neighbours(count, sibling, beyond, mirror):
    shape = (COLS, NY)
    even = lax.axis_index("lon") % 2 == 0
    row, lane = iota(shape, 0), iota(shape, 1)
    lc = count[...].astype(f32)
    north_tile = mirror[COLS:2 * COLS]

    def around(field, west, east, north):
        return (
            jnp.where(row == COLS - 1, east, roll(field, -1, 0)),
            jnp.where(row == 0, west, roll(field, 1, 0)),
            jnp.where(lane == NY - 1, north, roll(field, -1, 1)),
            jnp.where(lane == 0, 0.0, roll(field, 1, 1)),
        )

    def edges(at):
        a, b = sibling[at:at + 1], beyond[at:at + 1]
        return jnp.where(even, b, a), jnp.where(even, a, b)

    def padded(field, base, k, sign):
        at = LANE_MT + base * K + k
        return around(field, *edges(2 * COLS + base * K + k), sign * north_tile[:, at:at + 1])

    west_lc, east_lc = edges(64)
    north_lc = north_tile[:, LANE_LC:LANE_LC + 1]

    def mask_sum(mask, k):
        inside = [(c > k).astype(f32) for c in (west_lc, east_lc, north_lc)]
        return sum(around(mask, *inside))

    return lc, padded, mask_sum


def tracer_kernel(
    tracer, zonal, meridional, count, diffusivity, sibling, beyond, mirror, after, tracer_next
):
    lc, padded, mask_sum = neighbours(count, sibling, beyond, mirror)
    diff = diffusivity[...]

    def masked(k):
        if k < 0 or k >= K:
            return jnp.zeros_like(lc), jnp.zeros_like(lc)
        mask = (lc > k).astype(f32)
        return mask, mask * tracer[k]

    below, here = masked(-1), masked(0)
    for k in range(K):
        above = masked(k + 1)
        mask, mt = here
        t, u, v = tracer[k], zonal[k], meridional[k]
        te, tw, tn, ts = padded(mt, 0, k, 1.0)
        vertical = above[1] + below[1] - (above[0] + below[0]) * t
        tracer_next[k] = mask * (
            t
            + diff * (te + tw + tn + ts - mask_sum(mask, k) * t)
            + vertical_mix * vertical
            - advection * (u * (te - tw) + v * (tn - ts))
        )
        below, here = here, above


def flow_kernel(
    zonal, meridional, count, diffusivity, sibling, beyond, mirror, after,
    zonal_step, meridional_step, levels,
):
    lc, padded, mask_sum = neighbours(count, sibling, beyond, mirror)
    diff = diffusivity[...]
    turn = planetary(lc.shape)
    levels[...] = lc
    for k in range(K):
        mask = (lc > k).astype(f32)
        u, v = zonal[k], meridional[k]
        sides = mask_sum(mask, k)
        zonal_sum = sum(padded(mask * u, 1, k, -1.0))
        meridional_sum = sum(padded(mask * v, 2, k, -1.0))
        zonal_step[k] = mask * (u + diff * (zonal_sum - sides * u) + turn * v)
        meridional_step[k] = mask * (v + diff * (meridional_sum - sides * v) - turn * u)


def call(kernel, shapes, *args, flops=0, after=None, scratch=(), stay=0):
    moved = 4 * sum(a.size for a in args) + 4 * sum(
        functools.reduce(lambda x, y: x * y, s, 1) for s in shapes
    )
    space = pl.BlockSpec(memory_space=pltpu.VMEM)
    anywhere = pl.BlockSpec(memory_space=pl.ANY)
    in_specs = [space] * (len(args) - stay) + [pl.BlockSpec(memory_space=pltpu.HBM)] * stay
    here = len(args) - stay
    args = args[:here] + tuple(
        pltpu.with_memory_space_constraint(a, pltpu.HBM) for a in args[here:]
    )
    if after is not None:
        in_specs.append(anywhere)
        args = args + (after,)
    return pl.pallas_call(
        kernel,
        out_shape=[jax.ShapeDtypeStruct(s, f32) for s in shapes],
        in_specs=in_specs,
        out_specs=[space] * len(shapes),
        scratch_shapes=list(scratch),
        compiler_params=pltpu.CompilerParams(vmem_limit_bytes=32 * 1024 * 1024),
        cost_estimate=pl.CostEstimate(flops=flops, bytes_accessed=moved, transcendentals=0),
    )(*args)


def body(tracer, zonal, meridional, count, diffusivity, surface):
    size = lax.axis_size("lon")
    block = (K, COLS, NY)

    def permute(value, pairs):
        return lax.ppermute(value, "lon", pairs)

    siblings = [(i, i ^ 1) for i in range(size)]
    outward = [(i, (i + 1 if i % 2 else i - 1) % size) for i in range(size)]
    mirrored = [(i, size - 1 - i) for i in range(size)]
    arguments = (tracer, zonal, meridional, count, diffusivity, surface)
    inner, outer = call(
        pack_kernel, [(PACK, NY)] * 2, *arguments,
        scratch=[pltpu.VMEM(a.shape, a.dtype) for a in arguments]
        + [pltpu.SemaphoreType.DMA((3 + 3 * CHUNKS,))], stay=len(arguments),
    )
    beyond = permute(outer, outward)
    sibling = permute(inner, siblings)
    forcing, coded, tile, flipped = call(
        halo_kernel,
        [(EXT, NY), (EXT, NY), (EXT, LANES), (EXT, LANES)],
        inner, outer, sibling, beyond,
    )
    mirror = permute(flipped, mirrored)
    vectors, gram = call(
        basis_kernel,
        [(ITERS * EXT, NY + LANES), (COLS, LANES)],
        forcing, coded, tile, mirror,
    )
    sums = [gram]
    reach = 1
    while reach < size:
        other = permute(sums[-1], [(i, i ^ (reach ^ 1 if reach > 1 else 1)) for i in range(size)])
        sums.append(jnp.concatenate([sums[-1], other], axis=0))
        reach *= 2
    halos = (sibling, beyond, mirror)
    tracer_next, = call(
        tracer_kernel, [block],
        tracer, zonal, meridional, count, diffusivity, *halos,
        flops=65536 * 40, after=sums[min(2, len(sums) - 1)],
    )
    zonal_step, meridional_step, levels = call(
        flow_kernel, [block, block, (COLS, NY)],
        zonal, meridional, count, diffusivity, *halos,
        flops=65536 * 40, after=sums[min(3, len(sums) - 1)],
    )
    zonal_next, meridional_next, height = call(
        finish_kernel, [block, block, (COLS, NY)],
        sums[-1], vectors, zonal_step, meridional_step, levels,
    )
    return tracer_next, zonal_next, meridional_next, height


def solution(mesh):
    column = P("lon", None)
    field = P("ens", "lon", None)
    return jax.shard_map(
        body,
        mesh=mesh,
        in_specs=(field, field, field, column, column, column),
        out_specs=(field, field, field, P("lon", "ens")),
        check_vma=False,
    )
```

```python
import functools

import jax
import jax.numpy as jnp
from jax import lax
from jax.experimental import pallas as pl
from jax.experimental.pallas import tpu as pltpu
from jax.sharding import PartitionSpec as P

K = 16
NY = 512
ITERS = 6
COLS = 8
EXT = 3 * COLS
LANES = 128
PACK = 80
BASIS = ITERS + 1
CHUNKS = 4

vertical_mix = 0.1
advection = 0.25
coriolis_scale = 0.3
gravity = 0.5
corner_weight = 0.25
shift = 5.0
scale = 4.0
LANE_P = 16
LANE_LC = 32
LANE_DIFF = 33
LANE_MT = 40
LANE_MU = 56
LANE_MV = 72
LANE_EDGE = 88

f32 = jnp.float32


def iota(shape, dim):
    return lax.broadcasted_iota(jnp.int32, shape, dim)


def thickness(k):
    return 0.5 * (0.5 + k / K)


def planetary(shape):
    latitude = (iota(shape, 1).astype(f32) + 0.5) / NY
    return coriolis_scale * (2.0 * latitude - 1.0)


def roll(value, amount, axis):
    return pltpu.roll(value, amount % value.shape[axis], axis)


def level_sum(value):
    weight = 0.5 * (0.5 + iota(value.shape, 0).astype(f32) / K)
    return jnp.sum(weight * value, axis=0, keepdims=True)


def two_sum(a, b):
    s = a + b
    t = s - a
    return s, (a - (s - t)) + (b - t)


def fast_two_sum(a, b):
    s = a + b
    return s, b - (s - a)


def split(a):
    c = 4097.0 * a
    high = c - (c - a)
    return high, a - high


def two_prod(a, b, a_parts=None, b_parts=None):
    ah, al = split(a) if a_parts is None else a_parts
    bh, bl = split(b) if b_parts is None else b_parts
    p = a * b
    return p, ((ah * bh - p) + ah * bl + al * bh) + al * bl


def pair_mul(a, b):
    p, e = two_prod(a[0], b[0])
    return p, e + (a[0] * b[1] + a[1] * b[0])


def pair_add(a, b):
    s, e = two_sum(a[0], b[0])
    return s, e + (a[1] + b[1])


def pair_norm(a):
    return fast_two_sum(a[0], a[1])


def pair_scale(a, factor):
    p, e = two_prod(a[0], factor)
    return p, e + a[1] * factor


def pair_tree(terms):
    while len(terms) > 1:
        pairs = [pair_add(terms[i], terms[i + 1]) for i in range(0, len(terms) - 1, 2)]
        terms = pairs + terms[len(terms) - len(terms) % 2:]
    return terms[0]


def pair_rows(a):
    for step in (4, 2, 1):
        a = pair_add(a, (roll(a[0], step, 0), roll(a[1], step, 0)))
    return a


def pack_kernel(
    tracer_in, zonal_in, meridional_in, count_in, diffusivity_in, surface_in, inner, outer,
    tracer, zonal, meridional, count, diffusivity, surface, sems,
):
    shape = (COLS, NY)
    even = is_even()
    small = [
        pltpu.make_async_copy(a, b, sems.at[i])
        for i, (a, b) in enumerate(
            ((count_in, count), (diffusivity_in, diffusivity), (surface_in, surface))
        )
    ]
    large = []
    for c in range(CHUNKS):
        part = pl.ds(c * K // CHUNKS, K // CHUNKS)
        large.append(
            [
                pltpu.make_async_copy(a.at[part], b.at[part], sems.at[3 + 3 * c + i])
                for i, (a, b) in enumerate(
                    ((zonal_in, zonal), (meridional_in, meridional), (tracer_in, tracer))
                )
            ]
        )
    for copy in small + sum(large, []):
        copy.start()
    for copy in small:
        copy.wait()
    lc = count[...].astype(f32)
    diff = diffusivity[...]
    row, lane = iota(shape, 0), iota(shape, 1)
    tile_lane = iota((COLS, LANES), 1)
    total = jnp.zeros(shape, f32)
    turn = jnp.zeros(shape, f32)
    flux_x = jnp.zeros(shape, f32)
    flux_y = jnp.zeros(shape, f32)
    fold = jnp.zeros((COLS, LANES), f32)

    def put(tile, at, column):
        return jnp.where(tile_lane == at, column, tile)

    for k in range(K):
        if k % (K // CHUNKS) == 0:
            for copy in large[k // (K // CHUNKS)]:
                copy.wait()
        mask = (lc > k).astype(f32)
        u, v = zonal[k], meridional[k]
        mt, mu, mv = mask * tracer[k], mask * u, mask * v
        p = mu + mv
        total += thickness(k) * p
        turn += thickness(k) * (mv - mu)
        flux_x += thickness(k) * (mask * roll(p, -1, 0) - roll(mask, -1, 0) * p)
        flux_y += thickness(k) * (mask * roll(p, -1, 1) - roll(mask, -1, 1) * p)
        fold = put(fold, LANE_P + k, p[:, NY - 1:])
        for base, field in ((0, mt), (1, mu), (2, mv)):
            west, east = field[:1], field[COLS - 1:]
            at = 2 * COLS + base * K + k
            inner[at:at + 1] = jnp.where(even, east, west)
            outer[at:at + 1] = jnp.where(even, west, east)
            fold = put(fold, LANE_MT + base * K + k, field[:, NY - 1:])
    fold = put(fold, LANE_LC, lc[:, NY - 1:])
    fold = put(fold, LANE_DIFF, diff[:, NY - 1:])
    flux_x = jnp.where(row == COLS - 1, 0.0, flux_x)
    flux_y = jnp.where(lane == NY - 1, 0.0, flux_y)
    west_flux = jnp.where(row == 0, 0.0, roll(flux_x, 1, 0))
    south_flux = jnp.where(lane == 0, 0.0, roll(flux_y, 1, 1))
    forcing = total + planetary(shape) * turn + diff * (
        flux_x - west_flux + flux_y - south_flux
    )
    coded = jnp.where(lc > 0, surface[...], -1.0)
    zeros = jnp.zeros((COLS, NY - LANES), f32)
    for pack, mine, other in ((inner, COLS - 1, 0), (outer, 0, COLS - 1)):
        pack[0:COLS] = forcing
        pack[COLS:2 * COLS] = coded
        edge_lc = jnp.where(even, lc[mine:mine + 1], lc[other:other + 1])
        edge_diff = jnp.where(even, diff[mine:mine + 1], diff[other:other + 1])
        pack[64:72] = jnp.where(row == 0, edge_lc, jnp.where(row == 1, edge_diff, 0.0))
        pack[72:80] = jnp.concatenate([fold, zeros], axis=1)


def interface_flux(mine, theirs):
    level = iota((K, NY), 0).astype(f32)
    p_mine = mine[32:48] + mine[48:64]
    p_theirs = theirs[32:48] + theirs[48:64]
    return level_sum(
        jnp.where(level < mine[64:65], p_theirs, 0.0)
        - jnp.where(level < theirs[64:65], p_mine, 0.0)
    )


def is_even():
    return lax.axis_index("lon") % 2 == 0


def beside(even, west, east):
    return jnp.concatenate([jnp.where(even, west, east), jnp.where(even, east, west)], axis=0)


def chip_kernel(inner, outer, sibling, forcing, coded, tile, flipped):
    even = is_even()
    flux = interface_flux(inner, sibling)
    own, far = inner[65:66] * flux, -sibling[65:66] * flux
    row = iota((2 * COLS, NY), 0)
    change = jnp.where(
        row == COLS - 1,
        jnp.where(even, own, far),
        jnp.where(row == COLS, jnp.where(even, far, own), 0.0),
    )
    full = beside(even, inner[:COLS], sibling[:COLS]) + change
    code = beside(even, inner[COLS:2 * COLS], sibling[COLS:2 * COLS])
    fold = beside(even, inner[72:80, :LANES], sibling[72:80, :LANES])
    forcing[...] = full
    coded[...] = code
    tile[...] = fold
    lane = iota((2 * COLS, LANES), 1)
    for j in range(COLS):
        at = NY - 1 - j
        fold = jnp.where(lane == j, full[:, at:at + 1], fold)
        fold = jnp.where(lane == COLS + j, code[:, at:at + 1], fold)
    fold = jnp.concatenate(
        [fold[i:i + 1] for i in range(2 * COLS - 1, -1, -1)], axis=0
    )
    edge = outer[32:48, NY - LANES:] + outer[48:64, NY - LANES:]
    for j in range(COLS):
        at = LANES - 1 - j
        fold = jnp.where(lane == LANE_EDGE + j, edge[:, at:at + 1], fold)
        for base, source in ((1, 64), (2, 65)):
            value = outer[source:source + 1, NY - 1 - j:NY - j]
            fold = jnp.where(lane == LANE_EDGE + base * COLS + j, value, fold)
    flipped[...] = fold


def across_fold(even, chip, far):
    shape = (2 * COLS, LANES)
    level = iota(shape, 0).astype(f32)
    lane = iota((1, LANES), 1)
    flux = level_sum(
        jnp.where(level < roll(chip, -COLS, 1), far, 0.0)
        - jnp.where(level < roll(far, -COLS, 1), chip, 0.0)
    )

    def change(tile):
        return jnp.where(lane < COLS, roll(roll(tile[:1], -2 * COLS, 1) * flux, -LANE_EDGE, 1), 0.0)

    chip_change, far_change = change(chip), -change(far)
    tile = extend(even, far[COLS:], chip, far[:COLS])
    row = iota((EXT, LANES), 0)
    west = jnp.where(row == COLS - 1, far_change, jnp.where(row == COLS, chip_change, 0.0))
    east = jnp.where(
        row == 2 * COLS - 1, chip_change, jnp.where(row == 2 * COLS, far_change, 0.0)
    )
    return tile + jnp.where(even, west, east)


def extend(even, west, chip, east):
    return jnp.concatenate(
        [
            jnp.where(even, west, chip[:COLS]),
            jnp.where(even, chip[:COLS], chip[COLS:]),
            jnp.where(even, chip[COLS:], east),
        ],
        axis=0,
    )


def basis_kernel(outer, beyond, forcing, coded, tile, mirror, mirror_far, vectors, gram):
    width = NY + LANES
    even = is_even()
    lane = iota((EXT, LANES), 1)
    mine = beyond[72:80, :LANES]
    mine = extend(even, mine, tile[...], mine)
    theirs = across_fold(even, mirror[...], mirror_far[...])
    level = (lane - LANE_P).astype(f32)
    weight = jnp.where((lane >= LANE_P) & (lane < LANE_P + K), 0.5 * (0.5 + level / K), 0.0)
    mask_mine = (level < mine[:, LANE_LC:LANE_LC + 1]).astype(f32)
    mask_theirs = (level < theirs[:, LANE_LC:LANE_LC + 1]).astype(f32)
    flux = -jnp.sum(weight * (mask_mine * theirs + mask_theirs * mine), axis=1, keepdims=True)
    own_change = mine[:, LANE_DIFF:LANE_DIFF + 1] * flux
    far_change = theirs[:, LANE_DIFF:LANE_DIFF + 1] * flux
    flux_out = interface_flux(outer, beyond)
    own, far = outer[65:66] * flux_out, -beyond[65:66] * flux_out
    row = iota((EXT, NY), 0)
    west = jnp.where(row == COLS - 1, far, jnp.where(row == COLS, own, 0.0))
    east = jnp.where(row == 2 * COLS - 1, own, jnp.where(row == 2 * COLS, far, 0.0))
    far_forcing, far_code = beyond[:COLS], beyond[COLS:2 * COLS]
    south = extend(even, far_forcing, forcing[...], far_forcing) + jnp.where(even, west, east)
    south_code = extend(even, far_code, coded[...], far_code)
    north = jnp.where(lane < COLS, theirs, 0.0)
    north = north + jnp.where(lane == 0, far_change, 0.0)
    body_lane = iota((EXT, NY), 1)
    south = south + jnp.where(body_lane == NY - 1, own_change, 0.0)
    north_code = jnp.where(lane < COLS, roll(theirs, -COLS, 1), -1.0)
    code = jnp.concatenate([south_code, north_code], axis=1)
    ocean = code > 0
    centre = jnp.where(ocean, code / scale, 0.0)
    around = jnp.where(ocean, 1.0 / scale, 0.0)
    wide_lane = iota((EXT, width), 1)

    def operate(q):
        along = roll(q, -1, 1) + jnp.where(wide_lane == 0, 0.0, roll(q, 1, 1))
        side = q + corner_weight * along
        return centre * q - around * (along + roll(side, 1, 0) + roll(side, -1, 0))

    v = [jnp.concatenate([south, north], axis=1)]
    v.append(operate(v[0]))
    for j in range(2, BASIS):
        v.append(2.0 * operate(v[-1]) - v[-2])
    for j in range(ITERS):
        vectors[j * EXT:(j + 1) * EXT] = v[j]
    own = [[q[COLS:2 * COLS, c * LANES:(c + 1) * LANES] for c in range(NY // LANES)] for q in v]
    parts = [[split(q) for q in row] for row in own]
    sub = iota((COLS, LANES), 0)
    tile_lane = iota((COLS, LANES), 1)
    sums = {}
    for i in range(BASIS):
        for j in range(i, BASIS):
            terms = [
                two_prod(own[i][c], own[j][c], parts[i][c], parts[j][c])
                for c in range(NY // LANES)
            ]
            sums[i, j] = sums[j, i] = pair_rows(pair_tree(terms))
    out = jnp.zeros((COLS, LANES), f32)
    for i in range(BASIS):
        column = (jnp.zeros((COLS, LANES), f32), jnp.zeros((COLS, LANES), f32))
        for j in range(BASIS):
            column = tuple(jnp.where(sub == j, s, c) for s, c in zip(sums[i, j], column))
        step = LANES // 2
        while step:
            column = pair_add(column, (roll(column[0], step, 1), roll(column[1], step, 1)))
            step //= 2
        column = pair_norm(column)
        out = jnp.where(tile_lane == i, column[0], out)
        out = jnp.where(tile_lane == LANES // 2 + i, column[1], out)
    gram[...] = out


def coefficients(gram):
    shape = (COLS, LANES)
    tiles = [gram[i * COLS:(i + 1) * COLS] for i in range(gram.shape[0] // COLS)]
    total = pair_norm(pair_tree([(t, roll(t, LANES // 2, 1)) for t in tiles]))
    wide = lambda column: jnp.broadcast_to(column, shape)
    matrix = [tuple(wide(part[:, j:j + 1]) for part in total) for j in range(BASIS)]
    sub = iota(shape, 0)
    first = (sub == 0).astype(f32)
    zero = jnp.zeros(shape, f32)

    def apply(b):
        half = scale / 2
        up = [half * jnp.where(sub == 0, 0.0, roll(part, 1, 0)) for part in b]
        up = [jnp.where(sub == 1, 2.0 * part, part) for part in up]
        down = [half * jnp.where(sub == COLS - 1, 0.0, roll(part, -1, 0)) for part in b]
        four = tuple(4.0 * part for part in b)
        return pair_norm(pair_add(pair_add(four, b), pair_add(tuple(up), tuple(down))))

    def times(vector, count):
        terms = []
        for j in range(count):
            at = tuple(wide(part[j:j + 1]) for part in vector)
            terms.append(pair_mul(matrix[j], at))
        return pair_norm(pair_tree(terms))

    def dot(a, b):
        s = pair_rows(pair_mul(a, b))
        return s[0] + s[1]

    residual = (first, zero)
    image = matrix[0]
    direction = residual
    solution = zero
    norm_now = wide(matrix[0][0][:1])
    floor = 1e-13 * norm_now
    alive = norm_now > 0
    for iteration in range(ITERS):
        applied = apply(direction)
        applied_image = times(applied, iteration + 2)
        curvature = dot(direction, applied_image)
        alive = alive & (curvature > 0)
        step = jnp.where(alive, norm_now / jnp.where(alive, curvature, 1.0), 0.0)
        solution = solution + step * direction[0]
        if iteration + 1 < ITERS:
            back = -step
            residual = pair_norm(pair_add(residual, pair_scale(applied, back)))
            image = pair_norm(pair_add(image, pair_scale(applied_image, back)))
            norm_next = dot(residual, image)
            ratio = jnp.where(alive, norm_next / jnp.where(alive, norm_now, 1.0), 0.0)
            direction = pair_norm(pair_add(residual, pair_scale(direction, ratio)))
            norm_now = norm_next
            alive = alive & (norm_now > floor)
    return solution


def finish_kernel(gram, vectors, zonal, meridional, levels, zonal_next, meridional_next, height):
    x = coefficients(gram)
    total = jnp.zeros((EXT, NY + LANES), f32)
    for j in range(ITERS):
        total += x[j:j + 1, :1] * vectors[j * EXT:(j + 1) * EXT]
    own = total[COLS:2 * COLS, :NY]
    height[...] = own
    east = gravity * (roll(total, -1, 0)[COLS:2 * COLS, :NY] - own)
    north = gravity * (roll(total, -1, 1)[COLS:2 * COLS, :NY] - own)
    lc = levels[...]
    for k in range(K):
        zonal_next[k] = zonal[k] - jnp.where(lc > k, east, 0.0)
        meridional_next[k] = meridional[k] - jnp.where(lc > k, north, 0.0)


def neighbours(count, sibling, beyond, mirror):
    shape = (COLS, NY)
    even = is_even()
    row, lane = iota(shape, 0), iota(shape, 1)
    lc = count[...].astype(f32)
    north_tile = jnp.where(even, mirror[:COLS], mirror[COLS:])

    def around(field, west, east, north):
        return (
            jnp.where(row == COLS - 1, east, roll(field, -1, 0)),
            jnp.where(row == 0, west, roll(field, 1, 0)),
            jnp.where(lane == NY - 1, north, roll(field, -1, 1)),
            jnp.where(lane == 0, 0.0, roll(field, 1, 1)),
        )

    def edges(at):
        a, b = sibling[at:at + 1], beyond[at:at + 1]
        return jnp.where(even, b, a), jnp.where(even, a, b)

    def padded(field, base, k, sign):
        at = LANE_MT + base * K + k
        return around(field, *edges(2 * COLS + base * K + k), sign * north_tile[:, at:at + 1])

    west_lc, east_lc = edges(64)
    north_lc = north_tile[:, LANE_LC:LANE_LC + 1]

    def mask_sum(mask, k):
        inside = [(c > k).astype(f32) for c in (west_lc, east_lc, north_lc)]
        return sum(around(mask, *inside))

    return lc, padded, mask_sum


def tracer_kernel(
    tracer, zonal, meridional, count, diffusivity, sibling, beyond, mirror, after, tracer_next
):
    lc, padded, mask_sum = neighbours(count, sibling, beyond, mirror)
    diff = diffusivity[...]

    def masked(k):
        if k < 0 or k >= K:
            return jnp.zeros_like(lc), jnp.zeros_like(lc)
        mask = (lc > k).astype(f32)
        return mask, mask * tracer[k]

    below, here = masked(-1), masked(0)
    for k in range(K):
        above = masked(k + 1)
        mask, mt = here
        t, u, v = tracer[k], zonal[k], meridional[k]
        te, tw, tn, ts = padded(mt, 0, k, 1.0)
        vertical = above[1] + below[1] - (above[0] + below[0]) * t
        tracer_next[k] = mask * (
            t
            + diff * (te + tw + tn + ts - mask_sum(mask, k) * t)
            + vertical_mix * vertical
            - advection * (u * (te - tw) + v * (tn - ts))
        )
        below, here = here, above


def flow_kernel(
    zonal, meridional, count, diffusivity, sibling, beyond, mirror, after,
    zonal_step, meridional_step, levels,
):
    lc, padded, mask_sum = neighbours(count, sibling, beyond, mirror)
    diff = diffusivity[...]
    turn = planetary(lc.shape)
    levels[...] = lc
    for k in range(K):
        mask = (lc > k).astype(f32)
        u, v = zonal[k], meridional[k]
        sides = mask_sum(mask, k)
        zonal_sum = sum(padded(mask * u, 1, k, -1.0))
        meridional_sum = sum(padded(mask * v, 2, k, -1.0))
        zonal_step[k] = mask * (u + diff * (zonal_sum - sides * u) + turn * v)
        meridional_step[k] = mask * (v + diff * (meridional_sum - sides * v) - turn * u)


def call(kernel, shapes, *args, flops=0, after=None, scratch=(), stay=0):
    moved = 4 * sum(a.size for a in args) + 4 * sum(
        functools.reduce(lambda x, y: x * y, s, 1) for s in shapes
    )
    space = pl.BlockSpec(memory_space=pltpu.VMEM)
    anywhere = pl.BlockSpec(memory_space=pl.ANY)
    in_specs = [space] * (len(args) - stay) + [pl.BlockSpec(memory_space=pltpu.HBM)] * stay
    here = len(args) - stay
    args = args[:here] + tuple(
        pltpu.with_memory_space_constraint(a, pltpu.HBM) for a in args[here:]
    )
    if after is not None:
        in_specs.append(anywhere)
        args = args + (after,)
    return pl.pallas_call(
        kernel,
        out_shape=[jax.ShapeDtypeStruct(s, f32) for s in shapes],
        in_specs=in_specs,
        out_specs=[space] * len(shapes),
        scratch_shapes=list(scratch),
        compiler_params=pltpu.CompilerParams(vmem_limit_bytes=32 * 1024 * 1024),
        cost_estimate=pl.CostEstimate(flops=flops, bytes_accessed=moved, transcendentals=0),
    )(*args)


def body(tracer, zonal, meridional, count, diffusivity, surface):
    size = lax.axis_size("lon")
    block = (K, COLS, NY)

    def permute(value, pairs):
        return lax.ppermute(value, "lon", pairs)

    siblings = [(i, i ^ 1) for i in range(size)]
    outward = [(i, (i + 1 if i % 2 else i - 1) % size) for i in range(size)]
    mirrored = [(i, size - 1 - i) for i in range(size)]
    mirrored_far = [(i, (size - 2 * (i % 2) - i) % size) for i in range(size)]
    arguments = (tracer, zonal, meridional, count, diffusivity, surface)
    inner, outer = call(
        pack_kernel, [(PACK, NY)] * 2, *arguments,
        scratch=[pltpu.VMEM(a.shape, a.dtype) for a in arguments]
        + [pltpu.SemaphoreType.DMA((3 + 3 * CHUNKS,))], stay=len(arguments),
    )
    beyond = permute(outer, outward)
    sibling = permute(inner, siblings)
    chip = (2 * COLS, NY)
    forcing, coded, tile, flipped = call(
        chip_kernel, [chip, chip, (2 * COLS, LANES), (2 * COLS, LANES)], inner, outer, sibling
    )
    mirror = permute(flipped, mirrored)
    mirror_far = permute(flipped, mirrored_far)
    vectors, gram = call(
        basis_kernel,
        [(ITERS * EXT, NY + LANES), (COLS, LANES)],
        outer, beyond, forcing, coded, tile, mirror, mirror_far,
    )
    sums = [gram]
    reach = 1
    while reach < size:
        other = permute(sums[-1], [(i, i ^ (reach ^ 1 if reach > 1 else 1)) for i in range(size)])
        sums.append(jnp.concatenate([sums[-1], other], axis=0))
        reach *= 2
    halos = (sibling, beyond, mirror)
    tracer_next, = call(
        tracer_kernel, [block],
        tracer, zonal, meridional, count, diffusivity, *halos,
        flops=65536 * 40, after=sums[min(2, len(sums) - 1)],
    )
    zonal_step, meridional_step, levels = call(
        flow_kernel, [block, block, (COLS, NY)],
        zonal, meridional, count, diffusivity, *halos,
        flops=65536 * 40, after=sums[min(3, len(sums) - 1)],
    )
    zonal_next, meridional_next, height = call(
        finish_kernel, [block, block, (COLS, NY)],
        sums[-1], vectors, zonal_step, meridional_step, levels,
    )
    return tracer_next, zonal_next, meridional_next, height


def solution(mesh):
    column = P("lon", None)
    field = P("ens", "lon", None)
    return jax.shard_map(
        body,
        mesh=mesh,
        in_specs=(field, field, field, column, column, column),
        out_specs=(field, field, field, P("lon", "ens")),
        check_vma=False,
    )
```

```python
import functools

import jax
import jax.numpy as jnp
from jax import lax
from jax.experimental import pallas as pl
from jax.experimental.pallas import tpu as pltpu
from jax.sharding import PartitionSpec as P

K = 16
NY = 512
ITERS = 6
COLS = 8
EXT = 3 * COLS
LANES = 128
PACK = 80
BASIS = ITERS + 1
CHUNKS = 4

vertical_mix = 0.1
advection = 0.25
coriolis_scale = 0.3
gravity = 0.5
corner_weight = 0.25
shift = 5.0
scale = 4.0
LANE_P = 16
LANE_LC = 32
LANE_DIFF = 33
LANE_MT = 40
LANE_MU = 56
LANE_MV = 72
LANE_EDGE = 88

f32 = jnp.float32


def iota(shape, dim):
    return lax.broadcasted_iota(jnp.int32, shape, dim)


def thickness(k):
    return 0.5 * (0.5 + k / K)


def planetary(shape):
    latitude = (iota(shape, 1).astype(f32) + 0.5) / NY
    return coriolis_scale * (2.0 * latitude - 1.0)


def roll(value, amount, axis):
    return pltpu.roll(value, amount % value.shape[axis], axis)


def level_sum(value):
    weight = 0.5 * (0.5 + iota(value.shape, 0).astype(f32) / K)
    return jnp.sum(weight * value, axis=0, keepdims=True)


def two_sum(a, b):
    s = a + b
    t = s - a
    return s, (a - (s - t)) + (b - t)


def fast_two_sum(a, b):
    s = a + b
    return s, b - (s - a)


def split(a):
    c = 4097.0 * a
    high = c - (c - a)
    return high, a - high


def two_prod(a, b, a_parts=None, b_parts=None):
    ah, al = split(a) if a_parts is None else a_parts
    bh, bl = split(b) if b_parts is None else b_parts
    p = a * b
    return p, ((ah * bh - p) + ah * bl + al * bh) + al * bl


def pair_mul(a, b):
    p, e = two_prod(a[0], b[0])
    return p, e + (a[0] * b[1] + a[1] * b[0])


def pair_add(a, b):
    s, e = two_sum(a[0], b[0])
    return s, e + (a[1] + b[1])


def pair_norm(a):
    return fast_two_sum(a[0], a[1])


def pair_scale(a, factor):
    p, e = two_prod(a[0], factor)
    return p, e + a[1] * factor


def pair_tree(terms):
    while len(terms) > 1:
        pairs = [pair_add(terms[i], terms[i + 1]) for i in range(0, len(terms) - 1, 2)]
        terms = pairs + terms[len(terms) - len(terms) % 2:]
    return terms[0]


def pair_rows(a):
    for step in (4, 2, 1):
        a = pair_add(a, (roll(a[0], step, 0), roll(a[1], step, 0)))
    return a


def pack_kernel(
    tracer_in, zonal_in, meridional_in, count_in, diffusivity_in, surface_in, inner, outer,
    tracer, zonal, meridional, count, diffusivity, surface, sems,
):
    shape = (COLS, NY)
    even = is_even()
    small = [
        pltpu.make_async_copy(a, b, sems.at[i])
        for i, (a, b) in enumerate(
            ((count_in, count), (diffusivity_in, diffusivity), (surface_in, surface))
        )
    ]
    large = []
    for c in range(CHUNKS):
        part = pl.ds(c * K // CHUNKS, K // CHUNKS)
        large.append(
            [
                pltpu.make_async_copy(a.at[part], b.at[part], sems.at[3 + 3 * c + i])
                for i, (a, b) in enumerate(
                    ((zonal_in, zonal), (meridional_in, meridional), (tracer_in, tracer))
                )
            ]
        )
    for copy in small + sum(large, []):
        copy.start()
    for copy in small:
        copy.wait()
    lc = count[...].astype(f32)
    diff = diffusivity[...]
    row, lane = iota(shape, 0), iota(shape, 1)
    tile_lane = iota((COLS, LANES), 1)
    total = jnp.zeros(shape, f32)
    turn = jnp.zeros(shape, f32)
    flux_x = jnp.zeros(shape, f32)
    flux_y = jnp.zeros(shape, f32)
    fold = jnp.zeros((COLS, LANES), f32)

    def put(tile, at, column):
        return jnp.where(tile_lane == at, column, tile)

    for k in range(K):
        if k % (K // CHUNKS) == 0:
            for copy in large[k // (K // CHUNKS)]:
                copy.wait()
        mask = (lc > k).astype(f32)
        u, v = zonal[k], meridional[k]
        mt, mu, mv = mask * tracer[k], mask * u, mask * v
        p = mu + mv
        total += thickness(k) * p
        turn += thickness(k) * (mv - mu)
        flux_x += thickness(k) * (mask * roll(p, -1, 0) - roll(mask, -1, 0) * p)
        flux_y += thickness(k) * (mask * roll(p, -1, 1) - roll(mask, -1, 1) * p)
        fold = put(fold, LANE_P + k, p[:, NY - 1:])
        for base, field in ((0, mt), (1, mu), (2, mv)):
            west, east = field[:1], field[COLS - 1:]
            at = 2 * COLS + base * K + k
            inner[at:at + 1] = jnp.where(even, east, west)
            outer[at:at + 1] = jnp.where(even, west, east)
            fold = put(fold, LANE_MT + base * K + k, field[:, NY - 1:])
    fold = put(fold, LANE_LC, lc[:, NY - 1:])
    fold = put(fold, LANE_DIFF, diff[:, NY - 1:])
    flux_x = jnp.where(row == COLS - 1, 0.0, flux_x)
    flux_y = jnp.where(lane == NY - 1, 0.0, flux_y)
    west_flux = jnp.where(row == 0, 0.0, roll(flux_x, 1, 0))
    south_flux = jnp.where(lane == 0, 0.0, roll(flux_y, 1, 1))
    forcing = total + planetary(shape) * turn + diff * (
        flux_x - west_flux + flux_y - south_flux
    )
    coded = jnp.where(lc > 0, surface[...], -1.0)
    edge = jnp.zeros((K, LANES), f32)
    edge_lane = iota((K, LANES), 1)
    p = outer[32:48, NY - LANES:] + outer[48:64, NY - LANES:]
    edge_lc = jnp.where(even, lc[:1], lc[COLS - 1:])
    edge_diff = jnp.where(even, diff[:1], diff[COLS - 1:])
    for j in range(COLS):
        at = NY - 1 - j
        here = LANE_EDGE + j
        edge = jnp.where(edge_lane == here, p[:, LANES - 1 - j:LANES - j], edge)
        edge = jnp.where(edge_lane == here + COLS, edge_lc[:, at:at + 1], edge)
        edge = jnp.where(edge_lane == here + 2 * COLS, edge_diff[:, at:at + 1], edge)
    edge = [edge[:COLS], edge[COLS:]]
    zeros = jnp.zeros((COLS, NY - 3 * LANES), f32)
    for pack, mine, other in ((inner, COLS - 1, 0), (outer, 0, COLS - 1)):
        pack[0:COLS] = forcing
        pack[COLS:2 * COLS] = coded
        edge_lc = jnp.where(even, lc[mine:mine + 1], lc[other:other + 1])
        edge_diff = jnp.where(even, diff[mine:mine + 1], diff[other:other + 1])
        pack[64:72] = jnp.where(row == 0, edge_lc, jnp.where(row == 1, edge_diff, 0.0))
        pack[72:80] = jnp.concatenate([fold, *edge, zeros], axis=1)


def interface_flux(mine, theirs):
    level = iota((K, NY), 0).astype(f32)
    p_mine = mine[32:48] + mine[48:64]
    p_theirs = theirs[32:48] + theirs[48:64]
    return level_sum(
        jnp.where(level < mine[64:65], p_theirs, 0.0)
        - jnp.where(level < theirs[64:65], p_mine, 0.0)
    )


def is_even():
    return lax.axis_index("lon") % 2 == 0


def beside(even, west, east):
    return jnp.concatenate([jnp.where(even, west, east), jnp.where(even, east, west)], axis=0)


def chip_kernel(inner, sibling, forcing, coded, tile, near, far):
    even = is_even()
    flux = interface_flux(inner, sibling)
    own, other = inner[65:66] * flux, -sibling[65:66] * flux
    row = iota((2 * COLS, NY), 0)
    change = jnp.where(
        row == COLS - 1,
        jnp.where(even, own, other),
        jnp.where(row == COLS, jnp.where(even, other, own), 0.0),
    )
    full = beside(even, inner[:COLS], sibling[:COLS]) + change
    code = beside(even, inner[COLS:2 * COLS], sibling[COLS:2 * COLS])
    fold = beside(even, inner[72:80, :LANES], sibling[72:80, :LANES])
    forcing[...] = full
    coded[...] = code
    tile[...] = fold
    lane = iota((2 * COLS, LANES), 1)
    for j in range(COLS):
        at = NY - 1 - j
        fold = jnp.where(lane == j, full[:, at:at + 1], fold)
        fold = jnp.where(lane == COLS + j, code[:, at:at + 1], fold)
    fold = jnp.concatenate(
        [fold[i:i + 1] for i in range(2 * COLS - 1, -1, -1)], axis=0
    )
    for out, source in ((near, inner), (far, sibling)):
        edge = jnp.concatenate(
            [source[72:80, LANES:2 * LANES], source[72:80, 2 * LANES:3 * LANES]], axis=0
        )
        out[...] = jnp.where(lane >= LANE_EDGE, edge, fold)


def across_fold(even, chip, far):
    shape = (2 * COLS, LANES)
    level = iota(shape, 0).astype(f32)
    lane = iota((1, LANES), 1)
    flux = level_sum(
        jnp.where(level < roll(chip, -COLS, 1), far, 0.0)
        - jnp.where(level < roll(far, -COLS, 1), chip, 0.0)
    )

    def change(tile):
        return jnp.where(lane < COLS, roll(roll(tile[:1], -2 * COLS, 1) * flux, -LANE_EDGE, 1), 0.0)

    chip_change, far_change = change(chip), -change(far)
    tile = extend(even, far[COLS:], chip, far[:COLS])
    row = iota((EXT, LANES), 0)
    west = jnp.where(row == COLS - 1, far_change, jnp.where(row == COLS, chip_change, 0.0))
    east = jnp.where(
        row == 2 * COLS - 1, chip_change, jnp.where(row == 2 * COLS, far_change, 0.0)
    )
    return tile + jnp.where(even, west, east)


def extend(even, west, chip, east):
    return jnp.concatenate(
        [
            jnp.where(even, west, chip[:COLS]),
            jnp.where(even, chip[:COLS], chip[COLS:]),
            jnp.where(even, chip[COLS:], east),
        ],
        axis=0,
    )


def basis_kernel(outer, beyond, forcing, coded, tile, mirror, mirror_far, vectors, gram):
    width = NY + LANES
    even = is_even()
    lane = iota((EXT, LANES), 1)
    mine = beyond[72:80, :LANES]
    mine = extend(even, mine, tile[...], mine)
    theirs = across_fold(even, mirror[...], mirror_far[...])
    level = (lane - LANE_P).astype(f32)
    weight = jnp.where((lane >= LANE_P) & (lane < LANE_P + K), 0.5 * (0.5 + level / K), 0.0)
    mask_mine = (level < mine[:, LANE_LC:LANE_LC + 1]).astype(f32)
    mask_theirs = (level < theirs[:, LANE_LC:LANE_LC + 1]).astype(f32)
    flux = -jnp.sum(weight * (mask_mine * theirs + mask_theirs * mine), axis=1, keepdims=True)
    own_change = mine[:, LANE_DIFF:LANE_DIFF + 1] * flux
    far_change = theirs[:, LANE_DIFF:LANE_DIFF + 1] * flux
    flux_out = interface_flux(outer, beyond)
    own, far = outer[65:66] * flux_out, -beyond[65:66] * flux_out
    row = iota((EXT, NY), 0)
    west = jnp.where(row == COLS - 1, far, jnp.where(row == COLS, own, 0.0))
    east = jnp.where(row == 2 * COLS - 1, own, jnp.where(row == 2 * COLS, far, 0.0))
    far_forcing, far_code = beyond[:COLS], beyond[COLS:2 * COLS]
    south = extend(even, far_forcing, forcing[...], far_forcing) + jnp.where(even, west, east)
    south_code = extend(even, far_code, coded[...], far_code)
    north = jnp.where(lane < COLS, theirs, 0.0)
    north = north + jnp.where(lane == 0, far_change, 0.0)
    body_lane = iota((EXT, NY), 1)
    south = south + jnp.where(body_lane == NY - 1, own_change, 0.0)
    north_code = jnp.where(lane < COLS, roll(theirs, -COLS, 1), -1.0)
    code = jnp.concatenate([south_code, north_code], axis=1)
    ocean = code > 0
    centre = jnp.where(ocean, code / scale, 0.0)
    around = jnp.where(ocean, 1.0 / scale, 0.0)
    wide_lane = iota((EXT, width), 1)

    def operate(q):
        along = roll(q, -1, 1) + jnp.where(wide_lane == 0, 0.0, roll(q, 1, 1))
        side = q + corner_weight * along
        return centre * q - around * (along + roll(side, 1, 0) + roll(side, -1, 0))

    v = [jnp.concatenate([south, north], axis=1)]
    v.append(operate(v[0]))
    for j in range(2, BASIS):
        v.append(2.0 * operate(v[-1]) - v[-2])
    for j in range(ITERS):
        vectors[j * EXT:(j + 1) * EXT] = v[j]
    own = [[q[COLS:2 * COLS, c * LANES:(c + 1) * LANES] for c in range(NY // LANES)] for q in v]
    parts = [[split(q) for q in row] for row in own]
    sub = iota((COLS, LANES), 0)
    tile_lane = iota((COLS, LANES), 1)
    sums = {}
    for i in range(BASIS):
        for j in range(i, BASIS):
            terms = [
                two_prod(own[i][c], own[j][c], parts[i][c], parts[j][c])
                for c in range(NY // LANES)
            ]
            sums[i, j] = sums[j, i] = pair_rows(pair_tree(terms))
    out = jnp.zeros((COLS, LANES), f32)
    for i in range(BASIS):
        column = (jnp.zeros((COLS, LANES), f32), jnp.zeros((COLS, LANES), f32))
        for j in range(BASIS):
            column = tuple(jnp.where(sub == j, s, c) for s, c in zip(sums[i, j], column))
        step = LANES // 2
        while step:
            column = pair_add(column, (roll(column[0], step, 1), roll(column[1], step, 1)))
            step //= 2
        for part, base in zip(pair_norm(column), (0, LANES // 2)):
            out = jnp.where(tile_lane - (base + i * COLS) == sub, part, out)
    gram[...] = jnp.sum(out, axis=0, keepdims=True)


def coefficients(gram):
    shape = (COLS, LANES)
    tiles = [gram[i * COLS:(i + 1) * COLS] for i in range(gram.shape[0] // COLS)]
    total = pair_norm(pair_rows(pair_tree([(t, roll(t, LANES // 2, 1)) for t in tiles])))
    wide = lambda column: jnp.broadcast_to(column, shape)
    sub = iota(shape, 0)
    entry = iota(shape, 1) - sub
    matrix = [
        tuple(
            wide(jnp.sum(jnp.where(entry == j * COLS, part, 0.0), axis=1, keepdims=True))
            for part in total
        )
        for j in range(BASIS)
    ]
    first = (sub == 0).astype(f32)
    zero = jnp.zeros(shape, f32)

    def apply(b):
        half = scale / 2
        up = [half * jnp.where(sub == 0, 0.0, roll(part, 1, 0)) for part in b]
        up = [jnp.where(sub == 1, 2.0 * part, part) for part in up]
        down = [half * jnp.where(sub == COLS - 1, 0.0, roll(part, -1, 0)) for part in b]
        four = tuple(4.0 * part for part in b)
        return pair_norm(pair_add(pair_add(four, b), pair_add(tuple(up), tuple(down))))

    def times(vector, count):
        terms = []
        for j in range(count):
            at = tuple(wide(part[j:j + 1]) for part in vector)
            terms.append(pair_mul(matrix[j], at))
        return pair_norm(pair_tree(terms))

    def dot(a, b):
        s = pair_rows(pair_mul(a, b))
        return s[0] + s[1]

    residual = (first, zero)
    image = matrix[0]
    direction = residual
    solution = zero
    norm_now = wide(matrix[0][0][:1])
    floor = 1e-13 * norm_now
    alive = norm_now > 0
    for iteration in range(ITERS):
        applied = apply(direction)
        applied_image = times(applied, iteration + 2)
        curvature = dot(direction, applied_image)
        alive = alive & (curvature > 0)
        step = jnp.where(alive, norm_now / jnp.where(alive, curvature, 1.0), 0.0)
        solution = solution + step * direction[0]
        if iteration + 1 < ITERS:
            back = -step
            residual = pair_norm(pair_add(residual, pair_scale(applied, back)))
            image = pair_norm(pair_add(image, pair_scale(applied_image, back)))
            norm_next = dot(residual, image)
            ratio = jnp.where(alive, norm_next / jnp.where(alive, norm_now, 1.0), 0.0)
            direction = pair_norm(pair_add(residual, pair_scale(direction, ratio)))
            norm_now = norm_next
            alive = alive & (norm_now > floor)
    return solution


def finish_kernel(gram, vectors, zonal, meridional, levels, zonal_next, meridional_next, height):
    x = coefficients(gram)
    total = jnp.zeros((EXT, NY + LANES), f32)
    for j in range(ITERS):
        total += x[j:j + 1, :1] * vectors[j * EXT:(j + 1) * EXT]
    own = total[COLS:2 * COLS, :NY]
    height[...] = own
    east = gravity * (roll(total, -1, 0)[COLS:2 * COLS, :NY] - own)
    north = gravity * (roll(total, -1, 1)[COLS:2 * COLS, :NY] - own)
    lc = levels[...]
    for k in range(K):
        zonal_next[k] = zonal[k] - jnp.where(lc > k, east, 0.0)
        meridional_next[k] = meridional[k] - jnp.where(lc > k, north, 0.0)


def neighbours(count, sibling, beyond, mirror):
    shape = (COLS, NY)
    even = is_even()
    row, lane = iota(shape, 0), iota(shape, 1)
    lc = count[...].astype(f32)
    north_tile = jnp.where(even, mirror[:COLS], mirror[COLS:])

    def around(field, west, east, north):
        return (
            jnp.where(row == COLS - 1, east, roll(field, -1, 0)),
            jnp.where(row == 0, west, roll(field, 1, 0)),
            jnp.where(lane == NY - 1, north, roll(field, -1, 1)),
            jnp.where(lane == 0, 0.0, roll(field, 1, 1)),
        )

    def edges(at):
        a, b = sibling[at:at + 1], beyond[at:at + 1]
        return jnp.where(even, b, a), jnp.where(even, a, b)

    def padded(field, base, k, sign):
        at = LANE_MT + base * K + k
        return around(field, *edges(2 * COLS + base * K + k), sign * north_tile[:, at:at + 1])

    west_lc, east_lc = edges(64)
    north_lc = north_tile[:, LANE_LC:LANE_LC + 1]

    def mask_sum(mask, k):
        inside = [(c > k).astype(f32) for c in (west_lc, east_lc, north_lc)]
        return sum(around(mask, *inside))

    return lc, padded, mask_sum


def tracer_kernel(
    tracer, zonal, meridional, count, diffusivity, sibling, beyond, mirror, after, tracer_next
):
    lc, padded, mask_sum = neighbours(count, sibling, beyond, mirror)
    diff = diffusivity[...]

    def masked(k):
        if k < 0 or k >= K:
            return jnp.zeros_like(lc), jnp.zeros_like(lc)
        mask = (lc > k).astype(f32)
        return mask, mask * tracer[k]

    below, here = masked(-1), masked(0)
    for k in range(K):
        above = masked(k + 1)
        mask, mt = here
        t, u, v = tracer[k], zonal[k], meridional[k]
        te, tw, tn, ts = padded(mt, 0, k, 1.0)
        vertical = above[1] + below[1] - (above[0] + below[0]) * t
        tracer_next[k] = mask * (
            t
            + diff * (te + tw + tn + ts - mask_sum(mask, k) * t)
            + vertical_mix * vertical
            - advection * (u * (te - tw) + v * (tn - ts))
        )
        below, here = here, above


def flow_kernel(
    zonal, meridional, count, diffusivity, sibling, beyond, mirror, after,
    zonal_step, meridional_step, levels,
):
    lc, padded, mask_sum = neighbours(count, sibling, beyond, mirror)
    diff = diffusivity[...]
    turn = planetary(lc.shape)
    levels[...] = lc
    for k in range(K):
        mask = (lc > k).astype(f32)
        u, v = zonal[k], meridional[k]
        sides = mask_sum(mask, k)
        zonal_sum = sum(padded(mask * u, 1, k, -1.0))
        meridional_sum = sum(padded(mask * v, 2, k, -1.0))
        zonal_step[k] = mask * (u + diff * (zonal_sum - sides * u) + turn * v)
        meridional_step[k] = mask * (v + diff * (meridional_sum - sides * v) - turn * u)


def call(kernel, shapes, *args, flops=0, after=None, scratch=(), stay=0):
    moved = 4 * sum(a.size for a in args) + 4 * sum(
        functools.reduce(lambda x, y: x * y, s, 1) for s in shapes
    )
    space = pl.BlockSpec(memory_space=pltpu.VMEM)
    anywhere = pl.BlockSpec(memory_space=pl.ANY)
    in_specs = [space] * (len(args) - stay) + [pl.BlockSpec(memory_space=pltpu.HBM)] * stay
    here = len(args) - stay
    args = args[:here] + tuple(
        pltpu.with_memory_space_constraint(a, pltpu.HBM) for a in args[here:]
    )
    if after is not None:
        in_specs.append(anywhere)
        args = args + (after,)
    return pl.pallas_call(
        kernel,
        out_shape=[jax.ShapeDtypeStruct(s, f32) for s in shapes],
        in_specs=in_specs,
        out_specs=[space] * len(shapes),
        scratch_shapes=list(scratch),
        compiler_params=pltpu.CompilerParams(vmem_limit_bytes=32 * 1024 * 1024),
        cost_estimate=pl.CostEstimate(flops=flops, bytes_accessed=moved, transcendentals=0),
    )(*args)


def body(tracer, zonal, meridional, count, diffusivity, surface):
    size = lax.axis_size("lon")
    block = (K, COLS, NY)

    def permute(value, pairs):
        return lax.ppermute(value, "lon", pairs)

    siblings = [(i, i ^ 1) for i in range(size)]
    outward = [(i, (i + 1 if i % 2 else i - 1) % size) for i in range(size)]
    mirrored = [(i, size - 1 - i) for i in range(size)]
    mirrored_far = [((size + 1 - 4 * (i % 2) - i) % size, i) for i in range(size)]
    arguments = (tracer, zonal, meridional, count, diffusivity, surface)
    inner, outer = call(
        pack_kernel, [(PACK, NY)] * 2, *arguments,
        scratch=[pltpu.VMEM(a.shape, a.dtype) for a in arguments]
        + [pltpu.SemaphoreType.DMA((3 + 3 * CHUNKS,))], stay=len(arguments),
    )
    beyond = permute(outer, outward)
    sibling = permute(inner, siblings)
    chip = (2 * COLS, NY)
    forcing, coded, tile, near, far = call(
        chip_kernel, [chip, chip] + [(2 * COLS, LANES)] * 3, inner, sibling
    )
    mirror = permute(near, mirrored)
    mirror_far = permute(far, mirrored_far)
    vectors, gram = call(
        basis_kernel,
        [(ITERS * EXT, NY + LANES), (1, LANES)],
        outer, beyond, forcing, coded, tile, mirror, mirror_far,
    )
    halos = (sibling, beyond, mirror)
    reach = 1
    tracer_next = None
    while reach < size:
        if 8 * reach >= size and tracer_next is None and reach > 1:
            tracer_next, = call(
                tracer_kernel, [block],
                tracer, zonal, meridional, count, diffusivity, *halos,
                flops=65536 * 40, after=gram,
            )
        other = permute(gram, [(i, i ^ (reach ^ 1 if reach > 1 else 1)) for i in range(size)])
        gram = jnp.concatenate([gram, other], axis=0)
        reach *= 2
        if 2 * reach == size:
            gram, tracer_next = lax.optimization_barrier((gram, tracer_next))
            zonal_step, meridional_step, levels = call(
                flow_kernel, [block, block, (COLS, NY)],
                zonal, meridional, count, diffusivity, *halos,
                flops=65536 * 40, after=gram,
            )
    zonal_next, meridional_next, height = call(
        finish_kernel, [block, block, (COLS, NY)],
        gram, vectors, zonal_step, meridional_step, levels,
    )
    return tracer_next, zonal_next, meridional_next, height


def solution(mesh):
    column = P("lon", None)
    field = P("ens", "lon", None)
    return jax.shard_map(
        body,
        mesh=mesh,
        in_specs=(field, field, field, column, column, column),
        out_specs=(field, field, field, P("lon", "ens")),
        check_vma=False,
    )
```

```python
import functools

import jax
import jax.numpy as jnp
from jax import lax
from jax.experimental import pallas as pl
from jax.experimental.pallas import tpu as pltpu
from jax.sharding import PartitionSpec as P

K = 16
NY = 512
ITERS = 6
COLS = 8
EXT = 3 * COLS
LANES = 128
PACK = 80
BASIS = ITERS + 1
NEAR = 384
GROUPS = (BASIS * (BASIS + 1) // 2 + COLS - 1) // COLS
CHUNKS = 2

vertical_mix = 0.1
advection = 0.25
coriolis_scale = 0.3
gravity = 0.5
corner_weight = 0.25
shift = 5.0
scale = 4.0
LANE_P = 16
LANE_LC = 32
LANE_DIFF = 33
LANE_MT = 40
LANE_MU = 56
LANE_MV = 72
LANE_EDGE = 88

f32 = jnp.float32


def iota(shape, dim):
    return lax.broadcasted_iota(jnp.int32, shape, dim)


def thickness(k):
    return 0.5 * (0.5 + k / K)


def planetary(shape):
    latitude = (iota(shape, 1).astype(f32) + 0.5) / NY
    return coriolis_scale * (2.0 * latitude - 1.0)


def roll(value, amount, axis):
    return pltpu.roll(value, amount % value.shape[axis], axis)


def level_sum(value):
    weight = 0.5 * (0.5 + iota(value.shape, 0).astype(f32) / K)
    return jnp.sum(weight * value, axis=0, keepdims=True)


def two_sum(a, b):
    s = a + b
    t = s - a
    return s, (a - (s - t)) + (b - t)


def fast_two_sum(a, b):
    s = a + b
    return s, b - (s - a)


def split(a):
    c = 4097.0 * a
    high = c - (c - a)
    return high, a - high


def two_prod(a, b, a_parts=None, b_parts=None):
    ah, al = split(a) if a_parts is None else a_parts
    bh, bl = split(b) if b_parts is None else b_parts
    p = a * b
    return p, ((ah * bh - p) + ah * bl + al * bh) + al * bl


def pair_mul(a, b):
    p, e = two_prod(a[0], b[0])
    return p, e + (a[0] * b[1] + a[1] * b[0])


def pair_add(a, b):
    s, e = two_sum(a[0], b[0])
    return s, e + (a[1] + b[1])


def pair_norm(a):
    return fast_two_sum(a[0], a[1])


def pair_scale(a, factor):
    p, e = two_prod(a[0], factor)
    return p, e + a[1] * factor


def pair_tree(terms):
    while len(terms) > 1:
        pairs = [pair_add(terms[i], terms[i + 1]) for i in range(0, len(terms) - 1, 2)]
        terms = pairs + terms[len(terms) - len(terms) % 2:]
    return terms[0]


def pair_rows(a):
    for step in (4, 2, 1):
        a = pair_add(a, (roll(a[0], step, 0), roll(a[1], step, 0)))
    return a


def pair_pack(terms):
    shape = (COLS, LANES)
    sub = iota(shape, 0)
    zero = (jnp.zeros(shape, f32),) * 2
    terms = terms + [zero] * (COLS - len(terms))
    for step in (4, 2, 1):
        low = (sub & step) == 0
        merged = []
        for x, y in zip(terms[:step], terms[step:]):
            a = tuple(jnp.where(low, p, q) for p, q in zip(x, y))
            b = tuple(
                jnp.where(low, roll(p, -step, 0), roll(q, step, 0)) for p, q in zip(x, y)
            )
            merged.append(pair_add(a, b))
        terms = merged
    return terms[0]


def pack_kernel(
    tracer_in, zonal_in, meridional_in, count_in, diffusivity_in, surface_in, inner, outer,
    tracer, zonal, meridional, count, diffusivity, surface, edges, sems,
):
    shape = (COLS, NY)
    even = is_even()
    small = [
        pltpu.make_async_copy(a, b, sems.at[i])
        for i, (a, b) in enumerate(
            ((count_in, count), (diffusivity_in, diffusivity), (surface_in, surface))
        )
    ]
    large = []
    for c in range(CHUNKS):
        part = pl.ds(c * K // CHUNKS, K // CHUNKS)
        large.append(
            [
                pltpu.make_async_copy(a.at[part], b.at[part], sems.at[3 + 3 * c + i])
                for i, (a, b) in enumerate(
                    ((zonal_in, zonal), (meridional_in, meridional), (tracer_in, tracer))
                )
            ]
        )
    rows = [
        pltpu.make_async_copy(
            field.at[:, x], edges.at[2 * base + i], sems.at[3 + 3 * CHUNKS + 2 * base + i]
        )
        for base, field in enumerate((tracer_in, zonal_in, meridional_in))
        for i, x in enumerate((0, COLS - 1))
    ]
    for copy in small + sum(large, []) + rows:
        copy.start()
    for copy in small:
        copy.wait()
    lc = count[...].astype(f32)
    diff = diffusivity[...]
    row, lane = iota(shape, 0), iota(shape, 1)
    tile_lane = iota((COLS, LANES), 1)
    lc_east, lc_north = roll(lc, -1, 0), roll(lc, -1, 1)
    total = jnp.zeros(shape, f32)
    turn = jnp.zeros(shape, f32)
    flux_x = jnp.zeros(shape, f32)
    flux_y = jnp.zeros(shape, f32)
    fold = jnp.zeros((COLS, LANES), f32)
    for k in range(K):
        if k % (K // CHUNKS) == 0:
            for copy in large[k // (K // CHUNKS)]:
                copy.wait()
        mask = lc > k
        t, u, v = tracer[k], zonal[k], meridional[k]
        for base, field in ((LANE_MT, t), (LANE_MU, u), (LANE_MV, v)):
            fold = jnp.where(tile_lane == base + k, field[:, NY - 1:], fold)
        mu, mv = jnp.where(mask, u, 0.0), jnp.where(mask, v, 0.0)
        p = thickness(k) * (mu + mv)
        total += p
        turn += thickness(k) * (mv - mu)
        flux_x += jnp.where(mask, roll(p, -1, 0), 0.0) - jnp.where(lc_east > k, p, 0.0)
        flux_y += jnp.where(mask, roll(p, -1, 1), 0.0) - jnp.where(lc_north > k, p, 0.0)
    lc_fold = lc[:, NY - 1:]
    level = tile_lane - jnp.where(
        tile_lane < LANE_MU, LANE_MT, jnp.where(tile_lane < LANE_MV, LANE_MU, LANE_MV)
    )
    fold = jnp.where(level.astype(f32) < lc_fold, fold, 0.0)
    momentum = roll(fold, LANE_P - LANE_MU, 1) + roll(fold, LANE_P - LANE_MV, 1)
    fold = jnp.where((tile_lane >= LANE_P) & (tile_lane < LANE_P + K), momentum, fold)
    fold = jnp.where(tile_lane == LANE_LC, lc_fold, fold)
    fold = jnp.where(tile_lane == LANE_DIFF, diff[:, NY - 1:], fold)
    edge_level = iota((K, NY), 0).astype(f32)
    for copy in rows:
        copy.wait()
    for base in range(3):
        west, east = edges[2 * base], edges[2 * base + 1]
        west = jnp.where(edge_level < lc[:1], west, 0.0)
        east = jnp.where(edge_level < lc[COLS - 1:], east, 0.0)
        at = pl.ds(2 * COLS + base * K, K)
        inner[at] = jnp.where(even, east, west)
        outer[at] = jnp.where(even, west, east)
    flux_x = jnp.where(row == COLS - 1, 0.0, flux_x)
    flux_y = jnp.where(lane == NY - 1, 0.0, flux_y)
    west_flux = jnp.where(row == 0, 0.0, roll(flux_x, 1, 0))
    south_flux = jnp.where(lane == 0, 0.0, roll(flux_y, 1, 1))
    forcing = total + planetary(shape) * turn + diff * (
        flux_x - west_flux + flux_y - south_flux
    )
    coded = jnp.where(lc > 0, surface[...], -1.0)
    edge = jnp.zeros((K, LANES), f32)
    edge_lane = iota((K, LANES), 1)
    p = outer[32:48, NY - LANES:] + outer[48:64, NY - LANES:]
    edge_lc = jnp.where(even, lc[:1], lc[COLS - 1:])
    edge_diff = jnp.where(even, diff[:1], diff[COLS - 1:])
    for j in range(COLS):
        at = NY - 1 - j
        here = LANE_EDGE + j
        edge = jnp.where(edge_lane == here, p[:, LANES - 1 - j:LANES - j], edge)
        edge = jnp.where(edge_lane == here + COLS, edge_lc[:, at:at + 1], edge)
        edge = jnp.where(edge_lane == here + 2 * COLS, edge_diff[:, at:at + 1], edge)
    edge = [edge[:COLS], edge[COLS:]]
    zeros = jnp.zeros((COLS, NY - 3 * LANES), f32)
    for pack, mine, other in ((inner, COLS - 1, 0), (outer, 0, COLS - 1)):
        pack[0:COLS] = forcing
        pack[COLS:2 * COLS] = coded
        edge_lc = jnp.where(even, lc[mine:mine + 1], lc[other:other + 1])
        edge_diff = jnp.where(even, diff[mine:mine + 1], diff[other:other + 1])
        pack[64:72] = jnp.where(row == 0, edge_lc, jnp.where(row == 1, edge_diff, 0.0))
        pack[72:80] = jnp.concatenate([fold, *edge, zeros], axis=1)


def interface_flux(mine, theirs):
    level = iota((K, NY), 0).astype(f32)
    p_mine = mine[32:48] + mine[48:64]
    p_theirs = theirs[32:48] + theirs[48:64]
    return level_sum(
        jnp.where(level < mine[64:65], p_theirs, 0.0)
        - jnp.where(level < theirs[64:65], p_mine, 0.0)
    )


def is_even():
    return lax.axis_index("lon") % 2 == 0


def beside(even, west, east):
    return jnp.concatenate([jnp.where(even, west, east), jnp.where(even, east, west)], axis=0)


def chip_kernel(inner, sibling, forcing, coded, tile, near, far):
    even = is_even()
    flux = interface_flux(inner, sibling)
    own, other = inner[65:66] * flux, -sibling[65:66] * flux
    row = iota((2 * COLS, NY), 0)
    change = jnp.where(
        row == COLS - 1,
        jnp.where(even, own, other),
        jnp.where(row == COLS, jnp.where(even, other, own), 0.0),
    )
    full = beside(even, inner[:COLS], sibling[:COLS]) + change
    code = beside(even, inner[COLS:2 * COLS], sibling[COLS:2 * COLS])
    fold = beside(even, inner[72:80, :LANES], sibling[72:80, :LANES])
    forcing[...] = full
    coded[...] = code
    tile[...] = fold
    lane = iota((2 * COLS, LANES), 1)
    for j in range(COLS):
        at = NY - 1 - j
        fold = jnp.where(lane == j, full[:, at:at + 1], fold)
        fold = jnp.where(lane == COLS + j, code[:, at:at + 1], fold)
    fold = jnp.concatenate(
        [fold[i:i + 1] for i in range(2 * COLS - 1, -1, -1)], axis=0
    )
    for out, source in ((near, inner), (far, sibling)):
        edge = jnp.concatenate(
            [source[72:80, LANES:2 * LANES], source[72:80, 2 * LANES:3 * LANES]], axis=0
        )
        out[...] = jnp.where(lane >= LANE_EDGE, edge, fold)


def across_fold(even, chip, far):
    shape = (2 * COLS, LANES)
    level = iota(shape, 0).astype(f32)
    lane = iota((1, LANES), 1)
    flux = level_sum(
        jnp.where(level < roll(chip, -COLS, 1), far, 0.0)
        - jnp.where(level < roll(far, -COLS, 1), chip, 0.0)
    )

    def change(tile):
        return jnp.where(lane < COLS, roll(roll(tile[:1], -2 * COLS, 1) * flux, -LANE_EDGE, 1), 0.0)

    chip_change, far_change = change(chip), -change(far)
    tile = extend(even, far[COLS:], chip, far[:COLS])
    row = iota((EXT, LANES), 0)
    west = jnp.where(row == COLS - 1, far_change, jnp.where(row == COLS, chip_change, 0.0))
    east = jnp.where(
        row == 2 * COLS - 1, chip_change, jnp.where(row == 2 * COLS, far_change, 0.0)
    )
    return tile + jnp.where(even, west, east)


def extend(even, west, chip, east):
    return jnp.concatenate(
        [
            jnp.where(even, west, chip[:COLS]),
            jnp.where(even, chip[:COLS], chip[COLS:]),
            jnp.where(even, chip[COLS:], east),
        ],
        axis=0,
    )


def basis(start, code):
    ocean = code > 0
    centre = jnp.where(ocean, code / scale, 0.0)
    around = jnp.where(ocean, 1.0 / scale, 0.0)
    lane = iota(start.shape, 1)

    def operate(q):
        along = roll(q, -1, 1) + jnp.where(lane == 0, 0.0, roll(q, 1, 1))
        side = q + corner_weight * along
        return centre * q - around * (along + roll(side, 1, 0) + roll(side, -1, 0))

    v = [start, operate(start)]
    for j in range(2, BASIS):
        v.append(2.0 * operate(v[-1]) - v[-2])
    return v


def gram_rows(v, blocks):
    own = [[q[COLS:2 * COLS, c * LANES:(c + 1) * LANES] for c in blocks] for q in v]
    parts = [[split(q) for q in row] for row in own]
    entries = []
    for i in range(BASIS):
        for j in range(i, BASIS):
            terms = [
                two_prod(own[i][c], own[j][c], parts[i][c], parts[j][c])
                for c in range(len(blocks))
            ]
            entries.append(pair_tree(terms))
    return [pair_pack(entries[g:g + COLS]) for g in range(0, len(entries), COLS)]


def inner_kernel(outer, beyond, forcing, coded, last, last_code, vectors, partial):
    even = is_even()
    flux_out = interface_flux(outer, beyond)
    own, far = outer[65:66] * flux_out, -beyond[65:66] * flux_out
    row = iota((EXT, NY), 0)
    west = jnp.where(row == COLS - 1, far, jnp.where(row == COLS, own, 0.0))
    east = jnp.where(row == 2 * COLS - 1, own, jnp.where(row == 2 * COLS, far, 0.0))
    far_forcing, far_code = beyond[:COLS], beyond[COLS:2 * COLS]
    south = extend(even, far_forcing, forcing[...], far_forcing) + jnp.where(even, west, east)
    code = extend(even, far_code, coded[...], far_code)
    last[...] = south[:, NEAR - LANES:]
    last_code[...] = code[:, NEAR - LANES:]
    v = basis(south, code)
    for j in range(ITERS):
        vectors[j * EXT:(j + 1) * EXT] = v[j][:, :NEAR]
    for g, pair in enumerate(gram_rows(v, range(NEAR // LANES))):
        for at, part in zip((0, GROUPS * COLS), pair):
            partial[at + g * COLS:at + (g + 1) * COLS] = part


def fold_kernel(last, last_code, beyond, tile, mirror, mirror_far, partial, vectors, gram):
    even = is_even()
    lane = iota((EXT, LANES), 1)
    mine = beyond[72:80, :LANES]
    mine = extend(even, mine, tile[...], mine)
    theirs = across_fold(even, mirror[...], mirror_far[...])
    level = (lane - LANE_P).astype(f32)
    weight = jnp.where((lane >= LANE_P) & (lane < LANE_P + K), 0.5 * (0.5 + level / K), 0.0)
    mask_mine = (level < mine[:, LANE_LC:LANE_LC + 1]).astype(f32)
    mask_theirs = (level < theirs[:, LANE_LC:LANE_LC + 1]).astype(f32)
    flux = -jnp.sum(weight * (mask_mine * theirs + mask_theirs * mine), axis=1, keepdims=True)
    own_change = mine[:, LANE_DIFF:LANE_DIFF + 1] * flux
    far_change = theirs[:, LANE_DIFF:LANE_DIFF + 1] * flux
    north = jnp.where(lane < COLS, theirs, 0.0)
    north = north + jnp.where(lane == 0, far_change, 0.0)
    width = NY - NEAR + LANES
    south = last[...] + jnp.where(iota((EXT, width), 1) == width - 1, own_change, 0.0)
    north_code = jnp.where(lane < COLS, roll(theirs, -COLS, 1), -1.0)
    v = basis(
        jnp.concatenate([south, north], axis=1),
        jnp.concatenate([last_code[...], north_code], axis=1),
    )
    for j in range(ITERS):
        vectors[j * EXT:(j + 1) * EXT] = v[j][:, LANES:]
    sub = iota((COLS, LANES), 0)
    tile_lane = iota((COLS, LANES), 1)
    out = jnp.zeros((COLS, LANES), f32)
    for g, pair in enumerate(gram_rows(v, range(1, width // LANES))):
        at, low = g * COLS, (GROUPS + g) * COLS
        pair = pair_add(pair, (partial[at:at + COLS], partial[low:low + COLS]))
        step = LANES // 2
        while step:
            pair = pair_add(pair, tuple(roll(part, step, 1) for part in pair))
            step //= 2
        for part, base in zip(pair_norm(pair), (at, low)):
            out = jnp.where(tile_lane - base == sub, part, out)
    gram[...] = jnp.sum(out, axis=0, keepdims=True)


def coefficients(gram):
    shape = (COLS, LANES)
    tiles = [gram[i * COLS:(i + 1) * COLS] for i in range(gram.shape[0] // COLS)]
    total = pair_norm(pair_rows(pair_tree([(t, roll(t, -GROUPS * COLS, 1)) for t in tiles])))
    wide = lambda column: jnp.broadcast_to(column, shape)
    sub = iota(shape, 0)
    tile_lane = iota(shape, 1)

    def column(j):
        low, high = jnp.minimum(sub, j), jnp.maximum(sub, j)
        entry = ((low * (2 * BASIS - 1 - low)) >> 1) + high
        here = (tile_lane == entry) & (sub < BASIS)
        return tuple(
            wide(jnp.sum(jnp.where(here, part, 0.0), axis=1, keepdims=True)) for part in total
        )

    matrix = [column(j) for j in range(BASIS)]
    first = (sub == 0).astype(f32)
    zero = jnp.zeros(shape, f32)

    def apply(b):
        half = scale / 2
        up = [half * jnp.where(sub == 0, 0.0, roll(part, 1, 0)) for part in b]
        up = [jnp.where(sub == 1, 2.0 * part, part) for part in up]
        down = [half * jnp.where(sub == COLS - 1, 0.0, roll(part, -1, 0)) for part in b]
        four = tuple(4.0 * part for part in b)
        return pair_add(pair_add(four, b), pair_add(tuple(up), tuple(down)))

    def times(vector, count):
        terms = []
        for j in range(count):
            at = tuple(wide(part[j:j + 1]) for part in vector)
            terms.append(pair_mul(matrix[j], at))
        return pair_tree(terms)

    def dot(a, b):
        s = pair_rows(pair_mul(a, b))
        return s[0] + s[1]

    residual = (first, zero)
    image = matrix[0]
    direction = residual
    solution = zero
    norm_now = wide(matrix[0][0][:1])
    floor = 1e-13 * norm_now
    alive = norm_now > 0
    for iteration in range(ITERS):
        applied = apply(direction)
        applied_image = times(applied, iteration + 2)
        curvature = dot(direction, applied_image)
        alive = alive & (curvature > 0)
        step = jnp.where(alive, norm_now / jnp.where(alive, curvature, 1.0), 0.0)
        solution = solution + step * direction[0]
        if iteration + 1 < ITERS:
            back = -step
            residual = pair_norm(pair_add(residual, pair_scale(applied, back)))
            image = pair_norm(pair_add(image, pair_scale(applied_image, back)))
            norm_next = dot(residual, image)
            ratio = jnp.where(alive, norm_next / jnp.where(alive, norm_now, 1.0), 0.0)
            direction = pair_norm(pair_add(residual, pair_scale(direction, ratio)))
            norm_now = norm_next
            alive = alive & (norm_now > floor)
    return solution


def finish_kernel(
    gram, vectors, vectors_last, zonal, meridional, levels, zonal_next, meridional_next, height
):
    x = coefficients(gram)
    total = []
    for part in (vectors, vectors_last):
        at = [x[j:j + 1, :1] * part[j * EXT:(j + 1) * EXT] for j in range(ITERS)]
        total.append(sum(at[1:], at[0]))
    total = jnp.concatenate(total, axis=1)
    own = total[COLS:2 * COLS, :NY]
    height[...] = own
    east = gravity * (roll(total, -1, 0)[COLS:2 * COLS, :NY] - own)
    north = gravity * (roll(total, -1, 1)[COLS:2 * COLS, :NY] - own)
    lc = levels[...]
    for k in range(K):
        zonal_next[k] = zonal[k] - jnp.where(lc > k, east, 0.0)
        meridional_next[k] = meridional[k] - jnp.where(lc > k, north, 0.0)


def neighbours(count, sibling, beyond, mirror):
    shape = (COLS, NY)
    even = is_even()
    row, lane = iota(shape, 0), iota(shape, 1)
    lc = count[...].astype(f32)
    north_tile = jnp.where(even, mirror[:COLS], mirror[COLS:])

    def around(field, west, east, north):
        return (
            jnp.where(row == COLS - 1, east, roll(field, -1, 0)),
            jnp.where(row == 0, west, roll(field, 1, 0)),
            jnp.where(lane == NY - 1, north, roll(field, -1, 1)),
            jnp.where(lane == 0, 0.0, roll(field, 1, 1)),
        )

    def edges(at):
        a, b = sibling[at:at + 1], beyond[at:at + 1]
        return jnp.where(even, b, a), jnp.where(even, a, b)

    def padded(field, base, k, sign):
        at = LANE_MT + base * K + k
        return around(field, *edges(2 * COLS + base * K + k), sign * north_tile[:, at:at + 1])

    west_lc, east_lc = edges(64)
    north_lc = north_tile[:, LANE_LC:LANE_LC + 1]

    def mask_sum(mask, k):
        inside = [(c > k).astype(f32) for c in (west_lc, east_lc, north_lc)]
        return sum(around(mask, *inside))

    return lc, padded, mask_sum


def tracer_kernel(
    tracer, zonal, meridional, count, diffusivity, sibling, beyond, mirror, after, tracer_next
):
    lc, padded, mask_sum = neighbours(count, sibling, beyond, mirror)
    diff = diffusivity[...]

    def masked(k):
        if k < 0 or k >= K:
            return jnp.zeros_like(lc), jnp.zeros_like(lc)
        mask = (lc > k).astype(f32)
        return mask, mask * tracer[k]

    below, here = masked(-1), masked(0)
    for k in range(K):
        above = masked(k + 1)
        mask, mt = here
        t, u, v = tracer[k], zonal[k], meridional[k]
        te, tw, tn, ts = padded(mt, 0, k, 1.0)
        vertical = above[1] + below[1] - (above[0] + below[0]) * t
        tracer_next[k] = mask * (
            t
            + diff * (te + tw + tn + ts - mask_sum(mask, k) * t)
            + vertical_mix * vertical
            - advection * (u * (te - tw) + v * (tn - ts))
        )
        below, here = here, above


def flow_kernel(
    zonal, meridional, count, diffusivity, sibling, beyond, mirror, after,
    zonal_step, meridional_step, levels,
):
    lc, padded, mask_sum = neighbours(count, sibling, beyond, mirror)
    diff = diffusivity[...]
    turn = planetary(lc.shape)
    levels[...] = lc
    for k in range(K):
        mask = (lc > k).astype(f32)
        u, v = zonal[k], meridional[k]
        sides = mask_sum(mask, k)
        zonal_sum = sum(padded(mask * u, 1, k, -1.0))
        meridional_sum = sum(padded(mask * v, 2, k, -1.0))
        zonal_step[k] = mask * (u + diff * (zonal_sum - sides * u) + turn * v)
        meridional_step[k] = mask * (v + diff * (meridional_sum - sides * v) - turn * u)


def call(kernel, shapes, *args, flops=0, after=None, scratch=(), stay=0):
    moved = 4 * sum(a.size for a in args) + 4 * sum(
        functools.reduce(lambda x, y: x * y, s, 1) for s in shapes
    )
    space = pl.BlockSpec(memory_space=pltpu.VMEM)
    anywhere = pl.BlockSpec(memory_space=pl.ANY)
    in_specs = [space] * (len(args) - stay) + [pl.BlockSpec(memory_space=pltpu.HBM)] * stay
    here = len(args) - stay
    args = args[:here] + tuple(
        pltpu.with_memory_space_constraint(a, pltpu.HBM) for a in args[here:]
    )
    if after is not None:
        in_specs.append(anywhere)
        args = args + (after,)
    return pl.pallas_call(
        kernel,
        out_shape=[jax.ShapeDtypeStruct(s, f32) for s in shapes],
        in_specs=in_specs,
        out_specs=[space] * len(shapes),
        scratch_shapes=list(scratch),
        compiler_params=pltpu.CompilerParams(vmem_limit_bytes=32 * 1024 * 1024),
        cost_estimate=pl.CostEstimate(flops=flops, bytes_accessed=moved, transcendentals=0),
    )(*args)


def body(tracer, zonal, meridional, count, diffusivity, surface):
    size = lax.axis_size("lon")
    block = (K, COLS, NY)

    def permute(value, pairs):
        return lax.ppermute(value, "lon", pairs)

    siblings = [(i, i ^ 1) for i in range(size)]
    outward = [(i, (i + 1 if i % 2 else i - 1) % size) for i in range(size)]
    mirrored = [(i, size - 1 - i) for i in range(size)]
    mirrored_far = [((size + 1 - 4 * (i % 2) - i) % size, i) for i in range(size)]
    arguments = (tracer, zonal, meridional, count, diffusivity, surface)
    inner, outer = call(
        pack_kernel, [(PACK, NY)] * 2, *arguments,
        scratch=[pltpu.VMEM(a.shape, a.dtype) for a in arguments]
        + [pltpu.VMEM((6, K, NY), f32), pltpu.SemaphoreType.DMA((9 + 3 * CHUNKS,))], stay=len(arguments),
    )
    beyond = permute(outer, outward)
    sibling = permute(inner, siblings)
    chip = (2 * COLS, NY)
    forcing, coded, tile, near, far = call(
        chip_kernel, [chip, chip] + [(2 * COLS, LANES)] * 3, inner, sibling
    )
    mirror = permute(near, mirrored)
    mirror_far = permute(far, mirrored_far)
    last_rows = (EXT, NY - NEAR + LANES)
    last, last_code, vectors, partial = call(
        inner_kernel,
        [last_rows, last_rows, (ITERS * EXT, NEAR), (2 * GROUPS * COLS, LANES)],
        outer, beyond, forcing, coded, flops=8192 * 100,
    )
    vectors_last, gram = call(
        fold_kernel,
        [(ITERS * EXT, NY - NEAR + LANES), (1, LANES)],
        last, last_code, beyond, tile, mirror, mirror_far, partial,
    )
    halos = (sibling, beyond, mirror)
    reach = 1
    tracer_next = None
    while reach < size:
        if 8 * reach >= size and tracer_next is None and reach > 1:
            tracer_next, = call(
                tracer_kernel, [block],
                tracer, zonal, meridional, count, diffusivity, *halos,
                flops=65536 * 40, after=gram,
            )
        other = permute(gram, [(i, i ^ (reach ^ 1 if reach > 1 else 1)) for i in range(size)])
        gram = jnp.concatenate([gram, other], axis=0)
        reach *= 2
        if 2 * reach == size:
            gram, tracer_next = lax.optimization_barrier((gram, tracer_next))
            zonal_step, meridional_step, levels = call(
                flow_kernel, [block, block, (COLS, NY)],
                zonal, meridional, count, diffusivity, *halos,
                flops=65536 * 40, after=gram,
            )
    zonal_next, meridional_next, height = call(
        finish_kernel, [block, block, (COLS, NY)],
        gram, vectors, vectors_last, zonal_step, meridional_step, levels,
    )
    return tracer_next, zonal_next, meridional_next, height


def solution(mesh):
    column = P("lon", None)
    field = P("ens", "lon", None)
    return jax.shard_map(
        body,
        mesh=mesh,
        in_specs=(field, field, field, column, column, column),
        out_specs=(field, field, field, P("lon", "ens")),
        check_vma=False,
    )
```

```python
import functools

import jax
import jax.numpy as jnp
from jax import lax
from jax.experimental import pallas as pl
from jax.experimental.pallas import tpu as pltpu
from jax.sharding import PartitionSpec as P

K = 16
NY = 512
ITERS = 6
COLS = 8
EXT = 3 * COLS
LANES = 128
PACK = 80
BASIS = ITERS + 1
NEAR = 384
GROUPS = (BASIS * (BASIS + 1) // 2 + COLS - 1) // COLS
CHUNKS = 2

vertical_mix = 0.1
advection = 0.25
coriolis_scale = 0.3
gravity = 0.5
corner_weight = 0.25
shift = 5.0
scale = 4.0
LANE_P = 16
LANE_LC = 32
LANE_DIFF = 33
LANE_MT = 40
LANE_MU = 56
LANE_MV = 72
LANE_EDGE = 88

f32 = jnp.float32


def iota(shape, dim):
    return lax.broadcasted_iota(jnp.int32, shape, dim)


def thickness(k):
    return 0.5 * (0.5 + k / K)


def planetary(shape):
    latitude = (iota(shape, 1).astype(f32) + 0.5) / NY
    return coriolis_scale * (2.0 * latitude - 1.0)


def roll(value, amount, axis):
    return pltpu.roll(value, amount % value.shape[axis], axis)


def level_sum(value):
    weight = 0.5 * (0.5 + iota(value.shape, 0).astype(f32) / K)
    return jnp.sum(weight * value, axis=0, keepdims=True)


def two_sum(a, b):
    s = a + b
    t = s - a
    return s, (a - (s - t)) + (b - t)


def fast_two_sum(a, b):
    s = a + b
    return s, b - (s - a)


def split(a):
    c = 4097.0 * a
    high = c - (c - a)
    return high, a - high


def two_prod(a, b, a_parts=None, b_parts=None):
    ah, al = split(a) if a_parts is None else a_parts
    bh, bl = split(b) if b_parts is None else b_parts
    p = a * b
    return p, ((ah * bh - p) + ah * bl + al * bh) + al * bl


def pair_mul(a, b):
    p, e = two_prod(a[0], b[0])
    return p, e + (a[0] * b[1] + a[1] * b[0])


def pair_add(a, b):
    s, e = two_sum(a[0], b[0])
    return s, e + (a[1] + b[1])


def pair_norm(a):
    return fast_two_sum(a[0], a[1])


def pair_scale(a, factor):
    p, e = two_prod(a[0], factor)
    return p, e + a[1] * factor


def pair_tree(terms):
    while len(terms) > 1:
        pairs = [pair_add(terms[i], terms[i + 1]) for i in range(0, len(terms) - 1, 2)]
        terms = pairs + terms[len(terms) - len(terms) % 2:]
    return terms[0]


def pair_rows(a):
    for step in (4, 2, 1):
        a = pair_add(a, (roll(a[0], step, 0), roll(a[1], step, 0)))
    return a


def pair_pack(terms):
    shape = (COLS, LANES)
    sub = iota(shape, 0)
    zero = (jnp.zeros(shape, f32),) * 2
    terms = terms + [zero] * (COLS - len(terms))
    for step in (4, 2, 1):
        low = (sub & step) == 0
        merged = []
        for x, y in zip(terms[:step], terms[step:]):
            a = tuple(jnp.where(low, p, q) for p, q in zip(x, y))
            b = tuple(
                jnp.where(low, roll(p, -step, 0), roll(q, step, 0)) for p, q in zip(x, y)
            )
            merged.append(pair_add(a, b))
        terms = merged
    return terms[0]


def pack_kernel(
    tracer_in, zonal_in, meridional_in, count_in, diffusivity_in, surface_in, inner, outer,
    tracer, zonal, meridional, count, diffusivity, surface, edges, sems,
):
    shape = (COLS, NY)
    even = is_even()
    small = [
        pltpu.make_async_copy(a, b, sems.at[i])
        for i, (a, b) in enumerate(
            ((count_in, count), (diffusivity_in, diffusivity), (surface_in, surface))
        )
    ]
    large = []
    for c in range(CHUNKS):
        part = pl.ds(c * K // CHUNKS, K // CHUNKS)
        large.append(
            [
                pltpu.make_async_copy(a.at[part], b.at[part], sems.at[3 + 3 * c + i])
                for i, (a, b) in enumerate(
                    (
                        (zonal_in, zonal),
                        (meridional_in, meridional),
                        (tracer_in.at[:, :, NY - LANES:], tracer),
                    )
                )
            ]
        )
    rows = [
        pltpu.make_async_copy(
            field.at[:, x], edges.at[2 * base + i], sems.at[3 + 3 * CHUNKS + 2 * base + i]
        )
        for base, field in enumerate((tracer_in, zonal_in, meridional_in))
        for i, x in enumerate((0, COLS - 1))
    ]
    for copy in small + sum(large, []) + rows:
        copy.start()
    for copy in small:
        copy.wait()
    lc = count[...].astype(f32)
    diff = diffusivity[...]
    row, lane = iota(shape, 0), iota(shape, 1)
    tile_lane = iota((COLS, LANES), 1)
    lc_east, lc_north = roll(lc, -1, 0), roll(lc, -1, 1)
    total = jnp.zeros(shape, f32)
    turn = jnp.zeros(shape, f32)
    flux_x = jnp.zeros(shape, f32)
    flux_y = jnp.zeros(shape, f32)
    fold = jnp.zeros((COLS, LANES), f32)
    for k in range(K):
        if k % (K // CHUNKS) == 0:
            for copy in large[k // (K // CHUNKS)]:
                copy.wait()
        mask = lc > k
        t, u, v = tracer[k], zonal[k], meridional[k]
        for base, field in ((LANE_MT, t), (LANE_MU, u), (LANE_MV, v)):
            fold = jnp.where(tile_lane == base + k, field[:, -1:], fold)
        mu, mv = jnp.where(mask, u, 0.0), jnp.where(mask, v, 0.0)
        p = thickness(k) * (mu + mv)
        total += p
        turn += thickness(k) * (mv - mu)
        flux_x += jnp.where(mask, roll(p, -1, 0), 0.0) - jnp.where(lc_east > k, p, 0.0)
        flux_y += jnp.where(mask, roll(p, -1, 1), 0.0) - jnp.where(lc_north > k, p, 0.0)
    lc_fold = lc[:, NY - 1:]
    level = tile_lane - jnp.where(
        tile_lane < LANE_MU, LANE_MT, jnp.where(tile_lane < LANE_MV, LANE_MU, LANE_MV)
    )
    fold = jnp.where(level.astype(f32) < lc_fold, fold, 0.0)
    momentum = roll(fold, LANE_P - LANE_MU, 1) + roll(fold, LANE_P - LANE_MV, 1)
    fold = jnp.where((tile_lane >= LANE_P) & (tile_lane < LANE_P + K), momentum, fold)
    fold = jnp.where(tile_lane == LANE_LC, lc_fold, fold)
    fold = jnp.where(tile_lane == LANE_DIFF, diff[:, NY - 1:], fold)
    edge_level = iota((K, NY), 0).astype(f32)
    for copy in rows:
        copy.wait()
    for base in range(3):
        west, east = edges[2 * base], edges[2 * base + 1]
        west = jnp.where(edge_level < lc[:1], west, 0.0)
        east = jnp.where(edge_level < lc[COLS - 1:], east, 0.0)
        at = pl.ds(2 * COLS + base * K, K)
        inner[at] = jnp.where(even, east, west)
        outer[at] = jnp.where(even, west, east)
    flux_x = jnp.where(row == COLS - 1, 0.0, flux_x)
    flux_y = jnp.where(lane == NY - 1, 0.0, flux_y)
    west_flux = jnp.where(row == 0, 0.0, roll(flux_x, 1, 0))
    south_flux = jnp.where(lane == 0, 0.0, roll(flux_y, 1, 1))
    forcing = total + planetary(shape) * turn + diff * (
        flux_x - west_flux + flux_y - south_flux
    )
    coded = jnp.where(lc > 0, surface[...], -1.0)
    edge = jnp.zeros((K, LANES), f32)
    edge_lane = iota((K, LANES), 1)
    p = outer[32:48, NY - LANES:] + outer[48:64, NY - LANES:]
    edge_lc = jnp.where(even, lc[:1], lc[COLS - 1:])
    edge_diff = jnp.where(even, diff[:1], diff[COLS - 1:])
    for j in range(COLS):
        at = NY - 1 - j
        here = LANE_EDGE + j
        edge = jnp.where(edge_lane == here, p[:, LANES - 1 - j:LANES - j], edge)
        edge = jnp.where(edge_lane == here + COLS, edge_lc[:, at:at + 1], edge)
        edge = jnp.where(edge_lane == here + 2 * COLS, edge_diff[:, at:at + 1], edge)
    edge = [edge[:COLS], edge[COLS:]]
    zeros = jnp.zeros((COLS, NY - 3 * LANES), f32)
    for pack, mine, other in ((inner, COLS - 1, 0), (outer, 0, COLS - 1)):
        pack[0:COLS] = forcing
        pack[COLS:2 * COLS] = coded
        edge_lc = jnp.where(even, lc[mine:mine + 1], lc[other:other + 1])
        edge_diff = jnp.where(even, diff[mine:mine + 1], diff[other:other + 1])
        pack[64:72] = jnp.where(row == 0, edge_lc, jnp.where(row == 1, edge_diff, 0.0))
        pack[72:80] = jnp.concatenate([fold, *edge, zeros], axis=1)


def interface_flux(mine, theirs):
    level = iota((K, NY), 0).astype(f32)
    p_mine = mine[32:48] + mine[48:64]
    p_theirs = theirs[32:48] + theirs[48:64]
    return level_sum(
        jnp.where(level < mine[64:65], p_theirs, 0.0)
        - jnp.where(level < theirs[64:65], p_mine, 0.0)
    )


def is_even():
    return lax.axis_index("lon") % 2 == 0


def beside(even, west, east):
    return jnp.concatenate([jnp.where(even, west, east), jnp.where(even, east, west)], axis=0)


def chip_kernel(inner, sibling, forcing, coded, tile, near, far):
    even = is_even()
    flux = interface_flux(inner, sibling)
    own, other = inner[65:66] * flux, -sibling[65:66] * flux
    row = iota((2 * COLS, NY), 0)
    change = jnp.where(
        row == COLS - 1,
        jnp.where(even, own, other),
        jnp.where(row == COLS, jnp.where(even, other, own), 0.0),
    )
    full = beside(even, inner[:COLS], sibling[:COLS]) + change
    code = beside(even, inner[COLS:2 * COLS], sibling[COLS:2 * COLS])
    fold = beside(even, inner[72:80, :LANES], sibling[72:80, :LANES])
    forcing[...] = full
    coded[...] = code
    tile[...] = fold
    lane = iota((2 * COLS, LANES), 1)
    for j in range(COLS):
        at = NY - 1 - j
        fold = jnp.where(lane == j, full[:, at:at + 1], fold)
        fold = jnp.where(lane == COLS + j, code[:, at:at + 1], fold)
    fold = jnp.concatenate(
        [fold[i:i + 1] for i in range(2 * COLS - 1, -1, -1)], axis=0
    )
    for out, source in ((near, inner), (far, sibling)):
        edge = jnp.concatenate(
            [source[72:80, LANES:2 * LANES], source[72:80, 2 * LANES:3 * LANES]], axis=0
        )
        out[...] = jnp.where(lane >= LANE_EDGE, edge, fold)


def across_fold(even, chip, far):
    shape = (2 * COLS, LANES)
    level = iota(shape, 0).astype(f32)
    lane = iota((1, LANES), 1)
    flux = level_sum(
        jnp.where(level < roll(chip, -COLS, 1), far, 0.0)
        - jnp.where(level < roll(far, -COLS, 1), chip, 0.0)
    )

    def change(tile):
        return jnp.where(lane < COLS, roll(roll(tile[:1], -2 * COLS, 1) * flux, -LANE_EDGE, 1), 0.0)

    chip_change, far_change = change(chip), -change(far)
    tile = extend(even, far[COLS:], chip, far[:COLS])
    row = iota((EXT, LANES), 0)
    west = jnp.where(row == COLS - 1, far_change, jnp.where(row == COLS, chip_change, 0.0))
    east = jnp.where(
        row == 2 * COLS - 1, chip_change, jnp.where(row == 2 * COLS, far_change, 0.0)
    )
    return tile, jnp.where(even, west, east)


def extend(even, west, chip, east):
    return jnp.concatenate(
        [
            jnp.where(even, west, chip[:COLS]),
            jnp.where(even, chip[:COLS], chip[COLS:]),
            jnp.where(even, chip[COLS:], east),
        ],
        axis=0,
    )


def basis(start, code):
    ocean = code > 0
    centre = jnp.where(ocean, code / scale, 0.0)
    around = jnp.where(ocean, 1.0 / scale, 0.0)
    lane = iota(start.shape, 1)

    def operate(q):
        along = roll(q, -1, 1) + jnp.where(lane == 0, 0.0, roll(q, 1, 1))
        side = q + corner_weight * along
        return centre * q - around * (along + roll(side, 1, 0) + roll(side, -1, 0))

    v = [start, operate(start)]
    for j in range(2, BASIS):
        v.append(2.0 * operate(v[-1]) - v[-2])
    return v


def gram_rows(v, blocks):
    own = [[q[COLS:2 * COLS, c * LANES:(c + 1) * LANES] for c in blocks] for q in v]
    parts = [[split(q) for q in row] for row in own]
    entries = []
    for i in range(BASIS):
        for j in range(i, BASIS):
            terms = [
                two_prod(own[i][c], own[j][c], parts[i][c], parts[j][c])
                for c in range(len(blocks))
            ]
            entries.append(pair_tree(terms))
    return [pair_pack(entries[g:g + COLS]) for g in range(0, len(entries), COLS)]


def inner_kernel(outer, beyond, forcing, coded, last, last_code, vectors, partial):
    even = is_even()
    flux_out = interface_flux(outer, beyond)
    own, far = outer[65:66] * flux_out, -beyond[65:66] * flux_out
    row = iota((EXT, NY), 0)
    west = jnp.where(row == COLS - 1, far, jnp.where(row == COLS, own, 0.0))
    east = jnp.where(row == 2 * COLS - 1, own, jnp.where(row == 2 * COLS, far, 0.0))
    far_forcing, far_code = beyond[:COLS], beyond[COLS:2 * COLS]
    south = extend(even, far_forcing, forcing[...], far_forcing) + jnp.where(even, west, east)
    code = extend(even, far_code, coded[...], far_code)
    last[...] = south[:, NEAR - LANES:]
    last_code[...] = code[:, NEAR - LANES:]
    v = basis(south, code)
    for j in range(ITERS):
        vectors[j * EXT:(j + 1) * EXT] = v[j][:, :NEAR]
    for g, pair in enumerate(gram_rows(v, range(NEAR // LANES))):
        for at, part in zip((0, GROUPS * COLS), pair):
            partial[at + g * COLS:at + (g + 1) * COLS] = part


def fold_kernel(last, last_code, beyond, tile, mirror, mirror_far, partial, vectors, gram):
    even = is_even()
    lane = iota((EXT, LANES), 1)
    mine = beyond[72:80, :LANES]
    mine = extend(even, mine, tile[...], mine)
    theirs, between = across_fold(even, mirror[...], mirror_far[...])
    level = (lane - LANE_P).astype(f32)
    weight = jnp.where((lane >= LANE_P) & (lane < LANE_P + K), 0.5 * (0.5 + level / K), 0.0)
    mask_mine = (level < mine[:, LANE_LC:LANE_LC + 1]).astype(f32)
    mask_theirs = (level < theirs[:, LANE_LC:LANE_LC + 1]).astype(f32)
    flux = -jnp.sum(weight * (mask_mine * theirs + mask_theirs * mine), axis=1, keepdims=True)
    own_change = mine[:, LANE_DIFF:LANE_DIFF + 1] * flux
    far_change = theirs[:, LANE_DIFF:LANE_DIFF + 1] * flux
    north = jnp.where(lane < COLS, theirs, 0.0) + between
    north = north + jnp.where(lane == 0, far_change, 0.0)
    width = NY - NEAR + LANES
    south = last[...] + jnp.where(iota((EXT, width), 1) == width - 1, own_change, 0.0)
    north_code = jnp.where(lane < COLS, roll(theirs, -COLS, 1), -1.0)
    v = basis(
        jnp.concatenate([south, north], axis=1),
        jnp.concatenate([last_code[...], north_code], axis=1),
    )
    for j in range(ITERS):
        vectors[j * EXT:(j + 1) * EXT] = v[j][:, LANES:]
    size = GROUPS * COLS
    high, low = [], []
    for g, pair in enumerate(gram_rows(v, range(1, width // LANES))):
        at = g * COLS
        pair = pair_add(pair, (partial[at:at + COLS], partial[size + at:size + at + COLS]))
        high.append(pair[0])
        low.append(pair[1])
    turned = jnp.concatenate(high + low + [jnp.zeros((LANES - 2 * size, LANES), f32)], axis=0).T
    terms = [turned[i * COLS:(i + 1) * COLS] for i in range(LANES // COLS)]
    high, low = pair_norm(pair_rows(pair_tree([(t, roll(t, -size, 1)) for t in terms])))
    row = jnp.where(iota((COLS, LANES), 1) < size, high, roll(low, size, 1))
    gram[...] = row[:1]


def coefficients(gram):
    shape = (COLS, LANES)
    tiles = [gram[i * COLS:(i + 1) * COLS] for i in range(gram.shape[0] // COLS)]
    total = pair_norm(pair_rows(pair_tree([(t, roll(t, -GROUPS * COLS, 1)) for t in tiles])))
    wide = lambda column: jnp.broadcast_to(column, shape)
    sub = iota(shape, 0)
    tile_lane = iota(shape, 1)

    def column(j):
        low, high = jnp.minimum(sub, j), jnp.maximum(sub, j)
        entry = ((low * (2 * BASIS - 1 - low)) >> 1) + high
        here = (tile_lane == entry) & (sub < BASIS)
        return tuple(
            wide(jnp.sum(jnp.where(here, part, 0.0), axis=1, keepdims=True)) for part in total
        )

    matrix = [column(j) for j in range(BASIS)]
    first = (sub == 0).astype(f32)
    zero = jnp.zeros(shape, f32)

    def apply(b):
        half = scale / 2
        up = [half * jnp.where(sub == 0, 0.0, roll(part, 1, 0)) for part in b]
        up = [jnp.where(sub == 1, 2.0 * part, part) for part in up]
        down = [half * jnp.where(sub == COLS - 1, 0.0, roll(part, -1, 0)) for part in b]
        four = tuple(4.0 * part for part in b)
        return pair_add(pair_add(four, b), pair_add(tuple(up), tuple(down)))

    def times(vector, count):
        terms = []
        for j in range(count):
            at = tuple(wide(part[j:j + 1]) for part in vector)
            terms.append(pair_mul(matrix[j], at))
        return pair_tree(terms)

    def dot(a, b):
        s = pair_rows(pair_mul(a, b))
        return s[0] + s[1]

    residual = (first, zero)
    image = matrix[0]
    direction = residual
    solution = zero
    norm_now = wide(matrix[0][0][:1])
    floor = 1e-13 * norm_now
    alive = norm_now > 0
    for iteration in range(ITERS):
        applied = apply(direction)
        applied_image = times(applied, iteration + 2)
        curvature = dot(direction, applied_image)
        alive = alive & (curvature > 0)
        step = jnp.where(alive, norm_now / jnp.where(alive, curvature, 1.0), 0.0)
        solution = solution + step * direction[0]
        if iteration + 1 < ITERS:
            back = -step
            residual = pair_norm(pair_add(residual, pair_scale(applied, back)))
            image = pair_norm(pair_add(image, pair_scale(applied_image, back)))
            norm_next = dot(residual, image)
            ratio = jnp.where(alive, norm_next / jnp.where(alive, norm_now, 1.0), 0.0)
            direction = pair_norm(pair_add(residual, pair_scale(direction, ratio)))
            norm_now = norm_next
            alive = alive & (norm_now > floor)
    return solution


def finish_kernel(
    gram, vectors, vectors_last, zonal, meridional, levels, zonal_next, meridional_next, height
):
    x = coefficients(gram)
    total = []
    for part in (vectors, vectors_last):
        at = [x[j:j + 1, :1] * part[j * EXT:(j + 1) * EXT] for j in range(ITERS)]
        total.append(sum(at[1:], at[0]))
    total = jnp.concatenate(total, axis=1)
    own = total[COLS:2 * COLS, :NY]
    height[...] = own
    east = gravity * (roll(total, -1, 0)[COLS:2 * COLS, :NY] - own)
    north = gravity * (roll(total, -1, 1)[COLS:2 * COLS, :NY] - own)
    lc = levels[...]
    for k in range(K):
        zonal_next[k] = zonal[k] - jnp.where(lc > k, east, 0.0)
        meridional_next[k] = meridional[k] - jnp.where(lc > k, north, 0.0)


def neighbours(count, sibling, beyond, mirror):
    shape = (COLS, NY)
    even = is_even()
    row, lane = iota(shape, 0), iota(shape, 1)
    lc = count[...].astype(f32)
    north_tile = jnp.where(even, mirror[:COLS], mirror[COLS:])

    def around(field, west, east, north):
        return (
            jnp.where(row == COLS - 1, east, roll(field, -1, 0)),
            jnp.where(row == 0, west, roll(field, 1, 0)),
            jnp.where(lane == NY - 1, north, roll(field, -1, 1)),
            jnp.where(lane == 0, 0.0, roll(field, 1, 1)),
        )

    def edges(at):
        a, b = sibling[at:at + 1], beyond[at:at + 1]
        return jnp.where(even, b, a), jnp.where(even, a, b)

    def padded(field, base, k, sign):
        at = LANE_MT + base * K + k
        return around(field, *edges(2 * COLS + base * K + k), sign * north_tile[:, at:at + 1])

    west_lc, east_lc = edges(64)
    north_lc = north_tile[:, LANE_LC:LANE_LC + 1]

    def mask_sum(mask, k):
        inside = [(c > k).astype(f32) for c in (west_lc, east_lc, north_lc)]
        return sum(around(mask, *inside))

    return lc, padded, mask_sum


def tracer_kernel(
    tracer, zonal, meridional, count, diffusivity, sibling, beyond, mirror, after, tracer_next
):
    lc, padded, mask_sum = neighbours(count, sibling, beyond, mirror)
    diff = diffusivity[...]

    def masked(k):
        if k < 0 or k >= K:
            return jnp.zeros_like(lc), jnp.zeros_like(lc)
        mask = (lc > k).astype(f32)
        return mask, mask * tracer[k]

    below, here = masked(-1), masked(0)
    for k in range(K):
        above = masked(k + 1)
        mask, mt = here
        t, u, v = tracer[k], zonal[k], meridional[k]
        te, tw, tn, ts = padded(mt, 0, k, 1.0)
        vertical = above[1] + below[1] - (above[0] + below[0]) * t
        tracer_next[k] = mask * (
            t
            + diff * (te + tw + tn + ts - mask_sum(mask, k) * t)
            + vertical_mix * vertical
            - advection * (u * (te - tw) + v * (tn - ts))
        )
        below, here = here, above


def flow_kernel(
    zonal, meridional, count, diffusivity, sibling, beyond, mirror, after,
    zonal_step, meridional_step, levels,
):
    lc, padded, mask_sum = neighbours(count, sibling, beyond, mirror)
    diff = diffusivity[...]
    turn = planetary(lc.shape)
    levels[...] = lc
    for k in range(K):
        mask = (lc > k).astype(f32)
        u, v = zonal[k], meridional[k]
        sides = mask_sum(mask, k)
        zonal_sum = sum(padded(mask * u, 1, k, -1.0))
        meridional_sum = sum(padded(mask * v, 2, k, -1.0))
        zonal_step[k] = mask * (u + diff * (zonal_sum - sides * u) + turn * v)
        meridional_step[k] = mask * (v + diff * (meridional_sum - sides * v) - turn * u)


def call(kernel, shapes, *args, flops=0, after=None, scratch=(), stay=0):
    moved = 4 * sum(a.size for a in args) + 4 * sum(
        functools.reduce(lambda x, y: x * y, s, 1) for s in shapes
    )
    space = pl.BlockSpec(memory_space=pltpu.VMEM)
    anywhere = pl.BlockSpec(memory_space=pl.ANY)
    in_specs = [space] * (len(args) - stay) + [pl.BlockSpec(memory_space=pltpu.HBM)] * stay
    here = len(args) - stay
    args = args[:here] + tuple(
        pltpu.with_memory_space_constraint(a, pltpu.HBM) for a in args[here:]
    )
    if after is not None:
        in_specs.append(anywhere)
        args = args + (after,)
    return pl.pallas_call(
        kernel,
        out_shape=[jax.ShapeDtypeStruct(s, f32) for s in shapes],
        in_specs=in_specs,
        out_specs=[space] * len(shapes),
        scratch_shapes=list(scratch),
        compiler_params=pltpu.CompilerParams(vmem_limit_bytes=32 * 1024 * 1024),
        cost_estimate=pl.CostEstimate(flops=flops, bytes_accessed=moved, transcendentals=0),
    )(*args)


def body(tracer, zonal, meridional, count, diffusivity, surface):
    size = lax.axis_size("lon")
    block = (K, COLS, NY)

    def permute(value, pairs):
        return lax.ppermute(value, "lon", pairs)

    siblings = [(i, i ^ 1) for i in range(size)]
    outward = [(i, (i + 1 if i % 2 else i - 1) % size) for i in range(size)]
    mirrored = [(i, size - 1 - i) for i in range(size)]
    mirrored_far = [((size + 1 - 4 * (i % 2) - i) % size, i) for i in range(size)]
    arguments = (tracer, zonal, meridional, count, diffusivity, surface)
    inner, outer = call(
        pack_kernel, [(PACK, NY)] * 2, *arguments,
        scratch=[pltpu.VMEM((K, COLS, LANES), f32)]
        + [pltpu.VMEM(a.shape, a.dtype) for a in arguments[1:]]
        + [pltpu.VMEM((6, K, NY), f32), pltpu.SemaphoreType.DMA((9 + 3 * CHUNKS,))], stay=len(arguments),
    )
    beyond = permute(outer, outward)
    sibling = permute(inner, siblings)
    chip = (2 * COLS, NY)
    forcing, coded, tile, near, far = call(
        chip_kernel, [chip, chip] + [(2 * COLS, LANES)] * 3, inner, sibling
    )
    mirror = permute(near, mirrored)
    mirror_far = permute(far, mirrored_far)
    last_rows = (EXT, NY - NEAR + LANES)
    last, last_code, vectors, partial = call(
        inner_kernel,
        [last_rows, last_rows, (ITERS * EXT, NEAR), (2 * GROUPS * COLS, LANES)],
        outer, beyond, forcing, coded, flops=8192 * 100,
    )
    vectors_last, gram = call(
        fold_kernel,
        [(ITERS * EXT, NY - NEAR + LANES), (1, LANES)],
        last, last_code, beyond, tile, mirror, mirror_far, partial,
    )
    halos = (sibling, beyond, mirror)
    reach = 1
    tracer_next = None
    while reach < size:
        if 8 * reach >= size and tracer_next is None and reach > 1:
            tracer_next, = call(
                tracer_kernel, [block],
                tracer, zonal, meridional, count, diffusivity, *halos,
                flops=65536 * 40, after=gram,
            )
        other = permute(gram, [(i, i ^ (reach ^ 1 if reach > 1 else 1)) for i in range(size)])
        gram = jnp.concatenate([gram, other], axis=0)
        reach *= 2
        if 2 * reach == size:
            gram, tracer_next = lax.optimization_barrier((gram, tracer_next))
            zonal_step, meridional_step, levels = call(
                flow_kernel, [block, block, (COLS, NY)],
                zonal, meridional, count, diffusivity, *halos,
                flops=65536 * 40, after=gram,
            )
    zonal_next, meridional_next, height = call(
        finish_kernel, [block, block, (COLS, NY)],
        gram, vectors, vectors_last, zonal_step, meridional_step, levels,
    )
    return tracer_next, zonal_next, meridional_next, height


def solution(mesh):
    column = P("lon", None)
    field = P("ens", "lon", None)
    return jax.shard_map(
        body,
        mesh=mesh,
        in_specs=(field, field, field, column, column, column),
        out_specs=(field, field, field, P("lon", "ens")),
        check_vma=False,
    )
```

```python
import functools

import jax
import jax.numpy as jnp
from jax import lax
from jax.experimental import pallas as pl
from jax.experimental.pallas import tpu as pltpu
from jax.sharding import PartitionSpec as P

K = 16
NY = 512
ITERS = 6
COLS = 8
EXT = 3 * COLS
LANES = 128
PACK = 80
BASIS = ITERS + 1
NEAR = 384
GROUPS = (BASIS * (BASIS + 1) // 2 + COLS - 1) // COLS
CHUNKS = 2

vertical_mix = 0.1
advection = 0.25
coriolis_scale = 0.3
gravity = 0.5
corner_weight = 0.25
shift = 5.0
scale = 4.0
LANE_P = 16
LANE_LC = 32
LANE_DIFF = 33
LANE_MT = 40
LANE_MU = 56
LANE_MV = 72
LANE_EDGE = 88

f32 = jnp.float32


def iota(shape, dim):
    return lax.broadcasted_iota(jnp.int32, shape, dim)


def thickness(k):
    return 0.5 * (0.5 + k / K)


def planetary(shape):
    latitude = (iota(shape, 1).astype(f32) + 0.5) / NY
    return coriolis_scale * (2.0 * latitude - 1.0)


def roll(value, amount, axis):
    return pltpu.roll(value, amount % value.shape[axis], axis)


def level_sum(value):
    weight = 0.5 * (0.5 + iota(value.shape, 0).astype(f32) / K)
    return jnp.sum(weight * value, axis=0, keepdims=True)


def two_sum(a, b):
    s = a + b
    t = s - a
    return s, (a - (s - t)) + (b - t)


def fast_two_sum(a, b):
    s = a + b
    return s, b - (s - a)


def split(a):
    c = 4097.0 * a
    high = c - (c - a)
    return high, a - high


def two_prod(a, b, a_parts=None, b_parts=None):
    ah, al = split(a) if a_parts is None else a_parts
    bh, bl = split(b) if b_parts is None else b_parts
    p = a * b
    return p, ((ah * bh - p) + ah * bl + al * bh) + al * bl


def pair_mul(a, b):
    p, e = two_prod(a[0], b[0])
    return p, e + (a[0] * b[1] + a[1] * b[0])


def pair_add(a, b):
    s, e = two_sum(a[0], b[0])
    return s, e + (a[1] + b[1])


def pair_norm(a):
    return fast_two_sum(a[0], a[1])


def pair_scale(a, factor):
    p, e = two_prod(a[0], factor)
    return p, e + a[1] * factor


def pair_tree(terms):
    while len(terms) > 1:
        pairs = [pair_add(terms[i], terms[i + 1]) for i in range(0, len(terms) - 1, 2)]
        terms = pairs + terms[len(terms) - len(terms) % 2:]
    return terms[0]


def pair_rows(a):
    for step in (4, 2, 1):
        a = pair_add(a, (roll(a[0], step, 0), roll(a[1], step, 0)))
    return a


def pair_pack(terms):
    shape = (COLS, LANES)
    sub = iota(shape, 0)
    zero = (jnp.zeros(shape, f32),) * 2
    terms = terms + [zero] * (COLS - len(terms))
    for step in (4, 2, 1):
        low = (sub & step) == 0
        merged = []
        for x, y in zip(terms[:step], terms[step:]):
            a = tuple(jnp.where(low, p, q) for p, q in zip(x, y))
            b = tuple(
                jnp.where(low, roll(p, -step, 0), roll(q, step, 0)) for p, q in zip(x, y)
            )
            merged.append(pair_add(a, b))
        terms = merged
    return terms[0]


def pack_kernel(
    tracer_in, zonal_in, meridional_in, count_in, diffusivity_in, surface_in, inner, outer,
    tracer, zonal, meridional, count, diffusivity, surface, edges, sems,
):
    shape = (COLS, NY)
    even = is_even()
    small = [
        pltpu.make_async_copy(a, b, sems.at[i])
        for i, (a, b) in enumerate(
            ((count_in, count), (diffusivity_in, diffusivity), (surface_in, surface))
        )
    ]
    large = []
    for c in range(CHUNKS):
        part = pl.ds(c * K // CHUNKS, K // CHUNKS)
        large.append(
            [
                pltpu.make_async_copy(a.at[part], b.at[part], sems.at[3 + 3 * c + i])
                for i, (a, b) in enumerate(
                    (
                        (zonal_in, zonal),
                        (meridional_in, meridional),
                        (tracer_in.at[:, :, NY - LANES:], tracer),
                    )
                )
            ]
        )
    rows = [
        pltpu.make_async_copy(
            field.at[:, x], edges.at[2 * base + i], sems.at[3 + 3 * CHUNKS + 2 * base + i]
        )
        for base, field in enumerate((tracer_in, zonal_in, meridional_in))
        for i, x in enumerate((0, COLS - 1))
    ]
    for copy in small + sum(large, []) + rows:
        copy.start()
    for copy in small:
        copy.wait()
    lc = count[...].astype(f32)
    diff = diffusivity[...]
    row, lane = iota(shape, 0), iota(shape, 1)
    tile_lane = iota((COLS, LANES), 1)
    lc_east, lc_north = roll(lc, -1, 0), roll(lc, -1, 1)
    total = jnp.zeros(shape, f32)
    turn = jnp.zeros(shape, f32)
    flux_x = jnp.zeros(shape, f32)
    flux_y = jnp.zeros(shape, f32)
    fold = jnp.zeros((COLS, LANES), f32)
    for k in range(K):
        if k % (K // CHUNKS) == 0:
            for copy in large[k // (K // CHUNKS)]:
                copy.wait()
        mask = lc > k
        t, u, v = tracer[k], zonal[k], meridional[k]
        for base, field in ((LANE_MT, t), (LANE_MU, u), (LANE_MV, v)):
            fold = jnp.where(tile_lane == base + k, field[:, -1:], fold)
        mu, mv = jnp.where(mask, u, 0.0), jnp.where(mask, v, 0.0)
        p = thickness(k) * (mu + mv)
        total += p
        turn += thickness(k) * (mv - mu)
        flux_x += jnp.where(mask, roll(p, -1, 0), 0.0) - jnp.where(lc_east > k, p, 0.0)
        flux_y += jnp.where(mask, roll(p, -1, 1), 0.0) - jnp.where(lc_north > k, p, 0.0)
    lc_fold = lc[:, NY - 1:]
    level = tile_lane - jnp.where(
        tile_lane < LANE_MU, LANE_MT, jnp.where(tile_lane < LANE_MV, LANE_MU, LANE_MV)
    )
    fold = jnp.where(level.astype(f32) < lc_fold, fold, 0.0)
    momentum = roll(fold, LANE_P - LANE_MU, 1) + roll(fold, LANE_P - LANE_MV, 1)
    fold = jnp.where((tile_lane >= LANE_P) & (tile_lane < LANE_P + K), momentum, fold)
    fold = jnp.where(tile_lane == LANE_LC, lc_fold, fold)
    fold = jnp.where(tile_lane == LANE_DIFF, diff[:, NY - 1:], fold)
    edge_level = iota((K, NY), 0).astype(f32)
    for copy in rows:
        copy.wait()
    for base in range(3):
        west, east = edges[2 * base], edges[2 * base + 1]
        west = jnp.where(edge_level < lc[:1], west, 0.0)
        east = jnp.where(edge_level < lc[COLS - 1:], east, 0.0)
        at = pl.ds(2 * COLS + base * K, K)
        inner[at] = jnp.where(even, east, west)
        outer[at] = jnp.where(even, west, east)
    flux_x = jnp.where(row == COLS - 1, 0.0, flux_x)
    flux_y = jnp.where(lane == NY - 1, 0.0, flux_y)
    west_flux = jnp.where(row == 0, 0.0, roll(flux_x, 1, 0))
    south_flux = jnp.where(lane == 0, 0.0, roll(flux_y, 1, 1))
    forcing = total + planetary(shape) * turn + diff * (
        flux_x - west_flux + flux_y - south_flux
    )
    coded = jnp.where(lc > 0, surface[...], -1.0)
    edge = jnp.zeros((K, LANES), f32)
    edge_lane = iota((K, LANES), 1)
    p = outer[32:48, NY - LANES:] + outer[48:64, NY - LANES:]
    edge_lc = jnp.where(even, lc[:1], lc[COLS - 1:])
    edge_diff = jnp.where(even, diff[:1], diff[COLS - 1:])
    for j in range(COLS):
        at = NY - 1 - j
        here = LANE_EDGE + j
        edge = jnp.where(edge_lane == here, p[:, LANES - 1 - j:LANES - j], edge)
        edge = jnp.where(edge_lane == here + COLS, edge_lc[:, at:at + 1], edge)
        edge = jnp.where(edge_lane == here + 2 * COLS, edge_diff[:, at:at + 1], edge)
    edge = [edge[:COLS], edge[COLS:]]
    zeros = jnp.zeros((COLS, NY - 3 * LANES), f32)
    for pack, mine, other in ((inner, COLS - 1, 0), (outer, 0, COLS - 1)):
        pack[0:COLS] = forcing
        pack[COLS:2 * COLS] = coded
        edge_lc = jnp.where(even, lc[mine:mine + 1], lc[other:other + 1])
        edge_diff = jnp.where(even, diff[mine:mine + 1], diff[other:other + 1])
        pack[64:72] = jnp.where(row == 0, edge_lc, jnp.where(row == 1, edge_diff, 0.0))
        pack[72:80] = jnp.concatenate([fold, *edge, zeros], axis=1)


def interface_flux(mine, theirs):
    level = iota((K, NY), 0).astype(f32)
    p_mine = mine[32:48] + mine[48:64]
    p_theirs = theirs[32:48] + theirs[48:64]
    return level_sum(
        jnp.where(level < mine[64:65], p_theirs, 0.0)
        - jnp.where(level < theirs[64:65], p_mine, 0.0)
    )


def is_even():
    return lax.axis_index("lon") % 2 == 0


def beside(even, west, east):
    return jnp.concatenate([jnp.where(even, west, east), jnp.where(even, east, west)], axis=0)


def chip_kernel(inner, sibling, forcing, coded, tile, near, far):
    even = is_even()
    flux = interface_flux(inner, sibling)
    own, other = inner[65:66] * flux, -sibling[65:66] * flux
    row = iota((2 * COLS, NY), 0)
    change = jnp.where(
        row == COLS - 1,
        jnp.where(even, own, other),
        jnp.where(row == COLS, jnp.where(even, other, own), 0.0),
    )
    full = beside(even, inner[:COLS], sibling[:COLS]) + change
    code = beside(even, inner[COLS:2 * COLS], sibling[COLS:2 * COLS])
    fold = beside(even, inner[72:80, :LANES], sibling[72:80, :LANES])
    forcing[...] = full
    coded[...] = code
    tile[...] = fold
    lane = iota((2 * COLS, LANES), 1)
    for j in range(COLS):
        at = NY - 1 - j
        fold = jnp.where(lane == j, full[:, at:at + 1], fold)
        fold = jnp.where(lane == COLS + j, code[:, at:at + 1], fold)
    fold = jnp.concatenate(
        [fold[i:i + 1] for i in range(2 * COLS - 1, -1, -1)], axis=0
    )
    for out, source in ((near, inner), (far, sibling)):
        edge = jnp.concatenate(
            [source[72:80, LANES:2 * LANES], source[72:80, 2 * LANES:3 * LANES]], axis=0
        )
        out[...] = jnp.where(lane >= LANE_EDGE, edge, fold)


def across_fold(even, chip, far):
    shape = (2 * COLS, LANES)
    level = iota(shape, 0).astype(f32)
    lane = iota((1, LANES), 1)
    flux = level_sum(
        jnp.where(level < roll(chip, -COLS, 1), far, 0.0)
        - jnp.where(level < roll(far, -COLS, 1), chip, 0.0)
    )

    def change(tile):
        return jnp.where(lane < COLS, roll(roll(tile[:1], -2 * COLS, 1) * flux, -LANE_EDGE, 1), 0.0)

    chip_change, far_change = change(chip), -change(far)
    tile = extend(even, far[COLS:], chip, far[:COLS])
    row = iota((EXT, LANES), 0)
    west = jnp.where(row == COLS - 1, far_change, jnp.where(row == COLS, chip_change, 0.0))
    east = jnp.where(
        row == 2 * COLS - 1, chip_change, jnp.where(row == 2 * COLS, far_change, 0.0)
    )
    return tile, jnp.where(even, west, east)


def extend(even, west, chip, east):
    return jnp.concatenate(
        [
            jnp.where(even, west, chip[:COLS]),
            jnp.where(even, chip[:COLS], chip[COLS:]),
            jnp.where(even, chip[COLS:], east),
        ],
        axis=0,
    )


def basis(start, code):
    ocean = code > 0
    centre = jnp.where(ocean, code / scale, 0.0)
    around = jnp.where(ocean, 1.0 / scale, 0.0)
    lane = iota(start.shape, 1)

    def operate(q):
        along = roll(q, -1, 1) + jnp.where(lane == 0, 0.0, roll(q, 1, 1))
        side = q + corner_weight * along
        return centre * q - around * (along + roll(side, 1, 0) + roll(side, -1, 0))

    v = [start, operate(start)]
    for j in range(2, BASIS):
        v.append(2.0 * operate(v[-1]) - v[-2])
    return v


def gram_rows(v, blocks):
    own = [[q[COLS:2 * COLS, c * LANES:(c + 1) * LANES] for c in blocks] for q in v]
    parts = [[split(q) for q in row] for row in own]
    entries = []
    for i in range(BASIS):
        for j in range(i, BASIS):
            terms = [
                two_prod(own[i][c], own[j][c], parts[i][c], parts[j][c])
                for c in range(len(blocks))
            ]
            entries.append(pair_tree(terms))
    return [pair_pack(entries[g:g + COLS]) for g in range(0, len(entries), COLS)]


def inner_kernel(outer, beyond, forcing, coded, last, last_code, vectors, partial):
    even = is_even()
    flux_out = interface_flux(outer, beyond)
    own, far = outer[65:66] * flux_out, -beyond[65:66] * flux_out
    row = iota((EXT, NY), 0)
    west = jnp.where(row == COLS - 1, far, jnp.where(row == COLS, own, 0.0))
    east = jnp.where(row == 2 * COLS - 1, own, jnp.where(row == 2 * COLS, far, 0.0))
    far_forcing, far_code = beyond[:COLS], beyond[COLS:2 * COLS]
    south = extend(even, far_forcing, forcing[...], far_forcing) + jnp.where(even, west, east)
    code = extend(even, far_code, coded[...], far_code)
    last[...] = south[:, NEAR - LANES:]
    last_code[...] = code[:, NEAR - LANES:]
    v = basis(south, code)
    for j in range(ITERS):
        vectors[j * EXT:(j + 1) * EXT] = v[j][:, :NEAR]
    for g, pair in enumerate(gram_rows(v, range(NEAR // LANES))):
        for at, part in zip((0, GROUPS * COLS), pair):
            partial[at + g * COLS:at + (g + 1) * COLS] = part


def fold_kernel(last, last_code, beyond, tile, mirror, mirror_far, partial, vectors, gram):
    even = is_even()
    lane = iota((EXT, LANES), 1)
    mine = beyond[72:80, :LANES]
    mine = extend(even, mine, tile[...], mine)
    theirs, between = across_fold(even, mirror[...], mirror_far[...])
    level = (lane - LANE_P).astype(f32)
    weight = jnp.where((lane >= LANE_P) & (lane < LANE_P + K), 0.5 * (0.5 + level / K), 0.0)
    mask_mine = (level < mine[:, LANE_LC:LANE_LC + 1]).astype(f32)
    mask_theirs = (level < theirs[:, LANE_LC:LANE_LC + 1]).astype(f32)
    flux = -jnp.sum(weight * (mask_mine * theirs + mask_theirs * mine), axis=1, keepdims=True)
    own_change = mine[:, LANE_DIFF:LANE_DIFF + 1] * flux
    far_change = theirs[:, LANE_DIFF:LANE_DIFF + 1] * flux
    north = jnp.where(lane < COLS, theirs, 0.0) + between
    north = north + jnp.where(lane == 0, far_change, 0.0)
    width = NY - NEAR + LANES
    south = last[...] + jnp.where(iota((EXT, width), 1) == width - 1, own_change, 0.0)
    north_code = jnp.where(lane < COLS, roll(theirs, -COLS, 1), -1.0)
    v = basis(
        jnp.concatenate([south, north], axis=1),
        jnp.concatenate([last_code[...], north_code], axis=1),
    )
    for j in range(ITERS):
        vectors[j * EXT:(j + 1) * EXT] = v[j][:, LANES:]
    size = GROUPS * COLS
    high, low = [], []
    for g, pair in enumerate(gram_rows(v, range(1, width // LANES))):
        at = g * COLS
        pair = pair_add(pair, (partial[at:at + COLS], partial[size + at:size + at + COLS]))
        high.append(pair[0])
        low.append(pair[1])
    turned = jnp.concatenate(high + low + [jnp.zeros((LANES - 2 * size, LANES), f32)], axis=0).T
    terms = [turned[i * COLS:(i + 1) * COLS] for i in range(LANES // COLS)]
    high, low = pair_norm(pair_rows(pair_tree([(t, roll(t, -size, 1)) for t in terms])))
    row = jnp.where(iota((COLS, LANES), 1) < size, high, roll(low, size, 1))
    gram[...] = jnp.broadcast_to(row[:1], gram.shape)


def coefficients(gram):
    shape = (COLS, LANES)
    tiles = [gram[i * COLS:(i + 1) * COLS] for i in range(gram.shape[0] // COLS)]
    total = pair_norm(pair_rows(pair_tree([(t, roll(t, -GROUPS * COLS, 1)) for t in tiles])))
    wide = lambda column: jnp.broadcast_to(column, shape)
    sub = iota(shape, 0)
    tile_lane = iota(shape, 1)

    def column(j):
        low, high = jnp.minimum(sub, j), jnp.maximum(sub, j)
        entry = ((low * (2 * BASIS - 1 - low)) >> 1) + high
        here = (tile_lane == entry) & (sub < BASIS)
        return tuple(
            wide(jnp.sum(jnp.where(here, part, 0.0), axis=1, keepdims=True)) for part in total
        )

    matrix = [column(j) for j in range(BASIS)]
    first = (sub == 0).astype(f32)
    zero = jnp.zeros(shape, f32)

    def apply(b):
        half = scale / 2
        up = [half * jnp.where(sub == 0, 0.0, roll(part, 1, 0)) for part in b]
        up = [jnp.where(sub == 1, 2.0 * part, part) for part in up]
        down = [half * jnp.where(sub == COLS - 1, 0.0, roll(part, -1, 0)) for part in b]
        four = tuple(4.0 * part for part in b)
        return pair_add(pair_add(four, b), pair_add(tuple(up), tuple(down)))

    def times(vector, count):
        terms = []
        for j in range(count):
            at = tuple(wide(part[j:j + 1]) for part in vector)
            terms.append(pair_mul(matrix[j], at))
        return pair_tree(terms)

    def dot(a, b):
        s = pair_rows(pair_mul(a, b))
        return s[0] + s[1]

    residual = (first, zero)
    image = matrix[0]
    direction = residual
    solution = zero
    norm_now = wide(matrix[0][0][:1])
    floor = 1e-13 * norm_now
    alive = norm_now > 0
    for iteration in range(ITERS):
        applied = apply(direction)
        applied_image = times(applied, iteration + 2)
        curvature = dot(direction, applied_image)
        alive = alive & (curvature > 0)
        step = jnp.where(alive, norm_now / jnp.where(alive, curvature, 1.0), 0.0)
        solution = solution + step * direction[0]
        if iteration + 1 < ITERS:
            back = -step
            residual = pair_norm(pair_add(residual, pair_scale(applied, back)))
            image = pair_norm(pair_add(image, pair_scale(applied_image, back)))
            norm_next = dot(residual, image)
            ratio = jnp.where(alive, norm_next / jnp.where(alive, norm_now, 1.0), 0.0)
            direction = pair_norm(pair_add(residual, pair_scale(direction, ratio)))
            norm_now = norm_next
            alive = alive & (norm_now > floor)
    return solution


def finish_kernel(
    gram, vectors, vectors_last, zonal, meridional, levels, zonal_next, meridional_next, height
):
    x = coefficients(gram)
    total = []
    for part in (vectors, vectors_last):
        at = [x[j:j + 1, :1] * part[j * EXT:(j + 1) * EXT] for j in range(ITERS)]
        total.append(sum(at[1:], at[0]))
    total = jnp.concatenate(total, axis=1)
    own = total[COLS:2 * COLS, :NY]
    height[...] = own
    east = gravity * (roll(total, -1, 0)[COLS:2 * COLS, :NY] - own)
    north = gravity * (roll(total, -1, 1)[COLS:2 * COLS, :NY] - own)
    lc = levels[...]
    for k in range(K):
        zonal_next[k] = zonal[k] - jnp.where(lc > k, east, 0.0)
        meridional_next[k] = meridional[k] - jnp.where(lc > k, north, 0.0)


def neighbours(count, sibling, beyond, mirror):
    shape = (COLS, NY)
    even = is_even()
    row, lane = iota(shape, 0), iota(shape, 1)
    lc = count[...].astype(f32)
    north_tile = jnp.where(even, mirror[:COLS], mirror[COLS:])

    def around(field, west, east, north):
        return (
            jnp.where(row == COLS - 1, east, roll(field, -1, 0)),
            jnp.where(row == 0, west, roll(field, 1, 0)),
            jnp.where(lane == NY - 1, north, roll(field, -1, 1)),
            jnp.where(lane == 0, 0.0, roll(field, 1, 1)),
        )

    def edges(at):
        a, b = sibling[at:at + 1], beyond[at:at + 1]
        return jnp.where(even, b, a), jnp.where(even, a, b)

    def padded(field, base, k, sign):
        at = LANE_MT + base * K + k
        return around(field, *edges(2 * COLS + base * K + k), sign * north_tile[:, at:at + 1])

    west_lc, east_lc = edges(64)
    north_lc = north_tile[:, LANE_LC:LANE_LC + 1]

    def mask_sum(mask, k):
        inside = [(c > k).astype(f32) for c in (west_lc, east_lc, north_lc)]
        return sum(around(mask, *inside))

    return lc, padded, mask_sum


def tracer_kernel(
    tracer, zonal, meridional, count, diffusivity, sibling, beyond, mirror, tracer_next
):
    lc, padded, mask_sum = neighbours(count, sibling, beyond, mirror)
    diff = diffusivity[...]

    def masked(k):
        if k < 0 or k >= K:
            return jnp.zeros_like(lc), jnp.zeros_like(lc)
        mask = (lc > k).astype(f32)
        return mask, mask * tracer[k]

    below, here = masked(-1), masked(0)
    for k in range(K):
        above = masked(k + 1)
        mask, mt = here
        t, u, v = tracer[k], zonal[k], meridional[k]
        te, tw, tn, ts = padded(mt, 0, k, 1.0)
        vertical = above[1] + below[1] - (above[0] + below[0]) * t
        tracer_next[k] = mask * (
            t
            + diff * (te + tw + tn + ts - mask_sum(mask, k) * t)
            + vertical_mix * vertical
            - advection * (u * (te - tw) + v * (tn - ts))
        )
        below, here = here, above


def flow_kernel(
    zonal, meridional, count, diffusivity, sibling, beyond, mirror,
    zonal_step, meridional_step, levels,
):
    lc, padded, mask_sum = neighbours(count, sibling, beyond, mirror)
    diff = diffusivity[...]
    turn = planetary(lc.shape)
    levels[...] = lc
    for k in range(K):
        mask = (lc > k).astype(f32)
        u, v = zonal[k], meridional[k]
        sides = mask_sum(mask, k)
        zonal_sum = sum(padded(mask * u, 1, k, -1.0))
        meridional_sum = sum(padded(mask * v, 2, k, -1.0))
        zonal_step[k] = mask * (u + diff * (zonal_sum - sides * u) + turn * v)
        meridional_step[k] = mask * (v + diff * (meridional_sum - sides * v) - turn * u)


def call(kernel, shapes, *args, flops=0, scratch=(), stay=0):
    moved = 4 * sum(a.size for a in args) + 4 * sum(
        functools.reduce(lambda x, y: x * y, s, 1) for s in shapes
    )
    space = pl.BlockSpec(memory_space=pltpu.VMEM)
    in_specs = [space] * (len(args) - stay) + [pl.BlockSpec(memory_space=pltpu.HBM)] * stay
    here = len(args) - stay
    args = args[:here] + tuple(
        pltpu.with_memory_space_constraint(a, pltpu.HBM) for a in args[here:]
    )
    return pl.pallas_call(
        kernel,
        out_shape=[jax.ShapeDtypeStruct(s, f32) for s in shapes],
        in_specs=in_specs,
        out_specs=[space] * len(shapes),
        scratch_shapes=list(scratch),
        compiler_params=pltpu.CompilerParams(vmem_limit_bytes=32 * 1024 * 1024),
        cost_estimate=pl.CostEstimate(flops=flops, bytes_accessed=moved, transcendentals=0),
    )(*args)


def body(tracer, zonal, meridional, count, diffusivity, surface):
    size = lax.axis_size("lon")
    block = (K, COLS, NY)

    def permute(value, pairs):
        return lax.ppermute(value, "lon", pairs)

    siblings = [(i, i ^ 1) for i in range(size)]
    outward = [(i, (i + 1 if i % 2 else i - 1) % size) for i in range(size)]
    mirrored = [(i, size - 1 - i) for i in range(size)]
    mirrored_far = [((size + 1 - 4 * (i % 2) - i) % size, i) for i in range(size)]
    arguments = (tracer, zonal, meridional, count, diffusivity, surface)
    inner, outer = call(
        pack_kernel, [(PACK, NY)] * 2, *arguments,
        scratch=[pltpu.VMEM((K, COLS, LANES), f32)]
        + [pltpu.VMEM(a.shape, a.dtype) for a in arguments[1:]]
        + [pltpu.VMEM((6, K, NY), f32), pltpu.SemaphoreType.DMA((9 + 3 * CHUNKS,))], stay=len(arguments),
    )
    beyond = permute(outer, outward)
    sibling = permute(inner, siblings)
    chip = (2 * COLS, NY)
    forcing, coded, tile, near, far = call(
        chip_kernel, [chip, chip] + [(2 * COLS, LANES)] * 3, inner, sibling
    )
    mirror = permute(near, mirrored)
    mirror_far = permute(far, mirrored_far)
    last_rows = (EXT, NY - NEAR + LANES)
    last, last_code, vectors, partial = call(
        inner_kernel,
        [last_rows, last_rows, (ITERS * EXT, NEAR), (2 * GROUPS * COLS, LANES)],
        outer, beyond, forcing, coded, flops=8192 * 100,
    )
    vectors_last, gram = call(
        fold_kernel,
        [(ITERS * EXT, NY - NEAR + LANES), (size, LANES)],
        last, last_code, beyond, tile, mirror, mirror_far, partial,
    )
    halos = (sibling, beyond, mirror)
    tracer_next, = call(
        tracer_kernel, [block],
        tracer, zonal, meridional, count, diffusivity, *halos,
        flops=65536 * 40,
    )
    zonal_step, meridional_step, levels = call(
        flow_kernel, [block, block, (COLS, NY)],
        zonal, meridional, count, diffusivity, *halos,
        flops=65536 * 40,
    )
    group = [(i + size // 2 + 1) % size for i in range(size)]
    gram = lax.all_to_all(gram, "lon", 0, 0, tiled=True, axis_index_groups=[group])
    zonal_next, meridional_next, height = call(
        finish_kernel, [block, block, (COLS, NY)],
        gram, vectors, vectors_last, zonal_step, meridional_step, levels,
    )
    return tracer_next, zonal_next, meridional_next, height


def solution(mesh):
    column = P("lon", None)
    field = P("ens", "lon", None)
    return jax.shard_map(
        body,
        mesh=mesh,
        in_specs=(field, field, field, column, column, column),
        out_specs=(field, field, field, P("lon", "ens")),
        check_vma=False,
    )
```

```python
import functools

import jax
import jax.numpy as jnp
from jax import lax
from jax.experimental import pallas as pl
from jax.experimental.pallas import tpu as pltpu
from jax.sharding import PartitionSpec as P

K = 16
NY = 512
ITERS = 6
COLS = 8
EXT = 3 * COLS
LANES = 128
PACK = 80
BASIS = ITERS + 1
CUT = NY - COLS
GROUPS = (BASIS * (BASIS + 1) // 2 + COLS - 1) // COLS
CHUNKS = 2

vertical_mix = 0.1
advection = 0.25
coriolis_scale = 0.3
gravity = 0.5
corner_weight = 0.25
shift = 5.0
scale = 4.0
LANE_P = 16
LANE_LC = 32
LANE_DIFF = 33
LANE_MT = 40
LANE_MU = 56
LANE_MV = 72
LANE_EDGE = 88
LANE_CODE = LANES - 2 * COLS
LANE_F = LANES - COLS

f32 = jnp.float32


def iota(shape, dim):
    return lax.broadcasted_iota(jnp.int32, shape, dim)


def thickness(k):
    return 0.5 * (0.5 + k / K)


def planetary(shape):
    latitude = (iota(shape, 1).astype(f32) + 0.5) / NY
    return coriolis_scale * (2.0 * latitude - 1.0)


def roll(value, amount, axis):
    return pltpu.roll(value, amount % value.shape[axis], axis)


def level_sum(value):
    weight = 0.5 * (0.5 + iota(value.shape, 0).astype(f32) / K)
    return jnp.sum(weight * value, axis=0, keepdims=True)


def two_sum(a, b):
    s = a + b
    t = s - a
    return s, (a - (s - t)) + (b - t)


def fast_two_sum(a, b):
    s = a + b
    return s, b - (s - a)


def split(a):
    c = 4097.0 * a
    high = c - (c - a)
    return high, a - high


def two_prod(a, b, a_parts=None, b_parts=None):
    ah, al = split(a) if a_parts is None else a_parts
    bh, bl = split(b) if b_parts is None else b_parts
    p = a * b
    return p, ((ah * bh - p) + ah * bl + al * bh) + al * bl


def pair_mul(a, b):
    p, e = two_prod(a[0], b[0])
    return p, e + (a[0] * b[1] + a[1] * b[0])


def pair_add(a, b):
    s, e = two_sum(a[0], b[0])
    return s, e + (a[1] + b[1])


def pair_norm(a):
    return fast_two_sum(a[0], a[1])


def pair_scale(a, factor):
    p, e = two_prod(a[0], factor)
    return p, e + a[1] * factor


def pair_tree(terms):
    while len(terms) > 1:
        pairs = [pair_add(terms[i], terms[i + 1]) for i in range(0, len(terms) - 1, 2)]
        terms = pairs + terms[len(terms) - len(terms) % 2:]
    return terms[0]


def pair_rows(a):
    for step in (4, 2, 1):
        a = pair_add(a, (roll(a[0], step, 0), roll(a[1], step, 0)))
    return a


def pair_pack(terms):
    shape = (COLS, LANES)
    sub = iota(shape, 0)
    zero = (jnp.zeros(shape, f32),) * 2
    terms = terms + [zero] * (COLS - len(terms))
    for step in (4, 2, 1):
        low = (sub & step) == 0
        merged = []
        for x, y in zip(terms[:step], terms[step:]):
            a = tuple(jnp.where(low, p, q) for p, q in zip(x, y))
            b = tuple(
                jnp.where(low, roll(p, -step, 0), roll(q, step, 0)) for p, q in zip(x, y)
            )
            merged.append(pair_add(a, b))
        terms = merged
    return terms[0]


def pack_kernel(
    tracer_in, zonal_in, meridional_in, count_in, diffusivity_in, surface_in, inner, outer,
    tracer, zonal, meridional, count, diffusivity, surface, edges, sems,
):
    shape = (COLS, NY)
    even = is_even()
    small = [
        pltpu.make_async_copy(a, b, sems.at[i])
        for i, (a, b) in enumerate(
            ((count_in, count), (diffusivity_in, diffusivity), (surface_in, surface))
        )
    ]
    large = []
    for c in range(CHUNKS):
        part = pl.ds(c * K // CHUNKS, K // CHUNKS)
        large.append(
            [
                pltpu.make_async_copy(a.at[part], b.at[part], sems.at[3 + 3 * c + i])
                for i, (a, b) in enumerate(
                    (
                        (zonal_in, zonal),
                        (meridional_in, meridional),
                        (tracer_in.at[:, :, NY - LANES:], tracer),
                    )
                )
            ]
        )
    rows = [
        pltpu.make_async_copy(
            field.at[:, x], edges.at[2 * base + i], sems.at[3 + 3 * CHUNKS + 2 * base + i]
        )
        for base, field in enumerate((tracer_in, zonal_in, meridional_in))
        for i, x in enumerate((0, COLS - 1))
    ]
    for copy in small + sum(large, []) + rows:
        copy.start()
    for copy in small:
        copy.wait()
    lc = count[...].astype(f32)
    diff = diffusivity[...]
    row, lane = iota(shape, 0), iota(shape, 1)
    tile_lane = iota((COLS, LANES), 1)
    lc_east, lc_north = roll(lc, -1, 0), roll(lc, -1, 1)
    total = jnp.zeros(shape, f32)
    turn = jnp.zeros(shape, f32)
    flux_x = jnp.zeros(shape, f32)
    flux_y = jnp.zeros(shape, f32)
    fold = jnp.zeros((COLS, LANES), f32)
    for k in range(K):
        if k % (K // CHUNKS) == 0:
            for copy in large[k // (K // CHUNKS)]:
                copy.wait()
        mask = lc > k
        t, u, v = tracer[k], zonal[k], meridional[k]
        for base, field in ((LANE_MT, t), (LANE_MU, u), (LANE_MV, v)):
            fold = jnp.where(tile_lane == base + k, field[:, -1:], fold)
        mu, mv = jnp.where(mask, u, 0.0), jnp.where(mask, v, 0.0)
        p = thickness(k) * (mu + mv)
        total += p
        turn += thickness(k) * (mv - mu)
        flux_x += jnp.where(mask, roll(p, -1, 0), 0.0) - jnp.where(lc_east > k, p, 0.0)
        flux_y += jnp.where(mask, roll(p, -1, 1), 0.0) - jnp.where(lc_north > k, p, 0.0)
    lc_fold = lc[:, NY - 1:]
    level = tile_lane - jnp.where(
        tile_lane < LANE_MU, LANE_MT, jnp.where(tile_lane < LANE_MV, LANE_MU, LANE_MV)
    )
    fold = jnp.where(level.astype(f32) < lc_fold, fold, 0.0)
    momentum = roll(fold, LANE_P - LANE_MU, 1) + roll(fold, LANE_P - LANE_MV, 1)
    fold = jnp.where((tile_lane >= LANE_P) & (tile_lane < LANE_P + K), momentum, fold)
    fold = jnp.where(tile_lane == LANE_LC, lc_fold, fold)
    fold = jnp.where(tile_lane == LANE_DIFF, diff[:, NY - 1:], fold)
    edge_level = iota((K, NY), 0).astype(f32)
    for copy in rows:
        copy.wait()
    for base in range(3):
        west, east = edges[2 * base], edges[2 * base + 1]
        west = jnp.where(edge_level < lc[:1], west, 0.0)
        east = jnp.where(edge_level < lc[COLS - 1:], east, 0.0)
        at = pl.ds(2 * COLS + base * K, K)
        inner[at] = jnp.where(even, east, west)
        outer[at] = jnp.where(even, west, east)
    flux_x = jnp.where(row == COLS - 1, 0.0, flux_x)
    flux_y = jnp.where(lane == NY - 1, 0.0, flux_y)
    west_flux = jnp.where(row == 0, 0.0, roll(flux_x, 1, 0))
    south_flux = jnp.where(lane == 0, 0.0, roll(flux_y, 1, 1))
    forcing = total + planetary(shape) * turn + diff * (
        flux_x - west_flux + flux_y - south_flux
    )
    coded = jnp.where(lc > 0, surface[...], -1.0)
    edge = jnp.zeros((K, LANES), f32)
    edge_lane = iota((K, LANES), 1)
    p = outer[32:48, NY - LANES:] + outer[48:64, NY - LANES:]
    edge_lc = jnp.where(even, lc[:1], lc[COLS - 1:])
    edge_diff = jnp.where(even, diff[:1], diff[COLS - 1:])
    for j in range(COLS):
        at = NY - 1 - j
        here = LANE_EDGE + j
        edge = jnp.where(edge_lane == here, p[:, LANES - 1 - j:LANES - j], edge)
        edge = jnp.where(edge_lane == here + COLS, edge_lc[:, at:at + 1], edge)
        edge = jnp.where(edge_lane == here + 2 * COLS, edge_diff[:, at:at + 1], edge)
    edge = [edge[:COLS], edge[COLS:]]
    zeros = jnp.zeros((COLS, NY - 3 * LANES), f32)
    for pack, mine, other in ((inner, COLS - 1, 0), (outer, 0, COLS - 1)):
        pack[0:COLS] = forcing
        pack[COLS:2 * COLS] = coded
        edge_lc = jnp.where(even, lc[mine:mine + 1], lc[other:other + 1])
        edge_diff = jnp.where(even, diff[mine:mine + 1], diff[other:other + 1])
        pack[64:72] = jnp.where(row == 0, edge_lc, jnp.where(row == 1, edge_diff, 0.0))
        pack[72:80] = jnp.concatenate([fold, *edge, zeros], axis=1)


def interface_flux(mine, theirs):
    level = iota((K, NY), 0).astype(f32)
    p_mine = mine[32:48] + mine[48:64]
    p_theirs = theirs[32:48] + theirs[48:64]
    return level_sum(
        jnp.where(level < mine[64:65], p_theirs, 0.0)
        - jnp.where(level < theirs[64:65], p_mine, 0.0)
    )


def is_even():
    return lax.axis_index("lon") % 2 == 0


def beside(even, west, east):
    return jnp.concatenate([jnp.where(even, west, east), jnp.where(even, east, west)], axis=0)


def chip_kernel(inner, sibling, forcing, coded, tile, near, far):
    even = is_even()
    flux = interface_flux(inner, sibling)
    own, other = inner[65:66] * flux, -sibling[65:66] * flux
    row = iota((2 * COLS, NY), 0)
    change = jnp.where(
        row == COLS - 1,
        jnp.where(even, own, other),
        jnp.where(row == COLS, jnp.where(even, other, own), 0.0),
    )
    full = beside(even, inner[:COLS], sibling[:COLS]) + change
    code = beside(even, inner[COLS:2 * COLS], sibling[COLS:2 * COLS])
    fold = beside(even, inner[72:80, :LANES], sibling[72:80, :LANES])
    forcing[...] = full
    coded[...] = code
    tile[...] = fold
    lane = iota((2 * COLS, LANES), 1)
    for j in range(COLS):
        at = NY - 1 - j
        fold = jnp.where(lane == LANE_F + j, full[:, at:at + 1], fold)
        fold = jnp.where(lane == LANE_CODE + j, code[:, at:at + 1], fold)
    fold = jnp.concatenate(
        [fold[i:i + 1] for i in range(2 * COLS - 1, -1, -1)], axis=0
    )
    for out, source in ((near, inner), (far, sibling)):
        edge = jnp.concatenate(
            [source[72:80, LANES:2 * LANES], source[72:80, 2 * LANES:3 * LANES]], axis=0
        )
        out[...] = jnp.where((lane >= LANE_EDGE) & (lane < LANE_CODE), edge, fold)


def across_fold(even, chip, far):
    shape = (2 * COLS, LANES)
    level = iota(shape, 0).astype(f32)
    lane = iota((1, LANES), 1)
    flux = level_sum(
        jnp.where(level < roll(chip, -COLS, 1), far, 0.0)
        - jnp.where(level < roll(far, -COLS, 1), chip, 0.0)
    )

    def change(tile):
        product = roll(tile[:1], -2 * COLS, 1) * flux
        return jnp.where(lane >= LANE_F, roll(product, LANE_F - LANE_EDGE, 1), 0.0)

    chip_change, far_change = change(chip), -change(far)
    tile = extend(even, far[COLS:], chip, far[:COLS])
    row = iota((EXT, LANES), 0)
    west = jnp.where(row == COLS - 1, far_change, jnp.where(row == COLS, chip_change, 0.0))
    east = jnp.where(
        row == 2 * COLS - 1, chip_change, jnp.where(row == 2 * COLS, far_change, 0.0)
    )
    return tile, jnp.where(even, west, east)


def extend(even, west, chip, east):
    return jnp.concatenate(
        [
            jnp.where(even, west, chip[:COLS]),
            jnp.where(even, chip[:COLS], chip[COLS:]),
            jnp.where(even, chip[COLS:], east),
        ],
        axis=0,
    )


def basis(start, code):
    ocean = code > 0
    centre = jnp.where(ocean, code / scale, 0.0)
    around = jnp.where(ocean, 1.0 / scale, 0.0)
    lane = iota(start.shape, 1)

    def operate(q):
        along = roll(q, -1, 1) + jnp.where(lane == 0, 0.0, roll(q, 1, 1))
        side = q + corner_weight * along
        return centre * q - around * (along + roll(side, 1, 0) + roll(side, -1, 0))

    v = [start, operate(start)]
    for j in range(2, BASIS):
        v.append(2.0 * operate(v[-1]) - v[-2])
    return v


def gram_rows(blocks):
    parts = [[split(q) for q in row] for row in blocks]
    entries = []
    for i in range(BASIS):
        for j in range(i, BASIS):
            terms = [
                two_prod(a, b, a_parts, b_parts)
                for a, b, a_parts, b_parts in zip(blocks[i], blocks[j], parts[i], parts[j])
            ]
            entries.append(pair_tree(terms))
    return [pair_pack(entries[g:g + COLS]) for g in range(0, len(entries), COLS)]


def inner_kernel(outer, beyond, forcing, coded, last, last_code, vectors, partial):
    even = is_even()
    flux_out = interface_flux(outer, beyond)
    own, far = outer[65:66] * flux_out, -beyond[65:66] * flux_out
    row = iota((EXT, NY), 0)
    west = jnp.where(row == COLS - 1, far, jnp.where(row == COLS, own, 0.0))
    east = jnp.where(row == 2 * COLS - 1, own, jnp.where(row == 2 * COLS, far, 0.0))
    far_forcing, far_code = beyond[:COLS], beyond[COLS:2 * COLS]
    south = extend(even, far_forcing, forcing[...], far_forcing) + jnp.where(even, west, east)
    code = extend(even, far_code, coded[...], far_code)
    last[...] = roll(south[:, NY - LANES:], -COLS, 1)
    last_code[...] = roll(code[:, NY - LANES:], -COLS, 1)
    v = basis(south, code)
    lane = iota((COLS, LANES), 1)
    blocks = []
    for j, q in enumerate(v):
        if j < ITERS:
            vectors[j * EXT:(j + 1) * EXT] = q
        cut = [q[COLS:2 * COLS, c:c + LANES] for c in range(0, NY, LANES)]
        cut[-1] = jnp.where(lane < LANES - COLS, cut[-1], 0.0)
        blocks.append(cut)
    for g, pair in enumerate(gram_rows(blocks)):
        for at, part in zip((0, GROUPS * COLS), pair):
            partial[at + g * COLS:at + (g + 1) * COLS] = part


def fold_kernel(last, last_code, beyond, tile, mirror, mirror_far, partial, vectors, gram):
    even = is_even()
    lane = iota((EXT, LANES), 1)
    mine = beyond[72:80, :LANES]
    mine = extend(even, mine, tile[...], mine)
    theirs, between = across_fold(even, mirror[...], mirror_far[...])
    level = (lane - LANE_P).astype(f32)
    weight = jnp.where((lane >= LANE_P) & (lane < LANE_P + K), 0.5 * (0.5 + level / K), 0.0)
    mask_mine = (level < mine[:, LANE_LC:LANE_LC + 1]).astype(f32)
    mask_theirs = (level < theirs[:, LANE_LC:LANE_LC + 1]).astype(f32)
    flux = -jnp.sum(weight * (mask_mine * theirs + mask_theirs * mine), axis=1, keepdims=True)
    own_change = mine[:, LANE_DIFF:LANE_DIFF + 1] * flux
    far_change = theirs[:, LANE_DIFF:LANE_DIFF + 1] * flux
    beyond_fold = lane >= LANE_F
    start = jnp.where(beyond_fold, theirs, last[...]) + between
    start = start + jnp.where(
        lane == LANE_F, far_change, jnp.where(lane == LANE_F - 1, own_change, 0.0)
    )
    code = jnp.where(beyond_fold, roll(theirs, LANE_F - LANE_CODE, 1), last_code[...])
    v = basis(start, code)
    for j in range(ITERS):
        vectors[j * EXT:(j + 1) * EXT] = v[j]
    own_lane = lane[:COLS]
    summed = (own_lane >= LANE_F - COLS) & (own_lane < LANE_F)
    blocks = [[jnp.where(summed, q[COLS:2 * COLS], 0.0)] for q in v]
    size = GROUPS * COLS
    high, low = [], []
    for g, pair in enumerate(gram_rows(blocks)):
        at = g * COLS
        pair = pair_add(pair, (partial[at:at + COLS], partial[size + at:size + at + COLS]))
        high.append(pair[0])
        low.append(pair[1])
    turned = jnp.concatenate(high + low + [jnp.zeros((LANES - 2 * size, LANES), f32)], axis=0).T
    terms = [turned[i * COLS:(i + 1) * COLS] for i in range(LANES // COLS)]
    high, low = pair_norm(pair_rows(pair_tree([(t, roll(t, -size, 1)) for t in terms])))
    row = jnp.where(iota((COLS, LANES), 1) < size, high, roll(low, size, 1))
    gram[...] = jnp.broadcast_to(row[:1], gram.shape)


def coefficients(gram):
    shape = (COLS, LANES)
    tiles = [gram[i * COLS:(i + 1) * COLS] for i in range(gram.shape[0] // COLS)]
    total = pair_norm(pair_rows(pair_tree([(t, roll(t, -GROUPS * COLS, 1)) for t in tiles])))
    wide = lambda column: jnp.broadcast_to(column, shape)
    sub = iota(shape, 0)
    tile_lane = iota(shape, 1)

    def column(j):
        low, high = jnp.minimum(sub, j), jnp.maximum(sub, j)
        entry = ((low * (2 * BASIS - 1 - low)) >> 1) + high
        here = (tile_lane == entry) & (sub < BASIS)
        return tuple(
            wide(jnp.sum(jnp.where(here, part, 0.0), axis=1, keepdims=True)) for part in total
        )

    matrix = [column(j) for j in range(BASIS)]
    first = (sub == 0).astype(f32)
    zero = jnp.zeros(shape, f32)

    def apply(b):
        half = scale / 2
        up = [half * jnp.where(sub == 0, 0.0, roll(part, 1, 0)) for part in b]
        up = [jnp.where(sub == 1, 2.0 * part, part) for part in up]
        down = [half * jnp.where(sub == COLS - 1, 0.0, roll(part, -1, 0)) for part in b]
        four = tuple(4.0 * part for part in b)
        return pair_add(pair_add(four, b), pair_add(tuple(up), tuple(down)))

    def times(vector, count):
        terms = []
        for j in range(count):
            at = tuple(wide(part[j:j + 1]) for part in vector)
            terms.append(pair_mul(matrix[j], at))
        return pair_tree(terms)

    def dot(a, b):
        s = pair_rows(pair_mul(a, b))
        return s[0] + s[1]

    residual = (first, zero)
    image = matrix[0]
    direction = residual
    solution = zero
    norm_now = wide(matrix[0][0][:1])
    floor = 1e-13 * norm_now
    alive = norm_now > 0
    for iteration in range(ITERS):
        applied = apply(direction)
        applied_image = times(applied, iteration + 2)
        curvature = dot(direction, applied_image)
        alive = alive & (curvature > 0)
        step = jnp.where(alive, norm_now / jnp.where(alive, curvature, 1.0), 0.0)
        solution = solution + step * direction[0]
        if iteration + 1 < ITERS:
            back = -step
            residual = pair_norm(pair_add(residual, pair_scale(applied, back)))
            image = pair_norm(pair_add(image, pair_scale(applied_image, back)))
            norm_next = dot(residual, image)
            ratio = jnp.where(alive, norm_next / jnp.where(alive, norm_now, 1.0), 0.0)
            direction = pair_norm(pair_add(residual, pair_scale(direction, ratio)))
            norm_now = norm_next
            alive = alive & (norm_now > floor)
    return solution


def finish_kernel(
    gram, vectors, vectors_last, zonal, meridional, levels, zonal_next, meridional_next, height
):
    x = coefficients(gram)

    def combine(part):
        terms = [x[j:j + 1, :1] * part[j * EXT:(j + 1) * EXT] for j in range(ITERS)]
        return sum(terms[1:], terms[0])

    total, window = combine(vectors), combine(vectors_last)
    near = iota((COLS, LANES), 1) >= CUT - (NY - LANES)

    def finished(value, from_window):
        value = value[COLS:2 * COLS]
        moved = roll(from_window[COLS:2 * COLS], COLS, 1)
        last = jnp.where(near, moved, value[:, NY - LANES:])
        return jnp.concatenate([value[:, :NY - LANES], last], axis=1)

    def step(axis):
        return gravity * finished(roll(total, -1, axis) - total, roll(window, -1, axis) - window)

    height[...] = finished(total, window)
    east, north = step(0), step(1)
    lc = levels[...]
    for k in range(K):
        zonal_next[k] = zonal[k] - jnp.where(lc > k, east, 0.0)
        meridional_next[k] = meridional[k] - jnp.where(lc > k, north, 0.0)


def neighbours(count, sibling, beyond, mirror):
    shape = (COLS, NY)
    even = is_even()
    row, lane = iota(shape, 0), iota(shape, 1)
    lc = count[...].astype(f32)
    north_tile = jnp.where(even, mirror[:COLS], mirror[COLS:])

    def around(field, west, east, north):
        return (
            jnp.where(row == COLS - 1, east, roll(field, -1, 0)),
            jnp.where(row == 0, west, roll(field, 1, 0)),
            jnp.where(lane == NY - 1, north, roll(field, -1, 1)),
            jnp.where(lane == 0, 0.0, roll(field, 1, 1)),
        )

    def edges(at):
        a, b = sibling[at:at + 1], beyond[at:at + 1]
        return jnp.where(even, b, a), jnp.where(even, a, b)

    def padded(field, base, k, sign):
        at = LANE_MT + base * K + k
        return around(field, *edges(2 * COLS + base * K + k), sign * north_tile[:, at:at + 1])

    west_lc, east_lc = edges(64)
    north_lc = north_tile[:, LANE_LC:LANE_LC + 1]

    def mask_sum(mask, k):
        inside = [(c > k).astype(f32) for c in (west_lc, east_lc, north_lc)]
        return sum(around(mask, *inside))

    return lc, padded, mask_sum


def tracer_kernel(
    tracer, zonal, meridional, count, diffusivity, sibling, beyond, mirror, tracer_next
):
    lc, padded, mask_sum = neighbours(count, sibling, beyond, mirror)
    diff = diffusivity[...]

    def masked(k):
        if k < 0 or k >= K:
            return jnp.zeros_like(lc), jnp.zeros_like(lc)
        mask = (lc > k).astype(f32)
        return mask, mask * tracer[k]

    below, here = masked(-1), masked(0)
    for k in range(K):
        above = masked(k + 1)
        mask, mt = here
        t, u, v = tracer[k], zonal[k], meridional[k]
        te, tw, tn, ts = padded(mt, 0, k, 1.0)
        vertical = above[1] + below[1] - (above[0] + below[0]) * t
        tracer_next[k] = mask * (
            t
            + diff * (te + tw + tn + ts - mask_sum(mask, k) * t)
            + vertical_mix * vertical
            - advection * (u * (te - tw) + v * (tn - ts))
        )
        below, here = here, above


def flow_kernel(
    zonal, meridional, count, diffusivity, sibling, beyond, mirror,
    zonal_step, meridional_step, levels,
):
    lc, padded, mask_sum = neighbours(count, sibling, beyond, mirror)
    diff = diffusivity[...]
    turn = planetary(lc.shape)
    levels[...] = lc
    for k in range(K):
        mask = (lc > k).astype(f32)
        u, v = zonal[k], meridional[k]
        sides = mask_sum(mask, k)
        zonal_sum = sum(padded(mask * u, 1, k, -1.0))
        meridional_sum = sum(padded(mask * v, 2, k, -1.0))
        zonal_step[k] = mask * (u + diff * (zonal_sum - sides * u) + turn * v)
        meridional_step[k] = mask * (v + diff * (meridional_sum - sides * v) - turn * u)


def call(kernel, shapes, *args, flops=0, scratch=(), stay=0):
    moved = 4 * sum(a.size for a in args) + 4 * sum(
        functools.reduce(lambda x, y: x * y, s, 1) for s in shapes
    )
    space = pl.BlockSpec(memory_space=pltpu.VMEM)
    in_specs = [space] * (len(args) - stay) + [pl.BlockSpec(memory_space=pltpu.HBM)] * stay
    here = len(args) - stay
    args = args[:here] + tuple(
        pltpu.with_memory_space_constraint(a, pltpu.HBM) for a in args[here:]
    )
    return pl.pallas_call(
        kernel,
        out_shape=[jax.ShapeDtypeStruct(s, f32) for s in shapes],
        in_specs=in_specs,
        out_specs=[space] * len(shapes),
        scratch_shapes=list(scratch),
        compiler_params=pltpu.CompilerParams(vmem_limit_bytes=32 * 1024 * 1024),
        cost_estimate=pl.CostEstimate(flops=flops, bytes_accessed=moved, transcendentals=0),
    )(*args)


def body(tracer, zonal, meridional, count, diffusivity, surface):
    size = lax.axis_size("lon")
    block = (K, COLS, NY)

    def permute(value, pairs):
        return lax.ppermute(value, "lon", pairs)

    siblings = [(i, i ^ 1) for i in range(size)]
    outward = [(i, (i + 1 if i % 2 else i - 1) % size) for i in range(size)]
    mirrored = [(i, size - 1 - i) for i in range(size)]
    mirrored_far = [((size + 1 - 4 * (i % 2) - i) % size, i) for i in range(size)]
    arguments = (tracer, zonal, meridional, count, diffusivity, surface)
    inner, outer = call(
        pack_kernel, [(PACK, NY)] * 2, *arguments,
        scratch=[pltpu.VMEM((K, COLS, LANES), f32)]
        + [pltpu.VMEM(a.shape, a.dtype) for a in arguments[1:]]
        + [pltpu.VMEM((6, K, NY), f32), pltpu.SemaphoreType.DMA((9 + 3 * CHUNKS,))], stay=len(arguments),
    )
    beyond = permute(outer, outward)
    sibling = permute(inner, siblings)
    chip = (2 * COLS, NY)
    forcing, coded, tile, near, far = call(
        chip_kernel, [chip, chip] + [(2 * COLS, LANES)] * 3, inner, sibling
    )
    mirror = permute(near, mirrored)
    mirror_far = permute(far, mirrored_far)
    window = (EXT, LANES)
    last, last_code, vectors, partial = call(
        inner_kernel,
        [window, window, (ITERS * EXT, NY), (2 * GROUPS * COLS, LANES)],
        outer, beyond, forcing, coded, flops=8192 * 100,
    )
    vectors_last, gram = call(
        fold_kernel,
        [(ITERS * EXT, LANES), (size, LANES)],
        last, last_code, beyond, tile, mirror, mirror_far, partial,
    )
    halos = (sibling, beyond, mirror)
    tracer_next, = call(
        tracer_kernel, [block],
        tracer, zonal, meridional, count, diffusivity, *halos,
        flops=65536 * 40,
    )
    zonal_step, meridional_step, levels = call(
        flow_kernel, [block, block, (COLS, NY)],
        zonal, meridional, count, diffusivity, *halos,
        flops=65536 * 40,
    )
    group = [(i + size // 2 + 1) % size for i in range(size)]
    gram = lax.all_to_all(gram, "lon", 0, 0, tiled=True, axis_index_groups=[group])
    zonal_next, meridional_next, height = call(
        finish_kernel, [block, block, (COLS, NY)],
        gram, vectors, vectors_last, zonal_step, meridional_step, levels,
    )
    return tracer_next, zonal_next, meridional_next, height


def solution(mesh):
    column = P("lon", None)
    field = P("ens", "lon", None)
    return jax.shard_map(
        body,
        mesh=mesh,
        in_specs=(field, field, field, column, column, column),
        out_specs=(field, field, field, P("lon", "ens")),
        check_vma=False,
    )
```

```python
import functools

import jax
import jax.numpy as jnp
from jax import lax
from jax.experimental import pallas as pl
from jax.experimental.pallas import tpu as pltpu
from jax.sharding import PartitionSpec as P

K = 16
NY = 512
ITERS = 6
COLS = 8
EXT = 3 * COLS
LANES = 128
BASIS = ITERS + 1
CUT = NY - COLS
GROUPS = (BASIS * (BASIS + 1) // 2 + COLS - 1) // COLS
CHUNKS = 2

vertical_mix = 0.1
advection = 0.25
coriolis_scale = 0.3
gravity = 0.5
corner_weight = 0.25
shift = 5.0
scale = 4.0
LANE_P = 16
LANE_LC = 32
LANE_DIFF = 33
LANE_MT = 40
LANE_MU = 56
LANE_MV = 72
LANE_EDGE = 88
WIDE = 32
LANE_CODE = LANES - 2 * COLS
LANE_F = LANES - COLS

f32 = jnp.float32


def iota(shape, dim):
    return lax.broadcasted_iota(jnp.int32, shape, dim)


def thickness(k):
    return 0.5 * (0.5 + k / K)


def planetary(shape):
    latitude = (iota(shape, 1).astype(f32) + 0.5) / NY
    return coriolis_scale * (2.0 * latitude - 1.0)


def roll(value, amount, axis):
    return pltpu.roll(value, amount % value.shape[axis], axis)


def level_sum(value):
    weight = 0.5 * (0.5 + iota(value.shape, 0).astype(f32) / K)
    return jnp.sum(weight * value, axis=0, keepdims=True)


def two_sum(a, b):
    s = a + b
    t = s - a
    return s, (a - (s - t)) + (b - t)


def fast_two_sum(a, b):
    s = a + b
    return s, b - (s - a)


def split(a):
    c = 4097.0 * a
    high = c - (c - a)
    return high, a - high


def two_prod(a, b, a_parts=None, b_parts=None):
    ah, al = split(a) if a_parts is None else a_parts
    bh, bl = split(b) if b_parts is None else b_parts
    p = a * b
    return p, ((ah * bh - p) + ah * bl + al * bh) + al * bl


def pair_mul(a, b):
    p, e = two_prod(a[0], b[0])
    return p, e + (a[0] * b[1] + a[1] * b[0])


def pair_add(a, b):
    s, e = two_sum(a[0], b[0])
    return s, e + (a[1] + b[1])


def pair_norm(a):
    return fast_two_sum(a[0], a[1])


def pair_scale(a, factor):
    p, e = two_prod(a[0], factor)
    return p, e + a[1] * factor


def pair_tree(terms):
    while len(terms) > 1:
        pairs = [pair_add(terms[i], terms[i + 1]) for i in range(0, len(terms) - 1, 2)]
        terms = pairs + terms[len(terms) - len(terms) % 2:]
    return terms[0]


def pair_rows(a):
    for step in (4, 2, 1):
        a = pair_add(a, (roll(a[0], step, 0), roll(a[1], step, 0)))
    return a


def pair_pack(terms):
    shape = (COLS, LANES)
    sub = iota(shape, 0)
    zero = (jnp.zeros(shape, f32),) * 2
    terms = terms + [zero] * (COLS - len(terms))
    for step in (4, 2, 1):
        low = (sub & step) == 0
        merged = []
        for x, y in zip(terms[:step], terms[step:]):
            a = tuple(jnp.where(low, p, q) for p, q in zip(x, y))
            b = tuple(
                jnp.where(low, roll(p, -step, 0), roll(q, step, 0)) for p, q in zip(x, y)
            )
            merged.append(pair_add(a, b))
        terms = merged
    return terms[0]


def pack_kernel(
    tracer_in, zonal_in, meridional_in, count_in, diffusivity_in, surface_in,
    inner, outer,
    tracer, zonal, meridional, count, diffusivity, surface, edges, sems,
):
    shape = (COLS, NY)
    even = is_even()
    small = [
        pltpu.make_async_copy(a, b, sems.at[i])
        for i, (a, b) in enumerate(
            ((count_in, count), (diffusivity_in, diffusivity), (surface_in, surface))
        )
    ]
    large = []
    for c in range(CHUNKS):
        part = pl.ds(c * K // CHUNKS, K // CHUNKS)
        large.append(
            [
                pltpu.make_async_copy(a.at[part], b.at[part], sems.at[3 + 3 * c + i])
                for i, (a, b) in enumerate(
                    (
                        (zonal_in, zonal),
                        (meridional_in, meridional),
                        (tracer_in.at[:, :, NY - LANES:], tracer),
                    )
                )
            ]
        )
    rows = [
        pltpu.make_async_copy(
            field.at[:, x], edges.at[2 * base + i], sems.at[3 + 3 * CHUNKS + 2 * base + i]
        )
        for base, field in enumerate((tracer_in, zonal_in, meridional_in))
        for i, x in enumerate((0, COLS - 1))
    ]
    for copy in small + sum(large, []) + rows:
        copy.start()
    for copy in small:
        copy.wait()
    lc = count[...].astype(f32)
    diff = diffusivity[...]
    row, lane = iota(shape, 0), iota(shape, 1)
    tile_lane = iota((COLS, LANES), 1)
    lc_east, lc_north = roll(lc, -1, 0), roll(lc, -1, 1)
    total = jnp.zeros(shape, f32)
    turn = jnp.zeros(shape, f32)
    flux_x = jnp.zeros(shape, f32)
    flux_y = jnp.zeros(shape, f32)
    fold = jnp.zeros((COLS, LANES), f32)
    for k in range(K):
        if k % (K // CHUNKS) == 0:
            for copy in large[k // (K // CHUNKS)]:
                copy.wait()
        mask = lc > k
        t, u, v = tracer[k], zonal[k], meridional[k]
        for base, field in ((LANE_MT, t), (LANE_MU, u), (LANE_MV, v)):
            fold = jnp.where(tile_lane == base + k, field[:, -1:], fold)
        mu, mv = jnp.where(mask, u, 0.0), jnp.where(mask, v, 0.0)
        p = thickness(k) * (mu + mv)
        total += p
        turn += thickness(k) * (mv - mu)
        flux_x += jnp.where(mask, roll(p, -1, 0), 0.0) - jnp.where(lc_east > k, p, 0.0)
        flux_y += jnp.where(mask, roll(p, -1, 1), 0.0) - jnp.where(lc_north > k, p, 0.0)
    lc_fold = lc[:, NY - 1:]
    level = tile_lane - jnp.where(
        tile_lane < LANE_MU, LANE_MT, jnp.where(tile_lane < LANE_MV, LANE_MU, LANE_MV)
    )
    fold = jnp.where(level.astype(f32) < lc_fold, fold, 0.0)
    momentum = roll(fold, LANE_P - LANE_MU, 1) + roll(fold, LANE_P - LANE_MV, 1)
    fold = jnp.where((tile_lane >= LANE_P) & (tile_lane < LANE_P + K), momentum, fold)
    fold = jnp.where(tile_lane == LANE_LC, lc_fold, fold)
    fold = jnp.where(tile_lane == LANE_DIFF, diff[:, NY - 1:], fold)
    edge_level = iota((K, NY), 0).astype(f32)

    for copy in rows:
        copy.wait()
    for base in range(3):
        west, east = edges[2 * base], edges[2 * base + 1]
        west = jnp.where(edge_level < lc[:1], west, 0.0)
        east = jnp.where(edge_level < lc[COLS - 1:], east, 0.0)
        at = pl.ds(2 * COLS + base * K, K)
        inner[at] = jnp.where(even, east, west)
        outer[at] = jnp.where(even, west, east)
    flux_x = jnp.where(row == COLS - 1, 0.0, flux_x)
    flux_y = jnp.where(lane == NY - 1, 0.0, flux_y)
    west_flux = jnp.where(row == 0, 0.0, roll(flux_x, 1, 0))
    south_flux = jnp.where(lane == 0, 0.0, roll(flux_y, 1, 1))
    forcing = total + planetary(shape) * turn + diff * (
        flux_x - west_flux + flux_y - south_flux
    )
    coded = jnp.where(lc > 0, surface[...], -1.0)
    edge = jnp.zeros((K, LANES), f32)
    edge_lane = iota((K, LANES), 1)
    p = outer[32:48, NY - LANES:] + outer[48:64, NY - LANES:]
    sub = iota((COLS, LANES), 0)
    edge_lc = jnp.where(even, lc[:1], lc[COLS - 1:])
    edge_diff = jnp.where(even, diff[:1], diff[COLS - 1:])
    for j in range(COLS):
        at = NY - 1 - j
        here = LANE_EDGE + j
        edge = jnp.where(edge_lane == here, p[:, LANES - 1 - j:LANES - j], edge)
        edge = jnp.where(edge_lane == here + COLS, edge_lc[:, at:at + 1], edge)
        edge = jnp.where(edge_lane == here + 2 * COLS, edge_diff[:, at:at + 1], edge)
    blank = jnp.zeros((COLS, NY - 3 * LANES), f32)
    inner[72:80] = jnp.concatenate([fold, edge[:COLS], edge[COLS:], blank], axis=1)
    inner[0:COLS] = forcing
    inner[COLS:2 * COLS] = coded
    mine_lc = jnp.where(even, lc[COLS - 1:], lc[:1])
    mine_diff = jnp.where(even, diff[COLS - 1:], diff[:1])
    inner[64:72] = jnp.where(row == 0, mine_lc, jnp.where(row == 1, mine_diff, 0.0))
    far, next_far = jnp.where(even, COLS - 1, 0), jnp.where(even, COLS - 2, 1)
    used = jnp.where((tile_lane >= LANE_P) & (tile_lane < LANE_P + WIDE), fold, 0.0)
    moved = [
        jnp.sum(
            sum(
                jnp.where(sub == x, roll(used, (x - first) * WIDE - LANE_P, 1), 0.0)
                for x in range(first, first + LANES // WIDE)
            ),
            axis=0, keepdims=True,
        )
        for first in range(0, COLS, LANES // WIDE)
    ]
    tile_row = jnp.concatenate(moved + [jnp.zeros((1, NY - len(moved) * LANES), f32)], axis=1)
    outer[0:COLS] = jnp.where(row == far, edge_lc, jnp.where(row == next_far, tile_row, forcing))
    outer[COLS:2 * COLS] = jnp.where(row == far, edge_diff, coded)


def far_rows(pack, far, next_far):
    tile_row = jnp.where(next_far == 1, pack[1:2], pack[COLS - 2:COLS - 1])
    sub = iota((COLS, LANES), 0)
    tile = jnp.zeros((COLS, LANES), f32)
    for x in range(COLS):
        block, place = divmod(x * WIDE, LANES)
        piece = tile_row[:, block * LANES:(block + 1) * LANES]
        tile = jnp.where(sub == x, roll(piece, LANE_P - place, 1), tile)
    return (
        jnp.where(far == 0, pack[0:1], pack[COLS - 1:COLS]),
        jnp.where(far == 0, pack[COLS:COLS + 1], pack[2 * COLS - 1:2 * COLS]),
        tile,
    )


def interface_flux(mine, theirs, lc_mine, lc_theirs):
    p_mine = mine[32:48] + mine[48:64]
    p_theirs = theirs[32:48] + theirs[48:64]
    level = iota(p_mine.shape, 0).astype(f32)
    return level_sum(
        jnp.where(level < lc_mine, p_theirs, 0.0) - jnp.where(level < lc_theirs, p_mine, 0.0)
    )


def chip_forcing(even, inner, sibling):
    flux = interface_flux(inner, sibling, inner[64:65], sibling[64:65])
    own, other = inner[65:66] * flux, -sibling[65:66] * flux
    row = iota((2 * COLS, flux.shape[1]), 0)
    change = jnp.where(
        row == COLS - 1,
        jnp.where(even, own, other),
        jnp.where(row == COLS, jnp.where(even, other, own), 0.0),
    )
    return beside(even, inner[:COLS], sibling[:COLS]) + change


def is_even():
    return lax.axis_index("lon") % 2 == 0


def beside(even, west, east):
    return jnp.concatenate([jnp.where(even, west, east), jnp.where(even, east, west)], axis=0)


def chip_kernel(inner, sibling, tile, near, far):
    even = is_even()
    ours, theirs = (pack[:72, NY - LANES:] for pack in (inner, sibling))
    full = chip_forcing(even, ours, theirs)
    code = beside(even, ours[COLS:2 * COLS], theirs[COLS:2 * COLS])
    fold = beside(even, inner[72:80, :LANES], sibling[72:80, :LANES])
    tile[...] = fold
    lane = iota((2 * COLS, LANES), 1)
    for j in range(COLS):
        at = LANES - 1 - j
        fold = jnp.where(lane == LANE_F + j, full[:, at:at + 1], fold)
        fold = jnp.where(lane == LANE_CODE + j, code[:, at:at + 1], fold)
    fold = jnp.concatenate(
        [fold[i:i + 1] for i in range(2 * COLS - 1, -1, -1)], axis=0
    )
    for out, source in ((near, inner), (far, sibling)):
        edge = jnp.concatenate(
            [source[72:80, LANES:2 * LANES], source[72:80, 2 * LANES:3 * LANES]], axis=0
        )
        out[...] = jnp.where((lane >= LANE_EDGE) & (lane < LANE_CODE), edge, fold)


def across_fold(even, chip, far):
    shape = (2 * COLS, LANES)
    level = iota(shape, 0).astype(f32)
    lane = iota((1, LANES), 1)
    flux = level_sum(
        jnp.where(level < roll(chip, -COLS, 1), far, 0.0)
        - jnp.where(level < roll(far, -COLS, 1), chip, 0.0)
    )

    def change(tile):
        product = roll(tile[:1], -2 * COLS, 1) * flux
        return jnp.where(lane >= LANE_F, roll(product, LANE_F - LANE_EDGE, 1), 0.0)

    chip_change, far_change = change(chip), -change(far)
    tile = extend(even, far[COLS:], chip, far[:COLS])
    row = iota((EXT, LANES), 0)
    west = jnp.where(row == COLS - 1, far_change, jnp.where(row == COLS, chip_change, 0.0))
    east = jnp.where(
        row == 2 * COLS - 1, chip_change, jnp.where(row == 2 * COLS, far_change, 0.0)
    )
    return tile, jnp.where(even, west, east)


def extend(even, west, chip, east):
    return jnp.concatenate(
        [
            jnp.where(even, west, chip[:COLS]),
            jnp.where(even, chip[:COLS], chip[COLS:]),
            jnp.where(even, chip[COLS:], east),
        ],
        axis=0,
    )


def basis(start, code):
    ocean = code > 0
    centre = jnp.where(ocean, code / scale, 0.0)
    around = jnp.where(ocean, 1.0 / scale, 0.0)
    lane = iota(start.shape, 1)

    def operate(q):
        along = roll(q, -1, 1) + jnp.where(lane == 0, 0.0, roll(q, 1, 1))
        side = q + corner_weight * along
        return centre * q - around * (along + roll(side, 1, 0) + roll(side, -1, 0))

    v = [start, operate(start)]
    for j in range(2, BASIS):
        v.append(2.0 * operate(v[-1]) - v[-2])
    return v


def gram_rows(blocks):
    parts = [[split(q) for q in row] for row in blocks]
    entries = []
    for i in range(BASIS):
        for j in range(i, BASIS):
            terms = [
                two_prod(a, b, a_parts, b_parts)
                for a, b, a_parts, b_parts in zip(blocks[i], blocks[j], parts[i], parts[j])
            ]
            entries.append(pair_tree(terms))
    return [pair_pack(entries[g:g + COLS]) for g in range(0, len(entries), COLS)]


def inner_kernel(
    inner, outer, sibling, beyond, last, last_code, vectors, partial, far_tile,
):
    even = is_even()
    forcing = chip_forcing(even, inner, sibling)
    coded = beside(even, inner[COLS:2 * COLS], sibling[COLS:2 * COLS])
    at_east, at_west = jnp.where(even, 0, COLS - 1), jnp.where(even, COLS - 1, 0)
    lc_out, diff_out, _ = far_rows(outer, at_west, jnp.where(even, COLS - 2, 1))
    lc_far, diff_far, far_tile[...] = far_rows(beyond, at_east, jnp.where(even, 1, COLS - 2))
    flux_out = interface_flux(outer, beyond, lc_out, lc_far)
    own, far = diff_out * flux_out, -diff_far * flux_out
    row = iota((EXT, NY), 0)
    west = jnp.where(row == COLS - 1, far, jnp.where(row == COLS, own, 0.0))
    east = jnp.where(row == 2 * COLS - 1, own, jnp.where(row == 2 * COLS, far, 0.0))
    far_forcing, far_code = beyond[:COLS], beyond[COLS:2 * COLS]
    south = extend(even, far_forcing, forcing, far_forcing) + jnp.where(even, west, east)
    code = extend(even, far_code, coded, far_code)
    last[...] = roll(south[:, NY - LANES:], -COLS, 1)
    last_code[...] = roll(code[:, NY - LANES:], -COLS, 1)
    v = basis(south, code)
    lane = iota((COLS, LANES), 1)
    blocks = []
    for j, q in enumerate(v):
        if j < ITERS:
            vectors[j * EXT:(j + 1) * EXT] = q
        cut = [q[COLS:2 * COLS, c:c + LANES] for c in range(0, NY, LANES)]
        cut[-1] = jnp.where(lane < LANES - COLS, cut[-1], 0.0)
        blocks.append(cut)
    for g, pair in enumerate(gram_rows(blocks)):
        for at, part in zip((0, GROUPS * COLS), pair):
            partial[at + g * COLS:at + (g + 1) * COLS] = part


def fold_kernel(last, last_code, far_tile, tile, mirror, mirror_far, partial, vectors, gram):
    even = is_even()
    lane = iota((EXT, LANES), 1)
    mine = extend(even, far_tile[...], tile[...], far_tile[...])
    theirs, between = across_fold(even, mirror[...], mirror_far[...])
    level = (lane - LANE_P).astype(f32)
    weight = jnp.where((lane >= LANE_P) & (lane < LANE_P + K), 0.5 * (0.5 + level / K), 0.0)
    mask_mine = (level < mine[:, LANE_LC:LANE_LC + 1]).astype(f32)
    mask_theirs = (level < theirs[:, LANE_LC:LANE_LC + 1]).astype(f32)
    flux = -jnp.sum(weight * (mask_mine * theirs + mask_theirs * mine), axis=1, keepdims=True)
    own_change = mine[:, LANE_DIFF:LANE_DIFF + 1] * flux
    far_change = theirs[:, LANE_DIFF:LANE_DIFF + 1] * flux
    beyond_fold = lane >= LANE_F
    start = jnp.where(beyond_fold, theirs, last[...]) + between
    start = start + jnp.where(
        lane == LANE_F, far_change, jnp.where(lane == LANE_F - 1, own_change, 0.0)
    )
    code = jnp.where(beyond_fold, roll(theirs, LANE_F - LANE_CODE, 1), last_code[...])
    v = basis(start, code)
    for j in range(ITERS):
        vectors[j * EXT:(j + 1) * EXT] = v[j]
    own_lane = lane[:COLS]
    summed = (own_lane >= LANE_F - COLS) & (own_lane < LANE_F)
    blocks = [[jnp.where(summed, q[COLS:2 * COLS], 0.0)] for q in v]
    size = GROUPS * COLS
    high, low = [], []
    for g, pair in enumerate(gram_rows(blocks)):
        at = g * COLS
        pair = pair_add(pair, (partial[at:at + COLS], partial[size + at:size + at + COLS]))
        high.append(pair[0])
        low.append(pair[1])
    turned = jnp.concatenate(high + low + [jnp.zeros((LANES - 2 * size, LANES), f32)], axis=0).T
    terms = [turned[i * COLS:(i + 1) * COLS] for i in range(LANES // COLS)]
    high, low = pair_norm(pair_rows(pair_tree([(t, roll(t, -size, 1)) for t in terms])))
    row = jnp.where(iota((COLS, LANES), 1) < size, high, roll(low, size, 1))
    gram[...] = jnp.broadcast_to(row[:1], gram.shape)


def coefficients(gram):
    shape = (COLS, LANES)
    tiles = [gram[i * COLS:(i + 1) * COLS] for i in range(gram.shape[0] // COLS)]
    total = pair_norm(pair_rows(pair_tree([(t, roll(t, -GROUPS * COLS, 1)) for t in tiles])))
    wide = lambda column: jnp.broadcast_to(column, shape)
    sub = iota(shape, 0)
    tile_lane = iota(shape, 1)

    def column(j):
        low, high = jnp.minimum(sub, j), jnp.maximum(sub, j)
        entry = ((low * (2 * BASIS - 1 - low)) >> 1) + high
        here = (tile_lane == entry) & (sub < BASIS)
        return tuple(
            wide(jnp.sum(jnp.where(here, part, 0.0), axis=1, keepdims=True)) for part in total
        )

    matrix = [column(j) for j in range(BASIS)]
    zero = jnp.zeros(shape, f32)
    half = scale / 2

    def times_power(pair, factor):
        return tuple(factor * part for part in pair)

    def shifted(pair):
        return pair_add(times_power(pair, shift - 1.0), pair)

    def apply(b):
        up = [half * jnp.where(sub == 0, 0.0, roll(part, 1, 0)) for part in b]
        up = tuple(jnp.where(sub == 1, 2.0 * part, part) for part in up)
        down = tuple(half * jnp.where(sub == COLS - 1, 0.0, roll(part, -1, 0)) for part in b)
        return pair_add(shifted(b), pair_add(up, down))

    images = [pair_add(shifted(matrix[0]), times_power(matrix[1], scale))]
    for j in range(1, ITERS):
        sides = pair_add(matrix[j - 1], matrix[j + 1])
        images.append(pair_add(shifted(matrix[j]), times_power(sides, half)))

    def image_of(vector, count):
        terms = []
        for j in range(count):
            at = tuple(wide(part[j:j + 1]) for part in vector)
            terms.append(pair_mul(images[j], at))
        return pair_tree(terms)

    def dot(a, b):
        return pair_rows(pair_mul(a, b))

    residual = ((sub == 0).astype(f32), zero)
    direction = residual
    solution = zero
    norm_now = tuple(wide(part[:1]) for part in matrix[0])
    floor = 1e-13 * norm_now[0]
    alive = norm_now[0] > 0
    for iteration in range(ITERS):
        applied = apply(direction)
        if iteration == 0:
            image = images[0]
            curvature = tuple(wide(part[:1]) for part in image)
        else:
            image = image_of(direction, iteration + 1)
            curvature = dot(direction, image)
        size = curvature[0] + curvature[1]
        alive = alive & (size > 0)
        step = jnp.where(alive, (norm_now[0] + norm_now[1]) / jnp.where(alive, size, 1.0), 0.0)
        solution = solution + step * direction[0]
        if iteration + 1 < ITERS:
            crossed = curvature if iteration == 0 else dot(residual, image)
            squared = dot(applied, image)
            change = pair_add(
                pair_scale(squared, step), times_power(crossed, -2.0)
            )
            norm_next = pair_norm(pair_add(norm_now, pair_scale(pair_norm(change), step)))
            residual = pair_norm(pair_add(residual, pair_scale(applied, -step)))
            ratio = jnp.where(alive, norm_next[0] / jnp.where(alive, norm_now[0], 1.0), 0.0)
            direction = pair_norm(pair_add(residual, pair_scale(direction, ratio)))
            norm_now = norm_next
            alive = alive & (norm_now[0] > floor)
    return solution


def finish_kernel(
    gram, vectors, vectors_last, zonal, meridional, levels, zonal_next, meridional_next, height
):
    x = coefficients(gram)

    def combine(part):
        terms = [x[j:j + 1, :1] * part[j * EXT:(j + 1) * EXT] for j in range(ITERS)]
        return sum(terms[1:], terms[0])

    total, window = combine(vectors), combine(vectors_last)
    near = iota((COLS, LANES), 1) >= CUT - (NY - LANES)

    def finished(value, from_window):
        value = value[COLS:2 * COLS]
        moved = roll(from_window[COLS:2 * COLS], COLS, 1)
        last = jnp.where(near, moved, value[:, NY - LANES:])
        return jnp.concatenate([value[:, :NY - LANES], last], axis=1)

    def step(axis):
        return gravity * finished(roll(total, -1, axis) - total, roll(window, -1, axis) - window)

    height[...] = finished(total, window)
    east, north = step(0), step(1)
    lc = levels[...]
    for k in range(K):
        zonal_next[k] = zonal[k] - jnp.where(lc > k, east, 0.0)
        meridional_next[k] = meridional[k] - jnp.where(lc > k, north, 0.0)


def neighbours(count, sibling, beyond, mirror):
    shape = (COLS, NY)
    even = is_even()
    row, lane = iota(shape, 0), iota(shape, 1)
    lc = count[...].astype(f32)
    north_tile = jnp.where(even, mirror[:COLS], mirror[COLS:])

    def around(field, west, east, north):
        return (
            jnp.where(row == COLS - 1, east, roll(field, -1, 0)),
            jnp.where(row == 0, west, roll(field, 1, 0)),
            jnp.where(lane == NY - 1, north, roll(field, -1, 1)),
            jnp.where(lane == 0, 0.0, roll(field, 1, 1)),
        )

    def sides(a, b):
        return jnp.where(even, b, a), jnp.where(even, a, b)

    def edges(at):
        return sides(sibling[at:at + 1], beyond[at:at + 1])

    def padded(field, base, k, sign):
        at = LANE_MT + base * K + k
        return around(field, *edges(2 * COLS + base * K + k), sign * north_tile[:, at:at + 1])

    beyond_lc = jnp.where(even, beyond[0:1], beyond[COLS - 1:COLS])
    west_lc, east_lc = sides(sibling[64:65], beyond_lc)
    north_lc = north_tile[:, LANE_LC:LANE_LC + 1]

    def mask_sum(mask, k):
        inside = [(c > k).astype(f32) for c in (west_lc, east_lc, north_lc)]
        return sum(around(mask, *inside))

    return lc, padded, mask_sum


def tracer_kernel(
    tracer, zonal, meridional, count, diffusivity, sibling, beyond, mirror, tracer_next
):
    lc, padded, mask_sum = neighbours(count, sibling, beyond, mirror)
    diff = diffusivity[...]

    def masked(k):
        if k < 0 or k >= K:
            return jnp.zeros_like(lc), jnp.zeros_like(lc)
        mask = (lc > k).astype(f32)
        return mask, mask * tracer[k]

    below, here = masked(-1), masked(0)
    for k in range(K):
        above = masked(k + 1)
        mask, mt = here
        t, u, v = tracer[k], zonal[k], meridional[k]
        te, tw, tn, ts = padded(mt, 0, k, 1.0)
        vertical = above[1] + below[1] - (above[0] + below[0]) * t
        tracer_next[k] = mask * (
            t
            + diff * (te + tw + tn + ts - mask_sum(mask, k) * t)
            + vertical_mix * vertical
            - advection * (u * (te - tw) + v * (tn - ts))
        )
        below, here = here, above


def flow_kernel(
    zonal, meridional, count, diffusivity, sibling, beyond, mirror,
    zonal_step, meridional_step, levels,
):
    lc, padded, mask_sum = neighbours(count, sibling, beyond, mirror)
    diff = diffusivity[...]
    turn = planetary(lc.shape)
    levels[...] = lc
    for k in range(K):
        mask = (lc > k).astype(f32)
        u, v = zonal[k], meridional[k]
        sides = mask_sum(mask, k)
        zonal_sum = sum(padded(mask * u, 1, k, -1.0))
        meridional_sum = sum(padded(mask * v, 2, k, -1.0))
        zonal_step[k] = mask * (u + diff * (zonal_sum - sides * u) + turn * v)
        meridional_step[k] = mask * (v + diff * (meridional_sum - sides * v) - turn * u)


def call(kernel, shapes, *args, flops=0, scratch=(), stay=0):
    moved = 4 * sum(a.size for a in args) + 4 * sum(
        functools.reduce(lambda x, y: x * y, s, 1) for s in shapes
    )
    space = pl.BlockSpec(memory_space=pltpu.VMEM)
    in_specs = [space] * (len(args) - stay) + [pl.BlockSpec(memory_space=pltpu.HBM)] * stay
    here = len(args) - stay
    args = args[:here] + tuple(
        pltpu.with_memory_space_constraint(a, pltpu.HBM) for a in args[here:]
    )
    return pl.pallas_call(
        kernel,
        out_shape=[jax.ShapeDtypeStruct(s, f32) for s in shapes],
        in_specs=in_specs,
        out_specs=[space] * len(shapes),
        scratch_shapes=list(scratch),
        compiler_params=pltpu.CompilerParams(vmem_limit_bytes=32 * 1024 * 1024),
        cost_estimate=pl.CostEstimate(flops=flops, bytes_accessed=moved, transcendentals=0),
    )(*args)


def body(tracer, zonal, meridional, count, diffusivity, surface):
    size = lax.axis_size("lon")
    block = (K, COLS, NY)

    def permute(value, pairs):
        return lax.ppermute(value, "lon", pairs)

    siblings = [(i, i ^ 1) for i in range(size)]
    outward = [(i, (i + 1 if i % 2 else i - 1) % size) for i in range(size)]
    mirrored = [(i, size - 1 - i) for i in range(size)]
    mirrored_far = [((size + 1 - 4 * (i % 2) - i) % size, i) for i in range(size)]
    arguments = (tracer, zonal, meridional, count, diffusivity, surface)
    inner, outer = call(
        pack_kernel, [(80, NY), (64, NY)], *arguments,
        scratch=[pltpu.VMEM((K, COLS, LANES), f32)]
        + [pltpu.VMEM(a.shape, a.dtype) for a in arguments[1:]]
        + [pltpu.VMEM((6, K, NY), f32), pltpu.SemaphoreType.DMA((9 + 3 * CHUNKS,))], stay=len(arguments),
    )
    beyond = permute(outer, outward)
    sibling = permute(inner, siblings)
    patch = (2 * COLS, LANES)
    tile, near, far = call(chip_kernel, [patch] * 3, inner, sibling)
    mirror = permute(near, mirrored)
    mirror_far = permute(far, mirrored_far)
    window = (EXT, LANES)
    last, last_code, vectors, partial, far_tile = call(
        inner_kernel,
        [
            window, window, (ITERS * EXT, NY), (2 * GROUPS * COLS, LANES), (COLS, LANES),
        ],
        inner, outer, sibling, beyond, flops=8192 * 100,
    )
    vectors_last, gram = call(
        fold_kernel,
        [(ITERS * EXT, LANES), (size, LANES)],
        last, last_code, far_tile, tile, mirror, mirror_far, partial,
    )
    halos = (sibling, beyond, mirror)
    tracer_next, = call(
        tracer_kernel, [block],
        tracer, zonal, meridional, count, diffusivity, *halos,
        flops=65536 * 40,
    )
    zonal_step, meridional_step, levels = call(
        flow_kernel, [block, block, (COLS, NY)],
        zonal, meridional, count, diffusivity, *halos,
        flops=65536 * 40,
    )
    group = [(i + size // 2 + 1) % size for i in range(size)]
    gram = lax.all_to_all(gram, "lon", 0, 0, tiled=True, axis_index_groups=[group])
    zonal_next, meridional_next, height = call(
        finish_kernel, [block, block, (COLS, NY)],
        gram, vectors, vectors_last, zonal_step, meridional_step, levels,
    )
    return tracer_next, zonal_next, meridional_next, height


def solution(mesh):
    column = P("lon", None)
    field = P("ens", "lon", None)
    return jax.shard_map(
        body,
        mesh=mesh,
        in_specs=(field, field, field, column, column, column),
        out_specs=(field, field, field, P("lon", "ens")),
        check_vma=False,
    )
```

```python
import functools

import jax
import jax.numpy as jnp
from jax import lax
from jax.experimental import pallas as pl
from jax.experimental.pallas import tpu as pltpu
from jax.sharding import PartitionSpec as P

K = 16
NY = 512
ITERS = 6
COLS = 8
EXT = 3 * COLS
LANES = 128
BASIS = ITERS + 1
CUT = NY - COLS
GROUPS = (BASIS * (BASIS + 1) // 2 + COLS - 1) // COLS
CHUNKS = 2

vertical_mix = 0.1
advection = 0.25
coriolis_scale = 0.3
gravity = 0.5
corner_weight = 0.25
shift = 5.0
scale = 4.0
LANE_P = 16
LANE_LC = 32
LANE_DIFF = 33
LANE_MT = 40
LANE_MU = 56
LANE_MV = 72
LANE_EDGE = 88
WIDE = 32
LANE_CODE = LANES - 2 * COLS
LANE_F = LANES - COLS

f32 = jnp.float32


def iota(shape, dim):
    return lax.broadcasted_iota(jnp.int32, shape, dim)


def thickness(k):
    return 0.5 * (0.5 + k / K)


def planetary(shape):
    latitude = (iota(shape, 1).astype(f32) + 0.5) / NY
    return coriolis_scale * (2.0 * latitude - 1.0)


def roll(value, amount, axis):
    return pltpu.roll(value, amount % value.shape[axis], axis)


def level_sum(value):
    weight = 0.5 * (0.5 + iota(value.shape, 0).astype(f32) / K)
    return jnp.sum(weight * value, axis=0, keepdims=True)


def two_sum(a, b):
    s = a + b
    t = s - a
    return s, (a - (s - t)) + (b - t)


def fast_two_sum(a, b):
    s = a + b
    return s, b - (s - a)


def split(a):
    c = 4097.0 * a
    high = c - (c - a)
    return high, a - high


def two_prod(a, b, a_parts=None, b_parts=None):
    ah, al = split(a) if a_parts is None else a_parts
    bh, bl = split(b) if b_parts is None else b_parts
    p = a * b
    return p, ((ah * bh - p) + ah * bl + al * bh) + al * bl


def pair_mul(a, b):
    p, e = two_prod(a[0], b[0])
    return p, e + (a[0] * b[1] + a[1] * b[0])


def pair_add(a, b):
    s, e = two_sum(a[0], b[0])
    return s, e + (a[1] + b[1])


def pair_norm(a):
    return fast_two_sum(a[0], a[1])


def pair_scale(a, factor):
    p, e = two_prod(a[0], factor)
    return p, e + a[1] * factor


def pair_tree(terms):
    while len(terms) > 1:
        pairs = [pair_add(terms[i], terms[i + 1]) for i in range(0, len(terms) - 1, 2)]
        terms = pairs + terms[len(terms) - len(terms) % 2:]
    return terms[0]


def pair_rows(a):
    for step in (4, 2, 1):
        a = pair_add(a, (roll(a[0], step, 0), roll(a[1], step, 0)))
    return a


def pair_pack(terms):
    shape = (COLS, LANES)
    sub = iota(shape, 0)
    zero = (jnp.zeros(shape, f32),) * 2
    terms = terms + [zero] * (COLS - len(terms))
    for step in (4, 2, 1):
        low = (sub & step) == 0
        merged = []
        for x, y in zip(terms[:step], terms[step:]):
            a = tuple(jnp.where(low, p, q) for p, q in zip(x, y))
            b = tuple(
                jnp.where(low, roll(p, -step, 0), roll(q, step, 0)) for p, q in zip(x, y)
            )
            merged.append(pair_add(a, b))
        terms = merged
    return terms[0]


def pack_kernel(
    tracer_in, zonal_in, meridional_in, count_in, diffusivity_in, surface_in,
    inner, outer,
    tracer, zonal, meridional, count, diffusivity, surface, edges, sems,
):
    shape = (COLS, NY)
    even = is_even()
    small = [
        pltpu.make_async_copy(a, b, sems.at[i])
        for i, (a, b) in enumerate(
            ((count_in, count), (diffusivity_in, diffusivity), (surface_in, surface))
        )
    ]
    large = []
    for c in range(CHUNKS):
        part = pl.ds(c * K // CHUNKS, K // CHUNKS)
        large.append(
            [
                pltpu.make_async_copy(a.at[part], b.at[part], sems.at[3 + 3 * c + i])
                for i, (a, b) in enumerate(
                    (
                        (zonal_in, zonal),
                        (meridional_in, meridional),
                        (tracer_in.at[:, :, NY - LANES:], tracer),
                    )
                )
            ]
        )
    rows = [
        pltpu.make_async_copy(
            field.at[:, x], edges.at[2 * base + i], sems.at[3 + 3 * CHUNKS + 2 * base + i]
        )
        for base, field in enumerate((tracer_in, zonal_in, meridional_in))
        for i, x in enumerate((0, COLS - 1))
    ]
    for copy in small + sum(large, []) + rows:
        copy.start()
    for copy in small:
        copy.wait()
    lc = count[...].astype(f32)
    diff = diffusivity[...]
    row, lane = iota(shape, 0), iota(shape, 1)
    tile_lane = iota((COLS, LANES), 1)
    lc_east, lc_north = roll(lc, -1, 0), roll(lc, -1, 1)
    total = jnp.zeros(shape, f32)
    turn = jnp.zeros(shape, f32)
    flux_x = jnp.zeros(shape, f32)
    flux_y = jnp.zeros(shape, f32)
    fold = jnp.zeros((COLS, LANES), f32)
    for k in range(K):
        if k % (K // CHUNKS) == 0:
            for copy in large[k // (K // CHUNKS)]:
                copy.wait()
        mask = lc > k
        t, u, v = tracer[k], zonal[k], meridional[k]
        for base, field in ((LANE_MT, t), (LANE_MU, u), (LANE_MV, v)):
            fold = jnp.where(tile_lane == base + k, field[:, -1:], fold)
        mu, mv = jnp.where(mask, u, 0.0), jnp.where(mask, v, 0.0)
        p = thickness(k) * (mu + mv)
        total += p
        turn += thickness(k) * (mv - mu)
        flux_x += jnp.where(mask, roll(p, -1, 0), 0.0) - jnp.where(lc_east > k, p, 0.0)
        flux_y += jnp.where(mask, roll(p, -1, 1), 0.0) - jnp.where(lc_north > k, p, 0.0)
    lc_fold = lc[:, NY - 1:]
    level = tile_lane - jnp.where(
        tile_lane < LANE_MU, LANE_MT, jnp.where(tile_lane < LANE_MV, LANE_MU, LANE_MV)
    )
    fold = jnp.where(level.astype(f32) < lc_fold, fold, 0.0)
    momentum = roll(fold, LANE_P - LANE_MU, 1) + roll(fold, LANE_P - LANE_MV, 1)
    fold = jnp.where((tile_lane >= LANE_P) & (tile_lane < LANE_P + K), momentum, fold)
    fold = jnp.where(tile_lane == LANE_LC, lc_fold, fold)
    fold = jnp.where(tile_lane == LANE_DIFF, diff[:, NY - 1:], fold)
    edge_level = iota((K, NY), 0).astype(f32)

    for copy in rows:
        copy.wait()
    for base in range(3):
        west, east = edges[2 * base], edges[2 * base + 1]
        west = jnp.where(edge_level < lc[:1], west, 0.0)
        east = jnp.where(edge_level < lc[COLS - 1:], east, 0.0)
        at = pl.ds(2 * COLS + base * K, K)
        inner[at] = jnp.where(even, east, west)
        outer[at] = jnp.where(even, west, east)
    flux_x = jnp.where(row == COLS - 1, 0.0, flux_x)
    flux_y = jnp.where(lane == NY - 1, 0.0, flux_y)
    west_flux = jnp.where(row == 0, 0.0, roll(flux_x, 1, 0))
    south_flux = jnp.where(lane == 0, 0.0, roll(flux_y, 1, 1))
    forcing = total + planetary(shape) * turn + diff * (
        flux_x - west_flux + flux_y - south_flux
    )
    coded = jnp.where(lc > 0, surface[...], -1.0)
    edge = jnp.zeros((K, LANES), f32)
    edge_lane = iota((K, LANES), 1)
    p = outer[32:48, NY - LANES:] + outer[48:64, NY - LANES:]
    sub = iota((COLS, LANES), 0)
    edge_lc = jnp.where(even, lc[:1], lc[COLS - 1:])
    edge_diff = jnp.where(even, diff[:1], diff[COLS - 1:])
    for j in range(COLS):
        at = NY - 1 - j
        here = LANE_EDGE + j
        edge = jnp.where(edge_lane == here, p[:, LANES - 1 - j:LANES - j], edge)
        edge = jnp.where(edge_lane == here + COLS, edge_lc[:, at:at + 1], edge)
        edge = jnp.where(edge_lane == here + 2 * COLS, edge_diff[:, at:at + 1], edge)
    blank = jnp.zeros((COLS, NY - 3 * LANES), f32)
    inner[72:80] = jnp.concatenate([fold, edge[:COLS], edge[COLS:], blank], axis=1)
    inner[0:COLS] = forcing
    inner[COLS:2 * COLS] = coded
    mine_lc = jnp.where(even, lc[COLS - 1:], lc[:1])
    mine_diff = jnp.where(even, diff[COLS - 1:], diff[:1])
    inner[64:72] = jnp.where(row == 0, mine_lc, jnp.where(row == 1, mine_diff, 0.0))
    far, next_far = jnp.where(even, COLS - 1, 0), jnp.where(even, COLS - 2, 1)
    used = jnp.where((tile_lane >= LANE_P) & (tile_lane < LANE_P + WIDE), fold, 0.0)
    moved = [
        jnp.sum(
            sum(
                jnp.where(sub == x, roll(used, (x - first) * WIDE - LANE_P, 1), 0.0)
                for x in range(first, first + LANES // WIDE)
            ),
            axis=0, keepdims=True,
        )
        for first in range(0, COLS, LANES // WIDE)
    ]
    tile_row = jnp.concatenate(moved + [jnp.zeros((1, NY - len(moved) * LANES), f32)], axis=1)
    outer[0:COLS] = jnp.where(row == far, edge_lc, jnp.where(row == next_far, tile_row, forcing))
    outer[COLS:2 * COLS] = jnp.where(row == far, edge_diff, coded)


def far_rows(pack, far, next_far):
    tile_row = jnp.where(next_far == 1, pack[1:2], pack[COLS - 2:COLS - 1])
    sub = iota((COLS, LANES), 0)
    tile = jnp.zeros((COLS, LANES), f32)
    for x in range(COLS):
        block, place = divmod(x * WIDE, LANES)
        piece = tile_row[:, block * LANES:(block + 1) * LANES]
        tile = jnp.where(sub == x, roll(piece, LANE_P - place, 1), tile)
    return (
        jnp.where(far == 0, pack[0:1], pack[COLS - 1:COLS]),
        jnp.where(far == 0, pack[COLS:COLS + 1], pack[2 * COLS - 1:2 * COLS]),
        tile,
    )


def interface_flux(mine, theirs, lc_mine, lc_theirs):
    p_mine = mine[32:48] + mine[48:64]
    p_theirs = theirs[32:48] + theirs[48:64]
    level = iota(p_mine.shape, 0).astype(f32)
    return level_sum(
        jnp.where(level < lc_mine, p_theirs, 0.0) - jnp.where(level < lc_theirs, p_mine, 0.0)
    )


def chip_forcing(even, inner, sibling):
    flux = interface_flux(inner, sibling, inner[64:65], sibling[64:65])
    own, other = inner[65:66] * flux, -sibling[65:66] * flux
    row = iota((2 * COLS, flux.shape[1]), 0)
    change = jnp.where(
        row == COLS - 1,
        jnp.where(even, own, other),
        jnp.where(row == COLS, jnp.where(even, other, own), 0.0),
    )
    return beside(even, inner[:COLS], sibling[:COLS]) + change


def is_even():
    return lax.axis_index("lon") % 2 == 0


def beside(even, west, east):
    return jnp.concatenate([jnp.where(even, west, east), jnp.where(even, east, west)], axis=0)


def far_first():
    size, index = lax.axis_size("lon"), lax.axis_index("lon")
    odd = index % 2 == 1
    return odd & (index < size // 2), ~odd & (index >= size // 2)


def patch_order(one, two, near):
    size, index = lax.axis_size("lon"), lax.axis_index("lon")
    swapped = far_first()[1]
    own = (index == 0) | (index == size // 2)
    return jnp.where(swapped, two, one), jnp.where(own, near, jnp.where(swapped, one, two))


def chip_kernel(inner, sibling, tile, near, one, two):
    even = is_even()
    ours, theirs = (pack[:72, NY - LANES:] for pack in (inner, sibling))
    full = chip_forcing(even, ours, theirs)
    code = beside(even, ours[COLS:2 * COLS], theirs[COLS:2 * COLS])
    fold = beside(even, inner[72:80, :LANES], sibling[72:80, :LANES])
    tile[...] = fold
    lane = iota((2 * COLS, LANES), 1)
    for j in range(COLS):
        at = LANES - 1 - j
        fold = jnp.where(lane == LANE_F + j, full[:, at:at + 1], fold)
        fold = jnp.where(lane == LANE_CODE + j, code[:, at:at + 1], fold)
    fold = jnp.concatenate(
        [fold[i:i + 1] for i in range(2 * COLS - 1, -1, -1)], axis=0
    )
    patches = []
    for source in (inner, sibling):
        edge = jnp.concatenate(
            [source[72:80, LANES:2 * LANES], source[72:80, 2 * LANES:3 * LANES]], axis=0
        )
        patches.append(jnp.where((lane >= LANE_EDGE) & (lane < LANE_CODE), edge, fold))
    swapped = far_first()[0]
    near[...] = patches[0]
    one[...] = jnp.where(swapped, patches[1], patches[0])
    two[...] = jnp.where(swapped, patches[0], patches[1])


def across_fold(even, chip, far):
    shape = (2 * COLS, LANES)
    level = iota(shape, 0).astype(f32)
    lane = iota((1, LANES), 1)
    flux = level_sum(
        jnp.where(level < roll(chip, -COLS, 1), far, 0.0)
        - jnp.where(level < roll(far, -COLS, 1), chip, 0.0)
    )

    def change(tile):
        product = roll(tile[:1], -2 * COLS, 1) * flux
        return jnp.where(lane >= LANE_F, roll(product, LANE_F - LANE_EDGE, 1), 0.0)

    chip_change, far_change = change(chip), -change(far)
    tile = extend(even, far[COLS:], chip, far[:COLS])
    row = iota((EXT, LANES), 0)
    west = jnp.where(row == COLS - 1, far_change, jnp.where(row == COLS, chip_change, 0.0))
    east = jnp.where(
        row == 2 * COLS - 1, chip_change, jnp.where(row == 2 * COLS, far_change, 0.0)
    )
    return tile, jnp.where(even, west, east)


def extend(even, west, chip, east):
    return jnp.concatenate(
        [
            jnp.where(even, west, chip[:COLS]),
            jnp.where(even, chip[:COLS], chip[COLS:]),
            jnp.where(even, chip[COLS:], east),
        ],
        axis=0,
    )


def basis(start, code):
    ocean = code > 0
    centre = jnp.where(ocean, code / scale, 0.0)
    around = jnp.where(ocean, 1.0 / scale, 0.0)
    lane = iota(start.shape, 1)

    def operate(q):
        along = roll(q, -1, 1) + jnp.where(lane == 0, 0.0, roll(q, 1, 1))
        side = q + corner_weight * along
        return centre * q - around * (along + roll(side, 1, 0) + roll(side, -1, 0))

    v = [start, operate(start)]
    for j in range(2, BASIS):
        v.append(2.0 * operate(v[-1]) - v[-2])
    return v


def gram_rows(blocks):
    parts = [[split(q) for q in row] for row in blocks]
    entries = []
    for i in range(BASIS):
        for j in range(i, BASIS):
            terms = [
                two_prod(a, b, a_parts, b_parts)
                for a, b, a_parts, b_parts in zip(blocks[i], blocks[j], parts[i], parts[j])
            ]
            entries.append(pair_tree(terms))
    return [pair_pack(entries[g:g + COLS]) for g in range(0, len(entries), COLS)]


def inner_kernel(
    inner, outer, sibling, beyond, last, last_code, vectors, partial, far_tile,
):
    even = is_even()
    forcing = chip_forcing(even, inner, sibling)
    coded = beside(even, inner[COLS:2 * COLS], sibling[COLS:2 * COLS])
    at_east, at_west = jnp.where(even, 0, COLS - 1), jnp.where(even, COLS - 1, 0)
    lc_out, diff_out, _ = far_rows(outer, at_west, jnp.where(even, COLS - 2, 1))
    lc_far, diff_far, far_tile[...] = far_rows(beyond, at_east, jnp.where(even, 1, COLS - 2))
    flux_out = interface_flux(outer, beyond, lc_out, lc_far)
    own, far = diff_out * flux_out, -diff_far * flux_out
    row = iota((EXT, NY), 0)
    west = jnp.where(row == COLS - 1, far, jnp.where(row == COLS, own, 0.0))
    east = jnp.where(row == 2 * COLS - 1, own, jnp.where(row == 2 * COLS, far, 0.0))
    far_forcing, far_code = beyond[:COLS], beyond[COLS:2 * COLS]
    south = extend(even, far_forcing, forcing, far_forcing) + jnp.where(even, west, east)
    code = extend(even, far_code, coded, far_code)
    last[...] = roll(south[:, NY - LANES:], -COLS, 1)
    last_code[...] = roll(code[:, NY - LANES:], -COLS, 1)
    v = basis(south, code)
    lane = iota((COLS, LANES), 1)
    blocks = []
    for j, q in enumerate(v):
        if j < ITERS:
            vectors[j * EXT:(j + 1) * EXT] = q
        cut = [q[COLS:2 * COLS, c:c + LANES] for c in range(0, NY, LANES)]
        cut[-1] = jnp.where(lane < LANES - COLS, cut[-1], 0.0)
        blocks.append(cut)
    for g, pair in enumerate(gram_rows(blocks)):
        for at, part in zip((0, GROUPS * COLS), pair):
            partial[at + g * COLS:at + (g + 1) * COLS] = part


def fold_kernel(
    last, last_code, far_tile, tile, one, two, near, partial, vectors, gram
):
    even = is_even()
    lane = iota((EXT, LANES), 1)
    mine = extend(even, far_tile[...], tile[...], far_tile[...])
    theirs, between = across_fold(even, *patch_order(one[...], two[...], near[...]))
    level = (lane - LANE_P).astype(f32)
    weight = jnp.where((lane >= LANE_P) & (lane < LANE_P + K), 0.5 * (0.5 + level / K), 0.0)
    mask_mine = (level < mine[:, LANE_LC:LANE_LC + 1]).astype(f32)
    mask_theirs = (level < theirs[:, LANE_LC:LANE_LC + 1]).astype(f32)
    flux = -jnp.sum(weight * (mask_mine * theirs + mask_theirs * mine), axis=1, keepdims=True)
    own_change = mine[:, LANE_DIFF:LANE_DIFF + 1] * flux
    far_change = theirs[:, LANE_DIFF:LANE_DIFF + 1] * flux
    beyond_fold = lane >= LANE_F
    start = jnp.where(beyond_fold, theirs, last[...]) + between
    start = start + jnp.where(
        lane == LANE_F, far_change, jnp.where(lane == LANE_F - 1, own_change, 0.0)
    )
    code = jnp.where(beyond_fold, roll(theirs, LANE_F - LANE_CODE, 1), last_code[...])
    v = basis(start, code)
    for j in range(ITERS):
        vectors[j * EXT:(j + 1) * EXT] = v[j]
    own_lane = lane[:COLS]
    summed = (own_lane >= LANE_F - COLS) & (own_lane < LANE_F)
    blocks = [[jnp.where(summed, q[COLS:2 * COLS], 0.0)] for q in v]
    size = GROUPS * COLS
    high, low = [], []
    for g, pair in enumerate(gram_rows(blocks)):
        at = g * COLS
        pair = pair_add(pair, (partial[at:at + COLS], partial[size + at:size + at + COLS]))
        high.append(pair[0])
        low.append(pair[1])
    turned = jnp.concatenate(high + low + [jnp.zeros((LANES - 2 * size, LANES), f32)], axis=0).T
    terms = [turned[i * COLS:(i + 1) * COLS] for i in range(LANES // COLS)]
    high, low = pair_norm(pair_rows(pair_tree([(t, roll(t, -size, 1)) for t in terms])))
    row = jnp.where(iota((COLS, LANES), 1) < size, high, roll(low, size, 1))
    gram[...] = jnp.broadcast_to(row[:1], gram.shape)


def coefficients(gram):
    shape = (COLS, LANES)
    tiles = [gram[i * COLS:(i + 1) * COLS] for i in range(gram.shape[0] // COLS)]
    total = pair_norm(pair_rows(pair_tree([(t, roll(t, -GROUPS * COLS, 1)) for t in tiles])))
    wide = lambda column: jnp.broadcast_to(column, shape)
    sub = iota(shape, 0)
    tile_lane = iota(shape, 1)

    def column(j):
        low, high = jnp.minimum(sub, j), jnp.maximum(sub, j)
        entry = ((low * (2 * BASIS - 1 - low)) >> 1) + high
        here = (tile_lane == entry) & (sub < BASIS)
        return tuple(
            wide(jnp.sum(jnp.where(here, part, 0.0), axis=1, keepdims=True)) for part in total
        )

    matrix = [column(j) for j in range(BASIS)]
    zero = jnp.zeros(shape, f32)
    half = scale / 2

    def times_power(pair, factor):
        return tuple(factor * part for part in pair)

    def shifted(pair):
        return pair_add(times_power(pair, shift - 1.0), pair)

    def apply(b):
        up = [half * jnp.where(sub == 0, 0.0, roll(part, 1, 0)) for part in b]
        up = tuple(jnp.where(sub == 1, 2.0 * part, part) for part in up)
        down = tuple(half * jnp.where(sub == COLS - 1, 0.0, roll(part, -1, 0)) for part in b)
        return pair_add(shifted(b), pair_add(up, down))

    images = [pair_add(shifted(matrix[0]), times_power(matrix[1], scale))]
    for j in range(1, ITERS):
        sides = pair_add(matrix[j - 1], matrix[j + 1])
        images.append(pair_add(shifted(matrix[j]), times_power(sides, half)))

    def image_of(vector, count):
        terms = []
        for j in range(count):
            at = tuple(wide(part[j:j + 1]) for part in vector)
            terms.append(pair_mul(images[j], at))
        return pair_tree(terms)

    def dot(a, b):
        return pair_rows(pair_mul(a, b))

    residual = ((sub == 0).astype(f32), zero)
    direction = residual
    solution = zero
    norm_now = tuple(wide(part[:1]) for part in matrix[0])
    floor = 1e-13 * norm_now[0]
    alive = norm_now[0] > 0
    for iteration in range(ITERS):
        applied = apply(direction)
        if iteration == 0:
            image = images[0]
            curvature = tuple(wide(part[:1]) for part in image)
        else:
            image = image_of(direction, iteration + 1)
            curvature = dot(direction, image)
        size = curvature[0] + curvature[1]
        alive = alive & (size > 0)
        step = jnp.where(alive, (norm_now[0] + norm_now[1]) / jnp.where(alive, size, 1.0), 0.0)
        solution = solution + step * direction[0]
        if iteration + 1 < ITERS:
            crossed = curvature if iteration == 0 else dot(residual, image)
            squared = dot(applied, image)
            change = pair_add(
                pair_scale(squared, step), times_power(crossed, -2.0)
            )
            norm_next = pair_norm(pair_add(norm_now, pair_scale(pair_norm(change), step)))
            residual = pair_norm(pair_add(residual, pair_scale(applied, -step)))
            ratio = jnp.where(alive, norm_next[0] / jnp.where(alive, norm_now[0], 1.0), 0.0)
            direction = pair_norm(pair_add(residual, pair_scale(direction, ratio)))
            norm_now = norm_next
            alive = alive & (norm_now[0] > floor)
    return solution


def finish_kernel(
    gram, vectors, vectors_last, zonal, meridional, levels, zonal_next, meridional_next, height
):
    x = coefficients(gram)

    def combine(part):
        terms = [x[j:j + 1, :1] * part[j * EXT:(j + 1) * EXT] for j in range(ITERS)]
        return sum(terms[1:], terms[0])

    total, window = combine(vectors), combine(vectors_last)
    near = iota((COLS, LANES), 1) >= CUT - (NY - LANES)

    def finished(value, from_window):
        value = value[COLS:2 * COLS]
        moved = roll(from_window[COLS:2 * COLS], COLS, 1)
        last = jnp.where(near, moved, value[:, NY - LANES:])
        return jnp.concatenate([value[:, :NY - LANES], last], axis=1)

    def step(axis):
        return gravity * finished(roll(total, -1, axis) - total, roll(window, -1, axis) - window)

    height[...] = finished(total, window)
    east, north = step(0), step(1)
    lc = levels[...]
    for k in range(K):
        zonal_next[k] = zonal[k] - jnp.where(lc > k, east, 0.0)
        meridional_next[k] = meridional[k] - jnp.where(lc > k, north, 0.0)


def neighbours(count, sibling, beyond, one, two):
    shape = (COLS, NY)
    even = is_even()
    row, lane = iota(shape, 0), iota(shape, 1)
    lc = count[...].astype(f32)
    mirror = patch_order(one[...], two[...], one[...])[0]
    north_tile = jnp.where(even, mirror[:COLS], mirror[COLS:])

    def around(field, west, east, north):
        return (
            jnp.where(row == COLS - 1, east, roll(field, -1, 0)),
            jnp.where(row == 0, west, roll(field, 1, 0)),
            jnp.where(lane == NY - 1, north, roll(field, -1, 1)),
            jnp.where(lane == 0, 0.0, roll(field, 1, 1)),
        )

    def sides(a, b):
        return jnp.where(even, b, a), jnp.where(even, a, b)

    def edges(at):
        return sides(sibling[at:at + 1], beyond[at:at + 1])

    def padded(field, base, k, sign):
        at = LANE_MT + base * K + k
        return around(field, *edges(2 * COLS + base * K + k), sign * north_tile[:, at:at + 1])

    beyond_lc = jnp.where(even, beyond[0:1], beyond[COLS - 1:COLS])
    west_lc, east_lc = sides(sibling[64:65], beyond_lc)
    north_lc = north_tile[:, LANE_LC:LANE_LC + 1]

    def mask_sum(mask, k):
        inside = [(c > k).astype(f32) for c in (west_lc, east_lc, north_lc)]
        return sum(around(mask, *inside))

    return lc, padded, mask_sum


def tracer_kernel(
    tracer, zonal, meridional, count, diffusivity, sibling, beyond, one, two, tracer_next
):
    lc, padded, mask_sum = neighbours(count, sibling, beyond, one, two)
    diff = diffusivity[...]

    def masked(k):
        if k < 0 or k >= K:
            return jnp.zeros_like(lc), jnp.zeros_like(lc)
        mask = (lc > k).astype(f32)
        return mask, mask * tracer[k]

    below, here = masked(-1), masked(0)
    for k in range(K):
        above = masked(k + 1)
        mask, mt = here
        t, u, v = tracer[k], zonal[k], meridional[k]
        te, tw, tn, ts = padded(mt, 0, k, 1.0)
        vertical = above[1] + below[1] - (above[0] + below[0]) * t
        tracer_next[k] = mask * (
            t
            + diff * (te + tw + tn + ts - mask_sum(mask, k) * t)
            + vertical_mix * vertical
            - advection * (u * (te - tw) + v * (tn - ts))
        )
        below, here = here, above


def flow_kernel(
    zonal, meridional, count, diffusivity, sibling, beyond, one, two,
    zonal_step, meridional_step, levels,
):
    lc, padded, mask_sum = neighbours(count, sibling, beyond, one, two)
    diff = diffusivity[...]
    turn = planetary(lc.shape)
    levels[...] = lc
    for k in range(K):
        mask = (lc > k).astype(f32)
        u, v = zonal[k], meridional[k]
        sides = mask_sum(mask, k)
        zonal_sum = sum(padded(mask * u, 1, k, -1.0))
        meridional_sum = sum(padded(mask * v, 2, k, -1.0))
        zonal_step[k] = mask * (u + diff * (zonal_sum - sides * u) + turn * v)
        meridional_step[k] = mask * (v + diff * (meridional_sum - sides * v) - turn * u)


def call(kernel, shapes, *args, flops=0, scratch=(), stay=0):
    moved = 4 * sum(a.size for a in args) + 4 * sum(
        functools.reduce(lambda x, y: x * y, s, 1) for s in shapes
    )
    space = pl.BlockSpec(memory_space=pltpu.VMEM)
    in_specs = [space] * (len(args) - stay) + [pl.BlockSpec(memory_space=pltpu.HBM)] * stay
    here = len(args) - stay
    args = args[:here] + tuple(
        pltpu.with_memory_space_constraint(a, pltpu.HBM) for a in args[here:]
    )
    return pl.pallas_call(
        kernel,
        out_shape=[jax.ShapeDtypeStruct(s, f32) for s in shapes],
        in_specs=in_specs,
        out_specs=[space] * len(shapes),
        scratch_shapes=list(scratch),
        compiler_params=pltpu.CompilerParams(vmem_limit_bytes=32 * 1024 * 1024),
        cost_estimate=pl.CostEstimate(flops=flops, bytes_accessed=moved, transcendentals=0),
    )(*args)


def body(tracer, zonal, meridional, count, diffusivity, surface):
    size = lax.axis_size("lon")
    block = (K, COLS, NY)

    def permute(value, pairs):
        return lax.ppermute(value, "lon", pairs)

    siblings = [(i, i ^ 1) for i in range(size)]
    outward = [(i, (i + 1 if i % 2 else i - 1) % size) for i in range(size)]
    first = {i: size - 1 - i for i in range(size)}
    second = {(size + 1 - 4 * (i % 2) - i) % size: i for i in range(size)}
    for i in range(1, size // 2, 2):
        first[i], second[i] = second[i], first[i]
    first[1], second[size // 2 + 1] = size // 2, 0
    arguments = (tracer, zonal, meridional, count, diffusivity, surface)
    inner, outer = call(
        pack_kernel, [(80, NY), (64, NY)], *arguments,
        scratch=[pltpu.VMEM((K, COLS, LANES), f32)]
        + [pltpu.VMEM(a.shape, a.dtype) for a in arguments[1:]]
        + [pltpu.VMEM((6, K, NY), f32), pltpu.SemaphoreType.DMA((9 + 3 * CHUNKS,))], stay=len(arguments),
    )
    beyond = permute(outer, outward)
    sibling = permute(inner, siblings)
    patch = (2 * COLS, LANES)
    tile, near, one, two = call(chip_kernel, [patch] * 4, inner, sibling)
    one = permute(one, sorted(first.items()))
    two = permute(two, sorted(second.items()))
    window = (EXT, LANES)
    last, last_code, vectors, partial, far_tile = call(
        inner_kernel,
        [
            window, window, (ITERS * EXT, NY), (2 * GROUPS * COLS, LANES), (COLS, LANES),
        ],
        inner, outer, sibling, beyond, flops=8192 * 100,
    )
    vectors_last, gram = call(
        fold_kernel,
        [(ITERS * EXT, LANES), (size, LANES)],
        last, last_code, far_tile, tile, one, two, near, partial,
    )
    halos = (sibling, beyond, one, two)
    tracer_next, = call(
        tracer_kernel, [block],
        tracer, zonal, meridional, count, diffusivity, *halos,
        flops=65536 * 40,
    )
    zonal_step, meridional_step, levels = call(
        flow_kernel, [block, block, (COLS, NY)],
        zonal, meridional, count, diffusivity, *halos,
        flops=65536 * 40,
    )
    group = [(5 * i + size // 2 - 1) % size for i in range(size)]
    gram = lax.all_to_all(gram, "lon", 0, 0, tiled=True, axis_index_groups=[group])
    zonal_next, meridional_next, height = call(
        finish_kernel, [block, block, (COLS, NY)],
        gram, vectors, vectors_last, zonal_step, meridional_step, levels,
    )
    return tracer_next, zonal_next, meridional_next, height


def solution(mesh):
    column = P("lon", None)
    field = P("ens", "lon", None)
    return jax.shard_map(
        body,
        mesh=mesh,
        in_specs=(field, field, field, column, column, column),
        out_specs=(field, field, field, P("lon", "ens")),
        check_vma=False,
    )
```

```python
import functools

import jax
import jax.numpy as jnp
from jax import lax
from jax.experimental import pallas as pl
from jax.experimental.pallas import tpu as pltpu
from jax.sharding import PartitionSpec as P

K = 16
NY = 512
ITERS = 6
COLS = 8
EXT = 3 * COLS
LANES = 128
BASIS = ITERS + 1
CUT = NY - COLS
GROUPS = (BASIS * (BASIS + 1) // 2 + COLS - 1) // COLS
CHUNKS = 2

vertical_mix = 0.1
advection = 0.25
coriolis_scale = 0.3
gravity = 0.5
corner_weight = 0.25
shift = 5.0
scale = 4.0
LANE_P = 16
LANE_LC = 32
LANE_DIFF = 33
LANE_MT = 40
LANE_MU = 56
LANE_MV = 72
LANE_EDGE = 88
WIDE = 32
LANE_CODE = LANES - 2 * COLS
LANE_F = LANES - COLS

f32 = jnp.float32


def iota(shape, dim):
    return lax.broadcasted_iota(jnp.int32, shape, dim)


def thickness(k):
    return 0.5 * (0.5 + k / K)


def planetary(shape):
    latitude = (iota(shape, 1).astype(f32) + 0.5) / NY
    return coriolis_scale * (2.0 * latitude - 1.0)


def roll(value, amount, axis):
    return pltpu.roll(value, amount % value.shape[axis], axis)


def level_sum(value):
    weight = 0.5 * (0.5 + iota(value.shape, 0).astype(f32) / K)
    return jnp.sum(weight * value, axis=0, keepdims=True)


def two_sum(a, b):
    s = a + b
    t = s - a
    return s, (a - (s - t)) + (b - t)


def fast_two_sum(a, b):
    s = a + b
    return s, b - (s - a)


def split(a):
    c = 4097.0 * a
    high = c - (c - a)
    return high, a - high


def two_prod(a, b, a_parts=None, b_parts=None):
    ah, al = split(a) if a_parts is None else a_parts
    bh, bl = split(b) if b_parts is None else b_parts
    p = a * b
    return p, ((ah * bh - p) + ah * bl + al * bh) + al * bl


def pair_mul(a, b):
    p, e = two_prod(a[0], b[0])
    return p, e + (a[0] * b[1] + a[1] * b[0])


def pair_add(a, b):
    s, e = two_sum(a[0], b[0])
    return s, e + (a[1] + b[1])


def pair_norm(a):
    return fast_two_sum(a[0], a[1])


def pair_scale(a, factor):
    p, e = two_prod(a[0], factor)
    return p, e + a[1] * factor


def pair_tree(terms):
    while len(terms) > 1:
        pairs = [pair_add(terms[i], terms[i + 1]) for i in range(0, len(terms) - 1, 2)]
        terms = pairs + terms[len(terms) - len(terms) % 2:]
    return terms[0]


def pair_rows(a):
    for step in (4, 2, 1):
        a = pair_add(a, (roll(a[0], step, 0), roll(a[1], step, 0)))
    return a


def pair_pack(terms):
    shape = (COLS, LANES)
    sub = iota(shape, 0)
    zero = (jnp.zeros(shape, f32),) * 2
    terms = terms + [zero] * (COLS - len(terms))
    for step in (4, 2, 1):
        low = (sub & step) == 0
        merged = []
        for x, y in zip(terms[:step], terms[step:]):
            a = tuple(jnp.where(low, p, q) for p, q in zip(x, y))
            b = tuple(
                jnp.where(low, roll(p, -step, 0), roll(q, step, 0)) for p, q in zip(x, y)
            )
            merged.append(pair_add(a, b))
        terms = merged
    return terms[0]


def pack_kernel(
    tracer_in, zonal_in, meridional_in, count_in, diffusivity_in, surface_in,
    inner, outer,
    tracer, zonal, meridional, count, diffusivity, surface, edges, sems,
):
    shape = (COLS, NY)
    even = is_even()
    small = [
        pltpu.make_async_copy(a, b, sems.at[i])
        for i, (a, b) in enumerate(
            ((count_in, count), (diffusivity_in, diffusivity), (surface_in, surface))
        )
    ]
    large = []
    for c in range(CHUNKS):
        part = pl.ds(c * K // CHUNKS, K // CHUNKS)
        large.append(
            [
                pltpu.make_async_copy(a.at[part], b.at[part], sems.at[3 + 3 * c + i])
                for i, (a, b) in enumerate(
                    (
                        (zonal_in, zonal),
                        (meridional_in, meridional),
                        (tracer_in.at[:, :, NY - LANES:], tracer),
                    )
                )
            ]
        )
    rows = [
        pltpu.make_async_copy(
            field.at[:, x], edges.at[2 * base + i], sems.at[3 + 3 * CHUNKS + 2 * base + i]
        )
        for base, field in enumerate((tracer_in, zonal_in, meridional_in))
        for i, x in enumerate((0, COLS - 1))
    ]
    for copy in small + sum(large, []) + rows:
        copy.start()
    for copy in small:
        copy.wait()
    lc = count[...].astype(f32)
    diff = diffusivity[...]
    row, lane = iota(shape, 0), iota(shape, 1)
    tile_lane = iota((COLS, LANES), 1)
    lc_east, lc_north = roll(lc, -1, 0), roll(lc, -1, 1)
    total = jnp.zeros(shape, f32)
    turn = jnp.zeros(shape, f32)
    flux_x = jnp.zeros(shape, f32)
    flux_y = jnp.zeros(shape, f32)
    fold = jnp.zeros((COLS, LANES), f32)
    for k in range(K):
        if k % (K // CHUNKS) == 0:
            for copy in large[k // (K // CHUNKS)]:
                copy.wait()
        mask = lc > k
        t, u, v = tracer[k], zonal[k], meridional[k]
        for base, field in ((LANE_MT, t), (LANE_MU, u), (LANE_MV, v)):
            fold = jnp.where(tile_lane == base + k, field[:, -1:], fold)
        mu, mv = jnp.where(mask, u, 0.0), jnp.where(mask, v, 0.0)
        p = thickness(k) * (mu + mv)
        total += p
        turn += thickness(k) * (mv - mu)
        flux_x += jnp.where(mask, roll(p, -1, 0), 0.0) - jnp.where(lc_east > k, p, 0.0)
        flux_y += jnp.where(mask, roll(p, -1, 1), 0.0) - jnp.where(lc_north > k, p, 0.0)
    lc_fold = lc[:, NY - 1:]
    level = tile_lane - jnp.where(
        tile_lane < LANE_MU, LANE_MT, jnp.where(tile_lane < LANE_MV, LANE_MU, LANE_MV)
    )
    fold = jnp.where(level.astype(f32) < lc_fold, fold, 0.0)
    momentum = roll(fold, LANE_P - LANE_MU, 1) + roll(fold, LANE_P - LANE_MV, 1)
    fold = jnp.where((tile_lane >= LANE_P) & (tile_lane < LANE_P + K), momentum, fold)
    fold = jnp.where(tile_lane == LANE_LC, lc_fold, fold)
    fold = jnp.where(tile_lane == LANE_DIFF, diff[:, NY - 1:], fold)
    edge_level = iota((K, NY), 0).astype(f32)

    for copy in rows:
        copy.wait()
    for base in range(3):
        west, east = edges[2 * base], edges[2 * base + 1]
        west = jnp.where(edge_level < lc[:1], west, 0.0)
        east = jnp.where(edge_level < lc[COLS - 1:], east, 0.0)
        at = pl.ds(2 * COLS + base * K, K)
        inner[at] = jnp.where(even, east, west)
        outer[at] = jnp.where(even, west, east)
    flux_x = jnp.where(row == COLS - 1, 0.0, flux_x)
    flux_y = jnp.where(lane == NY - 1, 0.0, flux_y)
    west_flux = jnp.where(row == 0, 0.0, roll(flux_x, 1, 0))
    south_flux = jnp.where(lane == 0, 0.0, roll(flux_y, 1, 1))
    forcing = total + planetary(shape) * turn + diff * (
        flux_x - west_flux + flux_y - south_flux
    )
    coded = jnp.where(lc > 0, surface[...], -1.0)
    edge = jnp.zeros((K, LANES), f32)
    edge_lane = iota((K, LANES), 1)
    p = outer[32:48, NY - LANES:] + outer[48:64, NY - LANES:]
    sub = iota((COLS, LANES), 0)
    edge_lc = jnp.where(even, lc[:1], lc[COLS - 1:])
    edge_diff = jnp.where(even, diff[:1], diff[COLS - 1:])
    for j in range(COLS):
        at = NY - 1 - j
        here = LANE_EDGE + j
        edge = jnp.where(edge_lane == here, p[:, LANES - 1 - j:LANES - j], edge)
        edge = jnp.where(edge_lane == here + COLS, edge_lc[:, at:at + 1], edge)
        edge = jnp.where(edge_lane == here + 2 * COLS, edge_diff[:, at:at + 1], edge)
    blank = jnp.zeros((COLS, NY - 3 * LANES), f32)
    inner[72:80] = jnp.concatenate([fold, edge[:COLS], edge[COLS:], blank], axis=1)
    inner[0:COLS] = forcing
    inner[COLS:2 * COLS] = coded
    mine_lc = jnp.where(even, lc[COLS - 1:], lc[:1])
    mine_diff = jnp.where(even, diff[COLS - 1:], diff[:1])
    inner[64:72] = jnp.where(row == 0, mine_lc, jnp.where(row == 1, mine_diff, 0.0))
    far, next_far = jnp.where(even, COLS - 1, 0), jnp.where(even, COLS - 2, 1)
    used = jnp.where((tile_lane >= LANE_P) & (tile_lane < LANE_P + WIDE), fold, 0.0)
    moved = [
        jnp.sum(
            sum(
                jnp.where(sub == x, roll(used, (x - first) * WIDE - LANE_P, 1), 0.0)
                for x in range(first, first + LANES // WIDE)
            ),
            axis=0, keepdims=True,
        )
        for first in range(0, COLS, LANES // WIDE)
    ]
    tile_row = jnp.concatenate(moved + [jnp.zeros((1, NY - len(moved) * LANES), f32)], axis=1)
    outer[0:COLS] = jnp.where(row == far, edge_lc, jnp.where(row == next_far, tile_row, forcing))
    outer[COLS:2 * COLS] = jnp.where(row == far, edge_diff, coded)


def far_rows(pack, far, next_far):
    tile_row = jnp.where(next_far == 1, pack[1:2], pack[COLS - 2:COLS - 1])
    sub = iota((COLS, LANES), 0)
    tile = jnp.zeros((COLS, LANES), f32)
    for x in range(COLS):
        block, place = divmod(x * WIDE, LANES)
        piece = tile_row[:, block * LANES:(block + 1) * LANES]
        tile = jnp.where(sub == x, roll(piece, LANE_P - place, 1), tile)
    return (
        jnp.where(far == 0, pack[0:1], pack[COLS - 1:COLS]),
        jnp.where(far == 0, pack[COLS:COLS + 1], pack[2 * COLS - 1:2 * COLS]),
        tile,
    )


def interface_flux(mine, theirs, lc_mine, lc_theirs):
    p_mine = mine[32:48] + mine[48:64]
    p_theirs = theirs[32:48] + theirs[48:64]
    level = iota(p_mine.shape, 0).astype(f32)
    return level_sum(
        jnp.where(level < lc_mine, p_theirs, 0.0) - jnp.where(level < lc_theirs, p_mine, 0.0)
    )


def chip_forcing(even, inner, sibling):
    flux = interface_flux(inner, sibling, inner[64:65], sibling[64:65])
    own, other = inner[65:66] * flux, -sibling[65:66] * flux
    row = iota((2 * COLS, flux.shape[1]), 0)
    change = jnp.where(
        row == COLS - 1,
        jnp.where(even, own, other),
        jnp.where(row == COLS, jnp.where(even, other, own), 0.0),
    )
    return beside(even, inner[:COLS], sibling[:COLS]) + change


def is_even():
    return lax.axis_index("lon") % 2 == 0


def beside(even, west, east):
    return jnp.concatenate([jnp.where(even, west, east), jnp.where(even, east, west)], axis=0)


def far_first():
    size, index = lax.axis_size("lon"), lax.axis_index("lon")
    odd = index % 2 == 1
    return odd & (index < size // 2), ~odd & (index >= size // 2)


def patch_order(one, two, near):
    size, index = lax.axis_size("lon"), lax.axis_index("lon")
    swapped = far_first()[1]
    own = (index == 0) | (index == size // 2)
    return jnp.where(swapped, two, one), jnp.where(own, near, jnp.where(swapped, one, two))


def chip_kernel(inner, sibling, tile, near, one, two):
    even = is_even()
    ours, theirs = (pack[:72, NY - LANES:] for pack in (inner, sibling))
    full = chip_forcing(even, ours, theirs)
    code = beside(even, ours[COLS:2 * COLS], theirs[COLS:2 * COLS])
    fold = beside(even, inner[72:80, :LANES], sibling[72:80, :LANES])
    tile[...] = fold
    lane = iota((2 * COLS, LANES), 1)
    for j in range(COLS):
        at = LANES - 1 - j
        fold = jnp.where(lane == LANE_F + j, full[:, at:at + 1], fold)
        fold = jnp.where(lane == LANE_CODE + j, code[:, at:at + 1], fold)
    fold = jnp.concatenate(
        [fold[i:i + 1] for i in range(2 * COLS - 1, -1, -1)], axis=0
    )
    patches = []
    for source in (inner, sibling):
        edge = jnp.concatenate(
            [source[72:80, LANES:2 * LANES], source[72:80, 2 * LANES:3 * LANES]], axis=0
        )
        patches.append(jnp.where((lane >= LANE_EDGE) & (lane < LANE_CODE), edge, fold))
    swapped = far_first()[0]
    near[...] = patches[0]
    one[...] = jnp.where(swapped, patches[1], patches[0])
    two[...] = jnp.where(swapped, patches[0], patches[1])


def across_fold(even, chip, far):
    shape = (2 * COLS, LANES)
    level = iota(shape, 0).astype(f32)
    lane = iota((1, LANES), 1)
    flux = level_sum(
        jnp.where(level < roll(chip, -COLS, 1), far, 0.0)
        - jnp.where(level < roll(far, -COLS, 1), chip, 0.0)
    )

    def change(tile):
        product = roll(tile[:1], -2 * COLS, 1) * flux
        return jnp.where(lane >= LANE_F, roll(product, LANE_F - LANE_EDGE, 1), 0.0)

    chip_change, far_change = change(chip), -change(far)
    tile = extend(even, far[COLS:], chip, far[:COLS])
    row = iota((EXT, LANES), 0)
    west = jnp.where(row == COLS - 1, far_change, jnp.where(row == COLS, chip_change, 0.0))
    east = jnp.where(
        row == 2 * COLS - 1, chip_change, jnp.where(row == 2 * COLS, far_change, 0.0)
    )
    return tile, jnp.where(even, west, east)


def extend(even, west, chip, east):
    return jnp.concatenate(
        [
            jnp.where(even, west, chip[:COLS]),
            jnp.where(even, chip[:COLS], chip[COLS:]),
            jnp.where(even, chip[COLS:], east),
        ],
        axis=0,
    )


def basis(start, code):
    ocean = code > 0
    centre = jnp.where(ocean, code / scale, 0.0)
    around = jnp.where(ocean, 1.0 / scale, 0.0)
    lane = iota(start.shape, 1)

    def operate(q):
        along = roll(q, -1, 1) + jnp.where(lane == 0, 0.0, roll(q, 1, 1))
        side = q + corner_weight * along
        return centre * q - around * (along + roll(side, 1, 0) + roll(side, -1, 0))

    v = [start, operate(start)]
    for j in range(2, BASIS):
        v.append(2.0 * operate(v[-1]) - v[-2])
    return v


def gram_rows(blocks):
    parts = [[split(q) for q in row] for row in blocks]
    entries = []
    for i in range(BASIS):
        for j in range(i, BASIS):
            terms = [
                two_prod(a, b, a_parts, b_parts)
                for a, b, a_parts, b_parts in zip(blocks[i], blocks[j], parts[i], parts[j])
            ]
            entries.append(pair_tree(terms))
    return [pair_pack(entries[g:g + COLS]) for g in range(0, len(entries), COLS)]


def lane_sums(groups, first, last):
    size = GROUPS * COLS
    parts = [pair[0] for pair in groups] + [pair[1] for pair in groups]
    turned = jnp.concatenate(parts + [jnp.zeros((LANES - 2 * size, LANES), f32)], axis=0).T
    terms = [turned[i:i + COLS] for i in range(first, last, COLS)]
    return pair_norm(pair_rows(pair_tree([(t, roll(t, -size, 1)) for t in terms])))


def inner_kernel(
    inner, outer, sibling, beyond, tile, last, last_code, vectors, partial, ours,
):
    even = is_even()
    forcing = chip_forcing(even, inner, sibling)
    coded = beside(even, inner[COLS:2 * COLS], sibling[COLS:2 * COLS])
    at_east, at_west = jnp.where(even, 0, COLS - 1), jnp.where(even, COLS - 1, 0)
    lc_out, diff_out, _ = far_rows(outer, at_west, jnp.where(even, COLS - 2, 1))
    lc_far, diff_far, tile_far = far_rows(beyond, at_east, jnp.where(even, 1, COLS - 2))
    flux_out = interface_flux(outer, beyond, lc_out, lc_far)
    own, far = diff_out * flux_out, -diff_far * flux_out
    row = iota((EXT, NY), 0)
    west = jnp.where(row == COLS - 1, far, jnp.where(row == COLS, own, 0.0))
    east = jnp.where(row == 2 * COLS - 1, own, jnp.where(row == 2 * COLS, far, 0.0))
    far_forcing, far_code = beyond[:COLS], beyond[COLS:2 * COLS]
    south = extend(even, far_forcing, forcing, far_forcing) + jnp.where(even, west, east)
    code = extend(even, far_code, coded, far_code)
    last[...] = roll(south[:, NY - LANES:], -COLS, 1)
    last_code[...] = roll(code[:, NY - LANES:], -COLS, 1)
    v = basis(south, code)
    lane = iota((COLS, LANES), 1)
    blocks = []
    for j, q in enumerate(v):
        if j < ITERS:
            vectors[j * EXT:(j + 1) * EXT] = q
        cut = [q[COLS:2 * COLS, c:c + LANES] for c in range(0, NY, LANES)]
        cut[-1] = jnp.where(lane < LANES - COLS, cut[-1], 0.0)
        blocks.append(cut)
    high, low = lane_sums(gram_rows(blocks), 0, LANES)
    partial[:COLS] = high
    partial[COLS:] = low
    mine = extend(even, tile_far, tile[...], tile_far)
    lane = iota((EXT, LANES), 1)
    level = (lane - LANE_P).astype(f32)
    weight = jnp.where((lane >= LANE_P) & (lane < LANE_P + K), 0.5 * (0.5 + level / K), 0.0)
    ours[:EXT] = jnp.where(level < mine[:, LANE_LC:LANE_LC + 1], weight, 0.0)
    ours[EXT:2 * EXT] = weight * mine
    ours[2 * EXT:] = jnp.where(lane == LANE_F - 1, mine[:, LANE_DIFF:LANE_DIFF + 1], 0.0)


def fold_kernel(
    last, last_code, ours, one, two, near, partial, vectors, gram
):
    even = is_even()
    lane = iota((EXT, LANES), 1)
    theirs, between = across_fold(even, *patch_order(one[...], two[...], near[...]))
    level = (lane - LANE_P).astype(f32)
    flux = -jnp.sum(
        ours[:EXT] * theirs
        + jnp.where(level < theirs[:, LANE_LC:LANE_LC + 1], ours[EXT:2 * EXT], 0.0),
        axis=1, keepdims=True,
    )
    far_change = theirs[:, LANE_DIFF:LANE_DIFF + 1] * flux
    beyond_fold = lane >= LANE_F
    start = jnp.where(beyond_fold, theirs, last[...]) + between
    start = start + jnp.where(lane == LANE_F, far_change, ours[2 * EXT:] * flux)
    code = jnp.where(beyond_fold, roll(theirs, LANE_F - LANE_CODE, 1), last_code[...])
    v = basis(start, code)
    for j in range(ITERS):
        vectors[j * EXT:(j + 1) * EXT] = v[j]
    own_lane = lane[:COLS]
    summed = (own_lane >= LANE_F - COLS) & (own_lane < LANE_F)
    blocks = [[jnp.where(summed, q[COLS:2 * COLS], 0.0)] for q in v]
    sums = lane_sums(gram_rows(blocks), LANE_F - COLS, LANE_F)
    high, low = pair_norm(pair_add(sums, (partial[:COLS], partial[COLS:])))
    size = GROUPS * COLS
    row = jnp.where(iota((COLS, LANES), 1) < size, high, roll(low, size, 1))
    gram[...] = jnp.broadcast_to(row[:1], gram.shape)


def coefficients(gram):
    shape = (COLS, LANES)
    tiles = [gram[i * COLS:(i + 1) * COLS] for i in range(gram.shape[0] // COLS)]
    total = pair_norm(pair_rows(pair_tree([(t, roll(t, -GROUPS * COLS, 1)) for t in tiles])))
    wide = lambda column: jnp.broadcast_to(column, shape)
    sub = iota(shape, 0)
    tile_lane = iota(shape, 1)

    def column(j):
        low, high = jnp.minimum(sub, j), jnp.maximum(sub, j)
        entry = ((low * (2 * BASIS - 1 - low)) >> 1) + high
        here = (tile_lane == entry) & (sub < BASIS)
        return tuple(
            wide(jnp.sum(jnp.where(here, part, 0.0), axis=1, keepdims=True)) for part in total
        )

    matrix = [column(j) for j in range(BASIS)]
    zero = jnp.zeros(shape, f32)
    half = scale / 2

    def times_power(pair, factor):
        return tuple(factor * part for part in pair)

    def shifted(pair):
        return pair_add(times_power(pair, shift - 1.0), pair)

    def apply(b):
        up = [half * jnp.where(sub == 0, 0.0, roll(part, 1, 0)) for part in b]
        up = tuple(jnp.where(sub == 1, 2.0 * part, part) for part in up)
        down = tuple(half * jnp.where(sub == COLS - 1, 0.0, roll(part, -1, 0)) for part in b)
        return pair_add(shifted(b), pair_add(up, down))

    images = [pair_add(shifted(matrix[0]), times_power(matrix[1], scale))]
    for j in range(1, ITERS):
        sides = pair_add(matrix[j - 1], matrix[j + 1])
        images.append(pair_add(shifted(matrix[j]), times_power(sides, half)))

    def image_of(vector, count):
        terms = []
        for j in range(count):
            at = tuple(wide(part[j:j + 1]) for part in vector)
            terms.append(pair_mul(images[j], at))
        return pair_tree(terms)

    def dot(a, b):
        return pair_rows(pair_mul(a, b))

    residual = ((sub == 0).astype(f32), zero)
    direction = residual
    solution = zero
    norm_now = tuple(wide(part[:1]) for part in matrix[0])
    floor = 1e-13 * norm_now[0]
    alive = norm_now[0] > 0
    for iteration in range(ITERS):
        applied = apply(direction)
        if iteration == 0:
            image = images[0]
            curvature = tuple(wide(part[:1]) for part in image)
        else:
            image = image_of(direction, iteration + 1)
            curvature = dot(direction, image)
        size = curvature[0] + curvature[1]
        alive = alive & (size > 0)
        step = jnp.where(alive, (norm_now[0] + norm_now[1]) / jnp.where(alive, size, 1.0), 0.0)
        solution = solution + step * direction[0]
        if iteration + 1 < ITERS:
            crossed = curvature if iteration == 0 else dot(residual, image)
            squared = dot(applied, image)
            change = pair_add(
                pair_scale(squared, step), times_power(crossed, -2.0)
            )
            norm_next = pair_norm(pair_add(norm_now, pair_scale(pair_norm(change), step)))
            residual = pair_norm(pair_add(residual, pair_scale(applied, -step)))
            ratio = jnp.where(alive, norm_next[0] / jnp.where(alive, norm_now[0], 1.0), 0.0)
            direction = pair_norm(pair_add(residual, pair_scale(direction, ratio)))
            norm_now = norm_next
            alive = alive & (norm_now[0] > floor)
    return solution


def finish_kernel(
    gram, vectors, vectors_last, zonal, meridional, levels, zonal_next, meridional_next, height
):
    x = coefficients(gram)

    def combine(part):
        terms = [x[j:j + 1, :1] * part[j * EXT:(j + 1) * EXT] for j in range(ITERS)]
        return sum(terms[1:], terms[0])

    total, window = combine(vectors), combine(vectors_last)
    near = iota((COLS, LANES), 1) >= CUT - (NY - LANES)

    def finished(value, from_window):
        value = value[COLS:2 * COLS]
        moved = roll(from_window[COLS:2 * COLS], COLS, 1)
        last = jnp.where(near, moved, value[:, NY - LANES:])
        return jnp.concatenate([value[:, :NY - LANES], last], axis=1)

    def step(axis):
        return gravity * finished(roll(total, -1, axis) - total, roll(window, -1, axis) - window)

    height[...] = finished(total, window)
    east, north = step(0), step(1)
    lc = levels[...]
    for k in range(K):
        zonal_next[k] = zonal[k] - jnp.where(lc > k, east, 0.0)
        meridional_next[k] = meridional[k] - jnp.where(lc > k, north, 0.0)


def neighbours(count, sibling, beyond, one, two):
    shape = (COLS, NY)
    even = is_even()
    row, lane = iota(shape, 0), iota(shape, 1)
    lc = count[...].astype(f32)
    mirror = patch_order(one[...], two[...], one[...])[0]
    north_tile = jnp.where(even, mirror[:COLS], mirror[COLS:])

    def around(field, west, east, north):
        return (
            jnp.where(row == COLS - 1, east, roll(field, -1, 0)),
            jnp.where(row == 0, west, roll(field, 1, 0)),
            jnp.where(lane == NY - 1, north, roll(field, -1, 1)),
            jnp.where(lane == 0, 0.0, roll(field, 1, 1)),
        )

    def sides(a, b):
        return jnp.where(even, b, a), jnp.where(even, a, b)

    def edges(at):
        return sides(sibling[at:at + 1], beyond[at:at + 1])

    def padded(field, base, k, sign):
        at = LANE_MT + base * K + k
        return around(field, *edges(2 * COLS + base * K + k), sign * north_tile[:, at:at + 1])

    beyond_lc = jnp.where(even, beyond[0:1], beyond[COLS - 1:COLS])
    west_lc, east_lc = sides(sibling[64:65], beyond_lc)
    north_lc = north_tile[:, LANE_LC:LANE_LC + 1]

    def mask_sum(mask, k):
        inside = [(c > k).astype(f32) for c in (west_lc, east_lc, north_lc)]
        return sum(around(mask, *inside))

    return lc, padded, mask_sum


def tracer_kernel(
    tracer, zonal, meridional, count, diffusivity, sibling, beyond, one, two, tracer_next
):
    lc, padded, mask_sum = neighbours(count, sibling, beyond, one, two)
    diff = diffusivity[...]

    def masked(k):
        if k < 0 or k >= K:
            return jnp.zeros_like(lc), jnp.zeros_like(lc)
        mask = (lc > k).astype(f32)
        return mask, mask * tracer[k]

    below, here = masked(-1), masked(0)
    for k in range(K):
        above = masked(k + 1)
        mask, mt = here
        t, u, v = tracer[k], zonal[k], meridional[k]
        te, tw, tn, ts = padded(mt, 0, k, 1.0)
        vertical = above[1] + below[1] - (above[0] + below[0]) * t
        tracer_next[k] = mask * (
            t
            + diff * (te + tw + tn + ts - mask_sum(mask, k) * t)
            + vertical_mix * vertical
            - advection * (u * (te - tw) + v * (tn - ts))
        )
        below, here = here, above


def flow_kernel(
    zonal, meridional, count, diffusivity, sibling, beyond, one, two,
    zonal_step, meridional_step, levels,
):
    lc, padded, mask_sum = neighbours(count, sibling, beyond, one, two)
    diff = diffusivity[...]
    turn = planetary(lc.shape)
    levels[...] = lc
    for k in range(K):
        mask = (lc > k).astype(f32)
        u, v = zonal[k], meridional[k]
        sides = mask_sum(mask, k)
        zonal_sum = sum(padded(mask * u, 1, k, -1.0))
        meridional_sum = sum(padded(mask * v, 2, k, -1.0))
        zonal_step[k] = mask * (u + diff * (zonal_sum - sides * u) + turn * v)
        meridional_step[k] = mask * (v + diff * (meridional_sum - sides * v) - turn * u)


def call(kernel, shapes, *args, flops=0, scratch=(), stay=0):
    moved = 4 * sum(a.size for a in args) + 4 * sum(
        functools.reduce(lambda x, y: x * y, s, 1) for s in shapes
    )
    space = pl.BlockSpec(memory_space=pltpu.VMEM)
    in_specs = [space] * (len(args) - stay) + [pl.BlockSpec(memory_space=pltpu.HBM)] * stay
    here = len(args) - stay
    args = args[:here] + tuple(
        pltpu.with_memory_space_constraint(a, pltpu.HBM) for a in args[here:]
    )
    return pl.pallas_call(
        kernel,
        out_shape=[jax.ShapeDtypeStruct(s, f32) for s in shapes],
        in_specs=in_specs,
        out_specs=[space] * len(shapes),
        scratch_shapes=list(scratch),
        compiler_params=pltpu.CompilerParams(vmem_limit_bytes=32 * 1024 * 1024),
        cost_estimate=pl.CostEstimate(flops=flops, bytes_accessed=moved, transcendentals=0),
    )(*args)


def body(tracer, zonal, meridional, count, diffusivity, surface):
    size = lax.axis_size("lon")
    block = (K, COLS, NY)

    def permute(value, pairs):
        return lax.ppermute(value, "lon", pairs)

    siblings = [(i, i ^ 1) for i in range(size)]
    outward = [(i, (i + 1 if i % 2 else i - 1) % size) for i in range(size)]
    first = {i: size - 1 - i for i in range(size)}
    second = {(size + 1 - 4 * (i % 2) - i) % size: i for i in range(size)}
    for i in range(1, size // 2, 2):
        first[i], second[i] = second[i], first[i]
    first[1], second[size // 2 + 1] = size // 2, 0
    arguments = (tracer, zonal, meridional, count, diffusivity, surface)
    inner, outer = call(
        pack_kernel, [(80, NY), (64, NY)], *arguments,
        scratch=[pltpu.VMEM((K, COLS, LANES), f32)]
        + [pltpu.VMEM(a.shape, a.dtype) for a in arguments[1:]]
        + [pltpu.VMEM((6, K, NY), f32), pltpu.SemaphoreType.DMA((9 + 3 * CHUNKS,))], stay=len(arguments),
    )
    beyond = permute(outer, outward)
    sibling = permute(inner, siblings)
    patch = (2 * COLS, LANES)
    tile, near, one, two = call(chip_kernel, [patch] * 4, inner, sibling)
    one = permute(one, sorted(first.items()))
    two = permute(two, sorted(second.items()))
    window = (EXT, LANES)
    last, last_code, vectors, partial, ours = call(
        inner_kernel,
        [
            window, window, (ITERS * EXT, NY), (2 * COLS, LANES), (3 * EXT, LANES),
        ],
        inner, outer, sibling, beyond, tile, flops=8192 * 100,
    )
    vectors_last, gram = call(
        fold_kernel,
        [(ITERS * EXT, LANES), (size, LANES)],
        last, last_code, ours, one, two, near, partial,
    )
    halos = (sibling, beyond, one, two)
    tracer_next, = call(
        tracer_kernel, [block],
        tracer, zonal, meridional, count, diffusivity, *halos,
        flops=65536 * 40,
    )
    zonal_step, meridional_step, levels = call(
        flow_kernel, [block, block, (COLS, NY)],
        zonal, meridional, count, diffusivity, *halos,
        flops=65536 * 40,
    )
    group = [(5 * i + size // 2 - 1) % size for i in range(size)]
    gram = lax.all_to_all(gram, "lon", 0, 0, tiled=True, axis_index_groups=[group])
    zonal_next, meridional_next, height = call(
        finish_kernel, [block, block, (COLS, NY)],
        gram, vectors, vectors_last, zonal_step, meridional_step, levels,
    )
    return tracer_next, zonal_next, meridional_next, height


def solution(mesh):
    column = P("lon", None)
    field = P("ens", "lon", None)
    return jax.shard_map(
        body,
        mesh=mesh,
        in_specs=(field, field, field, column, column, column),
        out_specs=(field, field, field, P("lon", "ens")),
        check_vma=False,
    )
```

```python
import functools

import jax
import jax.numpy as jnp
from jax import lax
from jax.experimental import pallas as pl
from jax.experimental.pallas import tpu as pltpu
from jax.sharding import PartitionSpec as P

K = 16
NY = 512
ITERS = 6
COLS = 8
EXT = 3 * COLS
LANES = 128
BASIS = ITERS + 1
CUT = NY - COLS
GROUPS = (BASIS * (BASIS + 1) // 2 + COLS - 1) // COLS
CHUNKS = 2

vertical_mix = 0.1
advection = 0.25
coriolis_scale = 0.3
gravity = 0.5
corner_weight = 0.25
shift = 5.0
scale = 4.0
LANE_P = 16
LANE_LC = 32
LANE_DIFF = 33
LANE_MT = 40
LANE_MU = 56
LANE_MV = 72
LANE_EDGE = 88
WIDE = 32
LANE_CODE = LANES - 2 * COLS
LANE_F = LANES - COLS

f32 = jnp.float32


def iota(shape, dim):
    return lax.broadcasted_iota(jnp.int32, shape, dim)


def thickness(k):
    return 0.5 * (0.5 + k / K)


def planetary(shape):
    latitude = (iota(shape, 1).astype(f32) + 0.5) / NY
    return coriolis_scale * (2.0 * latitude - 1.0)


def roll(value, amount, axis):
    return pltpu.roll(value, amount % value.shape[axis], axis)


def level_sum(value):
    weight = 0.5 * (0.5 + iota(value.shape, 0).astype(f32) / K)
    return jnp.sum(weight * value, axis=0, keepdims=True)


def two_sum(a, b):
    s = a + b
    t = s - a
    return s, (a - (s - t)) + (b - t)


def fast_two_sum(a, b):
    s = a + b
    return s, b - (s - a)


def split(a):
    c = 4097.0 * a
    high = c - (c - a)
    return high, a - high


def two_prod(a, b, a_parts=None, b_parts=None):
    ah, al = split(a) if a_parts is None else a_parts
    bh, bl = split(b) if b_parts is None else b_parts
    p = a * b
    return p, ((ah * bh - p) + ah * bl + al * bh) + al * bl


def pair_mul(a, b):
    p, e = two_prod(a[0], b[0])
    return p, e + (a[0] * b[1] + a[1] * b[0])


def pair_add(a, b):
    s, e = two_sum(a[0], b[0])
    return s, e + (a[1] + b[1])


def pair_norm(a):
    return fast_two_sum(a[0], a[1])


def pair_scale(a, factor):
    p, e = two_prod(a[0], factor)
    return p, e + a[1] * factor


def pair_tree(terms):
    while len(terms) > 1:
        pairs = [pair_add(terms[i], terms[i + 1]) for i in range(0, len(terms) - 1, 2)]
        terms = pairs + terms[len(terms) - len(terms) % 2:]
    return terms[0]


def pair_rows(a):
    for step in (4, 2, 1):
        a = pair_add(a, (roll(a[0], step, 0), roll(a[1], step, 0)))
    return a


def pair_pack(terms):
    shape = (COLS, LANES)
    sub = iota(shape, 0)
    zero = (jnp.zeros(shape, f32),) * 2
    terms = terms + [zero] * (COLS - len(terms))
    for step in (4, 2, 1):
        low = (sub & step) == 0
        merged = []
        for x, y in zip(terms[:step], terms[step:]):
            a = tuple(jnp.where(low, p, q) for p, q in zip(x, y))
            b = tuple(
                jnp.where(low, roll(p, -step, 0), roll(q, step, 0)) for p, q in zip(x, y)
            )
            merged.append(pair_add(a, b))
        terms = merged
    return terms[0]


def pack_kernel(
    tracer_in, zonal_in, meridional_in, count_in, diffusivity_in, surface_in,
    inner, outer,
    tracer, zonal, meridional, count, diffusivity, surface, edges, sems,
):
    shape = (COLS, NY)
    even = is_even()
    small = [
        pltpu.make_async_copy(a, b, sems.at[i])
        for i, (a, b) in enumerate(
            ((count_in, count), (diffusivity_in, diffusivity), (surface_in, surface))
        )
    ]
    large = []
    for c in range(CHUNKS):
        part = pl.ds(c * K // CHUNKS, K // CHUNKS)
        large.append(
            [
                pltpu.make_async_copy(a.at[part], b.at[part], sems.at[3 + 3 * c + i])
                for i, (a, b) in enumerate(
                    (
                        (zonal_in, zonal),
                        (meridional_in, meridional),
                        (tracer_in.at[:, :, NY - LANES:], tracer),
                    )
                )
            ]
        )
    rows = [
        pltpu.make_async_copy(
            field.at[:, x], edges.at[2 * base + i], sems.at[3 + 3 * CHUNKS + 2 * base + i]
        )
        for base, field in enumerate((tracer_in, zonal_in, meridional_in))
        for i, x in enumerate((0, COLS - 1))
    ]
    for copy in small + sum(large, []) + rows:
        copy.start()
    for copy in small:
        copy.wait()
    lc = count[...].astype(f32)
    diff = diffusivity[...]
    row, lane = iota(shape, 0), iota(shape, 1)
    tile_lane = iota((COLS, LANES), 1)
    lc_east, lc_north = roll(lc, -1, 0), roll(lc, -1, 1)
    total = jnp.zeros(shape, f32)
    turn = jnp.zeros(shape, f32)
    flux_x = jnp.zeros(shape, f32)
    flux_y = jnp.zeros(shape, f32)
    fold = jnp.zeros((COLS, LANES), f32)
    for k in range(K):
        if k % (K // CHUNKS) == 0:
            for copy in large[k // (K // CHUNKS)]:
                copy.wait()
        mask = lc > k
        t, u, v = tracer[k], zonal[k], meridional[k]
        for base, field in ((LANE_MT, t), (LANE_MU, u), (LANE_MV, v)):
            fold = jnp.where(tile_lane == base + k, field[:, -1:], fold)
        mu, mv = jnp.where(mask, u, 0.0), jnp.where(mask, v, 0.0)
        p = thickness(k) * (mu + mv)
        total += p
        turn += thickness(k) * (mv - mu)
        flux_x += jnp.where(mask, roll(p, -1, 0), 0.0) - jnp.where(lc_east > k, p, 0.0)
        flux_y += jnp.where(mask, roll(p, -1, 1), 0.0) - jnp.where(lc_north > k, p, 0.0)
    lc_fold = lc[:, NY - 1:]
    level = tile_lane - jnp.where(
        tile_lane < LANE_MU, LANE_MT, jnp.where(tile_lane < LANE_MV, LANE_MU, LANE_MV)
    )
    fold = jnp.where(level.astype(f32) < lc_fold, fold, 0.0)
    momentum = roll(fold, LANE_P - LANE_MU, 1) + roll(fold, LANE_P - LANE_MV, 1)
    fold = jnp.where((tile_lane >= LANE_P) & (tile_lane < LANE_P + K), momentum, fold)
    fold = jnp.where(tile_lane == LANE_LC, lc_fold, fold)
    fold = jnp.where(tile_lane == LANE_DIFF, diff[:, NY - 1:], fold)
    edge_level = iota((K, NY), 0).astype(f32)

    for copy in rows:
        copy.wait()
    for base in range(3):
        west, east = edges[2 * base], edges[2 * base + 1]
        west = jnp.where(edge_level < lc[:1], west, 0.0)
        east = jnp.where(edge_level < lc[COLS - 1:], east, 0.0)
        at = pl.ds(2 * COLS + base * K, K)
        inner[at] = jnp.where(even, east, west)
        outer[at] = jnp.where(even, west, east)
    flux_x = jnp.where(row == COLS - 1, 0.0, flux_x)
    flux_y = jnp.where(lane == NY - 1, 0.0, flux_y)
    west_flux = jnp.where(row == 0, 0.0, roll(flux_x, 1, 0))
    south_flux = jnp.where(lane == 0, 0.0, roll(flux_y, 1, 1))
    forcing = total + planetary(shape) * turn + diff * (
        flux_x - west_flux + flux_y - south_flux
    )
    coded = jnp.where(lc > 0, surface[...], -1.0)
    edge = jnp.zeros((K, LANES), f32)
    edge_lane = iota((K, LANES), 1)
    p = outer[32:48, NY - LANES:] + outer[48:64, NY - LANES:]
    sub = iota((COLS, LANES), 0)
    edge_lc = jnp.where(even, lc[:1], lc[COLS - 1:])
    edge_diff = jnp.where(even, diff[:1], diff[COLS - 1:])
    for j in range(COLS):
        at = NY - 1 - j
        here = LANE_EDGE + j
        edge = jnp.where(edge_lane == here, p[:, LANES - 1 - j:LANES - j], edge)
        edge = jnp.where(edge_lane == here + COLS, edge_lc[:, at:at + 1], edge)
        edge = jnp.where(edge_lane == here + 2 * COLS, edge_diff[:, at:at + 1], edge)
    blank = jnp.zeros((COLS, NY - 3 * LANES), f32)
    inner[72:80] = jnp.concatenate([fold, edge[:COLS], edge[COLS:], blank], axis=1)
    inner[0:COLS] = forcing
    inner[COLS:2 * COLS] = coded
    mine_lc = jnp.where(even, lc[COLS - 1:], lc[:1])
    mine_diff = jnp.where(even, diff[COLS - 1:], diff[:1])
    inner[64:72] = jnp.where(row == 0, mine_lc, jnp.where(row == 1, mine_diff, 0.0))
    far, next_far = jnp.where(even, COLS - 1, 0), jnp.where(even, COLS - 2, 1)
    used = jnp.where((tile_lane >= LANE_P) & (tile_lane < LANE_P + WIDE), fold, 0.0)
    moved = [
        jnp.sum(
            sum(
                jnp.where(sub == x, roll(used, (x - first) * WIDE - LANE_P, 1), 0.0)
                for x in range(first, first + LANES // WIDE)
            ),
            axis=0, keepdims=True,
        )
        for first in range(0, COLS, LANES // WIDE)
    ]
    tile_row = jnp.concatenate(moved + [jnp.zeros((1, NY - len(moved) * LANES), f32)], axis=1)
    outer[0:COLS] = jnp.where(row == far, edge_lc, jnp.where(row == next_far, tile_row, forcing))
    outer[COLS:2 * COLS] = jnp.where(row == far, edge_diff, coded)


def far_rows(pack, far, next_far):
    tile_row = jnp.where(next_far == 1, pack[1:2], pack[COLS - 2:COLS - 1])
    sub = iota((COLS, LANES), 0)
    tile = jnp.zeros((COLS, LANES), f32)
    for x in range(COLS):
        block, place = divmod(x * WIDE, LANES)
        piece = tile_row[:, block * LANES:(block + 1) * LANES]
        tile = jnp.where(sub == x, roll(piece, LANE_P - place, 1), tile)
    return (
        jnp.where(far == 0, pack[0:1], pack[COLS - 1:COLS]),
        jnp.where(far == 0, pack[COLS:COLS + 1], pack[2 * COLS - 1:2 * COLS]),
        tile,
    )


def interface_flux(mine, theirs, lc_mine, lc_theirs):
    p_mine = mine[32:48] + mine[48:64]
    p_theirs = theirs[32:48] + theirs[48:64]
    level = iota(p_mine.shape, 0).astype(f32)
    return level_sum(
        jnp.where(level < lc_mine, p_theirs, 0.0) - jnp.where(level < lc_theirs, p_mine, 0.0)
    )


def chip_forcing(even, inner, sibling):
    flux = interface_flux(inner, sibling, inner[64:65], sibling[64:65])
    own, other = inner[65:66] * flux, -sibling[65:66] * flux
    row = iota((2 * COLS, flux.shape[1]), 0)
    change = jnp.where(
        row == COLS - 1,
        jnp.where(even, own, other),
        jnp.where(row == COLS, jnp.where(even, other, own), 0.0),
    )
    return beside(even, inner[:COLS], sibling[:COLS]) + change


def is_even():
    return lax.axis_index("lon") % 2 == 0


def beside(even, west, east):
    return jnp.concatenate([jnp.where(even, west, east), jnp.where(even, east, west)], axis=0)


def far_first():
    size, index = lax.axis_size("lon"), lax.axis_index("lon")
    odd = index % 2 == 1
    return odd & (index < size // 2), ~odd & (index >= size // 2)


def patch_order(one, two, near):
    size, index = lax.axis_size("lon"), lax.axis_index("lon")
    swapped = far_first()[1]
    own = (index == 0) | (index == size // 2)
    return jnp.where(swapped, two, one), jnp.where(own, near, jnp.where(swapped, one, two))


def chip_kernel(inner, sibling, tile, near, one, two):
    even = is_even()
    ours, theirs = (pack[:72, NY - LANES:] for pack in (inner, sibling))
    full = chip_forcing(even, ours, theirs)
    code = beside(even, ours[COLS:2 * COLS], theirs[COLS:2 * COLS])
    fold = beside(even, inner[72:80, :LANES], sibling[72:80, :LANES])
    tile[...] = fold
    lane = iota((2 * COLS, LANES), 1)
    for j in range(COLS):
        at = LANES - 1 - j
        fold = jnp.where(lane == LANE_F + j, full[:, at:at + 1], fold)
        fold = jnp.where(lane == LANE_CODE + j, code[:, at:at + 1], fold)
    fold = jnp.concatenate(
        [fold[i:i + 1] for i in range(2 * COLS - 1, -1, -1)], axis=0
    )
    patches = []
    for source in (inner, sibling):
        edge = jnp.concatenate(
            [source[72:80, LANES:2 * LANES], source[72:80, 2 * LANES:3 * LANES]], axis=0
        )
        patches.append(jnp.where((lane >= LANE_EDGE) & (lane < LANE_CODE), edge, fold))
    swapped = far_first()[0]
    near[...] = patches[0]
    one[...] = jnp.where(swapped, patches[1], patches[0])
    two[...] = jnp.where(swapped, patches[0], patches[1])


def across_fold(even, chip, far):
    shape = (2 * COLS, LANES)
    level = iota(shape, 0).astype(f32)
    lane = iota((1, LANES), 1)
    flux = level_sum(
        jnp.where(level < roll(chip, -COLS, 1), far, 0.0)
        - jnp.where(level < roll(far, -COLS, 1), chip, 0.0)
    )

    def change(tile):
        product = roll(tile[:1], -2 * COLS, 1) * flux
        return jnp.where(lane >= LANE_F, roll(product, LANE_F - LANE_EDGE, 1), 0.0)

    chip_change, far_change = change(chip), -change(far)
    tile = extend(even, far[COLS:], chip, far[:COLS])
    row = iota((EXT, LANES), 0)
    west = jnp.where(row == COLS - 1, far_change, jnp.where(row == COLS, chip_change, 0.0))
    east = jnp.where(
        row == 2 * COLS - 1, chip_change, jnp.where(row == 2 * COLS, far_change, 0.0)
    )
    return tile, jnp.where(even, west, east)


def extend(even, west, chip, east):
    return jnp.concatenate(
        [
            jnp.where(even, west, chip[:COLS]),
            jnp.where(even, chip[:COLS], chip[COLS:]),
            jnp.where(even, chip[COLS:], east),
        ],
        axis=0,
    )


def basis(start, code):
    ocean = code > 0
    centre = jnp.where(ocean, code / scale, 0.0)
    around = jnp.where(ocean, 1.0 / scale, 0.0)
    lane = iota(start.shape, 1)

    def operate(q):
        along = roll(q, -1, 1) + jnp.where(lane == 0, 0.0, roll(q, 1, 1))
        side = q + corner_weight * along
        return centre * q - around * (along + roll(side, 1, 0) + roll(side, -1, 0))

    v = [start, operate(start)]
    for j in range(2, BASIS):
        v.append(2.0 * operate(v[-1]) - v[-2])
    return v


def gram_rows(blocks):
    parts = [[split(q) for q in row] for row in blocks]
    entries = []
    for i in range(BASIS):
        for j in range(i, BASIS):
            terms = [
                two_prod(a, b, a_parts, b_parts)
                for a, b, a_parts, b_parts in zip(blocks[i], blocks[j], parts[i], parts[j])
            ]
            entries.append(pair_tree(terms))
    return [pair_pack(entries[g:g + COLS]) for g in range(0, len(entries), COLS)]


def lane_sums(groups, first, last):
    size = GROUPS * COLS
    parts = [pair[0] for pair in groups] + [pair[1] for pair in groups]
    turned = jnp.concatenate(parts + [jnp.zeros((LANES - 2 * size, LANES), f32)], axis=0).T
    terms = [turned[i:i + COLS] for i in range(first, last, COLS)]
    return pair_norm(pair_rows(pair_tree([(t, roll(t, -size, 1)) for t in terms])))


def inner_kernel(
    inner, outer, sibling, beyond, tile, last, last_code, vectors, partial, ours,
):
    even = is_even()
    forcing = chip_forcing(even, inner, sibling)
    coded = beside(even, inner[COLS:2 * COLS], sibling[COLS:2 * COLS])
    at_east, at_west = jnp.where(even, 0, COLS - 1), jnp.where(even, COLS - 1, 0)
    lc_out, diff_out, _ = far_rows(outer, at_west, jnp.where(even, COLS - 2, 1))
    lc_far, diff_far, tile_far = far_rows(beyond, at_east, jnp.where(even, 1, COLS - 2))
    flux_out = interface_flux(outer, beyond, lc_out, lc_far)
    own, far = diff_out * flux_out, -diff_far * flux_out
    row = iota((EXT, NY), 0)
    west = jnp.where(row == COLS - 1, far, jnp.where(row == COLS, own, 0.0))
    east = jnp.where(row == 2 * COLS - 1, own, jnp.where(row == 2 * COLS, far, 0.0))
    far_forcing, far_code = beyond[:COLS], beyond[COLS:2 * COLS]
    south = extend(even, far_forcing, forcing, far_forcing) + jnp.where(even, west, east)
    code = extend(even, far_code, coded, far_code)
    last[...] = roll(south[:, NY - LANES:], -COLS, 1)
    last_code[...] = roll(code[:, NY - LANES:], -COLS, 1)
    v = basis(south, code)
    lane = iota((COLS, LANES), 1)
    blocks = []
    for j, q in enumerate(v):
        if j < ITERS:
            vectors[j * EXT:(j + 1) * EXT] = q
        cut = [q[COLS:2 * COLS, c:c + LANES] for c in range(0, NY, LANES)]
        cut[-1] = jnp.where(lane < LANES - COLS, cut[-1], 0.0)
        blocks.append(cut)
    high, low = lane_sums(gram_rows(blocks), 0, LANES)
    partial[:COLS] = high
    partial[COLS:] = low
    mine = extend(even, tile_far, tile[...], tile_far)
    lane = iota((EXT, LANES), 1)
    level = (lane - LANE_P).astype(f32)
    weight = jnp.where((lane >= LANE_P) & (lane < LANE_P + K), 0.5 * (0.5 + level / K), 0.0)
    ours[:EXT] = jnp.where(level < mine[:, LANE_LC:LANE_LC + 1], weight, 0.0)
    ours[EXT:2 * EXT] = weight * mine
    ours[2 * EXT:] = jnp.where(lane == LANE_F - 1, mine[:, LANE_DIFF:LANE_DIFF + 1], 0.0)


def fold_kernel(
    last, last_code, ours, one, two, near, partial, vectors, gram
):
    even = is_even()
    lane = iota((EXT, LANES), 1)
    theirs, between = across_fold(even, *patch_order(one[...], two[...], near[...]))
    level = (lane - LANE_P).astype(f32)
    flux = -jnp.sum(
        ours[:EXT] * theirs
        + jnp.where(level < theirs[:, LANE_LC:LANE_LC + 1], ours[EXT:2 * EXT], 0.0),
        axis=1, keepdims=True,
    )
    far_change = theirs[:, LANE_DIFF:LANE_DIFF + 1] * flux
    beyond_fold = lane >= LANE_F
    start = jnp.where(beyond_fold, theirs, last[...]) + between
    start = start + jnp.where(lane == LANE_F, far_change, ours[2 * EXT:] * flux)
    code = jnp.where(beyond_fold, roll(theirs, LANE_F - LANE_CODE, 1), last_code[...])
    v = basis(start, code)
    for j in range(ITERS):
        vectors[j * EXT:(j + 1) * EXT] = v[j]
    own_lane = lane[:COLS]
    summed = (own_lane >= LANE_F - COLS) & (own_lane < LANE_F)
    blocks = [[jnp.where(summed, q[COLS:2 * COLS], 0.0)] for q in v]
    sums = lane_sums(gram_rows(blocks), LANE_F - COLS, LANE_F)
    high, low = pair_norm(pair_add(sums, (partial[:COLS], partial[COLS:])))
    size = GROUPS * COLS
    row = jnp.where(iota((COLS, LANES), 1) < size, high, roll(low, size, 1))
    gram[...] = jnp.broadcast_to(row[:1], gram.shape)


def coefficients(gram):
    shape = (COLS, LANES)
    tiles = [gram[i * COLS:(i + 1) * COLS] for i in range(gram.shape[0] // COLS)]
    total = pair_norm(pair_rows(pair_tree([(t, roll(t, -GROUPS * COLS, 1)) for t in tiles])))
    wide = lambda column: jnp.broadcast_to(column, shape)
    sub = iota(shape, 0)
    tile_lane = iota(shape, 1)

    def column(j):
        low, high = jnp.minimum(sub, j), jnp.maximum(sub, j)
        entry = ((low * (2 * BASIS - 1 - low)) >> 1) + high
        here = (tile_lane == entry) & (sub < BASIS)
        return tuple(
            wide(jnp.sum(jnp.where(here, part, 0.0), axis=1, keepdims=True)) for part in total
        )

    matrix = [column(j) for j in range(BASIS)]
    zero = jnp.zeros(shape, f32)
    half = scale / 2

    def times_power(pair, factor):
        return tuple(factor * part for part in pair)

    def shifted(pair):
        return pair_add(times_power(pair, shift - 1.0), pair)

    def apply(b):
        up = [half * jnp.where(sub == 0, 0.0, roll(part, 1, 0)) for part in b]
        up = tuple(jnp.where(sub == 1, 2.0 * part, part) for part in up)
        down = tuple(half * jnp.where(sub == COLS - 1, 0.0, roll(part, -1, 0)) for part in b)
        return pair_add(shifted(b), pair_add(up, down))

    images = [pair_add(shifted(matrix[0]), times_power(matrix[1], scale))]
    for j in range(1, ITERS):
        sides = pair_add(matrix[j - 1], matrix[j + 1])
        images.append(pair_add(shifted(matrix[j]), times_power(sides, half)))

    def image_of(vector, count):
        terms = []
        for j in range(count):
            at = tuple(wide(part[j:j + 1]) for part in vector)
            terms.append(pair_mul(images[j], at))
        return pair_tree(terms)

    def dot(a, b):
        return pair_rows(pair_mul(a, b))

    residual = ((sub == 0).astype(f32), zero)
    direction = residual
    solution = zero
    norm_now = tuple(wide(part[:1]) for part in matrix[0])
    floor = 1e-13 * norm_now[0]
    alive = norm_now[0] > 0
    for iteration in range(ITERS):
        applied = apply(direction)
        if iteration == 0:
            image = images[0]
            curvature = tuple(wide(part[:1]) for part in image)
        else:
            image = image_of(direction, iteration + 1)
            curvature = dot(direction, image)
        size = curvature[0] + curvature[1]
        alive = alive & (size > 0)
        step = jnp.where(alive, (norm_now[0] + norm_now[1]) / jnp.where(alive, size, 1.0), 0.0)
        solution = solution + step * direction[0]
        if iteration + 1 < ITERS:
            crossed = curvature if iteration == 0 else dot(residual, image)
            squared = dot(applied, image)
            change = pair_add(
                pair_scale(squared, step), times_power(crossed, -2.0)
            )
            norm_next = pair_norm(pair_add(norm_now, pair_scale(pair_norm(change), step)))
            residual = pair_norm(pair_add(residual, pair_scale(applied, -step)))
            ratio = jnp.where(alive, norm_next[0] / jnp.where(alive, norm_now[0], 1.0), 0.0)
            direction = pair_norm(pair_add(residual, pair_scale(direction, ratio)))
            norm_now = norm_next
            alive = alive & (norm_now[0] > floor)
    return solution


def slope_kernel(vectors, vectors_last, parts):
    near = iota((COLS, LANES), 1) >= CUT - (NY - LANES)

    def finished(value, from_window):
        value = value[COLS:2 * COLS]
        moved = roll(from_window[COLS:2 * COLS], COLS, 1)
        last = jnp.where(near, moved, value[:, NY - LANES:])
        return jnp.concatenate([value[:, :NY - LANES], last], axis=1)

    for j in range(ITERS):
        at = slice(j * EXT, (j + 1) * EXT)
        total, window = vectors[at], vectors_last[at]
        row = 3 * j * COLS
        parts[row:row + COLS] = finished(total, window)
        for axis in (0, 1):
            row += COLS
            parts[row:row + COLS] = gravity * finished(
                roll(total, -1, axis) - total, roll(window, -1, axis) - window
            )


def finish_kernel(gram, parts, zonal, meridional, levels, zonal_next, meridional_next, height):
    x = coefficients(gram)

    def combine(which):
        rows = [(3 * j + which) * COLS for j in range(ITERS)]
        terms = [x[j:j + 1, :1] * parts[row:row + COLS] for j, row in enumerate(rows)]
        pairs = [sum(terms[j + 1:j + 2], terms[j]) for j in range(0, ITERS, 2)]
        return sum(pairs[1:], pairs[0])

    height[...] = combine(0)
    east, north = combine(1), combine(2)
    lc = levels[...]
    for k in range(K):
        zonal_next[k] = zonal[k] - jnp.where(lc > k, east, 0.0)
        meridional_next[k] = meridional[k] - jnp.where(lc > k, north, 0.0)


def neighbours(count, sibling, beyond, one, two):
    shape = (COLS, NY)
    even = is_even()
    row, lane = iota(shape, 0), iota(shape, 1)
    lc = count[...].astype(f32)
    mirror = patch_order(one[...], two[...], one[...])[0]
    north_tile = jnp.where(even, mirror[:COLS], mirror[COLS:])

    def around(field, west, east, north):
        return (
            jnp.where(row == COLS - 1, east, roll(field, -1, 0)),
            jnp.where(row == 0, west, roll(field, 1, 0)),
            jnp.where(lane == NY - 1, north, roll(field, -1, 1)),
            jnp.where(lane == 0, 0.0, roll(field, 1, 1)),
        )

    def sides(a, b):
        return jnp.where(even, b, a), jnp.where(even, a, b)

    def edges(at):
        return sides(sibling[at:at + 1], beyond[at:at + 1])

    def padded(field, base, k, sign):
        at = LANE_MT + base * K + k
        return around(field, *edges(2 * COLS + base * K + k), sign * north_tile[:, at:at + 1])

    beyond_lc = jnp.where(even, beyond[0:1], beyond[COLS - 1:COLS])
    west_lc, east_lc = sides(sibling[64:65], beyond_lc)
    north_lc = north_tile[:, LANE_LC:LANE_LC + 1]

    def mask_sum(mask, k):
        inside = [(c > k).astype(f32) for c in (west_lc, east_lc, north_lc)]
        return sum(around(mask, *inside))

    return lc, padded, mask_sum


def tracer_kernel(
    tracer, zonal, meridional, count, diffusivity, sibling, beyond, one, two, tracer_next
):
    lc, padded, mask_sum = neighbours(count, sibling, beyond, one, two)
    diff = diffusivity[...]

    def masked(k):
        if k < 0 or k >= K:
            return jnp.zeros_like(lc), jnp.zeros_like(lc)
        mask = (lc > k).astype(f32)
        return mask, mask * tracer[k]

    below, here = masked(-1), masked(0)
    for k in range(K):
        above = masked(k + 1)
        mask, mt = here
        t, u, v = tracer[k], zonal[k], meridional[k]
        te, tw, tn, ts = padded(mt, 0, k, 1.0)
        vertical = above[1] + below[1] - (above[0] + below[0]) * t
        tracer_next[k] = mask * (
            t
            + diff * (te + tw + tn + ts - mask_sum(mask, k) * t)
            + vertical_mix * vertical
            - advection * (u * (te - tw) + v * (tn - ts))
        )
        below, here = here, above


def flow_kernel(
    zonal, meridional, count, diffusivity, sibling, beyond, one, two,
    zonal_step, meridional_step, levels,
):
    lc, padded, mask_sum = neighbours(count, sibling, beyond, one, two)
    diff = diffusivity[...]
    turn = planetary(lc.shape)
    levels[...] = lc
    for k in range(K):
        mask = (lc > k).astype(f32)
        u, v = zonal[k], meridional[k]
        sides = mask_sum(mask, k)
        zonal_sum = sum(padded(mask * u, 1, k, -1.0))
        meridional_sum = sum(padded(mask * v, 2, k, -1.0))
        zonal_step[k] = mask * (u + diff * (zonal_sum - sides * u) + turn * v)
        meridional_step[k] = mask * (v + diff * (meridional_sum - sides * v) - turn * u)


def call(kernel, shapes, *args, flops=0, scratch=(), stay=0):
    moved = 4 * sum(a.size for a in args) + 4 * sum(
        functools.reduce(lambda x, y: x * y, s, 1) for s in shapes
    )
    space = pl.BlockSpec(memory_space=pltpu.VMEM)
    in_specs = [space] * (len(args) - stay) + [pl.BlockSpec(memory_space=pltpu.HBM)] * stay
    here = len(args) - stay
    args = args[:here] + tuple(
        pltpu.with_memory_space_constraint(a, pltpu.HBM) for a in args[here:]
    )
    return pl.pallas_call(
        kernel,
        out_shape=[jax.ShapeDtypeStruct(s, f32) for s in shapes],
        in_specs=in_specs,
        out_specs=[space] * len(shapes),
        scratch_shapes=list(scratch),
        compiler_params=pltpu.CompilerParams(vmem_limit_bytes=32 * 1024 * 1024),
        cost_estimate=pl.CostEstimate(flops=flops, bytes_accessed=moved, transcendentals=0),
    )(*args)


def body(tracer, zonal, meridional, count, diffusivity, surface):
    size = lax.axis_size("lon")
    block = (K, COLS, NY)

    def permute(value, pairs):
        return lax.ppermute(value, "lon", pairs)

    siblings = [(i, i ^ 1) for i in range(size)]
    outward = [(i, (i + 1 if i % 2 else i - 1) % size) for i in range(size)]
    first = {i: size - 1 - i for i in range(size)}
    second = {(size + 1 - 4 * (i % 2) - i) % size: i for i in range(size)}
    for i in range(1, size // 2, 2):
        first[i], second[i] = second[i], first[i]
    first[1], second[size // 2 + 1] = size // 2, 0
    arguments = (tracer, zonal, meridional, count, diffusivity, surface)
    inner, outer = call(
        pack_kernel, [(80, NY), (64, NY)], *arguments,
        scratch=[pltpu.VMEM((K, COLS, LANES), f32)]
        + [pltpu.VMEM(a.shape, a.dtype) for a in arguments[1:]]
        + [pltpu.VMEM((6, K, NY), f32), pltpu.SemaphoreType.DMA((9 + 3 * CHUNKS,))], stay=len(arguments),
    )
    beyond = permute(outer, outward)
    sibling = permute(inner, siblings)
    patch = (2 * COLS, LANES)
    tile, near, one, two = call(chip_kernel, [patch] * 4, inner, sibling)
    one = permute(one, sorted(first.items()))
    two = permute(two, sorted(second.items()))
    window = (EXT, LANES)
    last, last_code, vectors, partial, ours = call(
        inner_kernel,
        [
            window, window, (ITERS * EXT, NY), (2 * COLS, LANES), (3 * EXT, LANES),
        ],
        inner, outer, sibling, beyond, tile, flops=8192 * 100,
    )
    vectors_last, gram = call(
        fold_kernel,
        [(ITERS * EXT, LANES), (size, LANES)],
        last, last_code, ours, one, two, near, partial,
    )
    halos = (sibling, beyond, one, two)
    tracer_next, = call(
        tracer_kernel, [block],
        tracer, zonal, meridional, count, diffusivity, *halos,
        flops=65536 * 40,
    )
    zonal_step, meridional_step, levels = call(
        flow_kernel, [block, block, (COLS, NY)],
        zonal, meridional, count, diffusivity, *halos,
        flops=65536 * 40,
    )
    group = [(5 * i + size // 2 - 1) % size for i in range(size)]
    gram = lax.all_to_all(gram, "lon", 0, 0, tiled=True, axis_index_groups=[group])
    parts, = call(slope_kernel, [(3 * ITERS * COLS, NY)], vectors, vectors_last, flops=8192 * 20)
    zonal_next, meridional_next, height = call(
        finish_kernel, [block, block, (COLS, NY)],
        gram, parts, zonal_step, meridional_step, levels,
    )
    return tracer_next, zonal_next, meridional_next, height


def solution(mesh):
    column = P("lon", None)
    field = P("ens", "lon", None)
    return jax.shard_map(
        body,
        mesh=mesh,
        in_specs=(field, field, field, column, column, column),
        out_specs=(field, field, field, P("lon", "ens")),
        check_vma=False,
    )
```

```python
import functools

import jax
import jax.numpy as jnp
from jax import lax
from jax.experimental import pallas as pl
from jax.experimental.pallas import tpu as pltpu
from jax.sharding import PartitionSpec as P

K = 16
NY = 512
ITERS = 6
COLS = 8
EXT = 3 * COLS
LANES = 128
BASIS = ITERS + 1
CUT = NY - COLS
GROUPS = (BASIS * (BASIS + 1) // 2 + COLS - 1) // COLS
CHUNKS = 2

vertical_mix = 0.1
advection = 0.25
coriolis_scale = 0.3
gravity = 0.5
corner_weight = 0.25
shift = 5.0
scale = 4.0
LANE_P = 16
LANE_LC = 32
LANE_DIFF = 33
LANE_MT = 40
LANE_MU = 56
LANE_MV = 72
LANE_EDGE = 88
WIDE = 32
LANE_CODE = LANES - 2 * COLS
LANE_F = LANES - COLS

f32 = jnp.float32


def iota(shape, dim):
    return lax.broadcasted_iota(jnp.int32, shape, dim)


def thickness(k):
    return 0.5 * (0.5 + k / K)


def planetary(shape):
    latitude = (iota(shape, 1).astype(f32) + 0.5) / NY
    return coriolis_scale * (2.0 * latitude - 1.0)


def roll(value, amount, axis):
    return pltpu.roll(value, amount % value.shape[axis], axis)


def level_sum(value):
    weight = 0.5 * (0.5 + iota(value.shape, 0).astype(f32) / K)
    return jnp.sum(weight * value, axis=0, keepdims=True)


def two_sum(a, b):
    s = a + b
    t = s - a
    return s, (a - (s - t)) + (b - t)


def fast_two_sum(a, b):
    s = a + b
    return s, b - (s - a)


def split(a):
    c = 4097.0 * a
    high = c - (c - a)
    return high, a - high


def two_prod(a, b, a_parts=None, b_parts=None):
    ah, al = split(a) if a_parts is None else a_parts
    bh, bl = split(b) if b_parts is None else b_parts
    p = a * b
    return p, ((ah * bh - p) + ah * bl + al * bh) + al * bl


def pair_mul(a, b):
    p, e = two_prod(a[0], b[0])
    return p, e + (a[0] * b[1] + a[1] * b[0])


def pair_add(a, b):
    s, e = two_sum(a[0], b[0])
    return s, e + (a[1] + b[1])


def pair_norm(a):
    return fast_two_sum(a[0], a[1])


def pair_scale(a, factor):
    p, e = two_prod(a[0], factor)
    return p, e + a[1] * factor


def pair_tree(terms):
    while len(terms) > 1:
        pairs = [pair_add(terms[i], terms[i + 1]) for i in range(0, len(terms) - 1, 2)]
        terms = pairs + terms[len(terms) - len(terms) % 2:]
    return terms[0]


def pair_rows(a):
    for step in (4, 2, 1):
        a = pair_add(a, (roll(a[0], step, 0), roll(a[1], step, 0)))
    return a


def pair_pack(terms):
    shape = (COLS, LANES)
    sub = iota(shape, 0)
    zero = (jnp.zeros(shape, f32),) * 2
    terms = terms + [zero] * (COLS - len(terms))
    for step in (4, 2, 1):
        low = (sub & step) == 0
        merged = []
        for x, y in zip(terms[:step], terms[step:]):
            a = tuple(jnp.where(low, p, q) for p, q in zip(x, y))
            b = tuple(
                jnp.where(low, roll(p, -step, 0), roll(q, step, 0)) for p, q in zip(x, y)
            )
            merged.append(pair_add(a, b))
        terms = merged
    return terms[0]


def pack_kernel(
    tracer_in, zonal_in, meridional_in, count_in, diffusivity_in, surface_in,
    inner, outer,
    tracer, zonal, meridional, count, diffusivity, surface, edges, sems,
):
    shape = (COLS, NY)
    even = is_even()
    small = [
        pltpu.make_async_copy(a, b, sems.at[i])
        for i, (a, b) in enumerate(
            ((count_in, count), (diffusivity_in, diffusivity), (surface_in, surface))
        )
    ]
    large = []
    for c in range(CHUNKS):
        part = pl.ds(c * K // CHUNKS, K // CHUNKS)
        large.append(
            [
                pltpu.make_async_copy(a.at[part], b.at[part], sems.at[3 + 3 * c + i])
                for i, (a, b) in enumerate(
                    (
                        (zonal_in, zonal),
                        (meridional_in, meridional),
                        (tracer_in.at[:, :, NY - LANES:], tracer),
                    )
                )
            ]
        )
    rows = [
        pltpu.make_async_copy(
            field.at[:, x], edges.at[2 * base + i], sems.at[3 + 3 * CHUNKS + 2 * base + i]
        )
        for base, field in enumerate((tracer_in, zonal_in, meridional_in))
        for i, x in enumerate((0, COLS - 1))
    ]
    for copy in small + sum(large, []) + rows:
        copy.start()
    for copy in small:
        copy.wait()
    lc = count[...].astype(f32)
    diff = diffusivity[...]
    row, lane = iota(shape, 0), iota(shape, 1)
    tile_lane = iota((COLS, LANES), 1)
    lc_east, lc_north = roll(lc, -1, 0), roll(lc, -1, 1)
    total = jnp.zeros(shape, f32)
    turn = jnp.zeros(shape, f32)
    flux_x = jnp.zeros(shape, f32)
    flux_y = jnp.zeros(shape, f32)
    fold = jnp.zeros((COLS, LANES), f32)
    for k in range(K):
        if k % (K // CHUNKS) == 0:
            for copy in large[k // (K // CHUNKS)]:
                copy.wait()
        mask = lc > k
        t, u, v = tracer[k], zonal[k], meridional[k]
        for base, field in ((LANE_MT, t), (LANE_MU, u), (LANE_MV, v)):
            fold = jnp.where(tile_lane == base + k, field[:, -1:], fold)
        mu, mv = jnp.where(mask, u, 0.0), jnp.where(mask, v, 0.0)
        p = thickness(k) * (mu + mv)
        total += p
        turn += thickness(k) * (mv - mu)
        flux_x += jnp.where(mask, roll(p, -1, 0), 0.0) - jnp.where(lc_east > k, p, 0.0)
        flux_y += jnp.where(mask, roll(p, -1, 1), 0.0) - jnp.where(lc_north > k, p, 0.0)
    lc_fold = lc[:, NY - 1:]
    level = tile_lane - jnp.where(
        tile_lane < LANE_MU, LANE_MT, jnp.where(tile_lane < LANE_MV, LANE_MU, LANE_MV)
    )
    fold = jnp.where(level.astype(f32) < lc_fold, fold, 0.0)
    momentum = roll(fold, LANE_P - LANE_MU, 1) + roll(fold, LANE_P - LANE_MV, 1)
    fold = jnp.where((tile_lane >= LANE_P) & (tile_lane < LANE_P + K), momentum, fold)
    fold = jnp.where(tile_lane == LANE_LC, lc_fold, fold)
    fold = jnp.where(tile_lane == LANE_DIFF, diff[:, NY - 1:], fold)
    edge_level = iota((K, NY), 0).astype(f32)

    for copy in rows:
        copy.wait()
    for base in range(3):
        west, east = edges[2 * base], edges[2 * base + 1]
        west = jnp.where(edge_level < lc[:1], west, 0.0)
        east = jnp.where(edge_level < lc[COLS - 1:], east, 0.0)
        at = pl.ds(2 * COLS + base * K, K)
        inner[at] = jnp.where(even, east, west)
        outer[at] = jnp.where(even, west, east)
    flux_x = jnp.where(row == COLS - 1, 0.0, flux_x)
    flux_y = jnp.where(lane == NY - 1, 0.0, flux_y)
    west_flux = jnp.where(row == 0, 0.0, roll(flux_x, 1, 0))
    south_flux = jnp.where(lane == 0, 0.0, roll(flux_y, 1, 1))
    forcing = total + planetary(shape) * turn + diff * (
        flux_x - west_flux + flux_y - south_flux
    )
    coded = jnp.where(lc > 0, surface[...], -1.0)
    edge = jnp.zeros((K, LANES), f32)
    edge_lane = iota((K, LANES), 1)
    p = outer[32:48, NY - LANES:] + outer[48:64, NY - LANES:]
    sub = iota((COLS, LANES), 0)
    edge_lc = jnp.where(even, lc[:1], lc[COLS - 1:])
    edge_diff = jnp.where(even, diff[:1], diff[COLS - 1:])
    for j in range(COLS):
        at = NY - 1 - j
        here = LANE_EDGE + j
        edge = jnp.where(edge_lane == here, p[:, LANES - 1 - j:LANES - j], edge)
        edge = jnp.where(edge_lane == here + COLS, edge_lc[:, at:at + 1], edge)
        edge = jnp.where(edge_lane == here + 2 * COLS, edge_diff[:, at:at + 1], edge)
    blank = jnp.zeros((COLS, NY - 3 * LANES), f32)
    inner[72:80] = jnp.concatenate([fold, edge[:COLS], edge[COLS:], blank], axis=1)
    inner[0:COLS] = forcing
    inner[COLS:2 * COLS] = coded
    mine_lc = jnp.where(even, lc[COLS - 1:], lc[:1])
    mine_diff = jnp.where(even, diff[COLS - 1:], diff[:1])
    inner[64:72] = jnp.where(row == 0, mine_lc, jnp.where(row == 1, mine_diff, 0.0))
    far, next_far = jnp.where(even, COLS - 1, 0), jnp.where(even, COLS - 2, 1)
    used = jnp.where((tile_lane >= LANE_P) & (tile_lane < LANE_P + WIDE), fold, 0.0)
    moved = [
        jnp.sum(
            sum(
                jnp.where(sub == x, roll(used, (x - first) * WIDE - LANE_P, 1), 0.0)
                for x in range(first, first + LANES // WIDE)
            ),
            axis=0, keepdims=True,
        )
        for first in range(0, COLS, LANES // WIDE)
    ]
    tile_row = jnp.concatenate(moved + [jnp.zeros((1, NY - len(moved) * LANES), f32)], axis=1)
    outer[0:COLS] = jnp.where(row == far, edge_lc, jnp.where(row == next_far, tile_row, forcing))
    outer[COLS:2 * COLS] = jnp.where(row == far, edge_diff, coded)


def far_rows(pack, far, next_far):
    tile_row = jnp.where(next_far == 1, pack[1:2], pack[COLS - 2:COLS - 1])
    sub = iota((COLS, LANES), 0)
    tile = jnp.zeros((COLS, LANES), f32)
    for x in range(COLS):
        block, place = divmod(x * WIDE, LANES)
        piece = tile_row[:, block * LANES:(block + 1) * LANES]
        tile = jnp.where(sub == x, roll(piece, LANE_P - place, 1), tile)
    return (
        jnp.where(far == 0, pack[0:1], pack[COLS - 1:COLS]),
        jnp.where(far == 0, pack[COLS:COLS + 1], pack[2 * COLS - 1:2 * COLS]),
        tile,
    )


def interface_flux(mine, theirs, lc_mine, lc_theirs):
    p_mine = mine[32:48] + mine[48:64]
    p_theirs = theirs[32:48] + theirs[48:64]
    level = iota(p_mine.shape, 0).astype(f32)
    return level_sum(
        jnp.where(level < lc_mine, p_theirs, 0.0) - jnp.where(level < lc_theirs, p_mine, 0.0)
    )


def chip_forcing(even, inner, sibling):
    flux = interface_flux(inner, sibling, inner[64:65], sibling[64:65])
    own, other = inner[65:66] * flux, -sibling[65:66] * flux
    row = iota((2 * COLS, flux.shape[1]), 0)
    change = jnp.where(
        row == COLS - 1,
        jnp.where(even, own, other),
        jnp.where(row == COLS, jnp.where(even, other, own), 0.0),
    )
    return beside(even, inner[:COLS], sibling[:COLS]) + change


def is_even():
    return lax.axis_index("lon") % 2 == 0


def beside(even, west, east):
    return jnp.concatenate([jnp.where(even, west, east), jnp.where(even, east, west)], axis=0)


def far_first():
    size, index = lax.axis_size("lon"), lax.axis_index("lon")
    odd = index % 2 == 1
    return odd & (index < size // 2), ~odd & (index >= size // 2)


def patch_order(one, two, near):
    size, index = lax.axis_size("lon"), lax.axis_index("lon")
    swapped = far_first()[1]
    own = (index == 0) | (index == size // 2)
    return jnp.where(swapped, two, one), jnp.where(own, near, jnp.where(swapped, one, two))


def chip_kernel(inner, sibling, tile, near, one, two):
    even = is_even()
    ours, theirs = (pack[:72, NY - LANES:] for pack in (inner, sibling))
    full = chip_forcing(even, ours, theirs)
    code = beside(even, ours[COLS:2 * COLS], theirs[COLS:2 * COLS])
    fold = beside(even, inner[72:80, :LANES], sibling[72:80, :LANES])
    tile[...] = fold
    lane = iota((2 * COLS, LANES), 1)
    for j in range(COLS):
        at = LANES - 1 - j
        fold = jnp.where(lane == LANE_F + j, full[:, at:at + 1], fold)
        fold = jnp.where(lane == LANE_CODE + j, code[:, at:at + 1], fold)
    fold = jnp.concatenate(
        [fold[i:i + 1] for i in range(2 * COLS - 1, -1, -1)], axis=0
    )
    patches = []
    for source in (inner, sibling):
        edge = jnp.concatenate(
            [source[72:80, LANES:2 * LANES], source[72:80, 2 * LANES:3 * LANES]], axis=0
        )
        patches.append(jnp.where((lane >= LANE_EDGE) & (lane < LANE_CODE), edge, fold))
    swapped = far_first()[0]
    near[...] = patches[0]
    one[...] = jnp.where(swapped, patches[1], patches[0])
    two[...] = jnp.where(swapped, patches[0], patches[1])


def across_fold(even, chip, far):
    shape = (2 * COLS, LANES)
    level = iota(shape, 0).astype(f32)
    lane = iota((1, LANES), 1)
    flux = level_sum(
        jnp.where(level < roll(chip, -COLS, 1), far, 0.0)
        - jnp.where(level < roll(far, -COLS, 1), chip, 0.0)
    )

    def change(tile):
        product = roll(tile[:1], -2 * COLS, 1) * flux
        return jnp.where(lane >= LANE_F, roll(product, LANE_F - LANE_EDGE, 1), 0.0)

    chip_change, far_change = change(chip), -change(far)
    tile = extend(even, far[COLS:], chip, far[:COLS])
    row = iota((EXT, LANES), 0)
    west = jnp.where(row == COLS - 1, far_change, jnp.where(row == COLS, chip_change, 0.0))
    east = jnp.where(
        row == 2 * COLS - 1, chip_change, jnp.where(row == 2 * COLS, far_change, 0.0)
    )
    return tile, jnp.where(even, west, east)


def extend(even, west, chip, east):
    return jnp.concatenate(
        [
            jnp.where(even, west, chip[:COLS]),
            jnp.where(even, chip[:COLS], chip[COLS:]),
            jnp.where(even, chip[COLS:], east),
        ],
        axis=0,
    )


def basis(start, code):
    ocean = code > 0
    centre = jnp.where(ocean, code / scale, 0.0)
    around = jnp.where(ocean, 1.0 / scale, 0.0)
    lane = iota(start.shape, 1)

    def operate(q):
        along = roll(q, -1, 1) + jnp.where(lane == 0, 0.0, roll(q, 1, 1))
        side = q + corner_weight * along
        return centre * q - around * (along + roll(side, 1, 0) + roll(side, -1, 0))

    v = [start, operate(start)]
    for j in range(2, BASIS):
        v.append(2.0 * operate(v[-1]) - v[-2])
    return v


def gram_rows(blocks):
    parts = [[split(q) for q in row] for row in blocks]
    entries = []
    for i in range(BASIS):
        for j in range(i, BASIS):
            terms = [
                two_prod(a, b, a_parts, b_parts)
                for a, b, a_parts, b_parts in zip(blocks[i], blocks[j], parts[i], parts[j])
            ]
            entries.append(pair_tree(terms))
    return [pair_pack(entries[g:g + COLS]) for g in range(0, len(entries), COLS)]


def lane_sums(groups, first, last):
    size = GROUPS * COLS
    parts = [pair[0] for pair in groups] + [pair[1] for pair in groups]
    turned = jnp.concatenate(parts + [jnp.zeros((LANES - 2 * size, LANES), f32)], axis=0).T
    terms = [turned[i:i + COLS] for i in range(first, last, COLS)]
    return pair_norm(pair_rows(pair_tree([(t, roll(t, -size, 1)) for t in terms])))


def inner_kernel(
    inner, outer, sibling, beyond, tile, last, last_code, vectors, partial, ours,
):
    even = is_even()
    forcing = chip_forcing(even, inner, sibling)
    coded = beside(even, inner[COLS:2 * COLS], sibling[COLS:2 * COLS])
    at_east, at_west = jnp.where(even, 0, COLS - 1), jnp.where(even, COLS - 1, 0)
    lc_out, diff_out, _ = far_rows(outer, at_west, jnp.where(even, COLS - 2, 1))
    lc_far, diff_far, tile_far = far_rows(beyond, at_east, jnp.where(even, 1, COLS - 2))
    flux_out = interface_flux(outer, beyond, lc_out, lc_far)
    own, far = diff_out * flux_out, -diff_far * flux_out
    row = iota((EXT, NY), 0)
    west = jnp.where(row == COLS - 1, far, jnp.where(row == COLS, own, 0.0))
    east = jnp.where(row == 2 * COLS - 1, own, jnp.where(row == 2 * COLS, far, 0.0))
    far_forcing, far_code = beyond[:COLS], beyond[COLS:2 * COLS]
    south = extend(even, far_forcing, forcing, far_forcing) + jnp.where(even, west, east)
    code = extend(even, far_code, coded, far_code)
    last[...] = roll(south[:, NY - LANES:], -COLS, 1)
    last_code[...] = roll(code[:, NY - LANES:], -COLS, 1)
    v = basis(south, code)
    lane = iota((COLS, LANES), 1)
    blocks = []
    for j, q in enumerate(v):
        if j < ITERS:
            vectors[j * EXT:(j + 1) * EXT] = q
        cut = [q[COLS:2 * COLS, c:c + LANES] for c in range(0, NY, LANES)]
        cut[-1] = jnp.where(lane < LANES - COLS, cut[-1], 0.0)
        blocks.append(cut)
    high, low = lane_sums(gram_rows(blocks), 0, LANES)
    partial[:COLS] = high
    partial[COLS:] = low
    mine = extend(even, tile_far, tile[...], tile_far)
    lane = iota((EXT, LANES), 1)
    level = (lane - LANE_P).astype(f32)
    weight = jnp.where((lane >= LANE_P) & (lane < LANE_P + K), 0.5 * (0.5 + level / K), 0.0)
    ours[:EXT] = jnp.where(level < mine[:, LANE_LC:LANE_LC + 1], weight, 0.0)
    ours[EXT:2 * EXT] = weight * mine
    ours[2 * EXT:] = jnp.where(lane == LANE_F - 1, mine[:, LANE_DIFF:LANE_DIFF + 1], 0.0)


def fold_kernel(
    last, last_code, ours, one, two, near, partial, vectors, gram
):
    even = is_even()
    lane = iota((EXT, LANES), 1)
    theirs, between = across_fold(even, *patch_order(one[...], two[...], near[...]))
    level = (lane - LANE_P).astype(f32)
    flux = -jnp.sum(
        ours[:EXT] * theirs
        + jnp.where(level < theirs[:, LANE_LC:LANE_LC + 1], ours[EXT:2 * EXT], 0.0),
        axis=1, keepdims=True,
    )
    far_change = theirs[:, LANE_DIFF:LANE_DIFF + 1] * flux
    beyond_fold = lane >= LANE_F
    start = jnp.where(beyond_fold, theirs, last[...]) + between
    start = start + jnp.where(lane == LANE_F, far_change, ours[2 * EXT:] * flux)
    code = jnp.where(beyond_fold, roll(theirs, LANE_F - LANE_CODE, 1), last_code[...])
    v = basis(start, code)
    for j in range(ITERS):
        vectors[j * EXT:(j + 1) * EXT] = v[j]
    own_lane = lane[:COLS]
    summed = (own_lane >= LANE_F - COLS) & (own_lane < LANE_F)
    blocks = [[jnp.where(summed, q[COLS:2 * COLS], 0.0)] for q in v]
    sums = lane_sums(gram_rows(blocks), LANE_F - COLS, LANE_F)
    high, low = pair_norm(pair_add(sums, (partial[:COLS], partial[COLS:])))
    size = GROUPS * COLS
    row = jnp.where(iota((COLS, LANES), 1) < size, high, roll(low, size, 1))
    gram[...] = jnp.broadcast_to(row[:1], gram.shape)


def coefficients(gram):
    shape = (COLS, LANES)
    tiles = [gram[i * COLS:(i + 1) * COLS] for i in range(gram.shape[0] // COLS)]
    total = pair_norm(pair_rows(pair_tree([(t, roll(t, -GROUPS * COLS, 1)) for t in tiles])))
    wide = lambda column: jnp.broadcast_to(column, shape)
    sub = iota(shape, 0)
    tile_lane = iota(shape, 1)

    def column(j):
        low, high = jnp.minimum(sub, j), jnp.maximum(sub, j)
        entry = ((low * (2 * BASIS - 1 - low)) >> 1) + high
        here = (tile_lane == entry) & (sub < BASIS)
        return tuple(
            wide(jnp.sum(jnp.where(here, part, 0.0), axis=1, keepdims=True)) for part in total
        )

    matrix = [column(j) for j in range(BASIS)]
    zero = jnp.zeros(shape, f32)
    half = scale / 2

    def times_power(pair, factor):
        return tuple(factor * part for part in pair)

    def shifted(pair):
        return pair_add(times_power(pair, shift - 1.0), pair)

    def apply(b):
        up = [half * jnp.where(sub == 0, 0.0, roll(part, 1, 0)) for part in b]
        up = tuple(jnp.where(sub == 1, 2.0 * part, part) for part in up)
        down = tuple(half * jnp.where(sub == COLS - 1, 0.0, roll(part, -1, 0)) for part in b)
        return pair_add(shifted(b), pair_add(up, down))

    images = [pair_add(shifted(matrix[0]), times_power(matrix[1], scale))]
    for j in range(1, ITERS):
        sides = pair_add(matrix[j - 1], matrix[j + 1])
        images.append(pair_add(shifted(matrix[j]), times_power(sides, half)))

    def image_of(vector, count):
        terms = []
        for j in range(count):
            at = tuple(wide(part[j:j + 1]) for part in vector)
            terms.append(pair_mul(images[j], at))
        return pair_tree(terms)

    def dot(a, b):
        return pair_rows(pair_mul(a, b))

    residual = ((sub == 0).astype(f32), zero)
    direction = residual
    solution = zero
    norm_now = tuple(wide(part[:1]) for part in matrix[0])
    floor = 1e-13 * norm_now[0]
    alive = norm_now[0] > 0
    for iteration in range(ITERS):
        applied = apply(direction)
        if iteration == 0:
            image = images[0]
            curvature = tuple(wide(part[:1]) for part in image)
        else:
            image = image_of(direction, iteration + 1)
            curvature = dot(direction, image)
        size = curvature[0] + curvature[1]
        alive = alive & (size > 0)
        step = jnp.where(alive, (norm_now[0] + norm_now[1]) / jnp.where(alive, size, 1.0), 0.0)
        solution = solution + step * direction[0]
        if iteration + 1 < ITERS:
            crossed = curvature if iteration == 0 else dot(residual, image)
            squared = dot(applied, image)
            change = pair_add(
                pair_scale(squared, step), times_power(crossed, -2.0)
            )
            norm_next = pair_norm(pair_add(norm_now, pair_scale(pair_norm(change), step)))
            residual = pair_norm(pair_add(residual, pair_scale(applied, -step)))
            ratio = jnp.where(alive, norm_next[0] / jnp.where(alive, norm_now[0], 1.0), 0.0)
            direction = pair_norm(pair_add(residual, pair_scale(direction, ratio)))
            norm_now = norm_next
            alive = alive & (norm_now[0] > floor)
    return solution


def slope_kernel(vectors, vectors_last, parts):
    near = iota((COLS, LANES), 1) >= CUT - (NY - LANES)

    def finished(value, from_window):
        value = value[COLS:2 * COLS]
        moved = roll(from_window[COLS:2 * COLS], COLS, 1)
        last = jnp.where(near, moved, value[:, NY - LANES:])
        return jnp.concatenate([value[:, :NY - LANES], last], axis=1)

    for j in range(ITERS):
        at = slice(j * EXT, (j + 1) * EXT)
        total, window = vectors[at], vectors_last[at]
        row = 3 * j * COLS
        parts[row:row + COLS] = finished(total, window)
        for axis in (0, 1):
            row += COLS
            parts[row:row + COLS] = gravity * finished(
                roll(total, -1, axis) - total, roll(window, -1, axis) - window
            )


def finish_kernel(gram, parts, zonal, meridional, levels, zonal_next, meridional_next, height):
    solution_rows = coefficients(gram)
    x = [
        jnp.concatenate(
            [jnp.broadcast_to(solution_rows[j:j + 1], (COLS, LANES))] * (NY // LANES), axis=1
        )
        for j in range(ITERS)
    ]

    def combine(which):
        rows = [(3 * j + which) * COLS for j in range(ITERS)]
        terms = [x[j] * parts[row:row + COLS] for j, row in enumerate(rows)]
        pairs = [sum(terms[j + 1:j + 2], terms[j]) for j in range(0, ITERS, 2)]
        return sum(pairs[1:], pairs[0])

    height[...] = combine(0)
    east, north = combine(1), combine(2)
    lc = levels[...]
    for k in range(K):
        zonal_next[k] = zonal[k] - jnp.where(lc > k, east, 0.0)
        meridional_next[k] = meridional[k] - jnp.where(lc > k, north, 0.0)


def neighbours(count, sibling, beyond, one, two):
    shape = (COLS, NY)
    even = is_even()
    row, lane = iota(shape, 0), iota(shape, 1)
    lc = count[...].astype(f32)
    mirror = patch_order(one[...], two[...], one[...])[0]
    north_tile = jnp.where(even, mirror[:COLS], mirror[COLS:])

    def around(field, west, east, north):
        return (
            jnp.where(row == COLS - 1, east, roll(field, -1, 0)),
            jnp.where(row == 0, west, roll(field, 1, 0)),
            jnp.where(lane == NY - 1, north, roll(field, -1, 1)),
            jnp.where(lane == 0, 0.0, roll(field, 1, 1)),
        )

    def sides(a, b):
        return jnp.where(even, b, a), jnp.where(even, a, b)

    def edges(at):
        return sides(sibling[at:at + 1], beyond[at:at + 1])

    def padded(field, base, k, sign):
        at = LANE_MT + base * K + k
        return around(field, *edges(2 * COLS + base * K + k), sign * north_tile[:, at:at + 1])

    beyond_lc = jnp.where(even, beyond[0:1], beyond[COLS - 1:COLS])
    west_lc, east_lc = sides(sibling[64:65], beyond_lc)
    north_lc = north_tile[:, LANE_LC:LANE_LC + 1]

    def mask_sum(mask, k):
        inside = [(c > k).astype(f32) for c in (west_lc, east_lc, north_lc)]
        return sum(around(mask, *inside))

    return lc, padded, mask_sum


def tracer_kernel(
    tracer, zonal, meridional, count, diffusivity, sibling, beyond, one, two, tracer_next
):
    lc, padded, mask_sum = neighbours(count, sibling, beyond, one, two)
    diff = diffusivity[...]

    def masked(k):
        if k < 0 or k >= K:
            return jnp.zeros_like(lc), jnp.zeros_like(lc)
        mask = (lc > k).astype(f32)
        return mask, mask * tracer[k]

    below, here = masked(-1), masked(0)
    for k in range(K):
        above = masked(k + 1)
        mask, mt = here
        t, u, v = tracer[k], zonal[k], meridional[k]
        te, tw, tn, ts = padded(mt, 0, k, 1.0)
        vertical = above[1] + below[1] - (above[0] + below[0]) * t
        tracer_next[k] = mask * (
            t
            + diff * (te + tw + tn + ts - mask_sum(mask, k) * t)
            + vertical_mix * vertical
            - advection * (u * (te - tw) + v * (tn - ts))
        )
        below, here = here, above


def flow_kernel(
    zonal, meridional, count, diffusivity, sibling, beyond, one, two,
    zonal_step, meridional_step, levels,
):
    lc, padded, mask_sum = neighbours(count, sibling, beyond, one, two)
    diff = diffusivity[...]
    turn = planetary(lc.shape)
    levels[...] = lc
    for k in range(K):
        mask = (lc > k).astype(f32)
        u, v = zonal[k], meridional[k]
        sides = mask_sum(mask, k)
        zonal_sum = sum(padded(mask * u, 1, k, -1.0))
        meridional_sum = sum(padded(mask * v, 2, k, -1.0))
        zonal_step[k] = mask * (u + diff * (zonal_sum - sides * u) + turn * v)
        meridional_step[k] = mask * (v + diff * (meridional_sum - sides * v) - turn * u)


def call(kernel, shapes, *args, flops=0, scratch=(), stay=0):
    moved = 4 * sum(a.size for a in args) + 4 * sum(
        functools.reduce(lambda x, y: x * y, s, 1) for s in shapes
    )
    space = pl.BlockSpec(memory_space=pltpu.VMEM)
    in_specs = [space] * (len(args) - stay) + [pl.BlockSpec(memory_space=pltpu.HBM)] * stay
    here = len(args) - stay
    args = args[:here] + tuple(
        pltpu.with_memory_space_constraint(a, pltpu.HBM) for a in args[here:]
    )
    return pl.pallas_call(
        kernel,
        out_shape=[jax.ShapeDtypeStruct(s, f32) for s in shapes],
        in_specs=in_specs,
        out_specs=[space] * len(shapes),
        scratch_shapes=list(scratch),
        compiler_params=pltpu.CompilerParams(vmem_limit_bytes=32 * 1024 * 1024),
        cost_estimate=pl.CostEstimate(flops=flops, bytes_accessed=moved, transcendentals=0),
    )(*args)


def body(tracer, zonal, meridional, count, diffusivity, surface):
    size = lax.axis_size("lon")
    block = (K, COLS, NY)

    def permute(value, pairs):
        return lax.ppermute(value, "lon", pairs)

    siblings = [(i, i ^ 1) for i in range(size)]
    outward = [(i, (i + 1 if i % 2 else i - 1) % size) for i in range(size)]
    first = {i: size - 1 - i for i in range(size)}
    second = {(size + 1 - 4 * (i % 2) - i) % size: i for i in range(size)}
    for i in range(1, size // 2, 2):
        first[i], second[i] = second[i], first[i]
    first[1], second[size // 2 + 1] = size // 2, 0
    arguments = (tracer, zonal, meridional, count, diffusivity, surface)
    inner, outer = call(
        pack_kernel, [(80, NY), (64, NY)], *arguments,
        scratch=[pltpu.VMEM((K, COLS, LANES), f32)]
        + [pltpu.VMEM(a.shape, a.dtype) for a in arguments[1:]]
        + [pltpu.VMEM((6, K, NY), f32), pltpu.SemaphoreType.DMA((9 + 3 * CHUNKS,))], stay=len(arguments),
    )
    beyond = permute(outer, outward)
    sibling = permute(inner, siblings)
    patch = (2 * COLS, LANES)
    tile, near, one, two = call(chip_kernel, [patch] * 4, inner, sibling)
    one = permute(one, sorted(first.items()))
    two = permute(two, sorted(second.items()))
    window = (EXT, LANES)
    last, last_code, vectors, partial, ours = call(
        inner_kernel,
        [
            window, window, (ITERS * EXT, NY), (2 * COLS, LANES), (3 * EXT, LANES),
        ],
        inner, outer, sibling, beyond, tile, flops=8192 * 100,
    )
    vectors_last, gram = call(
        fold_kernel,
        [(ITERS * EXT, LANES), (size, LANES)],
        last, last_code, ours, one, two, near, partial,
    )
    halos = (sibling, beyond, one, two)
    tracer_next, = call(
        tracer_kernel, [block],
        tracer, zonal, meridional, count, diffusivity, *halos,
        flops=65536 * 40,
    )
    zonal_step, meridional_step, levels = call(
        flow_kernel, [block, block, (COLS, NY)],
        zonal, meridional, count, diffusivity, *halos,
        flops=65536 * 40,
    )
    group = [(5 * i + size // 2 - 1) % size for i in range(size)]
    gram = lax.all_to_all(gram, "lon", 0, 0, tiled=True, axis_index_groups=[group])
    parts, = call(slope_kernel, [(3 * ITERS * COLS, NY)], vectors, vectors_last, flops=8192 * 20)
    zonal_next, meridional_next, height = call(
        finish_kernel, [block, block, (COLS, NY)],
        gram, parts, zonal_step, meridional_step, levels,
    )
    return tracer_next, zonal_next, meridional_next, height


def solution(mesh):
    column = P("lon", None)
    field = P("ens", "lon", None)
    return jax.shard_map(
        body,
        mesh=mesh,
        in_specs=(field, field, field, column, column, column),
        out_specs=(field, field, field, P("lon", "ens")),
        check_vma=False,
    )
```

```python
import functools

import jax
import jax.numpy as jnp
from jax import lax
from jax.experimental import pallas as pl
from jax.experimental.pallas import tpu as pltpu
from jax.sharding import PartitionSpec as P

K = 16
NY = 512
ITERS = 6
COLS = 8
EXT = 3 * COLS
LANES = 128
BASIS = ITERS + 1
CUT = NY - COLS
GROUPS = (BASIS * (BASIS + 1) // 2 + COLS - 1) // COLS
CHUNKS = 2

vertical_mix = 0.1
advection = 0.25
coriolis_scale = 0.3
gravity = 0.5
corner_weight = 0.25
shift = 5.0
scale = 4.0
LANE_P = 16
LANE_LC = 32
LANE_DIFF = 33
LANE_MT = 40
LANE_MU = 56
LANE_MV = 72
LANE_EDGE = 88
WIDE = 32
LANE_CODE = LANES - 2 * COLS
LANE_F = LANES - COLS

f32 = jnp.float32


def iota(shape, dim):
    return lax.broadcasted_iota(jnp.int32, shape, dim)


def thickness(k):
    return 0.5 * (0.5 + k / K)


def planetary(shape):
    latitude = (iota(shape, 1).astype(f32) + 0.5) / NY
    return coriolis_scale * (2.0 * latitude - 1.0)


def roll(value, amount, axis):
    return pltpu.roll(value, amount % value.shape[axis], axis)


def level_sum(value):
    weight = 0.5 * (0.5 + iota(value.shape, 0).astype(f32) / K)
    return jnp.sum(weight * value, axis=0, keepdims=True)


def two_sum(a, b):
    s = a + b
    t = s - a
    return s, (a - (s - t)) + (b - t)


def fast_two_sum(a, b):
    s = a + b
    return s, b - (s - a)


def split(a):
    c = 4097.0 * a
    high = c - (c - a)
    return high, a - high


def two_prod(a, b, a_parts=None, b_parts=None):
    ah, al = split(a) if a_parts is None else a_parts
    bh, bl = split(b) if b_parts is None else b_parts
    p = a * b
    return p, ((ah * bh - p) + ah * bl + al * bh) + al * bl


def pair_mul(a, b):
    p, e = two_prod(a[0], b[0])
    return p, e + (a[0] * b[1] + a[1] * b[0])


def pair_add(a, b):
    s, e = two_sum(a[0], b[0])
    return s, e + (a[1] + b[1])


def pair_norm(a):
    return fast_two_sum(a[0], a[1])


def pair_scale(a, factor):
    p, e = two_prod(a[0], factor)
    return p, e + a[1] * factor


def pair_tree(terms):
    while len(terms) > 1:
        pairs = [pair_add(terms[i], terms[i + 1]) for i in range(0, len(terms) - 1, 2)]
        terms = pairs + terms[len(terms) - len(terms) % 2:]
    return terms[0]


def pair_rows(a):
    for step in (4, 2, 1):
        a = pair_add(a, (roll(a[0], step, 0), roll(a[1], step, 0)))
    return a


def pair_pack(terms):
    shape = (COLS, LANES)
    sub = iota(shape, 0)
    zero = (jnp.zeros(shape, f32),) * 2
    terms = terms + [zero] * (COLS - len(terms))
    for step in (4, 2, 1):
        low = (sub & step) == 0
        merged = []
        for x, y in zip(terms[:step], terms[step:]):
            a = tuple(jnp.where(low, p, q) for p, q in zip(x, y))
            b = tuple(
                jnp.where(low, roll(p, -step, 0), roll(q, step, 0)) for p, q in zip(x, y)
            )
            merged.append(pair_add(a, b))
        terms = merged
    return terms[0]


def pack_kernel(
    tracer_in, zonal_in, meridional_in, count_in, diffusivity_in, surface_in,
    inner, outer,
    tracer, zonal, meridional, count, diffusivity, surface, edges, sems,
):
    shape = (COLS, NY)
    even = is_even()
    small = [
        pltpu.make_async_copy(a, b, sems.at[i])
        for i, (a, b) in enumerate(
            ((count_in, count), (diffusivity_in, diffusivity), (surface_in, surface))
        )
    ]
    large = []
    for c in range(CHUNKS):
        part = pl.ds(c * K // CHUNKS, K // CHUNKS)
        large.append(
            [
                pltpu.make_async_copy(a.at[part], b.at[part], sems.at[3 + 3 * c + i])
                for i, (a, b) in enumerate(
                    (
                        (zonal_in, zonal),
                        (meridional_in, meridional),
                        (tracer_in.at[:, :, NY - LANES:], tracer),
                    )
                )
            ]
        )
    rows = [
        pltpu.make_async_copy(
            field.at[:, x], edges.at[2 * base + i], sems.at[3 + 3 * CHUNKS + 2 * base + i]
        )
        for base, field in enumerate((tracer_in, zonal_in, meridional_in))
        for i, x in enumerate((0, COLS - 1))
    ]
    for copy in small + sum(large, []) + rows:
        copy.start()
    for copy in small:
        copy.wait()
    lc = count[...].astype(f32)
    diff = diffusivity[...]
    row, lane = iota(shape, 0), iota(shape, 1)
    tile_lane = iota((COLS, LANES), 1)
    lc_east, lc_north = roll(lc, -1, 0), roll(lc, -1, 1)
    total = jnp.zeros(shape, f32)
    turn = jnp.zeros(shape, f32)
    flux_x = jnp.zeros(shape, f32)
    flux_y = jnp.zeros(shape, f32)
    fold = jnp.zeros((COLS, LANES), f32)
    for k in range(K):
        if k % (K // CHUNKS) == 0:
            for copy in large[k // (K // CHUNKS)]:
                copy.wait()
        mask = lc > k
        t, u, v = tracer[k], zonal[k], meridional[k]
        for base, field in ((LANE_MT, t), (LANE_MU, u), (LANE_MV, v)):
            fold = jnp.where(tile_lane == base + k, field[:, -1:], fold)
        mu, mv = jnp.where(mask, u, 0.0), jnp.where(mask, v, 0.0)
        p = thickness(k) * (mu + mv)
        total += p
        turn += thickness(k) * (mv - mu)
        flux_x += jnp.where(mask, roll(p, -1, 0), 0.0) - jnp.where(lc_east > k, p, 0.0)
        flux_y += jnp.where(mask, roll(p, -1, 1), 0.0) - jnp.where(lc_north > k, p, 0.0)
    lc_fold = lc[:, NY - 1:]
    level = tile_lane - jnp.where(
        tile_lane < LANE_MU, LANE_MT, jnp.where(tile_lane < LANE_MV, LANE_MU, LANE_MV)
    )
    fold = jnp.where(level.astype(f32) < lc_fold, fold, 0.0)
    momentum = roll(fold, LANE_P - LANE_MU, 1) + roll(fold, LANE_P - LANE_MV, 1)
    fold = jnp.where((tile_lane >= LANE_P) & (tile_lane < LANE_P + K), momentum, fold)
    fold = jnp.where(tile_lane < K, jnp.where(tile_lane.astype(f32) < lc_fold, 1.0, 0.0), fold)
    fold = jnp.where(tile_lane == LANE_LC, lc_fold, fold)
    fold = jnp.where(tile_lane == LANE_DIFF, diff[:, NY - 1:], fold)
    edge_level = iota((K, NY), 0).astype(f32)

    for copy in rows:
        copy.wait()
    for base in range(3):
        west, east = edges[2 * base], edges[2 * base + 1]
        west = jnp.where(edge_level < lc[:1], west, 0.0)
        east = jnp.where(edge_level < lc[COLS - 1:], east, 0.0)
        at = pl.ds(2 * COLS + base * K, K)
        inner[at] = jnp.where(even, east, west)
        outer[at] = jnp.where(even, west, east)
    flux_x = jnp.where(row == COLS - 1, 0.0, flux_x)
    flux_y = jnp.where(lane == NY - 1, 0.0, flux_y)
    west_flux = jnp.where(row == 0, 0.0, roll(flux_x, 1, 0))
    south_flux = jnp.where(lane == 0, 0.0, roll(flux_y, 1, 1))
    forcing = total + planetary(shape) * turn + diff * (
        flux_x - west_flux + flux_y - south_flux
    )
    coded = jnp.where(lc > 0, surface[...], -1.0)
    edge = jnp.zeros((K, LANES), f32)
    edge_lane = iota((K, LANES), 1)
    p = outer[32:48, NY - LANES:] + outer[48:64, NY - LANES:]
    sub = iota((COLS, LANES), 0)
    edge_lc = jnp.where(even, lc[:1], lc[COLS - 1:])
    edge_diff = jnp.where(even, diff[:1], diff[COLS - 1:])
    for j in range(COLS):
        at = NY - 1 - j
        here = LANE_EDGE + j
        edge = jnp.where(edge_lane == here, p[:, LANES - 1 - j:LANES - j], edge)
        edge = jnp.where(edge_lane == here + COLS, edge_lc[:, at:at + 1], edge)
        edge = jnp.where(edge_lane == here + 2 * COLS, edge_diff[:, at:at + 1], edge)
    blank = jnp.zeros((COLS, NY - 3 * LANES), f32)
    inner[72:80] = jnp.concatenate([fold, edge[:COLS], edge[COLS:], blank], axis=1)
    inner[0:COLS] = forcing
    inner[COLS:2 * COLS] = coded
    mine_lc = jnp.where(even, lc[COLS - 1:], lc[:1])
    mine_diff = jnp.where(even, diff[COLS - 1:], diff[:1])
    inner[64:72] = jnp.where(row == 0, mine_lc, jnp.where(row == 1, mine_diff, 0.0))
    far, next_far = jnp.where(even, COLS - 1, 0), jnp.where(even, COLS - 2, 1)
    used = jnp.where((tile_lane >= LANE_P) & (tile_lane < LANE_P + WIDE), fold, 0.0)
    moved = [
        jnp.sum(
            sum(
                jnp.where(sub == x, roll(used, (x - first) * WIDE - LANE_P, 1), 0.0)
                for x in range(first, first + LANES // WIDE)
            ),
            axis=0, keepdims=True,
        )
        for first in range(0, COLS, LANES // WIDE)
    ]
    tile_row = jnp.concatenate(moved + [jnp.zeros((1, NY - len(moved) * LANES), f32)], axis=1)
    outer[0:COLS] = jnp.where(row == far, edge_lc, jnp.where(row == next_far, tile_row, forcing))
    outer[COLS:2 * COLS] = jnp.where(row == far, edge_diff, coded)


def far_rows(pack, far, next_far):
    tile_row = jnp.where(next_far == 1, pack[1:2], pack[COLS - 2:COLS - 1])
    sub = iota((COLS, LANES), 0)
    tile = jnp.zeros((COLS, LANES), f32)
    for x in range(COLS):
        block, place = divmod(x * WIDE, LANES)
        piece = tile_row[:, block * LANES:(block + 1) * LANES]
        tile = jnp.where(sub == x, roll(piece, LANE_P - place, 1), tile)
    return (
        jnp.where(far == 0, pack[0:1], pack[COLS - 1:COLS]),
        jnp.where(far == 0, pack[COLS:COLS + 1], pack[2 * COLS - 1:2 * COLS]),
        tile,
    )


def interface_flux(mine, theirs, lc_mine, lc_theirs):
    p_mine = mine[32:48] + mine[48:64]
    p_theirs = theirs[32:48] + theirs[48:64]
    level = iota(p_mine.shape, 0).astype(f32)
    return level_sum(
        jnp.where(level < lc_mine, p_theirs, 0.0) - jnp.where(level < lc_theirs, p_mine, 0.0)
    )


def chip_forcing(even, inner, sibling):
    flux = interface_flux(inner, sibling, inner[64:65], sibling[64:65])
    own, other = inner[65:66] * flux, -sibling[65:66] * flux
    row = iota((2 * COLS, flux.shape[1]), 0)
    change = jnp.where(
        row == COLS - 1,
        jnp.where(even, own, other),
        jnp.where(row == COLS, jnp.where(even, other, own), 0.0),
    )
    return beside(even, inner[:COLS], sibling[:COLS]) + change


def is_even():
    return lax.axis_index("lon") % 2 == 0


def beside(even, west, east):
    return jnp.concatenate([jnp.where(even, west, east), jnp.where(even, east, west)], axis=0)


def far_first():
    size, index = lax.axis_size("lon"), lax.axis_index("lon")
    odd = index % 2 == 1
    return odd & (index < size // 2), ~odd & (index >= size // 2)


def patch_order(one, two, near):
    size, index = lax.axis_size("lon"), lax.axis_index("lon")
    swapped = far_first()[1]
    own = (index == 0) | (index == size // 2)
    return jnp.where(swapped, two, one), jnp.where(own, near, jnp.where(swapped, one, two))


def chip_kernel(inner, sibling, tile, near, one, two):
    even = is_even()
    ours, theirs = (pack[:72, NY - LANES:] for pack in (inner, sibling))
    full = chip_forcing(even, ours, theirs)
    code = beside(even, ours[COLS:2 * COLS], theirs[COLS:2 * COLS])
    fold = beside(even, inner[72:80, :LANES], sibling[72:80, :LANES])
    tile[...] = fold
    lane = iota((2 * COLS, LANES), 1)
    for j in range(COLS):
        at = LANES - 1 - j
        fold = jnp.where(lane == LANE_F + j, full[:, at:at + 1], fold)
        fold = jnp.where(lane == LANE_CODE + j, code[:, at:at + 1], fold)
    fold = jnp.concatenate(
        [fold[i:i + 1] for i in range(2 * COLS - 1, -1, -1)], axis=0
    )
    patches = []
    for source in (inner, sibling):
        edge = jnp.concatenate(
            [source[72:80, LANES:2 * LANES], source[72:80, 2 * LANES:3 * LANES]], axis=0
        )
        patches.append(jnp.where((lane >= LANE_EDGE) & (lane < LANE_CODE), edge, fold))
    swapped = far_first()[0]
    near[...] = patches[0]
    one[...] = jnp.where(swapped, patches[1], patches[0])
    two[...] = jnp.where(swapped, patches[0], patches[1])


def across_fold(even, chip, far):
    shape = (2 * COLS, LANES)
    level = iota(shape, 0).astype(f32)
    lane = iota((1, LANES), 1)
    flux = level_sum(
        jnp.where(level < roll(chip, -COLS, 1), far, 0.0)
        - jnp.where(level < roll(far, -COLS, 1), chip, 0.0)
    )

    def change(tile):
        product = roll(tile[:1], -2 * COLS, 1) * flux
        return jnp.where(lane >= LANE_F, roll(product, LANE_F - LANE_EDGE, 1), 0.0)

    chip_change, far_change = change(chip), -change(far)
    tile = extend(even, far[COLS:], chip, far[:COLS])
    row = iota((EXT, LANES), 0)
    west = jnp.where(row == COLS - 1, far_change, jnp.where(row == COLS, chip_change, 0.0))
    east = jnp.where(
        row == 2 * COLS - 1, chip_change, jnp.where(row == 2 * COLS, far_change, 0.0)
    )
    return tile, jnp.where(even, west, east)


def extend(even, west, chip, east):
    return jnp.concatenate(
        [
            jnp.where(even, west, chip[:COLS]),
            jnp.where(even, chip[:COLS], chip[COLS:]),
            jnp.where(even, chip[COLS:], east),
        ],
        axis=0,
    )


def basis(start, code):
    ocean = code > 0
    centre = jnp.where(ocean, code / scale, 0.0)
    around = jnp.where(ocean, 1.0 / scale, 0.0)
    lane = iota(start.shape, 1)

    def operate(q):
        along = roll(q, -1, 1) + jnp.where(lane == 0, 0.0, roll(q, 1, 1))
        side = q + corner_weight * along
        return centre * q - around * (along + roll(side, 1, 0) + roll(side, -1, 0))

    v = [start, operate(start)]
    for j in range(2, BASIS):
        v.append(2.0 * operate(v[-1]) - v[-2])
    return v


def gram_rows(blocks):
    parts = [[split(q) for q in row] for row in blocks]
    entries = []
    for i in range(BASIS):
        for j in range(i, BASIS):
            terms = [
                two_prod(a, b, a_parts, b_parts)
                for a, b, a_parts, b_parts in zip(blocks[i], blocks[j], parts[i], parts[j])
            ]
            entries.append(pair_tree(terms))
    return [pair_pack(entries[g:g + COLS]) for g in range(0, len(entries), COLS)]


def lane_sums(groups, first, last):
    size = GROUPS * COLS
    parts = [pair[0] for pair in groups] + [pair[1] for pair in groups]
    turned = jnp.concatenate(parts + [jnp.zeros((LANES - 2 * size, LANES), f32)], axis=0).T
    terms = [turned[i:i + COLS] for i in range(first, last, COLS)]
    return pair_norm(pair_rows(pair_tree([(t, roll(t, -size, 1)) for t in terms])))


def inner_kernel(
    inner, outer, sibling, beyond, tile, last, last_code, vectors, partial, ours,
):
    even = is_even()
    forcing = chip_forcing(even, inner, sibling)
    coded = beside(even, inner[COLS:2 * COLS], sibling[COLS:2 * COLS])
    at_east, at_west = jnp.where(even, 0, COLS - 1), jnp.where(even, COLS - 1, 0)
    lc_out, diff_out, _ = far_rows(outer, at_west, jnp.where(even, COLS - 2, 1))
    lc_far, diff_far, tile_far = far_rows(beyond, at_east, jnp.where(even, 1, COLS - 2))
    flux_out = interface_flux(outer, beyond, lc_out, lc_far)
    own, far = diff_out * flux_out, -diff_far * flux_out
    row = iota((EXT, NY), 0)
    west = jnp.where(row == COLS - 1, far, jnp.where(row == COLS, own, 0.0))
    east = jnp.where(row == 2 * COLS - 1, own, jnp.where(row == 2 * COLS, far, 0.0))
    far_forcing, far_code = beyond[:COLS], beyond[COLS:2 * COLS]
    south = extend(even, far_forcing, forcing, far_forcing) + jnp.where(even, west, east)
    code = extend(even, far_code, coded, far_code)
    last[...] = roll(south[:, NY - LANES:], -COLS, 1)
    last_code[...] = roll(code[:, NY - LANES:], -COLS, 1)
    v = basis(south, code)
    lane = iota((COLS, LANES), 1)
    blocks = []
    for j, q in enumerate(v):
        if j < ITERS:
            vectors[j * EXT:(j + 1) * EXT] = q
        cut = [q[COLS:2 * COLS, c:c + LANES] for c in range(0, NY, LANES)]
        cut[-1] = jnp.where(lane < LANES - COLS, cut[-1], 0.0)
        blocks.append(cut)
    high, low = lane_sums(gram_rows(blocks), 0, LANES)
    partial[:COLS] = high
    partial[COLS:] = low
    mine = extend(even, tile_far, tile[...], tile_far)
    lane = iota((EXT, LANES), 1)
    level = (lane - LANE_P).astype(f32)
    weight = jnp.where((lane >= LANE_P) & (lane < LANE_P + K), 0.5 * (0.5 + level / K), 0.0)
    ours[:EXT] = jnp.where(level < mine[:, LANE_LC:LANE_LC + 1], weight, 0.0) + roll(
        weight * mine, -LANE_P, 1
    )
    ours[EXT:] = jnp.where(lane == LANE_F - 1, mine[:, LANE_DIFF:LANE_DIFF + 1], 0.0)


def fold_kernel(
    last, last_code, ours, one, two, near, partial, vectors, gram
):
    even = is_even()
    lane = iota((EXT, LANES), 1)
    theirs, between = across_fold(even, *patch_order(one[...], two[...], near[...]))
    flux = -jnp.sum(ours[:EXT] * theirs, axis=1, keepdims=True)
    far_change = theirs[:, LANE_DIFF:LANE_DIFF + 1] * flux
    beyond_fold = lane >= LANE_F
    start = jnp.where(beyond_fold, theirs, last[...]) + between
    start = start + jnp.where(lane == LANE_F, far_change, ours[EXT:] * flux)
    code = jnp.where(beyond_fold, roll(theirs, LANE_F - LANE_CODE, 1), last_code[...])
    v = basis(start, code)
    for j in range(ITERS):
        vectors[j * EXT:(j + 1) * EXT] = v[j]
    own_lane = lane[:COLS]
    summed = (own_lane >= LANE_F - COLS) & (own_lane < LANE_F)
    blocks = [[jnp.where(summed, q[COLS:2 * COLS], 0.0)] for q in v]
    sums = lane_sums(gram_rows(blocks), LANE_F - COLS, LANE_F)
    high, low = pair_norm(pair_add(sums, (partial[:COLS], partial[COLS:])))
    size = GROUPS * COLS
    row = jnp.where(iota((COLS, LANES), 1) < size, high, roll(low, size, 1))
    gram[...] = jnp.broadcast_to(row[:1], gram.shape)


def coefficients(gram):
    shape = (COLS, LANES)
    tiles = [gram[i * COLS:(i + 1) * COLS] for i in range(gram.shape[0] // COLS)]
    total = pair_norm(pair_rows(pair_tree([(t, roll(t, -GROUPS * COLS, 1)) for t in tiles])))
    wide = lambda column: jnp.broadcast_to(column, shape)
    sub = iota(shape, 0)
    tile_lane = iota(shape, 1)

    def column(j):
        low, high = jnp.minimum(sub, j), jnp.maximum(sub, j)
        entry = ((low * (2 * BASIS - 1 - low)) >> 1) + high
        here = (tile_lane == entry) & (sub < BASIS)
        return tuple(
            wide(jnp.sum(jnp.where(here, part, 0.0), axis=1, keepdims=True)) for part in total
        )

    matrix = [column(j) for j in range(BASIS)]
    zero = jnp.zeros(shape, f32)
    half = scale / 2

    def times_power(pair, factor):
        return tuple(factor * part for part in pair)

    def shifted(pair):
        return pair_add(times_power(pair, shift - 1.0), pair)

    def apply(b):
        up = [half * jnp.where(sub == 0, 0.0, roll(part, 1, 0)) for part in b]
        up = tuple(jnp.where(sub == 1, 2.0 * part, part) for part in up)
        down = tuple(half * jnp.where(sub == COLS - 1, 0.0, roll(part, -1, 0)) for part in b)
        return pair_add(shifted(b), pair_add(up, down))

    images = [pair_add(shifted(matrix[0]), times_power(matrix[1], scale))]
    for j in range(1, ITERS):
        sides = pair_add(matrix[j - 1], matrix[j + 1])
        images.append(pair_add(shifted(matrix[j]), times_power(sides, half)))

    def image_of(vector, count):
        terms = []
        for j in range(count):
            at = tuple(wide(part[j:j + 1]) for part in vector)
            terms.append(pair_mul(images[j], at))
        return pair_tree(terms)

    def dot(a, b):
        return pair_rows(pair_mul(a, b))

    residual = ((sub == 0).astype(f32), zero)
    direction = residual
    solution = zero
    norm_now = tuple(wide(part[:1]) for part in matrix[0])
    floor = 1e-13 * norm_now[0]
    alive = norm_now[0] > 0
    for iteration in range(ITERS):
        applied = apply(direction)
        if iteration == 0:
            image = images[0]
            curvature = tuple(wide(part[:1]) for part in image)
        else:
            image = image_of(direction, iteration + 1)
            curvature = dot(direction, image)
        size = curvature[0] + curvature[1]
        alive = alive & (size > 0)
        step = jnp.where(alive, (norm_now[0] + norm_now[1]) / jnp.where(alive, size, 1.0), 0.0)
        solution = solution + step * direction[0]
        if iteration + 1 < ITERS:
            crossed = curvature if iteration == 0 else dot(residual, image)
            squared = dot(applied, image)
            change = pair_add(
                pair_scale(squared, step), times_power(crossed, -2.0)
            )
            norm_next = pair_norm(pair_add(norm_now, pair_scale(pair_norm(change), step)))
            residual = pair_norm(pair_add(residual, pair_scale(applied, -step)))
            ratio = jnp.where(alive, norm_next[0] / jnp.where(alive, norm_now[0], 1.0), 0.0)
            direction = pair_norm(pair_add(residual, pair_scale(direction, ratio)))
            norm_now = norm_next
            alive = alive & (norm_now[0] > floor)
    return solution


def slope_kernel(vectors, vectors_last, parts):
    near = iota((COLS, LANES), 1) >= CUT - (NY - LANES)

    def finished(value, from_window):
        value = value[COLS:2 * COLS]
        moved = roll(from_window[COLS:2 * COLS], COLS, 1)
        last = jnp.where(near, moved, value[:, NY - LANES:])
        return jnp.concatenate([value[:, :NY - LANES], last], axis=1)

    for j in range(ITERS):
        at = slice(j * EXT, (j + 1) * EXT)
        total, window = vectors[at], vectors_last[at]
        row = 3 * j * COLS
        parts[row:row + COLS] = finished(total, window)
        for axis in (0, 1):
            row += COLS
            parts[row:row + COLS] = gravity * finished(
                roll(total, -1, axis) - total, roll(window, -1, axis) - window
            )


def finish_kernel(gram, parts, zonal, meridional, levels, zonal_next, meridional_next, height):
    solution_rows = coefficients(gram)
    x = [
        jnp.concatenate(
            [jnp.broadcast_to(solution_rows[j:j + 1], (COLS, LANES))] * (NY // LANES), axis=1
        )
        for j in range(ITERS)
    ]

    def combine(which):
        rows = [(3 * j + which) * COLS for j in range(ITERS)]
        terms = [x[j] * parts[row:row + COLS] for j, row in enumerate(rows)]
        pairs = [sum(terms[j + 1:j + 2], terms[j]) for j in range(0, ITERS, 2)]
        return sum(pairs[1:], pairs[0])

    height[...] = combine(0)
    east, north = combine(1), combine(2)
    lc = levels[...]
    for k in range(K):
        zonal_next[k] = zonal[k] - jnp.where(lc > k, east, 0.0)
        meridional_next[k] = meridional[k] - jnp.where(lc > k, north, 0.0)


def neighbours(count, sibling, beyond, one, two):
    shape = (COLS, NY)
    even = is_even()
    row, lane = iota(shape, 0), iota(shape, 1)
    lc = count[...].astype(f32)
    mirror = patch_order(one[...], two[...], one[...])[0]
    north_tile = jnp.where(even, mirror[:COLS], mirror[COLS:])

    def around(field, west, east, north):
        return (
            jnp.where(row == COLS - 1, east, roll(field, -1, 0)),
            jnp.where(row == 0, west, roll(field, 1, 0)),
            jnp.where(lane == NY - 1, north, roll(field, -1, 1)),
            jnp.where(lane == 0, 0.0, roll(field, 1, 1)),
        )

    def sides(a, b):
        return jnp.where(even, b, a), jnp.where(even, a, b)

    def edges(at):
        return sides(sibling[at:at + 1], beyond[at:at + 1])

    def padded(field, base, k, sign):
        at = LANE_MT + base * K + k
        return around(field, *edges(2 * COLS + base * K + k), sign * north_tile[:, at:at + 1])

    beyond_lc = jnp.where(even, beyond[0:1], beyond[COLS - 1:COLS])
    west_lc, east_lc = sides(sibling[64:65], beyond_lc)
    north_lc = north_tile[:, LANE_LC:LANE_LC + 1]

    def mask_sum(mask, k):
        inside = [(c > k).astype(f32) for c in (west_lc, east_lc, north_lc)]
        return sum(around(mask, *inside))

    return lc, padded, mask_sum


def tracer_kernel(
    tracer, zonal, meridional, count, diffusivity, sibling, beyond, one, two, tracer_next
):
    lc, padded, mask_sum = neighbours(count, sibling, beyond, one, two)
    diff = diffusivity[...]

    def masked(k):
        if k < 0 or k >= K:
            return jnp.zeros_like(lc), jnp.zeros_like(lc)
        mask = (lc > k).astype(f32)
        return mask, mask * tracer[k]

    below, here = masked(-1), masked(0)
    for k in range(K):
        above = masked(k + 1)
        mask, mt = here
        t, u, v = tracer[k], zonal[k], meridional[k]
        te, tw, tn, ts = padded(mt, 0, k, 1.0)
        vertical = above[1] + below[1] - (above[0] + below[0]) * t
        tracer_next[k] = mask * (
            t
            + diff * (te + tw + tn + ts - mask_sum(mask, k) * t)
            + vertical_mix * vertical
            - advection * (u * (te - tw) + v * (tn - ts))
        )
        below, here = here, above


def flow_kernel(
    zonal, meridional, count, diffusivity, sibling, beyond, one, two,
    zonal_step, meridional_step, levels,
):
    lc, padded, mask_sum = neighbours(count, sibling, beyond, one, two)
    diff = diffusivity[...]
    turn = planetary(lc.shape)
    levels[...] = lc
    for k in range(K):
        mask = (lc > k).astype(f32)
        u, v = zonal[k], meridional[k]
        sides = mask_sum(mask, k)
        zonal_sum = sum(padded(mask * u, 1, k, -1.0))
        meridional_sum = sum(padded(mask * v, 2, k, -1.0))
        zonal_step[k] = mask * (u + diff * (zonal_sum - sides * u) + turn * v)
        meridional_step[k] = mask * (v + diff * (meridional_sum - sides * v) - turn * u)


def call(kernel, shapes, *args, flops=0, scratch=(), stay=0):
    moved = 4 * sum(a.size for a in args) + 4 * sum(
        functools.reduce(lambda x, y: x * y, s, 1) for s in shapes
    )
    space = pl.BlockSpec(memory_space=pltpu.VMEM)
    in_specs = [space] * (len(args) - stay) + [pl.BlockSpec(memory_space=pltpu.HBM)] * stay
    here = len(args) - stay
    args = args[:here] + tuple(
        pltpu.with_memory_space_constraint(a, pltpu.HBM) for a in args[here:]
    )
    return pl.pallas_call(
        kernel,
        out_shape=[jax.ShapeDtypeStruct(s, f32) for s in shapes],
        in_specs=in_specs,
        out_specs=[space] * len(shapes),
        scratch_shapes=list(scratch),
        compiler_params=pltpu.CompilerParams(vmem_limit_bytes=32 * 1024 * 1024),
        cost_estimate=pl.CostEstimate(flops=flops, bytes_accessed=moved, transcendentals=0),
    )(*args)


def body(tracer, zonal, meridional, count, diffusivity, surface):
    size = lax.axis_size("lon")
    block = (K, COLS, NY)

    def permute(value, pairs):
        return lax.ppermute(value, "lon", pairs)

    siblings = [(i, i ^ 1) for i in range(size)]
    outward = [(i, (i + 1 if i % 2 else i - 1) % size) for i in range(size)]
    first = {i: size - 1 - i for i in range(size)}
    second = {(size + 1 - 4 * (i % 2) - i) % size: i for i in range(size)}
    for i in range(1, size // 2, 2):
        first[i], second[i] = second[i], first[i]
    first[1], second[size // 2 + 1] = size // 2, 0
    arguments = (tracer, zonal, meridional, count, diffusivity, surface)
    inner, outer = call(
        pack_kernel, [(80, NY), (64, NY)], *arguments,
        scratch=[pltpu.VMEM((K, COLS, LANES), f32)]
        + [pltpu.VMEM(a.shape, a.dtype) for a in arguments[1:]]
        + [pltpu.VMEM((6, K, NY), f32), pltpu.SemaphoreType.DMA((9 + 3 * CHUNKS,))], stay=len(arguments),
    )
    beyond = permute(outer, outward)
    sibling = permute(inner, siblings)
    patch = (2 * COLS, LANES)
    tile, near, one, two = call(chip_kernel, [patch] * 4, inner, sibling)
    one = permute(one, sorted(first.items()))
    two = permute(two, sorted(second.items()))
    window = (EXT, LANES)
    last, last_code, vectors, partial, ours = call(
        inner_kernel,
        [
            window, window, (ITERS * EXT, NY), (2 * COLS, LANES), (2 * EXT, LANES),
        ],
        inner, outer, sibling, beyond, tile, flops=8192 * 100,
    )
    vectors_last, gram = call(
        fold_kernel,
        [(ITERS * EXT, LANES), (size, LANES)],
        last, last_code, ours, one, two, near, partial,
    )
    halos = (sibling, beyond, one, two)
    tracer_next, = call(
        tracer_kernel, [block],
        tracer, zonal, meridional, count, diffusivity, *halos,
        flops=65536 * 40,
    )
    zonal_step, meridional_step, levels = call(
        flow_kernel, [block, block, (COLS, NY)],
        zonal, meridional, count, diffusivity, *halos,
        flops=65536 * 40,
    )
    group = [(5 * i + size // 2 - 1) % size for i in range(size)]
    gram = lax.all_to_all(gram, "lon", 0, 0, tiled=True, axis_index_groups=[group])
    parts, = call(slope_kernel, [(3 * ITERS * COLS, NY)], vectors, vectors_last, flops=8192 * 20)
    zonal_next, meridional_next, height = call(
        finish_kernel, [block, block, (COLS, NY)],
        gram, parts, zonal_step, meridional_step, levels,
    )
    return tracer_next, zonal_next, meridional_next, height


def solution(mesh):
    column = P("lon", None)
    field = P("ens", "lon", None)
    return jax.shard_map(
        body,
        mesh=mesh,
        in_specs=(field, field, field, column, column, column),
        out_specs=(field, field, field, P("lon", "ens")),
        check_vma=False,
    )
```

```python
import functools

import jax
import jax.numpy as jnp
from jax import lax
from jax.experimental import pallas as pl
from jax.experimental.pallas import tpu as pltpu
from jax.sharding import PartitionSpec as P

K = 16
NY = 512
ITERS = 6
COLS = 8
EXT = 3 * COLS
LANES = 128
BASIS = ITERS + 1
CUT = NY - COLS
GROUPS = (BASIS * (BASIS + 1) // 2 + COLS - 1) // COLS
CHUNKS = 2

vertical_mix = 0.1
advection = 0.25
coriolis_scale = 0.3
gravity = 0.5
corner_weight = 0.25
shift = 5.0
scale = 4.0
LANE_P = 16
LANE_LC = 32
LANE_DIFF = 33
LANE_MT = 40
LANE_MU = 56
LANE_MV = 72
LANE_EDGE = 88
WIDE = 32
LANE_CODE = LANES - 2 * COLS
LANE_F = LANES - COLS

f32 = jnp.float32


def iota(shape, dim):
    return lax.broadcasted_iota(jnp.int32, shape, dim)


def thickness(k):
    return 0.5 * (0.5 + k / K)


def planetary(shape):
    latitude = (iota(shape, 1).astype(f32) + 0.5) / NY
    return coriolis_scale * (2.0 * latitude - 1.0)


def roll(value, amount, axis):
    return pltpu.roll(value, amount % value.shape[axis], axis)


def level_sum(value):
    weight = 0.5 * (0.5 + iota(value.shape, 0).astype(f32) / K)
    return jnp.sum(weight * value, axis=0, keepdims=True)


def two_sum(a, b):
    s = a + b
    t = s - a
    return s, (a - (s - t)) + (b - t)


def fast_two_sum(a, b):
    s = a + b
    return s, b - (s - a)


def split(a):
    c = 4097.0 * a
    high = c - (c - a)
    return high, a - high


def two_prod(a, b, a_parts=None, b_parts=None):
    ah, al = split(a) if a_parts is None else a_parts
    bh, bl = split(b) if b_parts is None else b_parts
    p = a * b
    return p, ((ah * bh - p) + ah * bl + al * bh) + al * bl


def pair_mul(a, b):
    p, e = two_prod(a[0], b[0])
    return p, e + (a[0] * b[1] + a[1] * b[0])


def pair_add(a, b):
    s, e = two_sum(a[0], b[0])
    return s, e + (a[1] + b[1])


def pair_norm(a):
    return fast_two_sum(a[0], a[1])


def pair_scale(a, factor):
    p, e = two_prod(a[0], factor)
    return p, e + a[1] * factor


def pair_tree(terms):
    while len(terms) > 1:
        pairs = [pair_add(terms[i], terms[i + 1]) for i in range(0, len(terms) - 1, 2)]
        terms = pairs + terms[len(terms) - len(terms) % 2:]
    return terms[0]


def pair_rows(a):
    for step in (4, 2, 1):
        a = pair_add(a, (roll(a[0], step, 0), roll(a[1], step, 0)))
    return a


def pair_pack(terms):
    shape = (COLS, LANES)
    sub = iota(shape, 0)
    zero = (jnp.zeros(shape, f32),) * 2
    terms = terms + [zero] * (COLS - len(terms))
    for step in (4, 2, 1):
        low = (sub & step) == 0
        merged = []
        for x, y in zip(terms[:step], terms[step:]):
            a = tuple(jnp.where(low, p, q) for p, q in zip(x, y))
            b = tuple(
                jnp.where(low, roll(p, -step, 0), roll(q, step, 0)) for p, q in zip(x, y)
            )
            merged.append(pair_add(a, b))
        terms = merged
    return terms[0]


def pack_kernel(
    tracer_in, zonal_in, meridional_in, count_in, diffusivity_in, surface_in,
    inner, outer,
    tracer, zonal, meridional, count, diffusivity, surface, edges, sems,
):
    shape = (COLS, NY)
    even = is_even()
    small = [
        pltpu.make_async_copy(a, b, sems.at[i])
        for i, (a, b) in enumerate(
            ((count_in, count), (diffusivity_in, diffusivity), (surface_in, surface))
        )
    ]
    large = []
    for c in range(CHUNKS):
        part = pl.ds(c * K // CHUNKS, K // CHUNKS)
        large.append(
            [
                pltpu.make_async_copy(a.at[part], b.at[part], sems.at[3 + 3 * c + i])
                for i, (a, b) in enumerate(
                    (
                        (zonal_in, zonal),
                        (meridional_in, meridional),
                        (tracer_in.at[:, :, NY - LANES:], tracer),
                    )
                )
            ]
        )
    rows = [
        pltpu.make_async_copy(
            field.at[:, x], edges.at[2 * base + i], sems.at[3 + 3 * CHUNKS + 2 * base + i]
        )
        for base, field in enumerate((tracer_in, zonal_in, meridional_in))
        for i, x in enumerate((0, COLS - 1))
    ]
    for copy in small + sum(large, []) + rows:
        copy.start()
    for copy in small:
        copy.wait()
    lc = count[...].astype(f32)
    diff = diffusivity[...]
    row, lane = iota(shape, 0), iota(shape, 1)
    tile_lane = iota((COLS, LANES), 1)
    lc_east, lc_north = roll(lc, -1, 0), roll(lc, -1, 1)
    total = jnp.zeros(shape, f32)
    turn = jnp.zeros(shape, f32)
    flux_x = jnp.zeros(shape, f32)
    flux_y = jnp.zeros(shape, f32)
    fold = jnp.zeros((COLS, LANES), f32)
    for k in range(K):
        if k % (K // CHUNKS) == 0:
            for copy in large[k // (K // CHUNKS)]:
                copy.wait()
        mask = lc > k
        t, u, v = tracer[k], zonal[k], meridional[k]
        for base, field in ((LANE_MT, t), (LANE_MU, u), (LANE_MV, v)):
            fold = jnp.where(tile_lane == base + k, field[:, -1:], fold)
        mu, mv = jnp.where(mask, u, 0.0), jnp.where(mask, v, 0.0)
        p = thickness(k) * (mu + mv)
        total += p
        turn += thickness(k) * (mv - mu)
        flux_x += jnp.where(mask, roll(p, -1, 0), 0.0) - jnp.where(lc_east > k, p, 0.0)
        flux_y += jnp.where(mask, roll(p, -1, 1), 0.0) - jnp.where(lc_north > k, p, 0.0)
    lc_fold = lc[:, NY - 1:]
    level = tile_lane - jnp.where(
        tile_lane < LANE_MU, LANE_MT, jnp.where(tile_lane < LANE_MV, LANE_MU, LANE_MV)
    )
    fold = jnp.where(level.astype(f32) < lc_fold, fold, 0.0)
    momentum = roll(fold, LANE_P - LANE_MU, 1) + roll(fold, LANE_P - LANE_MV, 1)
    fold = jnp.where((tile_lane >= LANE_P) & (tile_lane < LANE_P + K), momentum, fold)
    fold = jnp.where(tile_lane < K, jnp.where(tile_lane.astype(f32) < lc_fold, 1.0, 0.0), fold)
    fold = jnp.where(tile_lane == LANE_LC, lc_fold, fold)
    fold = jnp.where(tile_lane == LANE_DIFF, diff[:, NY - 1:], fold)
    edge_level = iota((K, NY), 0).astype(f32)

    for copy in rows:
        copy.wait()
    for base in range(3):
        west, east = edges[2 * base], edges[2 * base + 1]
        west = jnp.where(edge_level < lc[:1], west, 0.0)
        east = jnp.where(edge_level < lc[COLS - 1:], east, 0.0)
        at = pl.ds(2 * COLS + base * K, K)
        inner[at] = jnp.where(even, east, west)
        outer[at] = jnp.where(even, west, east)
    flux_x = jnp.where(row == COLS - 1, 0.0, flux_x)
    flux_y = jnp.where(lane == NY - 1, 0.0, flux_y)
    west_flux = jnp.where(row == 0, 0.0, roll(flux_x, 1, 0))
    south_flux = jnp.where(lane == 0, 0.0, roll(flux_y, 1, 1))
    forcing = total + planetary(shape) * turn + diff * (
        flux_x - west_flux + flux_y - south_flux
    )
    coded = jnp.where(lc > 0, surface[...], -1.0)
    edge = jnp.zeros((K, LANES), f32)
    edge_lane = iota((K, LANES), 1)
    p = outer[32:48, NY - LANES:] + outer[48:64, NY - LANES:]
    sub = iota((COLS, LANES), 0)
    edge_lc = jnp.where(even, lc[:1], lc[COLS - 1:])
    edge_diff = jnp.where(even, diff[:1], diff[COLS - 1:])
    for j in range(COLS):
        at = NY - 1 - j
        here = LANE_EDGE + j
        edge = jnp.where(edge_lane == here, p[:, LANES - 1 - j:LANES - j], edge)
        edge = jnp.where(edge_lane == here + COLS, edge_lc[:, at:at + 1], edge)
        edge = jnp.where(edge_lane == here + 2 * COLS, edge_diff[:, at:at + 1], edge)
    blank = jnp.zeros((COLS, NY - 3 * LANES), f32)
    inner[72:80] = jnp.concatenate([fold, edge[:COLS], edge[COLS:], blank], axis=1)
    inner[0:COLS] = forcing
    inner[COLS:2 * COLS] = coded
    mine_lc = jnp.where(even, lc[COLS - 1:], lc[:1])
    mine_diff = jnp.where(even, diff[COLS - 1:], diff[:1])
    inner[64:72] = jnp.where(row == 0, mine_lc, jnp.where(row == 1, mine_diff, 0.0))
    far, next_far = jnp.where(even, COLS - 1, 0), jnp.where(even, COLS - 2, 1)
    used = jnp.where((tile_lane >= LANE_P) & (tile_lane < LANE_P + WIDE), fold, 0.0)
    moved = [
        jnp.sum(
            sum(
                jnp.where(sub == x, roll(used, (x - first) * WIDE - LANE_P, 1), 0.0)
                for x in range(first, first + LANES // WIDE)
            ),
            axis=0, keepdims=True,
        )
        for first in range(0, COLS, LANES // WIDE)
    ]
    tile_row = jnp.concatenate(moved + [jnp.zeros((1, NY - len(moved) * LANES), f32)], axis=1)
    outer[0:COLS] = jnp.where(row == far, edge_lc, jnp.where(row == next_far, tile_row, forcing))
    outer[COLS:2 * COLS] = jnp.where(row == far, edge_diff, coded)


def far_rows(pack, far, next_far):
    tile_row = jnp.where(next_far == 1, pack[1:2], pack[COLS - 2:COLS - 1])
    sub = iota((COLS, LANES), 0)
    tile = jnp.zeros((COLS, LANES), f32)
    for x in range(COLS):
        block, place = divmod(x * WIDE, LANES)
        piece = tile_row[:, block * LANES:(block + 1) * LANES]
        tile = jnp.where(sub == x, roll(piece, LANE_P - place, 1), tile)
    return (
        jnp.where(far == 0, pack[0:1], pack[COLS - 1:COLS]),
        jnp.where(far == 0, pack[COLS:COLS + 1], pack[2 * COLS - 1:2 * COLS]),
        tile,
    )


def interface_flux(mine, theirs, lc_mine, lc_theirs):
    p_mine = mine[32:48] + mine[48:64]
    p_theirs = theirs[32:48] + theirs[48:64]
    level = iota(p_mine.shape, 0).astype(f32)
    return level_sum(
        jnp.where(level < lc_mine, p_theirs, 0.0) - jnp.where(level < lc_theirs, p_mine, 0.0)
    )


def chip_forcing(even, inner, sibling):
    flux = interface_flux(inner, sibling, inner[64:65], sibling[64:65])
    own, other = inner[65:66] * flux, -sibling[65:66] * flux
    row = iota((2 * COLS, flux.shape[1]), 0)
    change = jnp.where(
        row == COLS - 1,
        jnp.where(even, own, other),
        jnp.where(row == COLS, jnp.where(even, other, own), 0.0),
    )
    return beside(even, inner[:COLS], sibling[:COLS]) + change


def is_even():
    return lax.axis_index("lon") % 2 == 0


def beside(even, west, east):
    return jnp.concatenate([jnp.where(even, west, east), jnp.where(even, east, west)], axis=0)


def far_first():
    size, index = lax.axis_size("lon"), lax.axis_index("lon")
    odd = index % 2 == 1
    return odd & (index < size // 2), ~odd & (index >= size // 2)


def patch_order(one, two, near):
    size, index = lax.axis_size("lon"), lax.axis_index("lon")
    swapped = far_first()[1]
    own = (index == 0) | (index == size // 2)
    return jnp.where(swapped, two, one), jnp.where(own, near, jnp.where(swapped, one, two))


def chip_kernel(inner, sibling, tile, near, one, two):
    even = is_even()
    ours, theirs = (pack[:72, NY - LANES:] for pack in (inner, sibling))
    full = chip_forcing(even, ours, theirs)
    code = beside(even, ours[COLS:2 * COLS], theirs[COLS:2 * COLS])
    fold = beside(even, inner[72:80, :LANES], sibling[72:80, :LANES])
    tile[...] = fold
    lane = iota((2 * COLS, LANES), 1)
    for j in range(COLS):
        at = LANES - 1 - j
        fold = jnp.where(lane == LANE_F + j, full[:, at:at + 1], fold)
        fold = jnp.where(lane == LANE_CODE + j, code[:, at:at + 1], fold)
    fold = jnp.concatenate(
        [fold[i:i + 1] for i in range(2 * COLS - 1, -1, -1)], axis=0
    )
    patches = []
    for source in (inner, sibling):
        edge = jnp.concatenate(
            [source[72:80, LANES:2 * LANES], source[72:80, 2 * LANES:3 * LANES]], axis=0
        )
        patches.append(jnp.where((lane >= LANE_EDGE) & (lane < LANE_CODE), edge, fold))
    swapped = far_first()[0]
    near[...] = patches[0]
    one[...] = jnp.where(swapped, patches[1], patches[0])
    two[...] = jnp.where(swapped, patches[0], patches[1])


def across_fold(even, chip, far):
    shape = (2 * COLS, LANES)
    level = iota(shape, 0).astype(f32)
    lane = iota((1, LANES), 1)
    flux = level_sum(
        jnp.where(level < roll(chip, -COLS, 1), far, 0.0)
        - jnp.where(level < roll(far, -COLS, 1), chip, 0.0)
    )

    def change(tile):
        product = roll(tile[:1], -2 * COLS, 1) * flux
        return jnp.where(lane >= LANE_F, roll(product, LANE_F - LANE_EDGE, 1), 0.0)

    chip_change, far_change = change(chip), -change(far)
    tile = extend(even, far[COLS:], chip, far[:COLS])
    row = iota((EXT, LANES), 0)
    west = jnp.where(row == COLS - 1, far_change, jnp.where(row == COLS, chip_change, 0.0))
    east = jnp.where(
        row == 2 * COLS - 1, chip_change, jnp.where(row == 2 * COLS, far_change, 0.0)
    )
    return tile, jnp.where(even, west, east)


def extend(even, west, chip, east):
    return jnp.concatenate(
        [
            jnp.where(even, west, chip[:COLS]),
            jnp.where(even, chip[:COLS], chip[COLS:]),
            jnp.where(even, chip[COLS:], east),
        ],
        axis=0,
    )


def basis(start, code):
    ocean = code > 0
    centre = jnp.where(ocean, code / scale, 0.0)
    around = jnp.where(ocean, 1.0 / scale, 0.0)
    lane = iota(start.shape, 1)

    def operate(q):
        along = roll(q, -1, 1) + jnp.where(lane == 0, 0.0, roll(q, 1, 1))
        side = q + corner_weight * along
        return centre * q - around * (along + roll(side, 1, 0) + roll(side, -1, 0))

    v = [start, operate(start)]
    for j in range(2, BASIS):
        v.append(2.0 * operate(v[-1]) - v[-2])
    return v


def gram_rows(blocks):
    parts = [[split(q) for q in row] for row in blocks]
    entries = []
    for i in range(BASIS):
        for j in range(i, BASIS):
            terms = [
                two_prod(a, b, a_parts, b_parts)
                for a, b, a_parts, b_parts in zip(blocks[i], blocks[j], parts[i], parts[j])
            ]
            entries.append(pair_tree(terms))
    return [pair_pack(entries[g:g + COLS]) for g in range(0, len(entries), COLS)]


def lane_sums(groups, first, last):
    size = GROUPS * COLS
    parts = [pair[0] for pair in groups] + [pair[1] for pair in groups]
    turned = jnp.concatenate(parts + [jnp.zeros((LANES - 2 * size, LANES), f32)], axis=0).T
    terms = [turned[i:i + COLS] for i in range(first, last, COLS)]
    return pair_norm(pair_rows(pair_tree([(t, roll(t, -size, 1)) for t in terms])))


def inner_kernel(
    inner, outer, sibling, beyond, tile, last, last_code, vectors, partial, ours,
):
    even = is_even()
    forcing = chip_forcing(even, inner, sibling)
    coded = beside(even, inner[COLS:2 * COLS], sibling[COLS:2 * COLS])
    at_east, at_west = jnp.where(even, 0, COLS - 1), jnp.where(even, COLS - 1, 0)
    lc_out, diff_out, _ = far_rows(outer, at_west, jnp.where(even, COLS - 2, 1))
    lc_far, diff_far, tile_far = far_rows(beyond, at_east, jnp.where(even, 1, COLS - 2))
    flux_out = interface_flux(outer, beyond, lc_out, lc_far)
    own, far = diff_out * flux_out, -diff_far * flux_out
    row = iota((EXT, NY), 0)
    west = jnp.where(row == COLS - 1, far, jnp.where(row == COLS, own, 0.0))
    east = jnp.where(row == 2 * COLS - 1, own, jnp.where(row == 2 * COLS, far, 0.0))
    far_forcing, far_code = beyond[:COLS], beyond[COLS:2 * COLS]
    south = extend(even, far_forcing, forcing, far_forcing) + jnp.where(even, west, east)
    code = extend(even, far_code, coded, far_code)
    last[...] = roll(south[:, NY - LANES:], -COLS, 1)
    last_code[...] = roll(code[:, NY - LANES:], -COLS, 1)
    v = basis(south, code)
    lane = iota((COLS, LANES), 1)
    blocks = []
    for j, q in enumerate(v):
        if j < ITERS:
            vectors[j * EXT:(j + 1) * EXT] = q
        cut = [q[COLS:2 * COLS, c:c + LANES] for c in range(0, NY, LANES)]
        cut[-1] = jnp.where(lane < LANES - COLS, cut[-1], 0.0)
        blocks.append(cut)
    high, low = lane_sums(gram_rows(blocks), 0, LANES)
    partial[:COLS] = high
    partial[COLS:] = low
    mine = extend(even, tile_far, tile[...], tile_far)
    lane = iota((EXT, LANES), 1)
    level = (lane - LANE_P).astype(f32)
    weight = jnp.where((lane >= LANE_P) & (lane < LANE_P + K), 0.5 * (0.5 + level / K), 0.0)
    ours[:EXT] = jnp.where(level < mine[:, LANE_LC:LANE_LC + 1], weight, 0.0) + roll(
        weight * mine, -LANE_P, 1
    )
    ours[EXT:] = jnp.where(lane == LANE_F - 1, mine[:, LANE_DIFF:LANE_DIFF + 1], 0.0)


def fold_kernel(
    last, last_code, ours, one, two, near, partial, vectors, gram
):
    even = is_even()
    lane = iota((EXT, LANES), 1)
    theirs, between = across_fold(even, *patch_order(one[...], two[...], near[...]))
    flux = -jnp.sum(ours[:EXT] * theirs, axis=1, keepdims=True)
    far_change = theirs[:, LANE_DIFF:LANE_DIFF + 1] * flux
    beyond_fold = lane >= LANE_F
    start = jnp.where(beyond_fold, theirs, last[...]) + between
    start = start + jnp.where(lane == LANE_F, far_change, ours[EXT:] * flux)
    code = jnp.where(beyond_fold, roll(theirs, LANE_F - LANE_CODE, 1), last_code[...])
    v = basis(start, code)
    for j in range(ITERS):
        vectors[j * EXT:(j + 1) * EXT] = v[j]
    own_lane = lane[:COLS]
    summed = (own_lane >= LANE_F - COLS) & (own_lane < LANE_F)
    blocks = [[jnp.where(summed, q[COLS:2 * COLS], 0.0)] for q in v]
    sums = lane_sums(gram_rows(blocks), LANE_F - COLS, LANE_F)
    high, low = pair_norm(pair_add(sums, (partial[:COLS], partial[COLS:])))
    size = GROUPS * COLS
    row = jnp.where(iota((COLS, LANES), 1) < size, high, roll(low, size, 1))
    gram[...] = jnp.broadcast_to(row[:1], gram.shape)


def coefficients(gram):
    shape = (COLS, LANES)
    tiles = [gram[i * COLS:(i + 1) * COLS] for i in range(gram.shape[0] // COLS)]
    total = pair_norm(pair_rows(pair_tree([(t, roll(t, -GROUPS * COLS, 1)) for t in tiles])))
    wide = lambda column: jnp.broadcast_to(column, shape)
    sub = iota(shape, 0)
    zero = jnp.zeros(shape, f32)

    spread = {}
    for i in range(BASIS):
        for j in range(i, BASIS):
            at = i * (2 * BASIS - 1 - i) // 2 + j
            spread[i, j] = spread[j, i] = tuple(wide(part[:, at:at + 1]) for part in total)

    def column(j):
        result = (zero, zero)
        for i in range(BASIS):
            result = tuple(jnp.where(sub == i, a, b) for a, b in zip(spread[i, j], result))
        return result

    matrix = [column(j) for j in range(BASIS)]
    half = scale / 2

    def times_power(pair, factor):
        return tuple(factor * part for part in pair)

    def shifted(pair):
        return pair_add(times_power(pair, shift - 1.0), pair)

    def apply(b):
        up = [half * jnp.where(sub == 0, 0.0, roll(part, 1, 0)) for part in b]
        up = tuple(jnp.where(sub == 1, 2.0 * part, part) for part in up)
        down = tuple(half * jnp.where(sub == COLS - 1, 0.0, roll(part, -1, 0)) for part in b)
        return pair_add(shifted(b), pair_add(up, down))

    images = [pair_add(shifted(matrix[0]), times_power(matrix[1], scale))]
    for j in range(1, ITERS):
        sides = pair_add(matrix[j - 1], matrix[j + 1])
        images.append(pair_add(shifted(matrix[j]), times_power(sides, half)))

    def image_of(vector, count):
        terms = []
        for j in range(count):
            at = tuple(wide(part[j:j + 1]) for part in vector)
            terms.append(pair_mul(images[j], at))
        return pair_tree(terms)

    def dot(a, b):
        return pair_rows(pair_mul(a, b))

    residual = ((sub == 0).astype(f32), zero)
    direction = residual
    solution = zero
    norm_now = tuple(wide(part[:1]) for part in matrix[0])
    floor = 1e-13 * norm_now[0]
    alive = norm_now[0] > 0
    for iteration in range(ITERS):
        applied = apply(direction)
        if iteration == 0:
            image = images[0]
            curvature = tuple(wide(part[:1]) for part in image)
        else:
            image = image_of(direction, iteration + 1)
            curvature = dot(direction, image)
        size = curvature[0] + curvature[1]
        alive = alive & (size > 0)
        step = jnp.where(alive, (norm_now[0] + norm_now[1]) / jnp.where(alive, size, 1.0), 0.0)
        solution = solution + step * direction[0]
        if iteration + 1 < ITERS:
            crossed = curvature if iteration == 0 else dot(residual, image)
            squared = dot(applied, image)
            change = pair_add(
                pair_scale(squared, step), times_power(crossed, -2.0)
            )
            norm_next = pair_norm(pair_add(norm_now, pair_scale(pair_norm(change), step)))
            residual = pair_norm(pair_add(residual, pair_scale(applied, -step)))
            ratio = jnp.where(alive, norm_next[0] / jnp.where(alive, norm_now[0], 1.0), 0.0)
            direction = pair_norm(pair_add(residual, pair_scale(direction, ratio)))
            norm_now = norm_next
            alive = alive & (norm_now[0] > floor)
    return solution


def slope_kernel(vectors, vectors_last, parts):
    near = iota((COLS, LANES), 1) >= CUT - (NY - LANES)

    def finished(value, from_window):
        value = value[COLS:2 * COLS]
        moved = roll(from_window[COLS:2 * COLS], COLS, 1)
        last = jnp.where(near, moved, value[:, NY - LANES:])
        return jnp.concatenate([value[:, :NY - LANES], last], axis=1)

    for j in range(ITERS):
        at = slice(j * EXT, (j + 1) * EXT)
        total, window = vectors[at], vectors_last[at]
        row = 3 * j * COLS
        parts[row:row + COLS] = finished(total, window)
        for axis in (0, 1):
            row += COLS
            parts[row:row + COLS] = gravity * finished(
                roll(total, -1, axis) - total, roll(window, -1, axis) - window
            )


def finish_kernel(gram, parts, zonal, meridional, levels, zonal_next, meridional_next, height):
    solution_rows = coefficients(gram)
    x = [
        jnp.concatenate(
            [jnp.broadcast_to(solution_rows[j:j + 1], (COLS, LANES))] * (NY // LANES), axis=1
        )
        for j in range(ITERS)
    ]

    def combine(which):
        rows = [(3 * j + which) * COLS for j in range(ITERS)]
        terms = [x[j] * parts[row:row + COLS] for j, row in enumerate(rows)]
        pairs = [sum(terms[j + 1:j + 2], terms[j]) for j in range(0, ITERS, 2)]
        return sum(pairs[1:], pairs[0])

    height[...] = combine(0)
    east, north = combine(1), combine(2)
    lc = levels[...]
    for k in range(K):
        zonal_next[k] = zonal[k] - jnp.where(lc > k, east, 0.0)
        meridional_next[k] = meridional[k] - jnp.where(lc > k, north, 0.0)


def neighbours(count, sibling, beyond, one, two):
    shape = (COLS, NY)
    even = is_even()
    row, lane = iota(shape, 0), iota(shape, 1)
    lc = count[...].astype(f32)
    mirror = patch_order(one[...], two[...], one[...])[0]
    north_tile = jnp.where(even, mirror[:COLS], mirror[COLS:])

    def around(field, west, east, north):
        return (
            jnp.where(row == COLS - 1, east, roll(field, -1, 0)),
            jnp.where(row == 0, west, roll(field, 1, 0)),
            jnp.where(lane == NY - 1, north, roll(field, -1, 1)),
            jnp.where(lane == 0, 0.0, roll(field, 1, 1)),
        )

    def sides(a, b):
        return jnp.where(even, b, a), jnp.where(even, a, b)

    def edges(at):
        return sides(sibling[at:at + 1], beyond[at:at + 1])

    def padded(field, base, k, sign):
        at = LANE_MT + base * K + k
        return around(field, *edges(2 * COLS + base * K + k), sign * north_tile[:, at:at + 1])

    beyond_lc = jnp.where(even, beyond[0:1], beyond[COLS - 1:COLS])
    west_lc, east_lc = sides(sibling[64:65], beyond_lc)
    north_lc = north_tile[:, LANE_LC:LANE_LC + 1]

    def mask_sum(mask, k):
        inside = [(c > k).astype(f32) for c in (west_lc, east_lc, north_lc)]
        return sum(around(mask, *inside))

    return lc, padded, mask_sum


def tracer_kernel(
    tracer, zonal, meridional, count, diffusivity, sibling, beyond, one, two, tracer_next
):
    lc, padded, mask_sum = neighbours(count, sibling, beyond, one, two)
    diff = diffusivity[...]

    def masked(k):
        if k < 0 or k >= K:
            return jnp.zeros_like(lc), jnp.zeros_like(lc)
        mask = (lc > k).astype(f32)
        return mask, mask * tracer[k]

    below, here = masked(-1), masked(0)
    for k in range(K):
        above = masked(k + 1)
        mask, mt = here
        t, u, v = tracer[k], zonal[k], meridional[k]
        te, tw, tn, ts = padded(mt, 0, k, 1.0)
        vertical = above[1] + below[1] - (above[0] + below[0]) * t
        tracer_next[k] = mask * (
            t
            + diff * (te + tw + tn + ts - mask_sum(mask, k) * t)
            + vertical_mix * vertical
            - advection * (u * (te - tw) + v * (tn - ts))
        )
        below, here = here, above


def flow_kernel(
    zonal, meridional, count, diffusivity, sibling, beyond, one, two,
    zonal_step, meridional_step, levels,
):
    lc, padded, mask_sum = neighbours(count, sibling, beyond, one, two)
    diff = diffusivity[...]
    turn = planetary(lc.shape)
    levels[...] = lc
    for k in range(K):
        mask = (lc > k).astype(f32)
        u, v = zonal[k], meridional[k]
        sides = mask_sum(mask, k)
        zonal_sum = sum(padded(mask * u, 1, k, -1.0))
        meridional_sum = sum(padded(mask * v, 2, k, -1.0))
        zonal_step[k] = mask * (u + diff * (zonal_sum - sides * u) + turn * v)
        meridional_step[k] = mask * (v + diff * (meridional_sum - sides * v) - turn * u)


def call(kernel, shapes, *args, flops=0, scratch=(), stay=0):
    moved = 4 * sum(a.size for a in args) + 4 * sum(
        functools.reduce(lambda x, y: x * y, s, 1) for s in shapes
    )
    space = pl.BlockSpec(memory_space=pltpu.VMEM)
    in_specs = [space] * (len(args) - stay) + [pl.BlockSpec(memory_space=pltpu.HBM)] * stay
    here = len(args) - stay
    args = args[:here] + tuple(
        pltpu.with_memory_space_constraint(a, pltpu.HBM) for a in args[here:]
    )
    return pl.pallas_call(
        kernel,
        out_shape=[jax.ShapeDtypeStruct(s, f32) for s in shapes],
        in_specs=in_specs,
        out_specs=[space] * len(shapes),
        scratch_shapes=list(scratch),
        compiler_params=pltpu.CompilerParams(vmem_limit_bytes=32 * 1024 * 1024),
        cost_estimate=pl.CostEstimate(flops=flops, bytes_accessed=moved, transcendentals=0),
    )(*args)


def body(tracer, zonal, meridional, count, diffusivity, surface):
    size = lax.axis_size("lon")
    block = (K, COLS, NY)

    def permute(value, pairs):
        return lax.ppermute(value, "lon", pairs)

    siblings = [(i, i ^ 1) for i in range(size)]
    outward = [(i, (i + 1 if i % 2 else i - 1) % size) for i in range(size)]
    first = {i: size - 1 - i for i in range(size)}
    second = {(size + 1 - 4 * (i % 2) - i) % size: i for i in range(size)}
    for i in range(1, size // 2, 2):
        first[i], second[i] = second[i], first[i]
    first[1], second[size // 2 + 1] = size // 2, 0
    arguments = (tracer, zonal, meridional, count, diffusivity, surface)
    inner, outer = call(
        pack_kernel, [(80, NY), (64, NY)], *arguments,
        scratch=[pltpu.VMEM((K, COLS, LANES), f32)]
        + [pltpu.VMEM(a.shape, a.dtype) for a in arguments[1:]]
        + [pltpu.VMEM((6, K, NY), f32), pltpu.SemaphoreType.DMA((9 + 3 * CHUNKS,))], stay=len(arguments),
    )
    beyond = permute(outer, outward)
    sibling = permute(inner, siblings)
    patch = (2 * COLS, LANES)
    tile, near, one, two = call(chip_kernel, [patch] * 4, inner, sibling)
    one = permute(one, sorted(first.items()))
    two = permute(two, sorted(second.items()))
    window = (EXT, LANES)
    last, last_code, vectors, partial, ours = call(
        inner_kernel,
        [
            window, window, (ITERS * EXT, NY), (2 * COLS, LANES), (2 * EXT, LANES),
        ],
        inner, outer, sibling, beyond, tile, flops=8192 * 100,
    )
    vectors_last, gram = call(
        fold_kernel,
        [(ITERS * EXT, LANES), (size, LANES)],
        last, last_code, ours, one, two, near, partial,
    )
    halos = (sibling, beyond, one, two)
    tracer_next, = call(
        tracer_kernel, [block],
        tracer, zonal, meridional, count, diffusivity, *halos,
        flops=65536 * 40,
    )
    zonal_step, meridional_step, levels = call(
        flow_kernel, [block, block, (COLS, NY)],
        zonal, meridional, count, diffusivity, *halos,
        flops=65536 * 40,
    )
    group = [(5 * i + size // 2 - 1) % size for i in range(size)]
    gram = lax.all_to_all(gram, "lon", 0, 0, tiled=True, axis_index_groups=[group])
    parts, = call(slope_kernel, [(3 * ITERS * COLS, NY)], vectors, vectors_last, flops=8192 * 20)
    zonal_next, meridional_next, height = call(
        finish_kernel, [block, block, (COLS, NY)],
        gram, parts, zonal_step, meridional_step, levels,
    )
    return tracer_next, zonal_next, meridional_next, height


def solution(mesh):
    column = P("lon", None)
    field = P("ens", "lon", None)
    return jax.shard_map(
        body,
        mesh=mesh,
        in_specs=(field, field, field, column, column, column),
        out_specs=(field, field, field, P("lon", "ens")),
        check_vma=False,
    )
```
